32 devices in a mesh: dp: 8 (over z, y), seq: 4 (over x, core).
Axes of the slice: x: 2, y: 2, z: 4, core: 2. Of those that a mesh axis runs over, the one named last changes fastest.
Arguments:
- tokens: bfloat16 [16, 1024, 1536], P('dp', 'seq'), may hold values from -8 to 8
- segment_ids: int32 [16, 1024], P('dp'), may hold values from 0 to 32, as said below
- w_in: bfloat16 [1536, 6448], P('dp'), may hold values from -0.15625 to 0.15625
- w_out: bfloat16 [3072, 1536], P('dp'), may hold values from -0.109375 to 0.109375
- conv_weight: bfloat16 [3328, 4], P('dp'), may hold values from -3 to 3
- conv_bias: bfloat16 [3328], P('dp'), may hold values from -1.75 to 1.75
- norm_gain: bfloat16 [1536], P('dp'), may hold values from 0.5 to 1.5
- gated_gain: bfloat16 [3072], P('dp'), may hold values from 0.5 to 1.5
- dt_bias: float32 [48], replicated, may hold values from -7 to -2.5
- a_log: float32 [48], replicated, may hold values from 0 to 2.77
- skip_weight: float32 [48], replicated, may hold values from 0.5 to 1.5
- cotangent: bfloat16 [16, 1024, 1536], P('dp', 'seq'), may hold values from -6 to 6
Outputs:
- out: bfloat16 [16, 1024, 1536], P('dp', 'seq')
- tokens_grad: float32 [16, 1024, 1536], P('dp', 'seq')
- w_in_grad: float32 [1536, 6448], P('dp')
- w_out_grad: float32 [3072, 1536], P('dp')
- conv_weight_grad: float32 [3328, 4], P('dp')
- conv_bias_grad: float32 [3328], P('dp')
- norm_gain_grad: float32 [1536], P('dp')
- gated_gain_grad: float32 [3072], P('dp')
- dt_bias_grad: float32 [48], replicated
- a_log_grad: float32 [48], replicated
- skip_weight_grad: float32 [48], replicated
The draws below stay inside these ranges and needn't reach their ends.
Inputs may be any that keep to these rules, and one draw needn't show every extreme that they name: `segment_ids`: each row starts at 0 and rises by 0 or 1 from one token to the next; in each aligned group of 2 rows one row, which one varies, is a single document.
All inputs are finite; a program needn't handle non-finite values.
Results may differ from the reference program's by a relative error of at most 0.015.
Values may be sent and summed in bfloat16 or wider, within the bound.
A program may use at most 256 MiB of HBM per device.

```python
from functools import partial
import jax
import jax.numpy as jnp
from jax import lax

D = 1536
H = 48
P_SIZE = 64
N = 128
CONV = 4
SPAN = 256
SEQS_DEV = 2
DI = 3072
E = 6448
CH = 3328
LEN = 1024
BATCH = 16


def draw_segment_ids(key, part):
    key = jax.random.fold_in(key, 17)
    rate_key, cut_key, pick_key = jax.random.split(key, 3)
    shifts = jax.random.randint(rate_key, (BATCH, 1), 2, 9)
    limits = jnp.left_shift(jnp.ones((BATCH, 1), jnp.int32), shifts)
    cuts = jax.random.randint(cut_key, (BATCH, LEN), 0, limits)
    starts = (cuts == 0).astype(jnp.int32)
    picked = jax.random.randint(pick_key, (BATCH // SEQS_DEV,), 0, SEQS_DEV)
    row_ids = jnp.arange(BATCH, dtype=jnp.int32)
    whole = row_ids % SEQS_DEV == jnp.repeat(picked, SEQS_DEV)
    places = jnp.arange(LEN, dtype=jnp.int32)[None, :]
    ceiling = LEN // 32
    forced = (row_ids == (picked[0] + 1) % SEQS_DEV) & jnp.logical_not(whole)
    starts = jnp.where(forced[:, None] & (places >= 1) & (places <= ceiling), 1, starts)
    starts = jnp.where(whole[:, None] | (places == 0), 0, starts)
    return jnp.minimum(jnp.cumsum(starts, axis=1), ceiling).astype(jnp.int32)


def spiked(drawn, key, source, target, blocks, factor):
    def block_of(dim):
        return (jnp.arange(drawn.shape[dim]) // (drawn.shape[dim] // blocks)).reshape((-1,) + (1,) * (drawn.ndim - 1 - dim))

    one_side = jax.random.permutation(key, blocks)[block_of(target)]
    far = (block_of(target) + blocks // 2) % blocks
    return jnp.where((block_of(source) == one_side) | (block_of(source) == far), factor * drawn, drawn)


def shard_levels(rng, dims, cuts, low, high):
    level = 1.0
    for position, blocks in cuts:
        steps = jax.random.uniform(jax.random.fold_in(jax.random.fold_in(rng, 6), position), (blocks,), jnp.float32, low / len(cuts), high / len(cuts))
        level = level * jnp.repeat(jnp.exp(steps), dims[position] // blocks).reshape((-1,) + (1,) * (len(dims) - 1 - position))
    return level


def centred(stream_key, extent, scale, most, cuts=(), held_as=jnp.bfloat16):
    drawn = scale * jax.random.normal(stream_key, extent, jnp.float32)
    if cuts:
        drawn = drawn * shard_levels(stream_key, extent, cuts, -0.22, 0.18)
    return jnp.clip(drawn, -most, most).astype(held_as)


def bell_draw_with(stream_key, dims, deviation, bound, cuts, heavy, kind=jnp.bfloat16):
    values = deviation * jax.random.normal(stream_key, dims, jnp.float32)
    if cuts:
        values = values * shard_levels(stream_key, dims, cuts, -0.22, 0.18)
    return jnp.clip(spiked(values, jax.random.fold_in(stream_key, 3), *heavy), -bound, bound).astype(kind)


def setup_inputs(seed: int = 0) -> dict:
    splits = jax.random.split(jax.random.key(seed), 13)
    tokens = bell_draw_with(splits[0], (BATCH, LEN, D), 1.0, 8.0, ((0, 8), (1, 4)), (0, 2, 8, 2.0))
    segment_ids = draw_segment_ids(jax.random.fold_in(splits[12], 71), 0)
    w_in = centred(splits[2], (D, E), D ** -0.5, 0.15625, ((0, 8),))
    w_out = centred(splits[3], (DI, D), DI ** -0.5, 0.109375, ((0, 8),))
    conv_weight = centred(splits[4], (CH, CONV), CONV ** -0.5, 3.0, ((0, 8),))
    conv_bias = centred(splits[5], (CH,), 0.3, 1.75, ((0, 8),))
    norm_gain = jnp.clip(1.0 + 0.1 * jax.random.normal(splits[6], (D,), jnp.float32), 0.5, 1.5).astype(jnp.bfloat16)
    gated_gain = jnp.clip(1.0 + 0.1 * jax.random.normal(splits[7], (DI,), jnp.float32), 0.5, 1.5).astype(jnp.bfloat16)
    dt_bias = jnp.clip(jax.random.uniform(splits[8], (H,), jnp.float32, -7.0, -2.5), -7.0, -2.5)
    a_log = jnp.clip(jax.random.uniform(splits[9], (H,), jnp.float32, 0.0, 2.77), 0.0, 2.77)
    skip_weight = jnp.clip(jax.random.uniform(splits[10], (H,), jnp.float32, 0.5, 1.5), 0.5, 1.5)
    cotangent = centred(splits[11], (BATCH, LEN, D), 1.0, 6.0, ((0, 8), (1, 4)))
    return dict(tokens=tokens, segment_ids=segment_ids, w_in=w_in, w_out=w_out, conv_weight=conv_weight, conv_bias=conv_bias, norm_gain=norm_gain, gated_gain=gated_gain, dt_bias=dt_bias, a_log=a_log, skip_weight=skip_weight, cotangent=cotangent)


EPSILON = 1e-05
PRECISE = lax.Precision.HIGHEST

@jax.custom_vjp
def low(v):
    return lax.optimization_barrier(v.astype(jnp.bfloat16)).astype(jnp.float32)

@jax.custom_vjp
def low_back(v):
    return v

def low_keep(v):
    return (low(v), None)

def low_pass(kept, grad):
    return (grad,)

def back_keep(v):
    return (v, None)

def back_low(kept, grad):
    return (low(grad),)
low.defvjp(low_keep, low_pass)
low_back.defvjp(back_keep, back_low)

def conv_reset(inputs, kernel, offsets, segment):
    length = inputs.shape[0]
    tap_count = kernel.shape[1]
    summed = inputs * kernel[:, tap_count - 1] + offsets
    for distance in range(1, tap_count):
        earlier = jnp.pad(inputs, ((distance, 0), (0, 0)))[:length]
        earlier_seg = jnp.pad(segment, (distance, 0), constant_values=-1)[:length]
        keeper = (earlier_seg == segment).astype(jnp.float32)
        summed = summed + earlier * keeper[:, None] * kernel[:, tap_count - 1 - distance]
    return jax.nn.silu(summed)

def span_step(decay_rate, carried_in, pieces):
    memory, seg_before = carried_in
    values, b_block, c_block, deltas, seg_block = pieces
    width_q = seg_block.shape[0]
    log_decay = jnp.cumsum(deltas * decay_rate, axis=0)
    row_ids = lax.broadcasted_iota(jnp.int32, (width_q, width_q), 0)
    col_ids = lax.broadcasted_iota(jnp.int32, (width_q, width_q), 1)
    linked = (row_ids >= col_ids) & (seg_block[:, None] == seg_block[None, :])
    spread = jnp.where(linked[:, :, None], log_decay[:, None, :] - log_decay[None, :, :], -jnp.inf)
    scores = jnp.dot(c_block, b_block.T, precision=PRECISE)
    weights = jnp.exp(spread) * scores[:, :, None]
    driven = values * deltas[:, :, None]
    within = jnp.einsum('ijh,jhp->ihp', weights, driven, precision=PRECISE)
    entering = (seg_block == seg_before).astype(jnp.float32)
    carried = jnp.einsum('in,hpn->ihp', c_block, memory, precision=PRECISE) * (jnp.exp(log_decay) * entering[:, None])[:, :, None]
    seg_final = seg_block[width_q - 1]
    leaving = jnp.exp(jnp.where((seg_block == seg_final)[:, None], log_decay[width_q - 1][None, :] - log_decay, -jnp.inf))
    kept_share = jnp.exp(log_decay[width_q - 1]) * (seg_final == seg_before).astype(jnp.float32)
    memory = memory * kept_share[:, None, None] + jnp.einsum('jhp,jn->hpn', driven * leaving[:, :, None], b_block, precision=PRECISE)
    return ((memory, seg_final), within + carried)

def ssd_scan(values, b_rows, c_rows, deltas, decay_rate, segment):
    length, head_count, head_size = values.shape
    state_size = b_rows.shape[1]
    span_count = length // SPAN
    pieces = (values.reshape(span_count, SPAN, head_count, head_size), b_rows.reshape(span_count, SPAN, state_size), c_rows.reshape(span_count, SPAN, state_size), deltas.reshape(span_count, SPAN, head_count), segment.reshape(span_count, SPAN))
    initial = (jnp.zeros((head_count, head_size, state_size), jnp.float32), jnp.array(-1, jnp.int32))
    final_state, outputs = lax.scan(jax.checkpoint(partial(span_step, decay_rate)), initial, pieces)
    return outputs.reshape(length, head_count, head_size)

def mixer(gate_in, conv_in, dt_raw, bc_raw, segment, x_kernel, x_offsets, bc_kernel, bc_offsets, dt_bias, a_log, skip_weight):
    length, head_count, head_size = conv_in.shape
    values = conv_reset(conv_in.reshape(length, head_count * head_size), x_kernel, x_offsets, segment).reshape(length, head_count, head_size)
    bc_rows = conv_reset(bc_raw, bc_kernel, bc_offsets, segment)
    state_size = bc_rows.shape[1] // 2
    deltas = jax.nn.softplus(dt_raw + dt_bias)
    decay_rate = -jnp.exp(a_log)
    gated_out = ssd_scan(values, bc_rows[:, :state_size], bc_rows[:, state_size:], deltas, decay_rate, segment) + skip_weight[:, None] * values
    return gated_out * jax.nn.silu(gate_in)

def block_row(weights, row_tokens, row_segment):
    w_in, w_out, conv_weight, conv_bias, norm_gain, gated_gain, dt_bias, a_log, skip_weight = weights
    square = lax.optimization_barrier(jnp.mean(row_tokens * row_tokens, axis=-1, keepdims=True))
    normed = low(row_tokens * lax.rsqrt(square + EPSILON) * norm_gain)
    projected = low_back(low(jnp.dot(normed, w_in, precision=PRECISE)))
    length = row_tokens.shape[0]
    head_cols = projected[:, :2 * DI].reshape(length, H, 2 * P_SIZE)
    bc_raw = projected[:, 2 * DI:2 * DI + 2 * N]
    dt_raw = projected[:, 2 * DI + 2 * N:]
    gated = mixer(head_cols[:, :, :P_SIZE], head_cols[:, :, P_SIZE:], dt_raw, bc_raw, row_segment, conv_weight[:DI], conv_bias[:DI], conv_weight[DI:], conv_bias[DI:], dt_bias, a_log, skip_weight)
    flattened = gated.reshape(length, DI)
    gated_mean = lax.optimization_barrier(jnp.mean(flattened * flattened, axis=-1, keepdims=True))
    scaled = low_back(low(flattened * lax.rsqrt(gated_mean + EPSILON) * gated_gain))
    return row_tokens + jnp.dot(scaled, w_out, precision=PRECISE)

def reference(tokens, segment_ids, w_in, w_out, conv_weight, conv_bias, norm_gain, gated_gain, dt_bias, a_log, skip_weight, cotangent):
    inputs = tokens.astype(jnp.float32)
    weights = tuple((source.astype(jnp.float32) for source in (w_in, w_out, conv_weight, conv_bias, norm_gain, gated_gain, dt_bias, a_log, skip_weight)))
    checked = jax.checkpoint(block_row)

    def forward(token_rows, weight_set):

        def one_row(row_pair):
            return checked(weight_set, row_pair[0], row_pair[1])
        return lax.map(one_row, (token_rows, segment_ids))
    result, pullback = jax.vjp(forward, inputs, weights)
    input_grad, weight_grads = pullback(cotangent.astype(jnp.float32))
    return (result.astype(jnp.bfloat16), input_grad, weight_grads[0], weight_grads[1], weight_grads[2], weight_grads[3], weight_grads[4], weight_grads[5], weight_grads[6], weight_grads[7], weight_grads[8])
```

```python
import functools

import jax
import jax.numpy as jnp
from jax import lax
from jax.experimental import pallas as pl
from jax.experimental.pallas import tpu as pltpu
from jax.sharding import PartitionSpec as P

Q = 128
EXACT = lax.Precision.HIGHEST
EPSILON = 1e-05
LOG2E = 1.4426950408889634
RESET = 160.0
F32 = jnp.float32
BF16 = jnp.bfloat16


def sigmoid(x):
    return 0.5 * jnp.tanh(0.5 * x) + 0.5


def softplus(x):
    return jnp.maximum(x, 0.0) + jnp.log1p(jnp.exp(-jnp.abs(x)))


def nt(a, b):
    return lax.dot_general(a, b, (((1,), (1,)), ((), ())), preferred_element_type=F32)


def mm(a, b):
    return jnp.dot(a, b, preferred_element_type=F32)


def decays(pj, cols, hp, width):
    arg = pj[0, :, width + 256 : width + 384].astype(F32) + hp[0:1, :]
    dt = softplus(arg)
    rows = lax.broadcasted_iota(jnp.int32, (Q, Q), 0)
    lanes = lax.broadcasted_iota(jnp.int32, (Q, Q), 1)
    lower = (rows >= lanes).astype(F32)
    level = jnp.dot(lower, dt * hp[1:2, :], precision=EXACT, preferred_element_type=F32)
    level = level + cols[0, :, 3:4]
    return arg, dt, level, rows, lanes


def fwd_kernel(pairs, pj, cols, sg, hp, ch, pre, ys, gn, st, red, state, tail):
    width = pairs * 256
    inner = pairs * 128
    chunk = pl.program_id(1)

    @pl.when(chunk == 0)
    def _():
        state[...] = jnp.zeros_like(state)
        tail[...] = jnp.zeros_like(tail)

    _, dt, level, rows, lanes = decays(pj, cols, hp, width)
    level_t = level.T
    low = lanes < 64
    masks = [cols[0, :, d : d + 1] for d in range(3)]

    def conv(raw, at):
        ext = jnp.concatenate([tail[:, at : at + 128], raw], axis=0)
        total = raw * ch[3:4, at : at + 128] + ch[4:5, at : at + 128]
        for d in (1, 2, 3):
            moved = pltpu.roll(ext, d, 0)[8:]
            total = total + moved * masks[d - 1] * ch[3 - d : 4 - d, at : at + 128]
        tail[:, at : at + 128] = raw[Q - 8 :]
        pre[0, :, at : at + 128] = total
        return total * sigmoid(total)

    b_rows = conv(pj[0, :, width : width + 128].astype(F32), inner)
    c_rows = conv(pj[0, :, width + 128 : width + 256].astype(F32), inner + 128)
    b_t = b_rows.T.astype(BF16)
    b_low = b_rows.astype(BF16)
    c_low = c_rows.astype(BF16)
    scores = jnp.where(rows >= lanes, nt(c_low, b_low), 0.0)
    old = state[...].astype(BF16)
    st[0, 0] = old
    carried_all = mm(c_low, old)
    squares = jnp.zeros((Q, 128), F32)
    cross = jnp.zeros((Q, 128), F32)
    for p in range(pairs):
        at = p * 128
        one = pj[0, :, p * 256 : p * 256 + 128].astype(F32)
        two = pj[0, :, p * 256 + 128 : p * 256 + 256].astype(F32)
        z = jnp.where(low, one, pltpu.roll(two, 64, 1))
        v = jnp.where(low, pltpu.roll(one, 64, 1), two)
        xc = conv(v, at)
        l0 = jnp.broadcast_to(level[:, 2 * p : 2 * p + 1], (Q, Q))
        l1 = jnp.broadcast_to(level[:, 2 * p + 1 : 2 * p + 2], (Q, Q))
        le = jnp.where(low, l0, l1)
        dte = jnp.where(low, dt[:, 2 * p : 2 * p + 1], dt[:, 2 * p + 1 : 2 * p + 2])
        u = xc * dte
        w0 = jnp.exp2(jnp.minimum(l0 - level_t[2 * p : 2 * p + 1, :], 0.0)) * scores
        w1 = jnp.exp2(jnp.minimum(l1 - level_t[2 * p + 1 : 2 * p + 2, :], 0.0)) * scores
        wide = jnp.concatenate([w0.astype(BF16), w1.astype(BF16)], axis=1)
        blocks = jnp.concatenate(
            [jnp.where(low, u, 0.0).astype(BF16), jnp.where(low, 0.0, u).astype(BF16)], axis=0
        )
        part = mm(wide, blocks) + carried_all[:, at : at + 128] * jnp.exp2(le)
        ys[0, :, at : at + 128] = part
        gated = (part + ch[5:6, at : at + 128] * xc) * (z * sigmoid(z))
        scaled = gated * ch[6:7, at : at + 128]
        gn[0, :, at : at + 128] = scaled.astype(BF16)
        squares = squares + gated * gated
        cross = cross + sg[0, :, at : at + 128].astype(F32) * scaled
        last = le[Q - 1 : Q, :]
        ul = (u * jnp.exp2(last - le)).astype(BF16)
        state[:, at : at + 128] = state[:, at : at + 128] * jnp.exp2(last) + mm(b_t, ul)
    both = jnp.where(
        lanes == 0, jnp.sum(squares, axis=1, keepdims=True), jnp.sum(cross, axis=1, keepdims=True)
    )
    red[0] = both.T[0:8]


def mix_forward(pj, cols, sg, hp, ch, interpret=False):
    seqs, length, total = pj.shape
    width = total - 384
    inner = width // 2
    pairs = inner // 128
    chunks = length // Q

    def row(n):
        return pl.BlockSpec((1, Q, n), lambda s, c: (s, c, 0))

    def whole(a):
        return pl.BlockSpec(a.shape, lambda s, c: (0,) * a.ndim)

    return pl.pallas_call(
        functools.partial(fwd_kernel, pairs),
        grid=(seqs, chunks),
        in_specs=[row(total), row(128), row(inner), whole(hp), whole(ch)],
        out_specs=[
            row(inner + 256),
            row(inner),
            row(inner),
            pl.BlockSpec((1, 1, 128, inner), lambda s, c: (s, c, 0, 0)),
            pl.BlockSpec((1, 8, Q), lambda s, c: (s, 0, c)),
        ],
        out_shape=[
            jax.ShapeDtypeStruct((seqs, length, inner + 256), F32),
            jax.ShapeDtypeStruct((seqs, length, inner), F32),
            jax.ShapeDtypeStruct((seqs, length, inner), BF16),
            jax.ShapeDtypeStruct((seqs, chunks, 128, inner), BF16),
            jax.ShapeDtypeStruct((seqs, 8, length), F32),
        ],
        scratch_shapes=[pltpu.VMEM((128, inner), F32), pltpu.VMEM((8, inner + 256), F32)],
        compiler_params=pltpu.CompilerParams(vmem_limit_bytes=48 * 2**20),
        name="mix_forward",
    )(pj, cols, sg, hp, ch)


def bwd_kernel(
    pairs, pj, cols, cols2, sg, pre, ys, st, hp, ch, sel, pg, chacc, hacc,
    dstate, halo, edy_all, ul_all,
):
    width = pairs * 256
    inner = pairs * 128
    first = (pl.program_id(0) == 0) & (pl.program_id(1) == 0)

    @pl.when(pl.program_id(1) == 0)
    def _():
        dstate[...] = jnp.zeros_like(dstate)
        halo[...] = jnp.zeros_like(halo)

    @pl.when(first)
    def _():
        chacc[...] = jnp.zeros_like(chacc)
        hacc[...] = jnp.zeros_like(hacc)

    arg, dt, level, rows, lanes = decays(pj, cols, hp, width)
    level_t = level.T
    low = lanes < 64
    masks = [cols[0, :, 3 + d : 4 + d] for d in (1, 2, 3)]
    rho = jnp.broadcast_to(cols2[0, :, 0:1], (Q, 128))
    k2 = jnp.broadcast_to(cols2[0, :, 1:2], (Q, 128))

    def fold(x):
        return jnp.sum(x.reshape(Q // 8, 8, 128), axis=0)

    def conv_back(grad, raw, at):
        ext = jnp.concatenate([grad, halo[:, at : at + 128]], axis=0)
        out = grad * ch[3:4, at : at + 128]
        chacc[3, :, at : at + 128] += fold(grad * raw)
        chacc[4, :, at : at + 128] += fold(grad)
        for d in (1, 2, 3):
            moved = pltpu.roll(ext, Q + 8 - d, 0)[:Q] * masks[d - 1]
            out = out + moved * ch[3 - d : 4 - d, at : at + 128]
            chacc[3 - d, :, at : at + 128] += fold(moved * raw)
        halo[:, at : at + 128] = grad[:8]
        return out

    pre_b = pre[0, :, inner : inner + 128]
    pre_c = pre[0, :, inner + 128 : inner + 256]
    sig_b, sig_c = sigmoid(pre_b), sigmoid(pre_c)
    b_rows, c_rows = pre_b * sig_b, pre_c * sig_c
    b_low, c_low = b_rows.astype(BF16), c_rows.astype(BF16)
    c_t = c_rows.T.astype(BF16)
    upper = lanes >= rows
    scores = jnp.where(upper, nt(b_low, c_low), 0.0)
    dlow = dstate[...].astype(BF16)
    dsb_all = mm(b_low, dlow)
    dscores = jnp.zeros((Q, Q), F32)
    sums = jnp.zeros((6 * Q, 128), F32)
    keep = jnp.zeros((8, 128), F32)
    for p in range(pairs):
        at = p * 128
        one = pj[0, :, p * 256 : p * 256 + 128].astype(F32)
        two = pj[0, :, p * 256 + 128 : p * 256 + 256].astype(F32)
        z = jnp.where(low, one, pltpu.roll(two, 64, 1))
        v = jnp.where(low, pltpu.roll(one, 64, 1), two)
        pr = pre[0, :, at : at + 128]
        sp = sigmoid(pr)
        xc = pr * sp
        l0 = jnp.broadcast_to(level[:, 2 * p : 2 * p + 1], (Q, Q))
        l1 = jnp.broadcast_to(level[:, 2 * p + 1 : 2 * p + 2], (Q, Q))
        le = jnp.where(low, l0, l1)
        dte = jnp.where(low, dt[:, 2 * p : 2 * p + 1], dt[:, 2 * p + 1 : 2 * p + 2])
        u = xc * dte
        skip = ch[5:6, at : at + 128]
        part = ys[0, :, at : at + 128]
        y = part + skip * xc
        sz = sigmoid(z)
        silz = z * sz
        gated = y * silz
        graw = sg[0, :, at : at + 128].astype(F32)
        scaled_rho = graw * rho
        chacc[5, :, at : at + 128] += fold(scaled_rho * gated)
        gg = scaled_rho * ch[6:7, at : at + 128] - k2 * gated
        dy = gg * silz
        dz = gg * y * (sz + silz * (1.0 - sz))
        ulow = u.astype(BF16)
        dylow = dy.astype(BF16)
        w0 = jnp.exp2(jnp.minimum(level_t[2 * p : 2 * p + 1, :] - l0, 0.0))
        w1 = jnp.exp2(jnp.minimum(level_t[2 * p + 1 : 2 * p + 2, :] - l1, 0.0))
        wide = jnp.concatenate([(w0 * scores).astype(BF16), (w1 * scores).astype(BF16)], axis=1)
        dyb = jnp.concatenate(
            [jnp.where(low, dy, 0.0).astype(BF16), jnp.where(low, 0.0, dy).astype(BF16)], axis=0
        )
        ub = jnp.concatenate(
            [jnp.where(low, u, 0.0).astype(BF16), jnp.where(low, 0.0, u).astype(BF16)], axis=0
        )
        duw = mm(wide, dyb)
        gt = nt(ub, dylow)
        dscores = dscores + w0 * gt[:Q] + w1 * gt[Q:]
        last = le[Q - 1 : Q, :]
        lve = jnp.exp2(last - le)
        edy = (dy * jnp.exp2(le)).astype(BF16)
        ul = (u * lve).astype(BF16)
        edy_all[:, at : at + 128] = edy
        ul_all[:, at : at + 128] = ul
        dsb = dsb_all[:, at : at + 128]
        du = duw + lve * dsb
        r1 = dylow.astype(F32) * part - ulow.astype(F32) * duw
        r2 = ul.astype(F32) * dsb
        r1h, r2h = r1.astype(BF16), r2.astype(BF16)
        stacked = jnp.concatenate(
            [
                r1h,
                (r1 - r1h.astype(F32)).astype(BF16),
                r2h,
                (r2 - r2h.astype(F32)).astype(BF16),
                (dy * xc).astype(BF16),
                (du * xc).astype(BF16),
            ],
            axis=0,
        )
        sums = sums + mm(stacked, sel[p])
        decay = jnp.exp2(last)
        kept = fold(dlow[:, at : at + 128].astype(F32) * st[0, 0, :, at : at + 128].astype(F32)) * decay
        kept_high = kept.astype(BF16)
        keep = keep + mm(kept_high, sel[p]) + mm((kept - kept_high.astype(F32)).astype(BF16), sel[p])
        dstate[:, at : at + 128] = dstate[:, at : at + 128] * decay + mm(c_t, edy)
        dv = conv_back((du * dte + skip * dy) * (sp + xc * (1.0 - sp)), v, at)
        pg[0, :, p * 256 : p * 256 + 128] = jnp.where(low, dz, pltpu.roll(dv, 64, 1)).astype(BF16)
        pg[0, :, p * 256 + 128 : p * 256 + 256] = jnp.where(low, pltpu.roll(dz, 64, 1), dv).astype(BF16)
    dsc = jnp.where(upper, dscores, 0.0)
    db = mm(dsc.astype(BF16), c_low) + nt(ul_all[...], dlow)
    dc = mm(dsc.T.astype(BF16), b_low) + nt(edy_all[...], st[0, 0])
    raw_b = pj[0, :, width : width + 128].astype(F32)
    raw_c = pj[0, :, width + 128 : width + 256].astype(F32)
    pg[0, :, width : width + 128] = conv_back(
        db * (sig_b + b_rows * (1.0 - sig_b)), raw_b, inner
    ).astype(BF16)
    pg[0, :, width + 128 : width + 256] = conv_back(
        dc * (sig_c + c_rows * (1.0 - sig_c)), raw_c, inner + 128
    ).astype(BF16)
    r1 = sums[:Q] + sums[Q : 2 * Q]
    r2 = sums[2 * Q : 3 * Q] + sums[3 * Q : 4 * Q]
    da = (
        jnp.dot(upper.astype(F32), r1, precision=EXACT, preferred_element_type=F32)
        + jnp.dot((rows > lanes).astype(F32), r2, precision=EXACT, preferred_element_type=F32)
        + jnp.sum(keep, axis=0, keepdims=True)
    )
    ddt = da * hp[2:3, :] + sums[5 * Q :]
    ds = ddt * sigmoid(arg)
    pg[0, :, width + 256 : width + 384] = ds.astype(BF16)
    hacc[0] += fold(ds)
    hacc[1] += fold(da * dt)
    hacc[2] += fold(sums[4 * Q : 5 * Q])


def mix_backward(pj, cols, cols2, sg, pre, ys, st, hp, ch, sel):
    seqs, length, total = pj.shape
    width = total - 384
    inner = width // 2
    pairs = inner // 128
    chunks = length // Q

    def row(n):
        return pl.BlockSpec((1, Q, n), lambda s, c: (s, chunks - 1 - c, 0))

    def whole(shape):
        return pl.BlockSpec(shape, lambda s, c: (0,) * len(shape))

    return pl.pallas_call(
        functools.partial(bwd_kernel, pairs),
        grid=(seqs, chunks),
        in_specs=[
            row(total),
            row(128),
            row(128),
            row(inner),
            row(inner + 256),
            row(inner),
            pl.BlockSpec((1, 1, 128, inner), lambda s, c: (s, chunks - 1 - c, 0, 0)),
            whole(hp.shape),
            whole(ch.shape),
            whole(sel.shape),
        ],
        out_specs=[row(total), whole((6, 8, inner + 256)), whole((3, 8, 128))],
        out_shape=[
            jax.ShapeDtypeStruct((seqs, length, total), BF16),
            jax.ShapeDtypeStruct((6, 8, inner + 256), F32),
            jax.ShapeDtypeStruct((3, 8, 128), F32),
        ],
        scratch_shapes=[
            pltpu.VMEM((128, inner), F32),
            pltpu.VMEM((8, inner + 256), F32),
            pltpu.VMEM((Q, inner), BF16),
            pltpu.VMEM((Q, inner), BF16),
        ],
        compiler_params=pltpu.CompilerParams(vmem_limit_bytes=48 * 2**20),
        name="mix_backward",
    )(pj, cols, cols2, sg, pre, ys, st, hp, ch, sel)


def columns(seg):
    seqs, length = seg.shape
    back = [
        jnp.pad((seg[:, d:] == seg[:, :-d]).astype(F32), ((0, 0), (d, 0))) for d in (1, 2, 3)
    ]
    ahead = [
        jnp.pad((seg[:, d:] == seg[:, :-d]).astype(F32), ((0, 0), (0, d))) for d in (1, 2, 3)
    ]
    ends = seg.reshape(seqs, length // Q, Q)[:, :, -1]
    before = jnp.pad(ends[:, :-1], ((0, 0), (1, 0)))
    level = -RESET * (seg.reshape(seqs, length // Q, Q) - before[:, :, None]).astype(F32)
    stacked = jnp.stack([*back, level.reshape(seqs, length), *ahead], axis=-1)
    return jnp.pad(stacked, ((0, 0), (0, 0), (0, 121)))


def selectors(pairs):
    lane = lax.broadcasted_iota(jnp.int32, (pairs, 128, 128), 1)
    pair = lax.broadcasted_iota(jnp.int32, (pairs, 128, 128), 0)
    out = lax.broadcasted_iota(jnp.int32, (pairs, 128, 128), 2)
    return (out == 2 * pair + lane // 64).astype(BF16)


def local(
    tokens,
    segment_ids,
    w_in,
    w_out,
    conv_weight,
    conv_bias,
    norm_gain,
    gated_gain,
    dt_bias,
    a_log,
    skip_weight,
    cotangent,
):
    groups = lax.axis_size("seq")
    shards = lax.axis_size("dp")
    place = lax.axis_index("seq")
    owner = lax.axis_index("dp")
    seqs, part, model = tokens.shape
    length = part * groups
    rows_out = w_out.shape[0]
    wide = rows_out * shards
    heads = dt_bias.shape[0]
    size = wide // heads
    mine = heads // groups
    inner = mine * size
    span = 2 * inner
    taps = conv_weight.shape[1]
    state2 = w_in.shape[1] - 2 * wide - heads
    channels = wide + state2
    share = channels // shards
    small = jnp.concatenate(
        [conv_weight.reshape(-1), conv_bias, norm_gain, gated_gain]
    ).astype(F32)
    small = lax.all_gather(small, "dp", axis=0, tiled=False)
    cuts = [share * taps, share * (taps + 1), share * (taps + 1) + norm_gain.shape[0]]
    conv_w = small[:, : cuts[0]].reshape(channels, taps)
    conv_b = small[:, cuts[0] : cuts[1]].reshape(channels)
    norm_all = small[:, cuts[1] : cuts[2]].reshape(-1)
    gain_all = small[:, cuts[2] :].reshape(-1)

    def own(a):
        return lax.dynamic_slice_in_dim(a, place * inner, inner, 0)

    def own_heads(a):
        return lax.dynamic_slice_in_dim(a, place * mine, mine, 0)

    floats = tokens.astype(F32)
    inverse = lax.rsqrt(jnp.mean(floats * floats, axis=-1, keepdims=True) + EPSILON)
    unit = floats * inverse
    normed = lax.all_gather((unit * norm_all).astype(BF16), "seq", axis=1, tiled=True)
    cot = lax.all_gather(cotangent, "seq", axis=1, tiled=True)
    w_mine = jnp.concatenate(
        [
            lax.dynamic_slice_in_dim(w_in, place * span, span, 1),
            w_in[:, 2 * wide : 2 * wide + state2],
            jnp.pad(
                lax.dynamic_slice_in_dim(w_in, 2 * wide + state2 + place * mine, mine, 1),
                ((0, 0), (0, 128 - mine)),
            ),
        ],
        axis=1,
    )
    w_full = lax.all_gather(w_mine, "dp", axis=0, tiled=True)
    ratio = shards // groups
    held = jnp.where(
        (owner // ratio == place) & (jnp.arange(ratio)[:, None, None] == owner % ratio),
        w_out[None],
        jnp.zeros((), BF16),
    ).reshape(inner, model)
    wo = lax.psum(held, "dp")
    sg = jnp.einsum("std,cd->stc", cot, wo, preferred_element_type=F32).astype(BF16)
    pj = jnp.einsum("std,de->ste", normed, w_full, preferred_element_type=F32).astype(BF16)

    def pad(v):
        return jnp.pad(v, (0, 128 - mine))

    rate = -jnp.exp(own_heads(a_log))
    hp = jnp.stack([pad(own_heads(dt_bias)), pad(rate * LOG2E), pad(rate)] + [jnp.zeros(128)] * 5)
    blank = jnp.zeros((state2,), F32)
    ch = jnp.concatenate(
        [
            jnp.concatenate([own(conv_w), conv_w[wide:]]).T,
            jnp.concatenate([own(conv_b), conv_b[wide:]])[None],
            jnp.concatenate([jnp.repeat(own_heads(skip_weight), size), blank])[None],
            jnp.concatenate([own(gain_all), blank])[None],
            jnp.zeros((1, inner + state2), F32),
        ]
    )
    cols = columns(segment_ids)
    pre, ys, gn, st, red = mix_forward(pj, cols, sg, hp, ch)
    totals = lax.psum(red[:, :2], "seq")
    rho = lax.rsqrt(totals[:, 0] / wide + EPSILON)
    k2 = rho**3 * totals[:, 1] / wide
    cols2 = jnp.pad(jnp.stack([rho, k2], axis=-1), ((0, 0), (0, 0), (0, 126)))
    product = jnp.einsum("stc,cd->std", gn, wo, preferred_element_type=F32)
    product = (product * rho[:, :, None]).astype(BF16)
    result = (
        floats
        + lax.psum_scatter(product, "seq", scatter_dimension=1, tiled=True).astype(F32)
    ).astype(BF16)
    cot_rho = (cot.astype(F32) * rho[:, :, None]).astype(BF16)
    wo_grad = jnp.einsum("stc,std->cd", gn, cot_rho, preferred_element_type=F32).astype(BF16)
    wo_grad = lax.psum(wo_grad, "dp").reshape(ratio, rows_out, model)
    wo_grad = lax.dynamic_index_in_dim(wo_grad, owner % ratio, 0, False)
    wo_grad = lax.psum(jnp.where(owner // ratio == place, wo_grad, jnp.zeros((), BF16)), "seq")
    pg, chacc, hacc = mix_backward(
        pj, cols, cols2, sg, pre, ys, st, hp, ch, selectors(inner // 128)
    )
    win_grad = jnp.einsum("std,ste->de", normed, pg, preferred_element_type=F32).astype(BF16)
    win_grad = lax.psum_scatter(win_grad, "dp", scatter_dimension=0, tiled=True)
    win_grad = lax.all_gather(win_grad, "seq", axis=0, tiled=False).astype(F32)
    rows_in = win_grad.shape[1]
    w_in_grad = jnp.concatenate(
        [
            win_grad[:, :, :span].transpose(1, 0, 2).reshape(rows_in, 2 * wide),
            jnp.sum(win_grad[:, :, span : span + state2], axis=0),
            win_grad[:, :, span + state2 : span + state2 + mine]
            .transpose(1, 0, 2)
            .reshape(rows_in, heads),
        ],
        axis=1,
    )
    ngrad = jnp.einsum("ste,de->std", pg, w_full, preferred_element_type=F32).astype(BF16)
    ngrad = lax.psum_scatter(ngrad, "seq", scatter_dimension=1, tiled=True).astype(F32)
    unit_grad = ngrad * norm_all
    tokens_grad = cotangent.astype(F32) + inverse * (
        unit_grad - unit * jnp.mean(unit_grad * unit, axis=-1, keepdims=True)
    )
    chsum = jnp.sum(chacc, axis=1)
    hsum = jnp.sum(hacc, axis=1)[:, :mine]
    hsum = hsum * jnp.stack([jnp.ones((mine,)), rate, jnp.ones((mine,))])

    def spread(a, n, start):
        full = jnp.zeros(a.shape[:-1] + (n,), F32)
        return lax.dynamic_update_slice_in_dim(full, a, start, a.ndim - 1)

    chan = jnp.concatenate(
        [spread(chsum[:, :inner], wide, place * inner), chsum[:, inner:]], axis=1
    )
    packed = jnp.concatenate(
        [
            chan[: taps + 1].reshape(-1),
            chan[taps + 1, :wide],
            jnp.sum(ngrad * unit, axis=(0, 1)),
            spread(hsum, heads, place * mine).reshape(-1),
        ]
    )
    packed = lax.psum(packed, ("dp", "seq"))
    chan = packed[: (taps + 1) * channels].reshape(taps + 1, channels)
    chan = lax.dynamic_slice_in_dim(chan, owner * share, share, 1)
    at = (taps + 1) * channels
    gain_grad = lax.dynamic_slice_in_dim(packed[at : at + wide], owner * rows_out, rows_out, 0)
    at += wide
    norm_grad = lax.dynamic_slice_in_dim(packed[at : at + model], owner * rows_in, rows_in, 0)
    at += model
    return (
        result,
        tokens_grad,
        w_in_grad,
        wo_grad.astype(F32),
        chan[:taps].T,
        chan[taps],
        norm_grad,
        gain_grad,
        packed[at : at + heads],
        packed[at + heads : at + 2 * heads],
        packed[at + 2 * heads : at + 3 * heads],
    )


def solution(mesh):
    return jax.shard_map(
        local,
        mesh=mesh,
        in_specs=(
            P("dp", "seq", None),
            P("dp", None),
            P("dp", None),
            P("dp", None),
            P("dp", None),
            P("dp"),
            P("dp"),
            P("dp"),
            P(),
            P(),
            P(),
            P("dp", "seq", None),
        ),
        out_specs=(
            P("dp", "seq", None),
            P("dp", "seq", None),
            P("dp", None),
            P("dp", None),
            P("dp", None),
            P("dp"),
            P("dp"),
            P("dp"),
            P(),
            P(),
            P(),
        ),
        check_vma=False,
    )
```

```python
import functools

import jax
import jax.numpy as jnp
from jax import lax
from jax.experimental import pallas as pl
from jax.experimental.pallas import tpu as pltpu
from jax.sharding import PartitionSpec as P

Q = 128
EXACT = lax.Precision.HIGHEST
EPSILON = 1e-05
LOG2E = 1.4426950408889634
RESET = 160.0
F32 = jnp.float32
BF16 = jnp.bfloat16
LUMPS = 6
WOFF = 1
MESH = pl.DeviceIdType.MESH


def sigmoid(x):
    return 0.5 * jnp.tanh(0.5 * x) + 0.5


def softplus(x):
    return jnp.maximum(x, 0.0) + jnp.log1p(jnp.exp(-jnp.abs(x)))


def nt(a, b):
    return lax.dot_general(a, b, (((1,), (1,)), ((), ())), preferred_element_type=F32)


def mm(a, b):
    return jnp.dot(a, b, preferred_element_type=F32)


def decays(pj, cols, hp, width):
    arg = pj[0, :, width + 256 : width + 384].astype(F32) + hp[0:1, :]
    dt = softplus(arg)
    rows = lax.broadcasted_iota(jnp.int32, (Q, Q), 0)
    lanes = lax.broadcasted_iota(jnp.int32, (Q, Q), 1)
    lower = (rows >= lanes).astype(F32)
    level = jnp.dot(lower, dt * hp[1:2, :], precision=EXACT, preferred_element_type=F32)
    level = level + cols[0, :, 3:4]
    return arg, dt, level, rows, lanes


def fwd_kernel(pairs, pj, cols, sg, hp, ch, pre, ys, gn, st, red, state, tail):
    width = pairs * 256
    inner = pairs * 128
    chunk = pl.program_id(1)

    @pl.when(chunk == 0)
    def _():
        state[...] = jnp.zeros_like(state)
        tail[...] = jnp.zeros_like(tail)

    _, dt, level, rows, lanes = decays(pj, cols, hp, width)
    level_t = level.T
    low = lanes < 64
    masks = [cols[0, :, d : d + 1] for d in range(3)]

    def conv(raw, at):
        ext = jnp.concatenate([tail[:, at : at + 128], raw], axis=0)
        total = raw * ch[3:4, at : at + 128] + ch[4:5, at : at + 128]
        for d in (1, 2, 3):
            moved = pltpu.roll(ext, d, 0)[8:]
            total = total + moved * masks[d - 1] * ch[3 - d : 4 - d, at : at + 128]
        tail[:, at : at + 128] = raw[Q - 8 :]
        pre[0, :, at : at + 128] = total
        return total * sigmoid(total)

    b_rows = conv(pj[0, :, width : width + 128].astype(F32), inner)
    c_rows = conv(pj[0, :, width + 128 : width + 256].astype(F32), inner + 128)
    b_t = b_rows.T.astype(BF16)
    b_low = b_rows.astype(BF16)
    c_low = c_rows.astype(BF16)
    scores = jnp.where(rows >= lanes, nt(c_low, b_low), 0.0)
    old = state[...].astype(BF16)
    st[0, 0] = old
    carried_all = mm(c_low, old)
    squares = jnp.zeros((Q, 128), F32)
    cross = jnp.zeros((Q, 128), F32)
    for p in range(pairs):
        at = p * 128
        one = pj[0, :, p * 256 : p * 256 + 128].astype(F32)
        two = pj[0, :, p * 256 + 128 : p * 256 + 256].astype(F32)
        z = jnp.where(low, one, pltpu.roll(two, 64, 1))
        v = jnp.where(low, pltpu.roll(one, 64, 1), two)
        xc = conv(v, at)
        l0 = jnp.broadcast_to(level[:, 2 * p : 2 * p + 1], (Q, Q))
        l1 = jnp.broadcast_to(level[:, 2 * p + 1 : 2 * p + 2], (Q, Q))
        le = jnp.where(low, l0, l1)
        dte = jnp.where(low, dt[:, 2 * p : 2 * p + 1], dt[:, 2 * p + 1 : 2 * p + 2])
        u = xc * dte
        w0 = jnp.exp2(jnp.minimum(l0 - level_t[2 * p : 2 * p + 1, :], 0.0)) * scores
        w1 = jnp.exp2(jnp.minimum(l1 - level_t[2 * p + 1 : 2 * p + 2, :], 0.0)) * scores
        wide = jnp.concatenate([w0.astype(BF16), w1.astype(BF16)], axis=1)
        blocks = jnp.concatenate(
            [jnp.where(low, u, 0.0).astype(BF16), jnp.where(low, 0.0, u).astype(BF16)], axis=0
        )
        part = mm(wide, blocks) + carried_all[:, at : at + 128] * jnp.exp2(le)
        ys[0, :, at : at + 128] = part
        gated = (part + ch[5:6, at : at + 128] * xc) * (z * sigmoid(z))
        scaled = gated * ch[6:7, at : at + 128]
        gn[0, :, at : at + 128] = scaled.astype(BF16)
        squares = squares + gated * gated
        cross = cross + sg[0, :, at : at + 128].astype(F32) * scaled
        last = le[Q - 1 : Q, :]
        ul = (u * jnp.exp2(last - le)).astype(BF16)
        state[:, at : at + 128] = state[:, at : at + 128] * jnp.exp2(last) + mm(b_t, ul)
    both = jnp.where(
        lanes == 0, jnp.sum(squares, axis=1, keepdims=True), jnp.sum(cross, axis=1, keepdims=True)
    )
    red[0] = both.T[0:8]


def mix_forward(pj, cols, sg, hp, ch, interpret=False):
    seqs, length, total = pj.shape
    width = total - 384
    inner = width // 2
    pairs = inner // 128
    chunks = length // Q

    def row(n):
        return pl.BlockSpec((1, Q, n), lambda s, c: (s, c, 0))

    def whole(a):
        return pl.BlockSpec(a.shape, lambda s, c: (0,) * a.ndim)

    return pl.pallas_call(
        functools.partial(fwd_kernel, pairs),
        grid=(seqs, chunks),
        in_specs=[row(total), row(128), row(inner), whole(hp), whole(ch)],
        out_specs=[
            row(inner + 256),
            row(inner),
            row(inner),
            pl.BlockSpec((1, 1, 128, inner), lambda s, c: (s, c, 0, 0)),
            pl.BlockSpec((1, 8, Q), lambda s, c: (s, 0, c)),
        ],
        out_shape=[
            jax.ShapeDtypeStruct((seqs, length, inner + 256), F32),
            jax.ShapeDtypeStruct((seqs, length, inner), F32),
            jax.ShapeDtypeStruct((seqs, length, inner), BF16),
            jax.ShapeDtypeStruct((seqs, chunks, 128, inner), BF16),
            jax.ShapeDtypeStruct((seqs, 8, length), F32),
        ],
        scratch_shapes=[pltpu.VMEM((128, inner), F32), pltpu.VMEM((8, inner + 256), F32)],
        compiler_params=pltpu.CompilerParams(vmem_limit_bytes=48 * 2**20),
        name="mix_forward",
    )(pj, cols, sg, hp, ch)


def bwd_kernel(
    pairs, pj, cols, cols2, sg, pre, ys, st, hp, ch, sel, pg, chacc, hacc,
    dstate, halo, edy_all, ul_all,
):
    width = pairs * 256
    inner = pairs * 128
    first = (pl.program_id(0) == 0) & (pl.program_id(1) == 0)

    @pl.when(pl.program_id(1) == 0)
    def _():
        dstate[...] = jnp.zeros_like(dstate)
        halo[...] = jnp.zeros_like(halo)

    @pl.when(first)
    def _():
        chacc[...] = jnp.zeros_like(chacc)
        hacc[...] = jnp.zeros_like(hacc)

    arg, dt, level, rows, lanes = decays(pj, cols, hp, width)
    level_t = level.T
    low = lanes < 64
    masks = [cols[0, :, 3 + d : 4 + d] for d in (1, 2, 3)]
    rho = jnp.broadcast_to(cols2[0, :, 0:1], (Q, 128))
    k2 = jnp.broadcast_to(cols2[0, :, 1:2], (Q, 128))

    def fold(x):
        return jnp.sum(x.reshape(Q // 8, 8, 128), axis=0)

    def conv_back(grad, raw, at):
        ext = jnp.concatenate([grad, halo[:, at : at + 128]], axis=0)
        out = grad * ch[3:4, at : at + 128]
        chacc[3, :, at : at + 128] += fold(grad * raw)
        chacc[4, :, at : at + 128] += fold(grad)
        for d in (1, 2, 3):
            moved = pltpu.roll(ext, Q + 8 - d, 0)[:Q] * masks[d - 1]
            out = out + moved * ch[3 - d : 4 - d, at : at + 128]
            chacc[3 - d, :, at : at + 128] += fold(moved * raw)
        halo[:, at : at + 128] = grad[:8]
        return out

    pre_b = pre[0, :, inner : inner + 128]
    pre_c = pre[0, :, inner + 128 : inner + 256]
    sig_b, sig_c = sigmoid(pre_b), sigmoid(pre_c)
    b_rows, c_rows = pre_b * sig_b, pre_c * sig_c
    b_low, c_low = b_rows.astype(BF16), c_rows.astype(BF16)
    c_t = c_rows.T.astype(BF16)
    upper = lanes >= rows
    scores = jnp.where(upper, nt(b_low, c_low), 0.0)
    dlow = dstate[...].astype(BF16)
    dsb_all = mm(b_low, dlow)
    dscores = jnp.zeros((Q, Q), F32)
    sums = jnp.zeros((6 * Q, 128), F32)
    keep = jnp.zeros((8, 128), F32)
    for p in range(pairs):
        at = p * 128
        one = pj[0, :, p * 256 : p * 256 + 128].astype(F32)
        two = pj[0, :, p * 256 + 128 : p * 256 + 256].astype(F32)
        z = jnp.where(low, one, pltpu.roll(two, 64, 1))
        v = jnp.where(low, pltpu.roll(one, 64, 1), two)
        pr = pre[0, :, at : at + 128]
        sp = sigmoid(pr)
        xc = pr * sp
        l0 = jnp.broadcast_to(level[:, 2 * p : 2 * p + 1], (Q, Q))
        l1 = jnp.broadcast_to(level[:, 2 * p + 1 : 2 * p + 2], (Q, Q))
        le = jnp.where(low, l0, l1)
        dte = jnp.where(low, dt[:, 2 * p : 2 * p + 1], dt[:, 2 * p + 1 : 2 * p + 2])
        u = xc * dte
        skip = ch[5:6, at : at + 128]
        part = ys[0, :, at : at + 128]
        y = part + skip * xc
        sz = sigmoid(z)
        silz = z * sz
        gated = y * silz
        graw = sg[0, :, at : at + 128].astype(F32)
        scaled_rho = graw * rho
        chacc[5, :, at : at + 128] += fold(scaled_rho * gated)
        gg = scaled_rho * ch[6:7, at : at + 128] - k2 * gated
        dy = gg * silz
        dz = gg * y * (sz + silz * (1.0 - sz))
        ulow = u.astype(BF16)
        dylow = dy.astype(BF16)
        w0 = jnp.exp2(jnp.minimum(level_t[2 * p : 2 * p + 1, :] - l0, 0.0))
        w1 = jnp.exp2(jnp.minimum(level_t[2 * p + 1 : 2 * p + 2, :] - l1, 0.0))
        wide = jnp.concatenate([(w0 * scores).astype(BF16), (w1 * scores).astype(BF16)], axis=1)
        dyb = jnp.concatenate(
            [jnp.where(low, dy, 0.0).astype(BF16), jnp.where(low, 0.0, dy).astype(BF16)], axis=0
        )
        ub = jnp.concatenate(
            [jnp.where(low, u, 0.0).astype(BF16), jnp.where(low, 0.0, u).astype(BF16)], axis=0
        )
        duw = mm(wide, dyb)
        gt = nt(ub, dylow)
        dscores = dscores + w0 * gt[:Q] + w1 * gt[Q:]
        last = le[Q - 1 : Q, :]
        lve = jnp.exp2(last - le)
        edy = (dy * jnp.exp2(le)).astype(BF16)
        ul = (u * lve).astype(BF16)
        edy_all[:, at : at + 128] = edy
        ul_all[:, at : at + 128] = ul
        dsb = dsb_all[:, at : at + 128]
        du = duw + lve * dsb
        r1 = dylow.astype(F32) * part - ulow.astype(F32) * duw
        r2 = ul.astype(F32) * dsb
        r1h, r2h = r1.astype(BF16), r2.astype(BF16)
        stacked = jnp.concatenate(
            [
                r1h,
                (r1 - r1h.astype(F32)).astype(BF16),
                r2h,
                (r2 - r2h.astype(F32)).astype(BF16),
                (dy * xc).astype(BF16),
                (du * xc).astype(BF16),
            ],
            axis=0,
        )
        sums = sums + mm(stacked, sel[p])
        decay = jnp.exp2(last)
        kept = fold(dlow[:, at : at + 128].astype(F32) * st[0, 0, :, at : at + 128].astype(F32)) * decay
        kept_high = kept.astype(BF16)
        keep = keep + mm(kept_high, sel[p]) + mm((kept - kept_high.astype(F32)).astype(BF16), sel[p])
        dstate[:, at : at + 128] = dstate[:, at : at + 128] * decay + mm(c_t, edy)
        dv = conv_back((du * dte + skip * dy) * (sp + xc * (1.0 - sp)), v, at)
        pg[0, :, p * 256 : p * 256 + 128] = jnp.where(low, dz, pltpu.roll(dv, 64, 1)).astype(BF16)
        pg[0, :, p * 256 + 128 : p * 256 + 256] = jnp.where(low, pltpu.roll(dz, 64, 1), dv).astype(BF16)
    dsc = jnp.where(upper, dscores, 0.0)
    db = mm(dsc.astype(BF16), c_low) + nt(ul_all[...], dlow)
    dc = mm(dsc.T.astype(BF16), b_low) + nt(edy_all[...], st[0, 0])
    raw_b = pj[0, :, width : width + 128].astype(F32)
    raw_c = pj[0, :, width + 128 : width + 256].astype(F32)
    pg[0, :, width : width + 128] = conv_back(
        db * (sig_b + b_rows * (1.0 - sig_b)), raw_b, inner
    ).astype(BF16)
    pg[0, :, width + 128 : width + 256] = conv_back(
        dc * (sig_c + c_rows * (1.0 - sig_c)), raw_c, inner + 128
    ).astype(BF16)
    r1 = sums[:Q] + sums[Q : 2 * Q]
    r2 = sums[2 * Q : 3 * Q] + sums[3 * Q : 4 * Q]
    da = (
        jnp.dot(upper.astype(F32), r1, precision=EXACT, preferred_element_type=F32)
        + jnp.dot((rows > lanes).astype(F32), r2, precision=EXACT, preferred_element_type=F32)
        + jnp.sum(keep, axis=0, keepdims=True)
    )
    ddt = da * hp[2:3, :] + sums[5 * Q :]
    ds = ddt * sigmoid(arg)
    pg[0, :, width + 256 : width + 384] = ds.astype(BF16)
    hacc[0] += fold(ds)
    hacc[1] += fold(da * dt)
    hacc[2] += fold(sums[4 * Q : 5 * Q])


def mix_backward(pj, cols, cols2, sg, pre, ys, st, hp, ch, sel):
    seqs, length, total = pj.shape
    width = total - 384
    inner = width // 2
    pairs = inner // 128
    chunks = length // Q

    def row(n):
        return pl.BlockSpec((1, Q, n), lambda s, c: (s, chunks - 1 - c, 0))

    def whole(shape):
        return pl.BlockSpec(shape, lambda s, c: (0,) * len(shape))

    return pl.pallas_call(
        functools.partial(bwd_kernel, pairs),
        grid=(seqs, chunks),
        in_specs=[
            row(total),
            row(128),
            row(128),
            row(inner),
            row(inner + 256),
            row(inner),
            pl.BlockSpec((1, 1, 128, inner), lambda s, c: (s, chunks - 1 - c, 0, 0)),
            whole(hp.shape),
            whole(ch.shape),
            whole(sel.shape),
        ],
        out_specs=[row(total), whole((6, 8, inner + 256)), whole((3, 8, 128))],
        out_shape=[
            jax.ShapeDtypeStruct((seqs, length, total), BF16),
            jax.ShapeDtypeStruct((6, 8, inner + 256), F32),
            jax.ShapeDtypeStruct((3, 8, 128), F32),
        ],
        scratch_shapes=[
            pltpu.VMEM((128, inner), F32),
            pltpu.VMEM((8, inner + 256), F32),
            pltpu.VMEM((Q, inner), BF16),
            pltpu.VMEM((Q, inner), BF16),
        ],
        compiler_params=pltpu.CompilerParams(vmem_limit_bytes=48 * 2**20),
        name="mix_backward",
    )(pj, cols, cols2, sg, pre, ys, st, hp, ch, sel)


def columns(seg):
    seqs, length = seg.shape
    back = [
        jnp.pad((seg[:, d:] == seg[:, :-d]).astype(F32), ((0, 0), (d, 0))) for d in (1, 2, 3)
    ]
    ahead = [
        jnp.pad((seg[:, d:] == seg[:, :-d]).astype(F32), ((0, 0), (0, d))) for d in (1, 2, 3)
    ]
    ends = seg.reshape(seqs, length // Q, Q)[:, :, -1]
    before = jnp.pad(ends[:, :-1], ((0, 0), (1, 0)))
    level = -RESET * (seg.reshape(seqs, length // Q, Q) - before[:, :, None]).astype(F32)
    stacked = jnp.stack([*back, level.reshape(seqs, length), *ahead], axis=-1)
    return jnp.pad(stacked, ((0, 0), (0, 0), (0, 121)))


def selectors(pairs):
    lane = lax.broadcasted_iota(jnp.int32, (pairs, 128, 128), 1)
    pair = lax.broadcasted_iota(jnp.int32, (pairs, 128, 128), 0)
    out = lax.broadcasted_iota(jnp.int32, (pairs, 128, 128), 2)
    return (out == 2 * pair + lane // 64).astype(BF16)


def gather_kernel(
    dims, wm, wo_in, small_in, tok_in, cot_in,
    normed_o, cot_o, pj_o, sg_o, w_o, wo_o, small_o,
    tok, cot, wbig, wo, small, pjv, sgv,
    szu, szd, rz, sy, ry, wsu, wsd, wrz, wsy, wry, bx_s, bx_r, bc_s, bc_r, loc, out,
):
    deep, pieces, rows, inner, part, length = dims
    d = lax.axis_index("dp")
    s = lax.axis_index("seq")
    z = d // 2
    y = d % 2
    top = deep - 1
    up, down, side = (d + 2, s), (d - 2, s), (d + 1 - 2 * y, s)
    across, twin = (d, s + 2 - 4 * (s // 2)), (d, s + 1 - 2 * (s % 2))
    opposite = across[1]

    bar = pltpu.get_barrier_semaphore()

    @pl.when(z < top)
    def _():
        pl.semaphore_signal(bar, inc=1, device_id=up, device_id_type=MESH)

    @pl.when(z > 0)
    def _():
        pl.semaphore_signal(bar, inc=1, device_id=down, device_id_type=MESH)

    for who in (side, across, twin):
        pl.semaphore_signal(bar, inc=1, device_id=who, device_id_type=MESH)
    pl.semaphore_wait(bar, 3 + jnp.minimum(z, 1) + jnp.minimum(top - z, 1))

    def send(src, dst, ssem, rsem, who):
        return pltpu.make_async_remote_copy(
            src_ref=src, dst_ref=dst, send_sem=ssem, recv_sem=rsem,
            device_id=who, device_id_type=MESH,
        )

    width = 2 * inner

    def cols(k):
        return pl.ds(width, 384) if k == 1 else pl.ds((k - 2) * 256, 256)

    def held(k, owner):
        if k == 0:
            return small.at[owner]
        return wbig.at[pl.ds(pl.multiple_of(owner * rows, 16), rows), cols(k)]

    def source(k):
        return small_in.at[...] if k == 0 else wm.at[:, cols(k)]

    def own_send(k):
        src, dst = source(k), held(k, d)

        @pl.when(z < top)
        def _():
            send(src, dst, szu.at[k, z], rz.at[k, z], up).start()

        @pl.when(z > 0)
        def _():
            send(src, dst, szd.at[k, z], rz.at[k, z], down).start()

        send(src, dst, sy.at[k, z], ry.at[k, z], side).start()

    def hop(k, h):
        below, above = z - h, z + h

        @pl.when(below >= 0)
        def _():
            ref = held(k, below * 2 + y)
            send(ref, ref, szu.at[k, below], rz.at[k, below], up).wait_recv()

            @pl.when(z < top)
            def _():
                send(ref, ref, szu.at[k, below], rz.at[k, below], up).start()

            send(ref, ref, sy.at[k, below], ry.at[k, below], side).start()

        @pl.when(above <= top)
        def _():
            ref = held(k, above * 2 + y)
            send(ref, ref, szd.at[k, above], rz.at[k, above], down).wait_recv()

            @pl.when(z > 0)
            def _():
                send(ref, ref, szd.at[k, above], rz.at[k, above], down).start()

            send(ref, ref, sy.at[k, above], ry.at[k, above], side).start()

    def arrive(k):
        for e in range(deep):
            ref = held(k, e * 2 + 1 - y)
            send(ref, ref, sy.at[k, e], ry.at[k, e], side).wait_recv()

    def own_copy(src, dst, sem):
        return pltpu.make_async_copy(src, dst, sem)

    here = pl.multiple_of(s * part, 16)
    there = pl.multiple_of(opposite * part, 16)
    locals_ = [
        own_copy(small_in, small.at[d], loc.at[0]),
        own_copy(wm, wbig.at[pl.ds(pl.multiple_of(d * rows, 16), rows)], loc.at[1]),
    ]
    for q in range(2):
        locals_.append(own_copy(tok_in.at[q], tok.at[q, pl.ds(here, part)], loc.at[2 + q]))
        locals_.append(own_copy(cot_in.at[q], cot.at[q, pl.ds(here, part)], loc.at[4 + q]))
    half = wo_in.shape[0]
    mine = z == s

    def root_copy():
        return own_copy(wo_in, wo.at[pl.ds(pl.multiple_of(y * half, 16), half)], loc.at[6])

    def block_sends(which, src, dst, q):
        spot = dst.at[q, pl.ds(here, part)]
        i = which * 2 + q
        send(src.at[q], spot, bx_s.at[i], bx_r.at[i], across).start()
        send(src.at[q], spot, bc_s.at[0, i], bc_r.at[0, i], twin).start()

    def block_forward(which, dst, q):
        spot = dst.at[q, pl.ds(there, part)]
        i = which * 2 + q
        send(spot, spot, bx_s.at[i], bx_r.at[i], across).wait_recv()
        send(spot, spot, bc_s.at[1, i], bc_r.at[1, i], twin).start()

    def block_arrive(which, dst, q):
        i = which * 2 + q
        for n in range(2):
            spot = dst.at[q, pl.ds(here, part)]
            send(spot, spot, bc_s.at[n, i], bc_r.at[n, i], twin).wait_recv()

    lump = half // LUMPS

    def wo_piece(i, col):
        m = col * LUMPS + i
        return m, wo.at[pl.ds(pl.multiple_of(m * lump, 16), lump)]

    def wo_send(i, src=None):
        m, ref = wo_piece(i, y)
        src = ref if src is None else src

        @pl.when((z >= s) & (z < top))
        def _():
            send(src, ref, wsu.at[m], wrz.at[m], up).start()

        @pl.when((z <= s) & (z > 0))
        def _():
            send(src, ref, wsd.at[m], wrz.at[m], down).start()

        send(src, ref, wsy.at[m], wry.at[m], side).start()

    def wo_root(i):
        @pl.when(mine)
        def _():
            wo_send(i, wo_in.at[pl.ds(i * lump, lump)])

    def wo_hop(i, h):
        @pl.when((z - s == h) | (s - z == h))
        def _():
            m, ref = wo_piece(i, y)
            send(ref, ref, wsu.at[m], wrz.at[m], up).wait_recv()
            wo_send(i)

    def wo_arrive(i):
        m, ref = wo_piece(i, 1 - y)
        send(ref, ref, wsy.at[m], wry.at[m], side).wait_recv()

    tile = 256

    def project(k):
        c = cols(k)

        def step(i, _):
            q, r = i // (length // tile), i % (length // tile)
            at = pl.multiple_of(r * tile, tile)
            pjv[q, pl.ds(at, tile), c] = mm(tok[q, pl.ds(at, tile), :], wbig[:, c]).astype(BF16)
            return 0

        lax.fori_loop(0, 2 * length // tile, step, 0)
        own_copy(pjv.at[:, :, c], pj_o.at[:, :, c], out.at[k]).start()

    for c in locals_:
        c.start()

    @pl.when(mine)
    def _():
        root_copy().start()

    for q in range(2):
        block_sends(0, tok_in, tok, q)
    ahead = 3
    for k in range(ahead):
        own_send(k)
    done = []

    def hops(t):
        for h in range(1, deep):
            if 0 <= t - h < pieces:
                hop(t - h, h)
        for h in range(1, deep):
            if 0 <= t - h - WOFF < LUMPS:
                wo_hop(t - h - WOFF, h)
        if 0 <= t - WOFF < LUMPS:
            wo_root(t - WOFF)
        if ahead <= t + ahead - 1 < pieces:
            own_send(t + ahead - 1)

    steps = max(pieces, WOFF + LUMPS) + deep - 1
    count = dict(next=1)

    def ready(n):
        for _ in range(n):
            if count["next"] < pieces:
                arrive(count["next"])
                project(count["next"])
                count["next"] += 1

    share = tok.shape[2] // (2 * deep)

    def norm_step(i, _):
        q, r = i // (length // 64), i % (length // 64)
        at = pl.multiple_of(r * 64, 64)
        x = tok[q, pl.ds(at, 64), :].astype(F32)
        inv = lax.rsqrt(jnp.mean(x * x, axis=1, keepdims=True) + EPSILON)
        gains = jnp.concatenate([small[e, 0:1, :share] for e in range(2 * deep)], axis=1)
        tok[q, pl.ds(at, 64), :] = (x * inv * gains.astype(F32)).astype(BF16)
        return 0

    for t in range(1, steps):
        hops(t)
        if t == 3:
            block_forward(0, tok, 0)
        if t == 6:
            block_forward(0, tok, 1)
            for q in range(2):
                block_sends(1, cot_in, cot, q)
        if t == 7:
            for i in (0, 1, 2, 4):
                locals_[i].wait()
            block_arrive(0, tok, 0)
            block_arrive(0, tok, 1)
            for q in range(2):
                spot = tok.at[q, pl.ds(there, part)]
                send(spot, spot, bc_s.at[1, q], bc_r.at[1, q], twin).wait_send()
            arrive(0)
            own_copy(small, small_o, out.at[0]).start()
            lax.fori_loop(0, 2 * length // 64, norm_step, 0)
            own_copy(tok, normed_o, out.at[pieces]).start()
        if t > 7:
            ready(1)
    for i in range(LUMPS):
        wo_arrive(i)

    @pl.when(mine)
    def _():
        root_copy().wait()

    block_forward(1, cot, 0)
    ready(pieces)
    own_copy(wbig, w_o, out.at[pieces + 1]).start()
    own_copy(wo, wo_o, out.at[pieces + 2]).start()
    block_forward(1, cot, 1)
    locals_[3].wait()
    locals_[5].wait()
    block_arrive(1, cot, 0)
    block_arrive(1, cot, 1)
    own_copy(cot, cot_o, out.at[pieces + 3]).start()

    def grad_step(i, _):
        q, r = i // (length // tile), i % (length // tile)
        at = pl.multiple_of(r * tile, tile)
        sgv[q, pl.ds(at, tile), :] = nt(cot[q, pl.ds(at, tile), :], wo[...]).astype(BF16)
        return 0

    lax.fori_loop(0, 2 * length // tile, grad_step, 0)
    own_copy(sgv, sg_o, out.at[pieces + 4]).start()

    for k in range(pieces):
        for e in range(deep):
            ref = held(k, e * 2 + y)

            @pl.when((z >= e) & (z < top))
            def _():
                send(ref, ref, szu.at[k, e], rz.at[k, e], up).wait_send()

            @pl.when((z <= e) & (z > 0))
            def _():
                send(ref, ref, szd.at[k, e], rz.at[k, e], down).wait_send()

            send(ref, ref, sy.at[k, e], ry.at[k, e], side).wait_send()
    for i in range(LUMPS):
        m, ref = wo_piece(i, y)

        @pl.when((z >= s) & (z < top))
        def _():
            send(ref, ref, wsu.at[m], wrz.at[m], up).wait_send()

        @pl.when((z <= s) & (z > 0))
        def _():
            send(ref, ref, wsd.at[m], wrz.at[m], down).wait_send()

        send(ref, ref, wsy.at[m], wry.at[m], side).wait_send()
    for which, dst in ((0, tok), (1, cot)):
        for q in range(2):
            i = which * 2 + q
            spot = dst.at[q, pl.ds(here, part)]
            send(spot, spot, bx_s.at[i], bx_r.at[i], across).wait_send()
            for n in range(1 + which):
                send(spot, spot, bc_s.at[n, i], bc_r.at[n, i], twin).wait_send()
    own_copy(small, small_o, out.at[0]).wait()
    for k in range(1, pieces):
        own_copy(pjv.at[:, :, cols(k)], pj_o.at[:, :, cols(k)], out.at[k]).wait()
    own_copy(tok, normed_o, out.at[pieces]).wait()
    own_copy(wbig, w_o, out.at[pieces + 1]).wait()
    own_copy(wo, wo_o, out.at[pieces + 2]).wait()
    own_copy(cot, cot_o, out.at[pieces + 3]).wait()
    own_copy(sgv, sg_o, out.at[pieces + 4]).wait()


def gather(wm, w_out, small, tokens, cotangent, shards, groups):
    rows, total = wm.shape
    width = total - 384
    inner = width // 2
    seqs, part, model = tokens.shape
    length = part * groups
    deep = shards // 2
    pairs = inner // 128
    pieces = pairs + 2
    any_ = pl.BlockSpec(memory_space=pl.ANY)
    dma = pltpu.SemaphoreType.DMA
    small_rows, small_cols = small.shape
    full = (shards * rows, total)
    shapes = [
        (seqs, length, model), (seqs, length, model), (seqs, length, total), (seqs, length, inner),
        full, (inner, model), (shards, small_rows, small_cols),
    ]
    return pl.pallas_call(
        functools.partial(gather_kernel, (deep, pieces, rows, inner, part, length)),
        in_specs=[any_] * 5,
        out_specs=[any_] * 7,
        out_shape=[jax.ShapeDtypeStruct(n, BF16) for n in shapes],
        scratch_shapes=[
            pltpu.VMEM(shapes[0], BF16),
            pltpu.VMEM(shapes[0], BF16),
            pltpu.VMEM(full, BF16),
            pltpu.VMEM((inner, model), BF16),
            pltpu.VMEM(shapes[6], BF16),
            pltpu.VMEM(shapes[2], BF16),
            pltpu.VMEM(shapes[3], BF16),
            dma((pieces, deep)), dma((pieces, deep)), dma((pieces, deep)),
            dma((pieces, deep)), dma((pieces, deep)),
            *[dma((2 * LUMPS,))] * 5,
            dma((4,)), dma((4,)), dma((2, 4)), dma((2, 4)),
            dma((7,)), dma((pieces + 5,)),
        ],
        compiler_params=pltpu.CompilerParams(
            collective_id=1, has_side_effects=True, vmem_limit_bytes=56 * 2**20
        ),
        name="gather_project",
    )(wm, w_out, small, tokens, cotangent)


def local(
    tokens,
    segment_ids,
    w_in,
    w_out,
    conv_weight,
    conv_bias,
    norm_gain,
    gated_gain,
    dt_bias,
    a_log,
    skip_weight,
    cotangent,
):
    groups = lax.axis_size("seq")
    shards = lax.axis_size("dp")
    place = lax.axis_index("seq")
    owner = lax.axis_index("dp")
    seqs, part, model = tokens.shape
    length = part * groups
    rows_out = w_out.shape[0]
    wide = rows_out * shards
    heads = dt_bias.shape[0]
    size = wide // heads
    mine = heads // groups
    inner = mine * size
    span = 2 * inner
    taps = conv_weight.shape[1]
    state2 = w_in.shape[1] - 2 * wide - heads
    channels = wide + state2
    share = channels // shards
    ratio = shards // groups
    step_cols = jnp.pad(
        lax.dynamic_slice_in_dim(w_in, 2 * wide + state2 + place * mine, mine, 1),
        ((0, 0), (0, 128 - mine)),
    )
    w_mine = jnp.concatenate(
        [
            lax.dynamic_slice_in_dim(w_in, place * span, span, 1),
            w_in[:, 2 * wide : 2 * wide + state2],
            step_cols,
        ],
        axis=1,
    )

    def rows256(a):
        flat = a.reshape(-1)
        count = -(-flat.shape[0] // 256)
        return jnp.pad(flat, (0, count * 256 - flat.shape[0])).reshape(count, 256), count

    packs = [rows256(a) for a in (norm_gain, conv_bias, gated_gain, conv_weight)]
    small = jnp.concatenate([p[0] for p in packs])
    tall = -(-small.shape[0] // 16) * 16
    small = jnp.pad(small, ((0, tall - small.shape[0]), (0, 0)))
    floats = tokens.astype(F32)
    inverse = lax.rsqrt(jnp.mean(floats * floats, axis=-1, keepdims=True) + EPSILON)
    unit = floats * inverse
    if shards == 8 and groups == 4:
        normed, cot, pj, sg, w_full, wo, small_all = gather(
            w_mine, w_out, small, tokens, cotangent, shards, groups
        )
    else:
        small_all = lax.all_gather(small, "dp", axis=0, tiled=False)
    small_all = small_all.astype(F32)
    cut = [0]
    for pack in packs:
        cut.append(cut[-1] + pack[1])

    def unpack(i, count):
        return small_all[:, cut[i] : cut[i + 1]].reshape(shards, -1)[:, :count].reshape(-1)

    norm_all = unpack(0, norm_gain.shape[0])
    conv_b = unpack(1, share)
    gain_all = unpack(2, rows_out)
    conv_w = unpack(3, share * taps).reshape(channels, taps)
    if not (shards == 8 and groups == 4):
        normed = lax.all_gather((unit * norm_all).astype(BF16), "seq", axis=1, tiled=True)
        cot = lax.all_gather(cotangent, "seq", axis=1, tiled=True)
        w_full = lax.all_gather(w_mine, "dp", axis=0, tiled=True)
        held = jnp.where(
            (owner // ratio == place) & (jnp.arange(ratio)[:, None, None] == owner % ratio),
            w_out[None],
            jnp.zeros((), BF16),
        ).reshape(inner, model)
        wo = lax.psum(held, "dp")
        sg = jnp.einsum("std,cd->stc", cot, wo, preferred_element_type=F32).astype(BF16)
        pj = jnp.einsum("std,de->ste", normed, w_full, preferred_element_type=F32).astype(BF16)

    def own(a):
        return lax.dynamic_slice_in_dim(a, place * inner, inner, 0)

    def own_heads(a):
        return lax.dynamic_slice_in_dim(a, place * mine, mine, 0)

    def pad(v):
        return jnp.pad(v, (0, 128 - mine))

    rate = -jnp.exp(own_heads(a_log))
    hp = jnp.stack([pad(own_heads(dt_bias)), pad(rate * LOG2E), pad(rate)] + [jnp.zeros(128)] * 5)
    blank = jnp.zeros((state2,), F32)
    ch = jnp.concatenate(
        [
            jnp.concatenate([own(conv_w), conv_w[wide:]]).T,
            jnp.concatenate([own(conv_b), conv_b[wide:]])[None],
            jnp.concatenate([jnp.repeat(own_heads(skip_weight), size), blank])[None],
            jnp.concatenate([own(gain_all), blank])[None],
            jnp.zeros((1, inner + state2), F32),
        ]
    )
    cols = columns(segment_ids)
    pre, ys, gn, st, red = mix_forward(pj, cols, sg, hp, ch)
    totals = lax.psum(red[:, :2], "seq")
    rho = lax.rsqrt(totals[:, 0] / wide + EPSILON)
    k2 = rho**3 * totals[:, 1] / wide
    cols2 = jnp.pad(jnp.stack([rho, k2], axis=-1), ((0, 0), (0, 0), (0, 126)))
    product = jnp.einsum("stc,cd->std", gn, wo, preferred_element_type=F32)
    product = (product * rho[:, :, None]).astype(BF16)
    result = (
        floats
        + lax.psum_scatter(product, "seq", scatter_dimension=1, tiled=True).astype(F32)
    ).astype(BF16)
    cot_rho = (cot.astype(F32) * rho[:, :, None]).astype(BF16)
    wo_grad = jnp.einsum("stc,std->cd", gn, cot_rho, preferred_element_type=F32).astype(BF16)
    wo_grad = lax.psum(wo_grad, "dp").reshape(ratio, rows_out, model)
    wo_grad = lax.dynamic_index_in_dim(wo_grad, owner % ratio, 0, False)
    wo_grad = lax.psum(jnp.where(owner // ratio == place, wo_grad, jnp.zeros((), BF16)), "seq")
    pg, chacc, hacc = mix_backward(
        pj, cols, cols2, sg, pre, ys, st, hp, ch, selectors(inner // 128)
    )
    win_grad = jnp.einsum("std,ste->de", normed, pg, preferred_element_type=F32).astype(BF16)
    win_grad = lax.psum_scatter(win_grad, "dp", scatter_dimension=0, tiled=True)
    win_grad = lax.all_gather(win_grad, "seq", axis=0, tiled=False).astype(F32)
    rows_in = win_grad.shape[1]
    w_in_grad = jnp.concatenate(
        [
            win_grad[:, :, :span].transpose(1, 0, 2).reshape(rows_in, 2 * wide),
            jnp.sum(win_grad[:, :, span : span + state2], axis=0),
            win_grad[:, :, span + state2 : span + state2 + mine]
            .transpose(1, 0, 2)
            .reshape(rows_in, heads),
        ],
        axis=1,
    )
    ngrad = jnp.einsum("ste,de->std", pg, w_full, preferred_element_type=F32).astype(BF16)
    ngrad = lax.psum_scatter(ngrad, "seq", scatter_dimension=1, tiled=True).astype(F32)
    unit_grad = ngrad * norm_all
    tokens_grad = cotangent.astype(F32) + inverse * (
        unit_grad - unit * jnp.mean(unit_grad * unit, axis=-1, keepdims=True)
    )
    chsum = jnp.sum(chacc, axis=1)
    hsum = jnp.sum(hacc, axis=1)[:, :mine]
    hsum = hsum * jnp.stack([jnp.ones((mine,)), rate, jnp.ones((mine,))])

    def spread(a, n, start):
        full = jnp.zeros(a.shape[:-1] + (n,), F32)
        return lax.dynamic_update_slice_in_dim(full, a, start, a.ndim - 1)

    chan = jnp.concatenate(
        [spread(chsum[:, :inner], wide, place * inner), chsum[:, inner:]], axis=1
    )
    packed = jnp.concatenate(
        [
            chan[: taps + 1].reshape(-1),
            chan[taps + 1, :wide],
            jnp.sum(ngrad * unit, axis=(0, 1)),
            spread(hsum, heads, place * mine).reshape(-1),
        ]
    )
    packed = lax.psum(packed, ("dp", "seq"))
    chan = packed[: (taps + 1) * channels].reshape(taps + 1, channels)
    chan = lax.dynamic_slice_in_dim(chan, owner * share, share, 1)
    at = (taps + 1) * channels
    gain_grad = lax.dynamic_slice_in_dim(packed[at : at + wide], owner * rows_out, rows_out, 0)
    at += wide
    norm_grad = lax.dynamic_slice_in_dim(packed[at : at + model], owner * rows_in, rows_in, 0)
    at += model
    return (
        result,
        tokens_grad,
        w_in_grad,
        wo_grad.astype(F32),
        chan[:taps].T,
        chan[taps],
        norm_grad,
        gain_grad,
        packed[at : at + heads],
        packed[at + heads : at + 2 * heads],
        packed[at + 2 * heads : at + 3 * heads],
    )


def solution(mesh):
    return jax.shard_map(
        local,
        mesh=mesh,
        in_specs=(
            P("dp", "seq", None),
            P("dp", None),
            P("dp", None),
            P("dp", None),
            P("dp", None),
            P("dp"),
            P("dp"),
            P("dp"),
            P(),
            P(),
            P(),
            P("dp", "seq", None),
        ),
        out_specs=(
            P("dp", "seq", None),
            P("dp", "seq", None),
            P("dp", None),
            P("dp", None),
            P("dp", None),
            P("dp"),
            P("dp"),
            P("dp"),
            P(),
            P(),
            P(),
        ),
        check_vma=False,
    )
```

```python
import functools

import jax
import jax.numpy as jnp
from jax import lax
from jax.experimental import pallas as pl
from jax.experimental.pallas import tpu as pltpu
from jax.sharding import PartitionSpec as P

Q = 128
EXACT = lax.Precision.HIGHEST
EPSILON = 1e-05
LOG2E = 1.4426950408889634
RESET = 160.0
F32 = jnp.float32
BF16 = jnp.bfloat16
LUMPS = 6
PARTS = 5
WOFF = 1
MESH = pl.DeviceIdType.MESH


def sigmoid(x):
    return 0.5 * jnp.tanh(0.5 * x) + 0.5


def softplus(x):
    return jnp.maximum(x, 0.0) + jnp.log1p(jnp.exp(-jnp.abs(x)))


def nt(a, b):
    return lax.dot_general(a, b, (((1,), (1,)), ((), ())), preferred_element_type=F32)


def mm(a, b):
    return jnp.dot(a, b, preferred_element_type=F32)


def decays(pj, cols, hp, width):
    arg = pj[0, :, width + 256 : width + 384].astype(F32) + hp[0:1, :]
    dt = softplus(arg)
    rows = lax.broadcasted_iota(jnp.int32, (Q, Q), 0)
    lanes = lax.broadcasted_iota(jnp.int32, (Q, Q), 1)
    lower = (rows >= lanes).astype(F32)
    level = jnp.dot(lower, dt * hp[1:2, :], precision=EXACT, preferred_element_type=F32)
    level = level + cols[0, :, 3:4]
    return arg, dt, level, rows, lanes


def fwd_kernel(pairs, pj, cols, sg, hp, ch, pre, ys, st, red, state, tail):
    width = pairs * 256
    inner = pairs * 128
    chunk = pl.program_id(1)

    @pl.when(chunk == 0)
    def _():
        state[...] = jnp.zeros_like(state)
        tail[...] = jnp.zeros_like(tail)

    _, dt, level, rows, lanes = decays(pj, cols, hp, width)
    level_t = level.T
    low = lanes < 64
    masks = [cols[0, :, d : d + 1] for d in range(3)]

    def conv(raw, at):
        ext = jnp.concatenate([tail[:, at : at + 128], raw], axis=0)
        total = raw * ch[3:4, at : at + 128] + ch[4:5, at : at + 128]
        for d in (1, 2, 3):
            moved = pltpu.roll(ext, d, 0)[8:]
            total = total + moved * masks[d - 1] * ch[3 - d : 4 - d, at : at + 128]
        tail[:, at : at + 128] = raw[Q - 8 :]
        pre[0, :, at : at + 128] = total
        return total * sigmoid(total)

    b_rows = conv(pj[0, :, width : width + 128].astype(F32), inner)
    c_rows = conv(pj[0, :, width + 128 : width + 256].astype(F32), inner + 128)
    b_t = b_rows.T.astype(BF16)
    b_low = b_rows.astype(BF16)
    c_low = c_rows.astype(BF16)
    scores = jnp.where(rows >= lanes, nt(c_low, b_low), 0.0)
    old = state[...].astype(BF16)
    st[0, 0] = old
    carried_all = mm(c_low, old)
    squares = jnp.zeros((Q, 128), F32)
    cross = jnp.zeros((Q, 128), F32)
    for p in range(pairs):
        at = p * 128
        one = pj[0, :, p * 256 : p * 256 + 128].astype(F32)
        two = pj[0, :, p * 256 + 128 : p * 256 + 256].astype(F32)
        z = jnp.where(low, one, pltpu.roll(two, 64, 1))
        v = jnp.where(low, pltpu.roll(one, 64, 1), two)
        xc = conv(v, at)
        l0 = jnp.broadcast_to(level[:, 2 * p : 2 * p + 1], (Q, Q))
        l1 = jnp.broadcast_to(level[:, 2 * p + 1 : 2 * p + 2], (Q, Q))
        le = jnp.where(low, l0, l1)
        dte = jnp.where(low, dt[:, 2 * p : 2 * p + 1], dt[:, 2 * p + 1 : 2 * p + 2])
        u = xc * dte
        w0 = jnp.exp2(jnp.minimum(l0 - level_t[2 * p : 2 * p + 1, :], 0.0)) * scores
        w1 = jnp.exp2(jnp.minimum(l1 - level_t[2 * p + 1 : 2 * p + 2, :], 0.0)) * scores
        wide = jnp.concatenate([w0.astype(BF16), w1.astype(BF16)], axis=1)
        blocks = jnp.concatenate(
            [jnp.where(low, u, 0.0).astype(BF16), jnp.where(low, 0.0, u).astype(BF16)], axis=0
        )
        part = mm(wide, blocks) + carried_all[:, at : at + 128] * jnp.exp2(le)
        ys[0, :, at : at + 128] = part
        gated = (part + ch[5:6, at : at + 128] * xc) * (z * sigmoid(z))
        scaled = gated * ch[6:7, at : at + 128]
        squares = squares + gated * gated
        cross = cross + sg[0, :, at : at + 128].astype(F32) * scaled
        last = le[Q - 1 : Q, :]
        ul = (u * jnp.exp2(last - le)).astype(BF16)
        state[:, at : at + 128] = state[:, at : at + 128] * jnp.exp2(last) + mm(b_t, ul)
    both = jnp.where(
        lanes == 0, jnp.sum(squares, axis=1, keepdims=True), jnp.sum(cross, axis=1, keepdims=True)
    )
    red[0] = both.T[0:8]


def mix_forward(pj, cols, sg, hp, ch, interpret=False):
    seqs, length, total = pj.shape
    width = total - 384
    inner = width // 2
    pairs = inner // 128
    chunks = length // Q

    def row(n):
        return pl.BlockSpec((1, Q, n), lambda s, c: (s, c, 0))

    def whole(a):
        return pl.BlockSpec(a.shape, lambda s, c: (0,) * a.ndim)

    return pl.pallas_call(
        functools.partial(fwd_kernel, pairs),
        grid=(seqs, chunks),
        in_specs=[row(total), row(128), row(inner), whole(hp), whole(ch)],
        out_specs=[
            row(inner + 256),
            row(inner),
            pl.BlockSpec((1, 1, 128, inner), lambda s, c: (s, c, 0, 0)),
            pl.BlockSpec((1, 8, Q), lambda s, c: (s, 0, c)),
        ],
        out_shape=[
            jax.ShapeDtypeStruct((seqs, length, inner + 256), F32),
            jax.ShapeDtypeStruct((seqs, length, inner), F32),
            jax.ShapeDtypeStruct((seqs, chunks, 128, inner), BF16),
            jax.ShapeDtypeStruct((seqs, 8, length), F32),
        ],
        scratch_shapes=[pltpu.VMEM((128, inner), F32), pltpu.VMEM((8, inner + 256), F32)],
        compiler_params=pltpu.CompilerParams(vmem_limit_bytes=48 * 2**20),
        name="mix_forward",
    )(pj, cols, sg, hp, ch)


def bwd_kernel(
    pairs, pj, cols, rk, sg, pre, ys, st, hp, ch, sel, wo, wi, pg, chacc, hacc, sct, outp, ngp,
    dstate, halo, edy_all, ul_all, sc_all,
):
    width = pairs * 256
    inner = pairs * 128
    first = (pl.program_id(0) == 0) & (pl.program_id(1) == 0)

    @pl.when(pl.program_id(1) == 0)
    def _():
        dstate[...] = jnp.zeros_like(dstate)
        halo[...] = jnp.zeros_like(halo)

    @pl.when(first)
    def _():
        chacc[...] = jnp.zeros_like(chacc)
        hacc[...] = jnp.zeros_like(hacc)

    arg, dt, level, rows, lanes = decays(pj, cols, hp, width)
    level_t = level.T
    low = lanes < 64
    masks = [cols[0, :, 3 + d : 4 + d] for d in (1, 2, 3)]
    tall = jnp.concatenate([rk[0], jnp.zeros((Q - 8, Q), F32)], axis=0).T
    rho = jnp.broadcast_to(tall[:, 0:1], (Q, 128))
    k2 = jnp.broadcast_to(tall[:, 1:2], (Q, 128))

    def fold(x):
        return jnp.sum(x.reshape(Q // 8, 8, 128), axis=0)

    def conv_back(grad, raw, at):
        ext = jnp.concatenate([grad, halo[:, at : at + 128]], axis=0)
        out = grad * ch[3:4, at : at + 128]
        chacc[3, :, at : at + 128] += fold(grad * raw)
        chacc[4, :, at : at + 128] += fold(grad)
        for d in (1, 2, 3):
            moved = pltpu.roll(ext, Q + 8 - d, 0)[:Q] * masks[d - 1]
            out = out + moved * ch[3 - d : 4 - d, at : at + 128]
            chacc[3 - d, :, at : at + 128] += fold(moved * raw)
        halo[:, at : at + 128] = grad[:8]
        return out

    pre_b = pre[0, :, inner : inner + 128]
    pre_c = pre[0, :, inner + 128 : inner + 256]
    sig_b, sig_c = sigmoid(pre_b), sigmoid(pre_c)
    b_rows, c_rows = pre_b * sig_b, pre_c * sig_c
    b_low, c_low = b_rows.astype(BF16), c_rows.astype(BF16)
    c_t = c_rows.T.astype(BF16)
    upper = lanes >= rows
    scores = jnp.where(upper, nt(b_low, c_low), 0.0)
    dlow = dstate[...].astype(BF16)
    dsb_all = mm(b_low, dlow)
    dscores = jnp.zeros((Q, Q), F32)
    sums = jnp.zeros((6 * Q, 128), F32)
    keep = jnp.zeros((8, 128), F32)
    for p in range(pairs):
        at = p * 128
        one = pj[0, :, p * 256 : p * 256 + 128].astype(F32)
        two = pj[0, :, p * 256 + 128 : p * 256 + 256].astype(F32)
        z = jnp.where(low, one, pltpu.roll(two, 64, 1))
        v = jnp.where(low, pltpu.roll(one, 64, 1), two)
        pr = pre[0, :, at : at + 128]
        sp = sigmoid(pr)
        xc = pr * sp
        l0 = jnp.broadcast_to(level[:, 2 * p : 2 * p + 1], (Q, Q))
        l1 = jnp.broadcast_to(level[:, 2 * p + 1 : 2 * p + 2], (Q, Q))
        le = jnp.where(low, l0, l1)
        dte = jnp.where(low, dt[:, 2 * p : 2 * p + 1], dt[:, 2 * p + 1 : 2 * p + 2])
        u = xc * dte
        skip = ch[5:6, at : at + 128]
        part = ys[0, :, at : at + 128]
        y = part + skip * xc
        sz = sigmoid(z)
        silz = z * sz
        gated = y * silz
        graw = sg[0, :, at : at + 128].astype(F32)
        scaled_rho = graw * rho
        scaled = gated * rho * ch[6:7, at : at + 128]
        sct[at : at + 128, :] = scaled.T.astype(BF16)
        sc_all[:, at : at + 128] = scaled.astype(BF16)
        gg = scaled_rho * ch[6:7, at : at + 128] - k2 * gated
        dy = gg * silz
        dz = gg * y * (sz + silz * (1.0 - sz))
        ulow = u.astype(BF16)
        dylow = dy.astype(BF16)
        w0 = jnp.exp2(jnp.minimum(level_t[2 * p : 2 * p + 1, :] - l0, 0.0))
        w1 = jnp.exp2(jnp.minimum(level_t[2 * p + 1 : 2 * p + 2, :] - l1, 0.0))
        wide = jnp.concatenate([(w0 * scores).astype(BF16), (w1 * scores).astype(BF16)], axis=1)
        dyb = jnp.concatenate(
            [jnp.where(low, dy, 0.0).astype(BF16), jnp.where(low, 0.0, dy).astype(BF16)], axis=0
        )
        ub = jnp.concatenate(
            [jnp.where(low, u, 0.0).astype(BF16), jnp.where(low, 0.0, u).astype(BF16)], axis=0
        )
        duw = mm(wide, dyb)
        gt = nt(ub, dylow)
        dscores = dscores + w0 * gt[:Q] + w1 * gt[Q:]
        last = le[Q - 1 : Q, :]
        lve = jnp.exp2(last - le)
        edy = (dy * jnp.exp2(le)).astype(BF16)
        ul = (u * lve).astype(BF16)
        edy_all[:, at : at + 128] = edy
        ul_all[:, at : at + 128] = ul
        dsb = dsb_all[:, at : at + 128]
        du = duw + lve * dsb
        r1 = dylow.astype(F32) * part - ulow.astype(F32) * duw
        r2 = ul.astype(F32) * dsb
        r1h, r2h = r1.astype(BF16), r2.astype(BF16)
        stacked = jnp.concatenate(
            [
                r1h,
                (r1 - r1h.astype(F32)).astype(BF16),
                r2h,
                (r2 - r2h.astype(F32)).astype(BF16),
                (dy * xc).astype(BF16),
                (du * xc).astype(BF16),
            ],
            axis=0,
        )
        sums = sums + mm(stacked, sel[p])
        decay = jnp.exp2(last)
        kept = fold(dlow[:, at : at + 128].astype(F32) * st[0, 0, :, at : at + 128].astype(F32)) * decay
        kept_high = kept.astype(BF16)
        keep = keep + mm(kept_high, sel[p]) + mm((kept - kept_high.astype(F32)).astype(BF16), sel[p])
        dstate[:, at : at + 128] = dstate[:, at : at + 128] * decay + mm(c_t, edy)
        dv = conv_back((du * dte + skip * dy) * (sp + xc * (1.0 - sp)), v, at)
        pg[0, :, p * 256 : p * 256 + 128] = jnp.where(low, dz, pltpu.roll(dv, 64, 1)).astype(BF16)
        pg[0, :, p * 256 + 128 : p * 256 + 256] = jnp.where(low, pltpu.roll(dz, 64, 1), dv).astype(BF16)
    dsc = jnp.where(upper, dscores, 0.0)
    db = mm(dsc.astype(BF16), c_low) + nt(ul_all[...], dlow)
    dc = mm(dsc.T.astype(BF16), b_low) + nt(edy_all[...], st[0, 0])
    raw_b = pj[0, :, width : width + 128].astype(F32)
    raw_c = pj[0, :, width + 128 : width + 256].astype(F32)
    pg[0, :, width : width + 128] = conv_back(
        db * (sig_b + b_rows * (1.0 - sig_b)), raw_b, inner
    ).astype(BF16)
    pg[0, :, width + 128 : width + 256] = conv_back(
        dc * (sig_c + c_rows * (1.0 - sig_c)), raw_c, inner + 128
    ).astype(BF16)
    r1 = sums[:Q] + sums[Q : 2 * Q]
    r2 = sums[2 * Q : 3 * Q] + sums[3 * Q : 4 * Q]
    da = (
        jnp.dot(upper.astype(F32), r1, precision=EXACT, preferred_element_type=F32)
        + jnp.dot((rows > lanes).astype(F32), r2, precision=EXACT, preferred_element_type=F32)
        + jnp.sum(keep, axis=0, keepdims=True)
    )
    ddt = da * hp[2:3, :] + sums[5 * Q :]
    ds = ddt * sigmoid(arg)
    pg[0, :, width + 256 : width + 384] = ds.astype(BF16)
    hacc[0] += fold(ds)
    hacc[1] += fold(da * dt)
    hacc[2] += fold(sums[4 * Q : 5 * Q])
    outp[0] = mm(sc_all[...], wo[...]).astype(BF16)
    ngp[0] = nt(pg[0], wi[...]).astype(BF16)


def mix_backward(pj, cols, rk, sg, pre, ys, st, hp, ch, sel, wo, wi):
    seqs, length, total = pj.shape
    width = total - 384
    inner = width // 2
    pairs = inner // 128
    chunks = length // Q
    model = wo.shape[1]

    def row(n):
        return pl.BlockSpec((1, Q, n), lambda s, c: (s, chunks - 1 - c, 0))

    def whole(shape):
        return pl.BlockSpec(shape, lambda s, c: (0,) * len(shape))

    return pl.pallas_call(
        functools.partial(bwd_kernel, pairs),
        grid=(seqs, chunks),
        in_specs=[
            row(total),
            row(128),
            pl.BlockSpec((1, 8, Q), lambda s, c: (s, 0, chunks - 1 - c)),
            row(inner),
            row(inner + 256),
            row(inner),
            pl.BlockSpec((1, 1, 128, inner), lambda s, c: (s, chunks - 1 - c, 0, 0)),
            whole(hp.shape),
            whole(ch.shape),
            whole(sel.shape),
            whole(wo.shape),
            whole(wi.shape),
        ],
        out_specs=[
            row(total),
            whole((5, 8, inner + 256)),
            whole((3, 8, 128)),
            pl.BlockSpec((inner, Q), lambda s, c: (0, s * chunks + chunks - 1 - c)),
            row(model),
            row(model),
        ],
        out_shape=[
            jax.ShapeDtypeStruct((seqs, length, total), BF16),
            jax.ShapeDtypeStruct((5, 8, inner + 256), F32),
            jax.ShapeDtypeStruct((3, 8, 128), F32),
            jax.ShapeDtypeStruct((inner, seqs * length), BF16),
            jax.ShapeDtypeStruct((seqs, length, model), BF16),
            jax.ShapeDtypeStruct((seqs, length, model), BF16),
        ],
        scratch_shapes=[
            pltpu.VMEM((128, inner), F32),
            pltpu.VMEM((8, inner + 256), F32),
            pltpu.VMEM((Q, inner), BF16),
            pltpu.VMEM((Q, inner), BF16),
            pltpu.VMEM((Q, inner), BF16),
        ],
        compiler_params=pltpu.CompilerParams(vmem_limit_bytes=48 * 2**20),
        name="mix_backward",
    )(pj, cols, rk, sg, pre, ys, st, hp, ch, sel, wo, wi)


def columns(seg):
    seqs, length = seg.shape
    back = [
        jnp.pad((seg[:, d:] == seg[:, :-d]).astype(F32), ((0, 0), (d, 0))) for d in (1, 2, 3)
    ]
    ahead = [
        jnp.pad((seg[:, d:] == seg[:, :-d]).astype(F32), ((0, 0), (0, d))) for d in (1, 2, 3)
    ]
    ends = seg.reshape(seqs, length // Q, Q)[:, :, -1]
    before = jnp.pad(ends[:, :-1], ((0, 0), (1, 0)))
    level = -RESET * (seg.reshape(seqs, length // Q, Q) - before[:, :, None]).astype(F32)
    stacked = jnp.stack([*back, level.reshape(seqs, length), *ahead], axis=-1)
    return jnp.pad(stacked, ((0, 0), (0, 0), (0, 121)))


def selectors(pairs):
    lane = lax.broadcasted_iota(jnp.int32, (pairs, 128, 128), 1)
    pair = lax.broadcasted_iota(jnp.int32, (pairs, 128, 128), 0)
    out = lax.broadcasted_iota(jnp.int32, (pairs, 128, 128), 2)
    return (out == 2 * pair + lane // 64).astype(BF16)


def norm_kernel(wide, red, rk, got, ssem, rsem):
    d = lax.axis_index("dp")
    s = lax.axis_index("seq")
    groups = got.shape[0]
    bar = pltpu.get_barrier_semaphore()
    for j in range(1, groups):
        pl.semaphore_signal(bar, inc=1, device_id=(d, lax.rem(s + j, groups)), device_id_type=MESH)
    pl.semaphore_wait(bar, groups - 1)
    sends = [
        pltpu.make_async_remote_copy(
            src_ref=red, dst_ref=got.at[j], send_sem=ssem.at[j], recv_sem=rsem.at[j],
            device_id=(d, lax.rem(s + j, groups)), device_id_type=MESH,
        )
        for j in range(1, groups)
    ]
    for copy in sends:
        copy.start()
    total = red[...]
    for j, copy in enumerate(sends):
        copy.wait()
        total = total + got[j + 1]
    rho = lax.rsqrt(total[:, 0:1] / wide + EPSILON)
    rk[...] = jnp.concatenate(
        [rho, rho * rho * rho * total[:, 1:2] / wide, jnp.zeros_like(total[:, 2:])], axis=1
    )


def norms(red, wide, groups):
    vmem = pl.BlockSpec(memory_space=pltpu.VMEM)
    return pl.pallas_call(
        functools.partial(norm_kernel, wide),
        in_specs=[vmem],
        out_specs=vmem,
        out_shape=jax.ShapeDtypeStruct(red.shape, F32),
        scratch_shapes=[
            pltpu.VMEM((groups, *red.shape), F32),
            pltpu.SemaphoreType.DMA((groups,)),
            pltpu.SemaphoreType.DMA((groups,)),
        ],
        compiler_params=pltpu.CompilerParams(collective_id=3, has_side_effects=True),
        name="norms",
    )(red)


def gather_kernel(
    dims, wm, wo_in, small_in, tok_in, cot_in,
    turned_o, cot_o, pj_o, sg_o, w_o, wo_o, small_o,
    tok, cot, wbig, wo, small, pjv, sgv, turned,
    szu, szd, rz, sy, ry, wsu, wsd, wrz, wsy, wry, bx_s, bx_r, bc_s, bc_r, loc, out,
):
    deep, pieces, rows, inner, part, length = dims
    d = lax.axis_index("dp")
    s = lax.axis_index("seq")
    z = d // 2
    y = d % 2
    top = deep - 1
    up, down, side = (d + 2, s), (d - 2, s), (d + 1 - 2 * y, s)
    across, twin = (d, s + 2 - 4 * (s // 2)), (d, s + 1 - 2 * (s % 2))
    opposite = across[1]

    bar = pltpu.get_barrier_semaphore()

    @pl.when(z < top)
    def _():
        pl.semaphore_signal(bar, inc=1, device_id=up, device_id_type=MESH)

    @pl.when(z > 0)
    def _():
        pl.semaphore_signal(bar, inc=1, device_id=down, device_id_type=MESH)

    for who in (side, across, twin):
        pl.semaphore_signal(bar, inc=1, device_id=who, device_id_type=MESH)
    pl.semaphore_wait(bar, 3 + jnp.minimum(z, 1) + jnp.minimum(top - z, 1))

    def send(src, dst, ssem, rsem, who):
        return pltpu.make_async_remote_copy(
            src_ref=src, dst_ref=dst, send_sem=ssem, recv_sem=rsem,
            device_id=who, device_id_type=MESH,
        )

    width = 2 * inner

    def cols(k):
        return pl.ds(width, 384) if k == 1 else pl.ds((k - 2) * 256, 256)

    def held(k, owner):
        if k == 0:
            return small.at[owner]
        return wbig.at[pl.ds(pl.multiple_of(owner * rows, 16), rows), cols(k)]

    def source(k):
        return small_in.at[...] if k == 0 else wm.at[:, cols(k)]

    def own_send(k):
        src, dst = source(k), held(k, d)

        @pl.when(z < top)
        def _():
            send(src, dst, szu.at[k, z], rz.at[k, z], up).start()

        @pl.when(z > 0)
        def _():
            send(src, dst, szd.at[k, z], rz.at[k, z], down).start()

        send(src, dst, sy.at[k, z], ry.at[k, z], side).start()

    def hop(k, h):
        below, above = z - h, z + h

        @pl.when(below >= 0)
        def _():
            ref = held(k, below * 2 + y)
            send(ref, ref, szu.at[k, below], rz.at[k, below], up).wait_recv()

            @pl.when(z < top)
            def _():
                send(ref, ref, szu.at[k, below], rz.at[k, below], up).start()

            send(ref, ref, sy.at[k, below], ry.at[k, below], side).start()

        @pl.when(above <= top)
        def _():
            ref = held(k, above * 2 + y)
            send(ref, ref, szd.at[k, above], rz.at[k, above], down).wait_recv()

            @pl.when(z > 0)
            def _():
                send(ref, ref, szd.at[k, above], rz.at[k, above], down).start()

            send(ref, ref, sy.at[k, above], ry.at[k, above], side).start()

    def arrive(k):
        for e in range(deep):
            ref = held(k, e * 2 + 1 - y)
            send(ref, ref, sy.at[k, e], ry.at[k, e], side).wait_recv()

    def own_copy(src, dst, sem):
        return pltpu.make_async_copy(src, dst, sem)

    here = pl.multiple_of(s * part, 16)
    there = pl.multiple_of(opposite * part, 16)
    locals_ = [
        own_copy(small_in, small.at[d], loc.at[0]),
        own_copy(wm, wbig.at[pl.ds(pl.multiple_of(d * rows, 16), rows)], loc.at[1]),
    ]
    for q in range(2):
        locals_.append(own_copy(tok_in.at[q], tok.at[q, pl.ds(here, part)], loc.at[2 + q]))
        locals_.append(own_copy(cot_in.at[q], cot.at[q, pl.ds(here, part)], loc.at[4 + q]))
    half = wo_in.shape[0]
    mine = z == s

    def root_copy():
        return own_copy(wo_in, wo.at[pl.ds(pl.multiple_of(y * half, 16), half)], loc.at[6])

    def block_sends(which, src, dst, q):
        spot = dst.at[q, pl.ds(here, part)]
        i = which * 2 + q
        send(src.at[q], spot, bx_s.at[i], bx_r.at[i], across).start()
        send(src.at[q], spot, bc_s.at[0, i], bc_r.at[0, i], twin).start()

    def block_forward(which, dst, q):
        spot = dst.at[q, pl.ds(there, part)]
        i = which * 2 + q
        send(spot, spot, bx_s.at[i], bx_r.at[i], across).wait_recv()
        send(spot, spot, bc_s.at[1, i], bc_r.at[1, i], twin).start()

    def block_arrive(which, dst, q):
        i = which * 2 + q
        for n in range(2):
            spot = dst.at[q, pl.ds(here, part)]
            send(spot, spot, bc_s.at[n, i], bc_r.at[n, i], twin).wait_recv()

    lump = half // LUMPS

    def wo_piece(i, col):
        m = col * LUMPS + i
        return m, wo.at[pl.ds(pl.multiple_of(m * lump, 16), lump)]

    def wo_send(i, src=None):
        m, ref = wo_piece(i, y)
        src = ref if src is None else src

        @pl.when((z >= s) & (z < top))
        def _():
            send(src, ref, wsu.at[m], wrz.at[m], up).start()

        @pl.when((z <= s) & (z > 0))
        def _():
            send(src, ref, wsd.at[m], wrz.at[m], down).start()

        send(src, ref, wsy.at[m], wry.at[m], side).start()

    def wo_root(i):
        @pl.when(mine)
        def _():
            wo_send(i, wo_in.at[pl.ds(i * lump, lump)])

    def wo_hop(i, h):
        @pl.when((z - s == h) | (s - z == h))
        def _():
            m, ref = wo_piece(i, y)
            send(ref, ref, wsu.at[m], wrz.at[m], up).wait_recv()
            wo_send(i)

    def wo_arrive(i):
        m, ref = wo_piece(i, 1 - y)
        send(ref, ref, wsy.at[m], wry.at[m], side).wait_recv()

    tile = 256

    def project(k):
        c = cols(k)

        def step(i, _):
            q, r = i // (length // tile), i % (length // tile)
            at = pl.multiple_of(r * tile, tile)
            pjv[q, pl.ds(at, tile), c] = mm(tok[q, pl.ds(at, tile), :], wbig[:, c]).astype(BF16)
            return 0

        lax.fori_loop(0, 2 * length // tile, step, 0)
        own_copy(pjv.at[:, :, c], pj_o.at[:, :, c], out.at[k]).start()

    for c in locals_:
        c.start()

    @pl.when(mine)
    def _():
        root_copy().start()

    for q in range(2):
        block_sends(0, tok_in, tok, q)
    ahead = 3
    for k in range(ahead):
        own_send(k)
    done = []

    def hops(t):
        for h in range(1, deep):
            if 0 <= t - h < pieces:
                hop(t - h, h)
        for h in range(1, deep):
            if 0 <= t - h - WOFF < LUMPS:
                wo_hop(t - h - WOFF, h)
        if 0 <= t - WOFF < LUMPS:
            wo_root(t - WOFF)
        if ahead <= t + ahead - 1 < pieces:
            own_send(t + ahead - 1)

    steps = max(pieces, WOFF + LUMPS) + deep - 1
    count = dict(next=1)

    def ready(n):
        for _ in range(n):
            if count["next"] < pieces:
                arrive(count["next"])
                project(count["next"])
                count["next"] += 1

    share = tok.shape[2] // (2 * deep)

    def norm_step(i, _):
        q, r = i // (length // 64), i % (length // 64)
        at = pl.multiple_of(r * 64, 64)
        x = tok[q, pl.ds(at, 64), :].astype(F32)
        inv = lax.rsqrt(jnp.mean(x * x, axis=1, keepdims=True) + EPSILON)
        gains = jnp.concatenate([small[e, 0:1, :share] for e in range(2 * deep)], axis=1)
        tok[q, pl.ds(at, 64), :] = (x * inv * gains.astype(F32)).astype(BF16)
        return 0

    for t in range(1, steps):
        hops(t)
        if t == 3:
            block_forward(0, tok, 0)
        if t == 6:
            block_forward(0, tok, 1)
            for q in range(2):
                block_sends(1, cot_in, cot, q)
        if t == 7:
            for i in (0, 1, 2, 4):
                locals_[i].wait()
            block_arrive(0, tok, 0)
            block_arrive(0, tok, 1)
            for q in range(2):
                spot = tok.at[q, pl.ds(there, part)]
                send(spot, spot, bc_s.at[1, q], bc_r.at[1, q], twin).wait_send()
            arrive(0)
            own_copy(small, small_o, out.at[0]).start()
            lax.fori_loop(0, 2 * length // 64, norm_step, 0)
        if t > 7:
            ready(1)
    for i in range(LUMPS):
        wo_arrive(i)

    @pl.when(mine)
    def _():
        root_copy().wait()

    block_forward(1, cot, 0)
    ready(pieces)
    own_copy(wbig, w_o, out.at[pieces + 1]).start()
    own_copy(wo, wo_o, out.at[pieces + 2]).start()

    def turn_step(i, _):
        q, r = i // (length // tile), i % (length // tile)
        at = pl.multiple_of(r * tile, tile)
        to = pl.multiple_of(i * tile, tile)
        for j in range(0, tok.shape[2], 128):
            turned[j : j + 128, pl.ds(to, tile)] = tok[q, pl.ds(at, tile), j : j + 128].T
        return 0

    lax.fori_loop(0, 2 * length // tile, turn_step, 0)
    own_copy(turned, turned_o, out.at[pieces]).start()
    block_forward(1, cot, 1)
    locals_[3].wait()
    locals_[5].wait()
    block_arrive(1, cot, 0)
    block_arrive(1, cot, 1)
    own_copy(cot, cot_o, out.at[pieces + 3]).start()

    def grad_step(i, _):
        q, r = i // (length // tile), i % (length // tile)
        at = pl.multiple_of(r * tile, tile)
        sgv[q, pl.ds(at, tile), :] = nt(cot[q, pl.ds(at, tile), :], wo[...]).astype(BF16)
        return 0

    lax.fori_loop(0, 2 * length // tile, grad_step, 0)
    own_copy(sgv, sg_o, out.at[pieces + 4]).start()

    for k in range(pieces):
        for e in range(deep):
            ref = held(k, e * 2 + y)

            @pl.when((z >= e) & (z < top))
            def _():
                send(ref, ref, szu.at[k, e], rz.at[k, e], up).wait_send()

            @pl.when((z <= e) & (z > 0))
            def _():
                send(ref, ref, szd.at[k, e], rz.at[k, e], down).wait_send()

            send(ref, ref, sy.at[k, e], ry.at[k, e], side).wait_send()
    for i in range(LUMPS):
        m, ref = wo_piece(i, y)

        @pl.when((z >= s) & (z < top))
        def _():
            send(ref, ref, wsu.at[m], wrz.at[m], up).wait_send()

        @pl.when((z <= s) & (z > 0))
        def _():
            send(ref, ref, wsd.at[m], wrz.at[m], down).wait_send()

        send(ref, ref, wsy.at[m], wry.at[m], side).wait_send()
    for which, dst in ((0, tok), (1, cot)):
        for q in range(2):
            i = which * 2 + q
            spot = dst.at[q, pl.ds(here, part)]
            send(spot, spot, bx_s.at[i], bx_r.at[i], across).wait_send()
            for n in range(1 + which):
                send(spot, spot, bc_s.at[n, i], bc_r.at[n, i], twin).wait_send()
    own_copy(small, small_o, out.at[0]).wait()
    for k in range(1, pieces):
        own_copy(pjv.at[:, :, cols(k)], pj_o.at[:, :, cols(k)], out.at[k]).wait()
    own_copy(turned, turned_o, out.at[pieces]).wait()
    own_copy(wbig, w_o, out.at[pieces + 1]).wait()
    own_copy(wo, wo_o, out.at[pieces + 2]).wait()
    own_copy(cot, cot_o, out.at[pieces + 3]).wait()
    own_copy(sgv, sg_o, out.at[pieces + 4]).wait()


def gather(wm, w_out, small, tokens, cotangent, shards, groups):
    rows, total = wm.shape
    width = total - 384
    inner = width // 2
    seqs, part, model = tokens.shape
    length = part * groups
    deep = shards // 2
    pairs = inner // 128
    pieces = pairs + 2
    any_ = pl.BlockSpec(memory_space=pl.ANY)
    dma = pltpu.SemaphoreType.DMA
    small_rows, small_cols = small.shape
    full = (shards * rows, total)
    shapes = [
        (model, seqs * length), (seqs, length, model), (seqs, length, total), (seqs, length, inner),
        full, (inner, model), (shards, small_rows, small_cols),
    ]
    return pl.pallas_call(
        functools.partial(gather_kernel, (deep, pieces, rows, inner, part, length)),
        in_specs=[any_] * 5,
        out_specs=[any_] * 7,
        out_shape=[jax.ShapeDtypeStruct(n, BF16) for n in shapes],
        scratch_shapes=[
            pltpu.VMEM(shapes[1], BF16),
            pltpu.VMEM(shapes[1], BF16),
            pltpu.VMEM(full, BF16),
            pltpu.VMEM((inner, model), BF16),
            pltpu.VMEM(shapes[6], BF16),
            pltpu.VMEM(shapes[2], BF16),
            pltpu.VMEM(shapes[3], BF16),
            pltpu.VMEM(shapes[0], BF16),
            dma((pieces, deep)), dma((pieces, deep)), dma((pieces, deep)),
            dma((pieces, deep)), dma((pieces, deep)),
            *[dma((2 * LUMPS,))] * 5,
            dma((4,)), dma((4,)), dma((2, 4)), dma((2, 4)),
            dma((7,)), dma((pieces + 5,)),
        ],
        compiler_params=pltpu.CompilerParams(
            collective_id=1, has_side_effects=True, vmem_limit_bytes=56 * 2**20
        ),
        name="gather_project",
    )(wm, w_out, small, tokens, cotangent)


def greet(z, top, up, down, others):
    bar = pltpu.get_barrier_semaphore()

    @pl.when(z < top)
    def _():
        pl.semaphore_signal(bar, inc=1, device_id=up, device_id_type=MESH)

    @pl.when(z > 0)
    def _():
        pl.semaphore_signal(bar, inc=1, device_id=down, device_id_type=MESH)

    for who in others:
        pl.semaphore_signal(bar, inc=1, device_id=who, device_id_type=MESH)
    pl.semaphore_wait(bar, len(others) + jnp.minimum(z, 1) + jnp.minimum(top - z, 1))


def send(src, dst, ssem, rsem, who):
    return pltpu.make_async_remote_copy(
        src_ref=src, dst_ref=dst, send_sem=ssem, recv_sem=rsem, device_id=who, device_id_type=MESH
    )


def add_into(dst, src):
    count = dst.shape[0]
    some = next(n for n in (64, 48, 32, 16) if count % n == 0)

    def step(i, _):
        at = pl.ds(pl.multiple_of(i * some, 16), some)
        dst[at, :] = (dst[at, :].astype(F32) + src[at, :].astype(F32)).astype(BF16)
        return 0

    lax.fori_loop(0, count // some, step, 0)


def scatter_kernel(
    dims, nt_in, pg_in, st_in, cot_in, outp, ngp,
    gw_o, wo_o, out_o, ng_o,
    nt_v, pg_v, st_v, cot_v, pv, yb, zb, gath, tw, xr, stage, gw, ybw, zbw, wof,
    sy, ry, su, sd, rz, gx_s, gx_r, gc_s, gc_r, tw_s, tw_r, xr_s, xr_r,
    wy_s, wy_r, wu_s, wd_s, wz_r, bx_s, bx_r, bc_s, bc_r, loc, stg, out,
):
    deep, rows, part = dims
    d = lax.axis_index("dp")
    s = lax.axis_index("seq")
    z = d // 2
    y = d % 2
    x = s // 2
    c = s % 2
    top = deep - 1
    up, down, side = (d + 2, s), (d - 2, s), (d + 1 - 2 * y, s)
    across, twin = (d, s + 2 - 4 * x), (d, s + 1 - 2 * c)
    greet(z, top, up, down, (side, across, twin))
    wide = pv.shape[1] // PARTS

    def cut(k):
        return pl.ds(k * wide, wide)

    def lines(ref, i, count=rows):
        return ref.at[pl.ds(pl.multiple_of(i * count, 16), count)]

    loads = [
        pltpu.make_async_copy(nt_in, nt_v, loc.at[0]),
        *[
            pltpu.make_async_copy(pg_in.at[:, cut(k)], pg_v.at[:, cut(k)], loc.at[3 + k])
            for k in range(PARTS)
        ],
        pltpu.make_async_copy(st_in, st_v, loc.at[1]),
        pltpu.make_async_copy(cot_in, cot_v, loc.at[2]),
    ]
    for load in loads:
        load.start()

    both = ((0, outp, out_o), (1, ngp, ng_o))

    def token_rows(owner):
        return pl.ds(pl.multiple_of(owner * part, 16), part)

    def twin_send(n, ref, turn, q):
        half = 1 - x if turn == 0 else x
        return send(
            ref.at[q, token_rows(2 * half + 1 - c)], tw.at[n, turn, q],
            tw_s.at[n, turn, q], tw_r.at[n, turn, q], twin,
        )

    for n, ref, _ in both:
        for turn in range(2):
            for q in range(2):
                twin_send(n, ref, turn, q).start()

    def stage_copy(n, ref, turn, q):
        half = 1 - x if turn == 0 else x
        return pltpu.make_async_copy(ref.at[q, token_rows(2 * half + c)], stage.at[q], stg.at[q])

    def pair_sum(n, ref, turn):
        for q in range(2):
            stage_copy(n, ref, turn, q).start()
        for q in range(2):
            twin_send(n, ref, turn, q).wait_recv()
            stage_copy(n, ref, turn, q).wait()
            add_into(tw.at[n, turn, q], stage.at[q])

    def x_send(n, q):
        return send(tw.at[n, 0, q], xr.at[n, q], xr_s.at[n, q], xr_r.at[n, q], across)

    def x_start(n, ref):
        pair_sum(n, ref, 0)
        for q in range(2):
            x_send(n, q).start()

    def x_finish(n, dst):
        for q in range(2):
            x_send(n, q).wait_recv()
            add_into(xr.at[n, q], tw.at[n, 1, q])
            pltpu.make_async_copy(xr.at[n, q], dst.at[q], out.at[2 + 2 * n + q]).start()

    def weigh(k):
        def step(i, _):
            at = pl.ds(pl.multiple_of(i * rows, 16), rows)
            pv[at, cut(k)] = mm(nt_v[at, :], pg_v[:, cut(k)]).astype(BF16)
            return 0

        lax.fori_loop(0, 2 * deep, step, 0)

    def block(e, k):
        return pv.at[pl.ds(pl.multiple_of((2 * e + y) * rows, 16), rows), cut(k)]

    def y_send(k, e):
        src = pv.at[pl.ds(pl.multiple_of((2 * e + 1 - y) * rows, 16), rows), cut(k)]
        return send(src, lines(yb, e).at[:, cut(k)], sy.at[k, e], ry.at[k, e], side)

    def y_start(k):
        for e in range(deep):
            y_send(k, e).start()

    def y_add(k):
        for e in range(deep):
            y_send(k, e).wait_recv()
            add_into(block(e, k), lines(yb, e).at[:, cut(k)])

    def z_send(k, e, slot, sem, who):
        return send(block(e, k), lines(zb, slot).at[:, cut(k)], sem.at[k, e], rz.at[k, slot], who)

    def hop(k, h):
        @pl.when(z == h - 1)
        def _():
            for e in range(top, h - 1, -1):
                if h > 1:
                    z_send(k, e, e, su, up).wait_recv()
                    add_into(block(e, k), lines(zb, e).at[:, cut(k)])
                z_send(k, e, e, su, up).start()

        @pl.when(z == deep - h)
        def _():
            for e in range(deep - h):
                if h > 1:
                    z_send(k, e, e, sd, down).wait_recv()
                    add_into(block(e, k), lines(zb, e).at[:, cut(k)])
                z_send(k, e, deep if e == deep - h - 1 else e, sd, down).start()

    def g_spot(who, k):
        return gath.at[who, :, cut(k)]

    def finish(k):
        mine = block(z, k)

        @pl.when(z > 0)
        def _():
            z_send(k, z, z, su, up).wait_recv()
            add_into(mine, lines(zb, z).at[:, cut(k)])

        @pl.when(z < top)
        def _():
            z_send(k, z, deep, sd, down).wait_recv()
            add_into(mine, lines(zb, deep).at[:, cut(k)])

        send(mine, g_spot(s, k), gx_s.at[k], gx_r.at[k], across).start()
        send(mine, g_spot(s, k), gc_s.at[0, k], gc_r.at[0, k], twin).start()
        pltpu.make_async_copy(mine, g_spot(s, k), loc.at[3 + k]).start()

    def spread(k):
        spot = g_spot(across[1], k)
        send(spot, spot, gx_s.at[k], gx_r.at[k], across).wait_recv()
        send(spot, spot, gc_s.at[1, k], gc_r.at[1, k], twin).start()

    half = gw.shape[0] // 2
    lump = half // LUMPS

    def w_rows(col, i):
        return gw.at[pl.ds(pl.multiple_of(col * half + i * lump, 16), lump)]

    def piece(ref, i):
        return ref.at[pl.ds(i * lump, lump)]

    def wy_send(i):
        return send(w_rows(1 - y, i), piece(ybw, i), wy_s.at[i], wy_r.at[i], side)

    def w_compute():
        tall = 128

        def step(i, _):
            at = pl.ds(pl.multiple_of(i * tall, 16), tall)
            for j in range(0, cot_v.shape[1], 512):
                gw[at, j : j + 512] = mm(st_v[at, :], cot_v[:, j : j + 512]).astype(BF16)
            return 0

        lax.fori_loop(0, gw.shape[0] // tall, step, 0)
        for i in range(LUMPS):
            wy_send(i).start()

    def from_below(i):
        return send(w_rows(y, i), piece(zbw.at[0], i), wu_s.at[i], wz_r.at[0, i], up)

    def from_above(i):
        return send(w_rows(y, i), piece(zbw.at[1], i), wd_s.at[i], wz_r.at[1, i], down)

    def w_cast(i, who, ssem, rsem):
        return send(piece(wof, i), piece(wof, i), ssem.at[i], rsem.at[i], who)

    root = z == s

    def w_chain(i):
        wy_send(i).wait_recv()
        add_into(w_rows(y, i), piece(ybw, i))

        @pl.when((z <= s) & (z > 0))
        def _():
            from_below(i).wait_recv()
            add_into(w_rows(y, i), piece(zbw.at[0], i))

        @pl.when((z >= s) & (z < top))
        def _():
            from_above(i).wait_recv()
            add_into(w_rows(y, i), piece(zbw.at[1], i))

        @pl.when(z < s)
        def _():
            from_below(i).start()

        @pl.when(z > s)
        def _():
            from_above(i).start()

        @pl.when(root)
        def _():
            piece(wof, i)[...] = w_rows(y, i)[...]
            w_cast(i, across, bx_s, bx_r).start()
            w_cast(i, twin, bc_s, bc_r).start()

    def w_spread(i):
        @pl.when(across[1] == z)
        def _():
            w_cast(i, across, bx_s, bx_r).wait_recv()
            w_cast(i, twin, bc_s, bc_r).start()

        @pl.when((across[1] != z) & jnp.logical_not(root))
        def _():
            w_cast(i, twin, bc_s, bc_r).wait_recv()

    loads[0].wait()
    for t in range(PARTS):
        loads[1 + t].wait()
        weigh(t)
        y_start(t)
        if t == 0:
            x_start(0, outp)
            x_start(1, ngp)
        if t > 0:
            y_add(t - 1)
        for h in range(1, deep):
            if t - h >= 0:
                hop(t - h, h)
        if t - deep >= 0:
            finish(t - deep)
    loads[1 + PARTS].wait()
    loads[2 + PARTS].wait()
    w_compute()
    pair_sum(0, outp, 1)
    pair_sum(1, ngp, 1)
    for t in range(PARTS, PARTS + deep + 1):
        if t == PARTS:
            y_add(t - 1)
        for h in range(1, deep):
            if 0 <= t - h < PARTS:
                hop(t - h, h)
        if 0 <= t - deep < PARTS:
            finish(t - deep)
        if 0 <= t - deep - 1 < PARTS:
            spread(t - deep - 1)
    x_finish(0, out_o)
    for i in range(LUMPS):
        w_chain(i)
    x_finish(1, ng_o)
    for i in range(LUMPS):
        w_spread(i)
    wo_copy = pltpu.make_async_copy(wof, wo_o, out.at[1])
    wo_copy.start()
    for k in range(PARTS):
        for n in range(2):
            spot = g_spot(twin[1], k)
            send(spot, spot, gc_s.at[n, k], gc_r.at[n, k], twin).wait_recv()
        pltpu.make_async_copy(g_spot(s, k), g_spot(s, k), loc.at[3 + k]).wait()
    gw_copy = pltpu.make_async_copy(gath, gw_o, out.at[0])
    gw_copy.start()
    for n, ref, dst in both:
        for q in range(2):
            for turn in range(2):
                twin_send(n, ref, turn, q).wait_send()
            x_send(n, q).wait_send()
            pltpu.make_async_copy(xr.at[n, q], dst.at[q], out.at[2 + 2 * n + q]).wait()
    for k in range(PARTS):
        for e in range(deep):
            y_send(k, e).wait_send()

            @pl.when(z < e)
            def _():
                z_send(k, e, e, su, up).wait_send()

            @pl.when(z > e)
            def _():
                z_send(k, e, e, sd, down).wait_send()

        spot = g_spot(s, k)
        send(spot, spot, gx_s.at[k], gx_r.at[k], across).wait_send()
        for n in range(2):
            send(spot, spot, gc_s.at[n, k], gc_r.at[n, k], twin).wait_send()
    for i in range(LUMPS):
        wy_send(i).wait_send()

        @pl.when(z < s)
        def _():
            from_below(i).wait_send()

        @pl.when(z > s)
        def _():
            from_above(i).wait_send()

        @pl.when(root)
        def _():
            w_cast(i, across, bx_s, bx_r).wait_send()

        @pl.when(root | (across[1] == z))
        def _():
            w_cast(i, twin, bc_s, bc_r).wait_send()

    wo_copy.wait()
    gw_copy.wait()


def scatter(normed_t, pg, scaled_t, cot, outp, ngp, shards, groups):
    model, count = normed_t.shape
    total = pg.shape[1]
    inner = scaled_t.shape[0]
    seqs, length, _ = outp.shape
    part = length // groups
    deep = shards // 2
    rows = model // shards
    any_ = pl.BlockSpec(memory_space=pl.ANY)
    dma = pltpu.SemaphoreType.DMA
    v = pltpu.VMEM
    return pl.pallas_call(
        functools.partial(scatter_kernel, (deep, rows, part)),
        in_specs=[any_] * 6,
        out_specs=[any_] * 4,
        out_shape=[
            jax.ShapeDtypeStruct((groups, rows, total), BF16),
            jax.ShapeDtypeStruct((inner // 2, model), BF16),
            jax.ShapeDtypeStruct((seqs, part, model), BF16),
            jax.ShapeDtypeStruct((seqs, part, model), BF16),
        ],
        scratch_shapes=[
            v((model, count), BF16),
            v((count, total), BF16),
            v((inner, count), BF16),
            v((count, model), BF16),
            v((model, total), BF16),
            v((deep * rows, total), BF16),
            v(((deep + 1) * rows, total), BF16),
            v((groups, rows, total), BF16),
            v((2, 2, 2, part, model), BF16),
            v((2, 2, part, model), BF16),
            v((2, part, model), BF16),
            v((inner, model), BF16),
            v((inner // 2, model), BF16),
            v((2, inner // 2, model), BF16),
            v((inner // 2, model), BF16),
            dma((PARTS, deep)), dma((PARTS, deep)), dma((PARTS, deep)), dma((PARTS, deep)),
            dma((PARTS, deep + 1)),
            dma((PARTS,)), dma((PARTS,)), dma((2, PARTS)), dma((2, PARTS)),
            dma((2, 2, 2)), dma((2, 2, 2)), dma((2, 2)), dma((2, 2)),
            dma((LUMPS,)), dma((LUMPS,)), dma((LUMPS,)), dma((LUMPS,)), dma((2, LUMPS)),
            dma((LUMPS,)), dma((LUMPS,)), dma((LUMPS,)), dma((LUMPS,)),
            dma((3 + PARTS,)), dma((2,)), dma((6,)),
        ],
        compiler_params=pltpu.CompilerParams(
            collective_id=2, has_side_effects=True, vmem_limit_bytes=60 * 2**20
        ),
        name="weigh_scatter",
    )(normed_t, pg, scaled_t, cot, outp, ngp)


def local(
    tokens,
    segment_ids,
    w_in,
    w_out,
    conv_weight,
    conv_bias,
    norm_gain,
    gated_gain,
    dt_bias,
    a_log,
    skip_weight,
    cotangent,
):
    groups = lax.axis_size("seq")
    shards = lax.axis_size("dp")
    place = lax.axis_index("seq")
    owner = lax.axis_index("dp")
    seqs, part, model = tokens.shape
    length = part * groups
    rows_in = w_in.shape[0]
    rows_out = w_out.shape[0]
    wide = rows_out * shards
    heads = dt_bias.shape[0]
    size = wide // heads
    mine = heads // groups
    inner = mine * size
    span = 2 * inner
    taps = conv_weight.shape[1]
    state2 = w_in.shape[1] - 2 * wide - heads
    channels = wide + state2
    share = channels // shards
    ratio = shards // groups
    small_slice = groups == 4 and shards == 8

    def own(a):
        return lax.dynamic_slice_in_dim(a, place * inner, inner, 0)

    def own_heads(a):
        return lax.dynamic_slice_in_dim(a, place * mine, mine, 0)

    step_cols = jnp.pad(
        lax.dynamic_slice_in_dim(w_in, 2 * wide + state2 + place * mine, mine, 1),
        ((0, 0), (0, 128 - mine)),
    )
    w_mine = jnp.concatenate(
        [
            lax.dynamic_slice_in_dim(w_in, place * span, span, 1),
            w_in[:, 2 * wide : 2 * wide + state2],
            step_cols,
        ],
        axis=1,
    )

    def rows256(a):
        flat = a.reshape(-1)
        count = -(-flat.shape[0] // 256)
        return jnp.pad(flat, (0, count * 256 - flat.shape[0])).reshape(count, 256), count

    packs = [rows256(a) for a in (norm_gain, conv_bias, gated_gain, conv_weight)]
    small = jnp.concatenate([p[0] for p in packs])
    tall = -(-small.shape[0] // 16) * 16
    small = jnp.pad(small, ((0, tall - small.shape[0]), (0, 0)))
    floats = tokens.astype(F32)
    inverse = lax.rsqrt(jnp.mean(floats * floats, axis=-1, keepdims=True) + EPSILON)
    unit = floats * inverse
    if small_slice:
        turned, cot, pj, sg, w_full, wo, small_all = gather(
            w_mine, w_out, small, tokens, cotangent, shards, groups
        )
    else:
        small_all = lax.all_gather(small, "dp", axis=0, tiled=False)
    small_all = small_all.astype(F32)
    cut = [0]
    for pack in packs:
        cut.append(cut[-1] + pack[1])

    def unpack(i, count):
        return small_all[:, cut[i] : cut[i + 1]].reshape(shards, -1)[:, :count].reshape(-1)

    norm_all = unpack(0, rows_in)
    conv_b = unpack(1, share)
    gain_all = unpack(2, rows_out)
    conv_w = unpack(3, share * taps).reshape(channels, taps)
    if not small_slice:
        normed = lax.all_gather((unit * norm_all).astype(BF16), "seq", axis=1, tiled=True)
        cot = lax.all_gather(cotangent, "seq", axis=1, tiled=True)
        w_full = lax.all_gather(w_mine, "dp", axis=0, tiled=True)
        held = jnp.where(
            (owner // ratio == place) & (jnp.arange(ratio)[:, None, None] == owner % ratio),
            w_out[None],
            jnp.zeros((), BF16),
        ).reshape(inner, model)
        wo = lax.psum(held, "dp")
        sg = jnp.einsum("std,cd->stc", cot, wo, preferred_element_type=F32).astype(BF16)
        pj = jnp.einsum("std,de->ste", normed, w_full, preferred_element_type=F32).astype(BF16)

    def pad(v):
        return jnp.pad(v, (0, 128 - mine))

    rate = -jnp.exp(own_heads(a_log))
    hp = jnp.stack([pad(own_heads(dt_bias)), pad(rate * LOG2E), pad(rate)] + [jnp.zeros(128)] * 5)
    blank = jnp.zeros((state2,), F32)
    ch = jnp.concatenate(
        [
            jnp.concatenate([own(conv_w), conv_w[wide:]]).T,
            jnp.concatenate([own(conv_b), conv_b[wide:]])[None],
            jnp.concatenate([jnp.repeat(own_heads(skip_weight), size), blank])[None],
            jnp.concatenate([own(gain_all), blank])[None],
            jnp.zeros((1, inner + state2), F32),
        ]
    )
    cols = columns(segment_ids)
    pre, ys, st, red = mix_forward(pj, cols, sg, hp, ch)
    if small_slice:
        rk = norms(red, wide, groups)
    else:
        totals = lax.psum(red[:, :2], "seq")
        rho = lax.rsqrt(totals[:, 0] / wide + EPSILON)
        rk = jnp.stack([rho, rho**3 * totals[:, 1] / wide] + [jnp.zeros_like(rho)] * 6, axis=1)
    pg, chacc, hacc, scaled_t, outp, ngp = mix_backward(
        pj, cols, rk, sg, pre, ys, st, hp, ch, selectors(inner // 128), wo, w_full
    )
    chsum = jnp.sum(chacc, axis=1)
    hsum = jnp.sum(hacc, axis=1)[:, :mine]
    hsum = hsum * jnp.stack([jnp.ones((mine,)), rate, jnp.ones((mine,))])

    def spread(a, n, start):
        full = jnp.zeros(a.shape[:-1] + (n,), F32)
        return lax.dynamic_update_slice_in_dim(full, a, start, a.ndim - 1)

    chan = jnp.concatenate(
        [spread(chsum[:, :inner], wide, place * inner), chsum[:, inner:]], axis=1
    )
    packed = jnp.concatenate([chan.reshape(-1), spread(hsum, heads, place * mine).reshape(-1)])
    packed = lax.psum(packed, ("dp", "seq"))
    if small_slice:
        win_grad, wo_grad, out_sum, ngrad = scatter(
            turned,
            pg.reshape(seqs * length, -1),
            scaled_t,
            cot.reshape(seqs * length, -1),
            outp,
            ngp,
            shards,
            groups,
        )
    else:
        win_grad = jnp.einsum("std,ste->de", normed, pg, preferred_element_type=F32)
        win_grad = lax.psum_scatter(win_grad.astype(BF16), "dp", scatter_dimension=0, tiled=True)
        win_grad = lax.all_gather(win_grad, "seq", axis=0, tiled=False)
        wo_grad = jnp.dot(scaled_t, cot.reshape(seqs * length, -1), preferred_element_type=F32)
        wo_grad = lax.psum(wo_grad.astype(BF16), "dp").reshape(ratio, rows_out, model)
        wo_grad = lax.dynamic_index_in_dim(wo_grad, owner % ratio, 0, False)
        wo_grad = lax.psum(
            jnp.where(owner // ratio == place, wo_grad, jnp.zeros((), BF16)), "seq"
        )
        out_sum = lax.psum_scatter(outp, "seq", scatter_dimension=1, tiled=True)
        ngrad = lax.psum_scatter(ngp, "seq", scatter_dimension=1, tiled=True)
    win_grad = win_grad.astype(F32)
    wo_grad = wo_grad.astype(F32)
    w_in_grad = jnp.concatenate(
        [
            *[win_grad[g, :, :span] for g in range(groups)],
            jnp.sum(win_grad[:, :, span : span + state2], axis=0),
            *[win_grad[g, :, span + state2 : span + state2 + mine] for g in range(groups)],
        ],
        axis=1,
    )
    norm_grad = jnp.sum(w_in.astype(F32) * w_in_grad, axis=1) / norm_gain.astype(F32)
    gain_grad = jnp.sum(w_out.astype(F32) * wo_grad, axis=1) / gated_gain.astype(F32)
    result = (floats + out_sum.astype(F32)).astype(BF16)
    unit_grad = ngrad.astype(F32) * norm_all
    tokens_grad = cotangent.astype(F32) + inverse * (
        unit_grad - unit * jnp.mean(unit_grad * unit, axis=-1, keepdims=True)
    )
    chan = packed[: (taps + 1) * channels].reshape(taps + 1, channels)
    chan = lax.dynamic_slice_in_dim(chan, owner * share, share, 1)
    at = (taps + 1) * channels
    return (
        result,
        tokens_grad,
        w_in_grad,
        wo_grad,
        chan[:taps].T,
        chan[taps],
        norm_grad,
        gain_grad,
        packed[at : at + heads],
        packed[at + heads : at + 2 * heads],
        packed[at + 2 * heads : at + 3 * heads],
    )


def solution(mesh):
    return jax.shard_map(
        local,
        mesh=mesh,
        in_specs=(
            P("dp", "seq", None),
            P("dp", None),
            P("dp", None),
            P("dp", None),
            P("dp", None),
            P("dp"),
            P("dp"),
            P("dp"),
            P(),
            P(),
            P(),
            P("dp", "seq", None),
        ),
        out_specs=(
            P("dp", "seq", None),
            P("dp", "seq", None),
            P("dp", None),
            P("dp", None),
            P("dp", None),
            P("dp"),
            P("dp"),
            P("dp"),
            P(),
            P(),
            P(),
        ),
        check_vma=False,
    )
```

```python
import functools

import jax
import jax.numpy as jnp
from jax import lax
from jax.experimental import pallas as pl
from jax.experimental.pallas import tpu as pltpu
from jax.sharding import PartitionSpec as P

Q = 128
EXACT = lax.Precision.HIGHEST
EPSILON = 1e-05
LOG2E = 1.4426950408889634
RESET = 160.0
F32 = jnp.float32
BF16 = jnp.bfloat16
LUMPS = 6
WOFF = 1
MESH = pl.DeviceIdType.MESH


def sigmoid(x):
    return 0.5 * jnp.tanh(0.5 * x) + 0.5


def softplus(x):
    return jnp.maximum(x, 0.0) + jnp.log1p(jnp.exp(-jnp.abs(x)))


def nt(a, b):
    return lax.dot_general(a, b, (((1,), (1,)), ((), ())), preferred_element_type=F32)


def mm(a, b):
    return jnp.dot(a, b, preferred_element_type=F32)


def decays(pj, cols, hp, width):
    arg = pj[0, :, width + 256 : width + 384].astype(F32) + hp[0:1, :]
    dt = softplus(arg)
    rows = lax.broadcasted_iota(jnp.int32, (Q, Q), 0)
    lanes = lax.broadcasted_iota(jnp.int32, (Q, Q), 1)
    lower = (rows >= lanes).astype(F32)
    level = jnp.dot(lower, dt * hp[1:2, :], precision=EXACT, preferred_element_type=F32)
    level = level + cols[0, :, 3:4]
    return arg, dt, level, rows, lanes


def fwd_kernel(pairs, pj, cols, sg, hp, ch, pre, ys, st, red, state, tail):
    width = pairs * 256
    inner = pairs * 128
    chunk = pl.program_id(1)

    @pl.when(chunk == 0)
    def _():
        state[...] = jnp.zeros_like(state)
        tail[...] = jnp.zeros_like(tail)

    _, dt, level, rows, lanes = decays(pj, cols, hp, width)
    level_t = level.T
    low = lanes < 64
    masks = [cols[0, :, d : d + 1] for d in range(3)]

    def conv(raw, at):
        ext = jnp.concatenate([tail[:, at : at + 128], raw], axis=0)
        total = raw * ch[3:4, at : at + 128] + ch[4:5, at : at + 128]
        for d in (1, 2, 3):
            moved = pltpu.roll(ext, d, 0)[8:]
            total = total + moved * masks[d - 1] * ch[3 - d : 4 - d, at : at + 128]
        tail[:, at : at + 128] = raw[Q - 8 :]
        pre[0, :, at : at + 128] = total
        return total * sigmoid(total)

    b_rows = conv(pj[0, :, width : width + 128].astype(F32), inner)
    c_rows = conv(pj[0, :, width + 128 : width + 256].astype(F32), inner + 128)
    b_t = b_rows.T.astype(BF16)
    b_low = b_rows.astype(BF16)
    c_low = c_rows.astype(BF16)
    scores = jnp.where(rows >= lanes, nt(c_low, b_low), 0.0)
    old = state[...].astype(BF16)
    st[0, 0] = old
    carried_all = mm(c_low, old)
    squares = jnp.zeros((Q, 128), F32)
    cross = jnp.zeros((Q, 128), F32)
    for p in range(pairs):
        at = p * 128
        one = pj[0, :, p * 256 : p * 256 + 128].astype(F32)
        two = pj[0, :, p * 256 + 128 : p * 256 + 256].astype(F32)
        z = jnp.where(low, one, pltpu.roll(two, 64, 1))
        v = jnp.where(low, pltpu.roll(one, 64, 1), two)
        xc = conv(v, at)
        l0 = jnp.broadcast_to(level[:, 2 * p : 2 * p + 1], (Q, Q))
        l1 = jnp.broadcast_to(level[:, 2 * p + 1 : 2 * p + 2], (Q, Q))
        le = jnp.where(low, l0, l1)
        dte = jnp.where(low, dt[:, 2 * p : 2 * p + 1], dt[:, 2 * p + 1 : 2 * p + 2])
        u = xc * dte
        w0 = jnp.exp2(jnp.minimum(l0 - level_t[2 * p : 2 * p + 1, :], 0.0)) * scores
        w1 = jnp.exp2(jnp.minimum(l1 - level_t[2 * p + 1 : 2 * p + 2, :], 0.0)) * scores
        wide = jnp.concatenate([w0.astype(BF16), w1.astype(BF16)], axis=1)
        blocks = jnp.concatenate(
            [jnp.where(low, u, 0.0).astype(BF16), jnp.where(low, 0.0, u).astype(BF16)], axis=0
        )
        part = mm(wide, blocks) + carried_all[:, at : at + 128] * jnp.exp2(le)
        ys[0, :, at : at + 128] = part
        gated = (part + ch[5:6, at : at + 128] * xc) * (z * sigmoid(z))
        scaled = gated * ch[6:7, at : at + 128]
        squares = squares + gated * gated
        cross = cross + sg[0, :, at : at + 128].astype(F32) * scaled
        last = le[Q - 1 : Q, :]
        ul = (u * jnp.exp2(last - le)).astype(BF16)
        state[:, at : at + 128] = state[:, at : at + 128] * jnp.exp2(last) + mm(b_t, ul)
    both = jnp.where(
        lanes == 0, jnp.sum(squares, axis=1, keepdims=True), jnp.sum(cross, axis=1, keepdims=True)
    )
    red[0] = both.T[0:8]


def mix_forward(pj, cols, sg, hp, ch, interpret=False):
    seqs, length, total = pj.shape
    width = total - 384
    inner = width // 2
    pairs = inner // 128
    chunks = length // Q

    def row(n):
        return pl.BlockSpec((1, Q, n), lambda s, c: (s, c, 0))

    def whole(a):
        return pl.BlockSpec(a.shape, lambda s, c: (0,) * a.ndim)

    return pl.pallas_call(
        functools.partial(fwd_kernel, pairs),
        grid=(seqs, chunks),
        in_specs=[row(total), row(128), row(inner), whole(hp), whole(ch)],
        out_specs=[
            row(inner + 256),
            row(inner),
            pl.BlockSpec((1, 1, 128, inner), lambda s, c: (s, c, 0, 0)),
            pl.BlockSpec((1, 8, Q), lambda s, c: (s, 0, c)),
        ],
        out_shape=[
            jax.ShapeDtypeStruct((seqs, length, inner + 256), F32),
            jax.ShapeDtypeStruct((seqs, length, inner), F32),
            jax.ShapeDtypeStruct((seqs, chunks, 128, inner), BF16),
            jax.ShapeDtypeStruct((seqs, 8, length), F32),
        ],
        scratch_shapes=[pltpu.VMEM((128, inner), F32), pltpu.VMEM((8, inner + 256), F32)],
        compiler_params=pltpu.CompilerParams(vmem_limit_bytes=48 * 2**20),
        name="mix_forward",
    )(pj, cols, sg, hp, ch)


def bwd_kernel(
    pairs, pj, cols, rk, sg, pre, ys, st, hp, ch, sel, pg, chacc, hacc, sct, scl,
    dstate, halo, edy_all, ul_all,
):
    width = pairs * 256
    inner = pairs * 128
    first = (pl.program_id(0) == 0) & (pl.program_id(1) == 0)

    @pl.when(pl.program_id(1) == 0)
    def _():
        dstate[...] = jnp.zeros_like(dstate)
        halo[...] = jnp.zeros_like(halo)

    @pl.when(first)
    def _():
        chacc[...] = jnp.zeros_like(chacc)
        hacc[...] = jnp.zeros_like(hacc)

    arg, dt, level, rows, lanes = decays(pj, cols, hp, width)
    level_t = level.T
    low = lanes < 64
    masks = [cols[0, :, 3 + d : 4 + d] for d in (1, 2, 3)]
    tall = jnp.concatenate([rk[0], jnp.zeros((Q - 8, Q), F32)], axis=0).T
    rho = jnp.broadcast_to(tall[:, 0:1], (Q, 128))
    k2 = jnp.broadcast_to(tall[:, 1:2], (Q, 128))

    def fold(x):
        return jnp.sum(x.reshape(Q // 8, 8, 128), axis=0)

    def conv_back(grad, raw, at):
        ext = jnp.concatenate([grad, halo[:, at : at + 128]], axis=0)
        out = grad * ch[3:4, at : at + 128]
        chacc[3, :, at : at + 128] += fold(grad * raw)
        chacc[4, :, at : at + 128] += fold(grad)
        for d in (1, 2, 3):
            moved = pltpu.roll(ext, Q + 8 - d, 0)[:Q] * masks[d - 1]
            out = out + moved * ch[3 - d : 4 - d, at : at + 128]
            chacc[3 - d, :, at : at + 128] += fold(moved * raw)
        halo[:, at : at + 128] = grad[:8]
        return out

    pre_b = pre[0, :, inner : inner + 128]
    pre_c = pre[0, :, inner + 128 : inner + 256]
    sig_b, sig_c = sigmoid(pre_b), sigmoid(pre_c)
    b_rows, c_rows = pre_b * sig_b, pre_c * sig_c
    b_low, c_low = b_rows.astype(BF16), c_rows.astype(BF16)
    c_t = c_rows.T.astype(BF16)
    upper = lanes >= rows
    scores = jnp.where(upper, nt(b_low, c_low), 0.0)
    dlow = dstate[...].astype(BF16)
    dsb_all = mm(b_low, dlow)
    dscores = jnp.zeros((Q, Q), F32)
    sums = jnp.zeros((6 * Q, 128), F32)
    keep = jnp.zeros((8, 128), F32)
    for p in range(pairs):
        at = p * 128
        one = pj[0, :, p * 256 : p * 256 + 128].astype(F32)
        two = pj[0, :, p * 256 + 128 : p * 256 + 256].astype(F32)
        z = jnp.where(low, one, pltpu.roll(two, 64, 1))
        v = jnp.where(low, pltpu.roll(one, 64, 1), two)
        pr = pre[0, :, at : at + 128]
        sp = sigmoid(pr)
        xc = pr * sp
        l0 = jnp.broadcast_to(level[:, 2 * p : 2 * p + 1], (Q, Q))
        l1 = jnp.broadcast_to(level[:, 2 * p + 1 : 2 * p + 2], (Q, Q))
        le = jnp.where(low, l0, l1)
        dte = jnp.where(low, dt[:, 2 * p : 2 * p + 1], dt[:, 2 * p + 1 : 2 * p + 2])
        u = xc * dte
        skip = ch[5:6, at : at + 128]
        part = ys[0, :, at : at + 128]
        y = part + skip * xc
        sz = sigmoid(z)
        silz = z * sz
        gated = y * silz
        graw = sg[0, :, at : at + 128].astype(F32)
        scaled_rho = graw * rho
        scaled = gated * rho * ch[6:7, at : at + 128]
        sct[at : at + 128, :] = scaled.T.astype(BF16)
        scl[0, :, at : at + 128] = scaled.astype(BF16)
        gg = scaled_rho * ch[6:7, at : at + 128] - k2 * gated
        dy = gg * silz
        dz = gg * y * (sz + silz * (1.0 - sz))
        ulow = u.astype(BF16)
        dylow = dy.astype(BF16)
        w0 = jnp.exp2(jnp.minimum(level_t[2 * p : 2 * p + 1, :] - l0, 0.0))
        w1 = jnp.exp2(jnp.minimum(level_t[2 * p + 1 : 2 * p + 2, :] - l1, 0.0))
        wide = jnp.concatenate([(w0 * scores).astype(BF16), (w1 * scores).astype(BF16)], axis=1)
        dyb = jnp.concatenate(
            [jnp.where(low, dy, 0.0).astype(BF16), jnp.where(low, 0.0, dy).astype(BF16)], axis=0
        )
        ub = jnp.concatenate(
            [jnp.where(low, u, 0.0).astype(BF16), jnp.where(low, 0.0, u).astype(BF16)], axis=0
        )
        duw = mm(wide, dyb)
        gt = nt(ub, dylow)
        dscores = dscores + w0 * gt[:Q] + w1 * gt[Q:]
        last = le[Q - 1 : Q, :]
        lve = jnp.exp2(last - le)
        edy = (dy * jnp.exp2(le)).astype(BF16)
        ul = (u * lve).astype(BF16)
        edy_all[:, at : at + 128] = edy
        ul_all[:, at : at + 128] = ul
        dsb = dsb_all[:, at : at + 128]
        du = duw + lve * dsb
        r1 = dylow.astype(F32) * part - ulow.astype(F32) * duw
        r2 = ul.astype(F32) * dsb
        r1h, r2h = r1.astype(BF16), r2.astype(BF16)
        stacked = jnp.concatenate(
            [
                r1h,
                (r1 - r1h.astype(F32)).astype(BF16),
                r2h,
                (r2 - r2h.astype(F32)).astype(BF16),
                (dy * xc).astype(BF16),
                (du * xc).astype(BF16),
            ],
            axis=0,
        )
        sums = sums + mm(stacked, sel[p])
        decay = jnp.exp2(last)
        kept = fold(dlow[:, at : at + 128].astype(F32) * st[0, 0, :, at : at + 128].astype(F32)) * decay
        kept_high = kept.astype(BF16)
        keep = keep + mm(kept_high, sel[p]) + mm((kept - kept_high.astype(F32)).astype(BF16), sel[p])
        dstate[:, at : at + 128] = dstate[:, at : at + 128] * decay + mm(c_t, edy)
        dv = conv_back((du * dte + skip * dy) * (sp + xc * (1.0 - sp)), v, at)
        pg[0, :, p * 256 : p * 256 + 128] = jnp.where(low, dz, pltpu.roll(dv, 64, 1)).astype(BF16)
        pg[0, :, p * 256 + 128 : p * 256 + 256] = jnp.where(low, pltpu.roll(dz, 64, 1), dv).astype(BF16)
    dsc = jnp.where(upper, dscores, 0.0)
    db = mm(dsc.astype(BF16), c_low) + nt(ul_all[...], dlow)
    dc = mm(dsc.T.astype(BF16), b_low) + nt(edy_all[...], st[0, 0])
    raw_b = pj[0, :, width : width + 128].astype(F32)
    raw_c = pj[0, :, width + 128 : width + 256].astype(F32)
    pg[0, :, width : width + 128] = conv_back(
        db * (sig_b + b_rows * (1.0 - sig_b)), raw_b, inner
    ).astype(BF16)
    pg[0, :, width + 128 : width + 256] = conv_back(
        dc * (sig_c + c_rows * (1.0 - sig_c)), raw_c, inner + 128
    ).astype(BF16)
    r1 = sums[:Q] + sums[Q : 2 * Q]
    r2 = sums[2 * Q : 3 * Q] + sums[3 * Q : 4 * Q]
    da = (
        jnp.dot(upper.astype(F32), r1, precision=EXACT, preferred_element_type=F32)
        + jnp.dot((rows > lanes).astype(F32), r2, precision=EXACT, preferred_element_type=F32)
        + jnp.sum(keep, axis=0, keepdims=True)
    )
    ddt = da * hp[2:3, :] + sums[5 * Q :]
    ds = ddt * sigmoid(arg)
    pg[0, :, width + 256 : width + 384] = ds.astype(BF16)
    hacc[0] += fold(ds)
    hacc[1] += fold(da * dt)
    hacc[2] += fold(sums[4 * Q : 5 * Q])


def mix_backward(pj, cols, rk, sg, pre, ys, st, hp, ch, sel):
    seqs, length, total = pj.shape
    width = total - 384
    inner = width // 2
    pairs = inner // 128
    chunks = length // Q

    def row(n):
        return pl.BlockSpec((1, Q, n), lambda s, c: (s, chunks - 1 - c, 0))

    def whole(shape):
        return pl.BlockSpec(shape, lambda s, c: (0,) * len(shape))

    return pl.pallas_call(
        functools.partial(bwd_kernel, pairs),
        grid=(seqs, chunks),
        in_specs=[
            row(total),
            row(128),
            pl.BlockSpec((1, 8, Q), lambda s, c: (s, 0, chunks - 1 - c)),
            row(inner),
            row(inner + 256),
            row(inner),
            pl.BlockSpec((1, 1, 128, inner), lambda s, c: (s, chunks - 1 - c, 0, 0)),
            whole(hp.shape),
            whole(ch.shape),
            whole(sel.shape),
        ],
        out_specs=[
            row(total),
            whole((5, 8, inner + 256)),
            whole((3, 8, 128)),
            pl.BlockSpec((inner, Q), lambda s, c: (0, s * chunks + chunks - 1 - c)),
            row(inner),
        ],
        out_shape=[
            jax.ShapeDtypeStruct((seqs, length, total), BF16),
            jax.ShapeDtypeStruct((5, 8, inner + 256), F32),
            jax.ShapeDtypeStruct((3, 8, 128), F32),
            jax.ShapeDtypeStruct((inner, seqs * length), BF16),
            jax.ShapeDtypeStruct((seqs, length, inner), BF16),
        ],
        scratch_shapes=[
            pltpu.VMEM((128, inner), F32),
            pltpu.VMEM((8, inner + 256), F32),
            pltpu.VMEM((Q, inner), BF16),
            pltpu.VMEM((Q, inner), BF16),
        ],
        compiler_params=pltpu.CompilerParams(vmem_limit_bytes=48 * 2**20),
        name="mix_backward",
    )(pj, cols, rk, sg, pre, ys, st, hp, ch, sel)


def columns(seg):
    seqs, length = seg.shape
    back = [
        jnp.pad((seg[:, d:] == seg[:, :-d]).astype(F32), ((0, 0), (d, 0))) for d in (1, 2, 3)
    ]
    ahead = [
        jnp.pad((seg[:, d:] == seg[:, :-d]).astype(F32), ((0, 0), (0, d))) for d in (1, 2, 3)
    ]
    ends = seg.reshape(seqs, length // Q, Q)[:, :, -1]
    before = jnp.pad(ends[:, :-1], ((0, 0), (1, 0)))
    level = -RESET * (seg.reshape(seqs, length // Q, Q) - before[:, :, None]).astype(F32)
    stacked = jnp.stack([*back, level.reshape(seqs, length), *ahead], axis=-1)
    return jnp.pad(stacked, ((0, 0), (0, 0), (0, 121)))


def selectors(pairs):
    lane = lax.broadcasted_iota(jnp.int32, (pairs, 128, 128), 1)
    pair = lax.broadcasted_iota(jnp.int32, (pairs, 128, 128), 0)
    out = lax.broadcasted_iota(jnp.int32, (pairs, 128, 128), 2)
    return (out == 2 * pair + lane // 64).astype(BF16)


def norm_kernel(wide, red, rk, got, ssem, rsem):
    d = lax.axis_index("dp")
    s = lax.axis_index("seq")
    groups = got.shape[0]
    bar = pltpu.get_barrier_semaphore()
    for j in range(1, groups):
        pl.semaphore_signal(bar, inc=1, device_id=(d, lax.rem(s + j, groups)), device_id_type=MESH)
    pl.semaphore_wait(bar, groups - 1)
    sends = [
        pltpu.make_async_remote_copy(
            src_ref=red, dst_ref=got.at[j], send_sem=ssem.at[j], recv_sem=rsem.at[j],
            device_id=(d, lax.rem(s + j, groups)), device_id_type=MESH,
        )
        for j in range(1, groups)
    ]
    for copy in sends:
        copy.start()
    total = red[...]
    for j, copy in enumerate(sends):
        copy.wait()
        total = total + got[j + 1]
    rho = lax.rsqrt(total[:, 0:1] / wide + EPSILON)
    rk[...] = jnp.concatenate(
        [rho, rho * rho * rho * total[:, 1:2] / wide, jnp.zeros_like(total[:, 2:])], axis=1
    )


def norms(red, wide, groups):
    vmem = pl.BlockSpec(memory_space=pltpu.VMEM)
    return pl.pallas_call(
        functools.partial(norm_kernel, wide),
        in_specs=[vmem],
        out_specs=vmem,
        out_shape=jax.ShapeDtypeStruct(red.shape, F32),
        scratch_shapes=[
            pltpu.VMEM((groups, *red.shape), F32),
            pltpu.SemaphoreType.DMA((groups,)),
            pltpu.SemaphoreType.DMA((groups,)),
        ],
        compiler_params=pltpu.CompilerParams(collective_id=3, has_side_effects=True),
        name="norms",
    )(red)


def final_kernel(
    groups, span, mine, gw, w_in, wog, w_out, osum, ngrad, tok, cot, gains,
    res, tgrad, wig, wgr, nsum, gsum,
):
    total = jnp.zeros((w_in.shape[0], 1), F32)
    for g in range(groups):
        here = slice(g * span, (g + 1) * span)
        grad = gw[g, :, :span].astype(F32)
        wig[:, here] = grad
        total = total + jnp.sum(grad * w_in[:, here].astype(F32), axis=1, keepdims=True)
    at = groups * span
    width = gw.shape[2] - 128
    shared = gw[0, :, span:width].astype(F32)
    steps = gw[0, :, width:].astype(F32)
    for g in range(1, groups):
        shared = shared + gw[g, :, span:width].astype(F32)
        steps = steps + pltpu.roll(gw[g, :, width:].astype(F32), g * mine, 1)
    mid = at + width - span
    wig[:, at:mid] = shared
    wig[:, mid:] = steps[:, : groups * mine]
    total = total + jnp.sum(shared * w_in[:, at:mid].astype(F32), axis=1, keepdims=True)
    total = total + jnp.sum(
        steps[:, : groups * mine] * w_in[:, mid:].astype(F32), axis=1, keepdims=True
    )
    nsum[...] = jnp.broadcast_to(total, nsum.shape)
    grad = wog[...].astype(F32)
    wgr[...] = grad
    gsum[...] = jnp.broadcast_to(
        jnp.sum(grad * w_out[...].astype(F32), axis=1, keepdims=True), gsum.shape
    )
    x = tok[...].astype(F32)
    res[...] = (x + osum[...].astype(F32)).astype(BF16)
    inverse = lax.rsqrt(jnp.mean(x * x, axis=1, keepdims=True) + EPSILON)
    unit = x * inverse
    grad = ngrad[...].astype(F32) * gains[0:1, :]
    tgrad[...] = cot[...].astype(F32) + inverse * (
        grad - unit * jnp.mean(grad * unit, axis=1, keepdims=True)
    )


def final(gw, w_in, wog, w_out, osum, ngrad, tok, cot, gains, span, mine):
    groups, rows, total = gw.shape
    steps = next(n for n in (4, 2, 1) if rows % (16 * n) == 0)

    def part(a):
        return pl.BlockSpec((a.shape[0] // steps, a.shape[1]), lambda i: (i, 0))

    tall = [w_in, wog, w_out, osum, ngrad, tok, cot]
    shapes = [
        (tok.shape, BF16), (tok.shape, F32), (w_in.shape, F32), (wog.shape, F32),
        ((rows, 128), F32), ((wog.shape[0], 128), F32),
    ]
    outs = [jax.ShapeDtypeStruct(*n) for n in shapes]
    return pl.pallas_call(
        functools.partial(final_kernel, groups, span, mine),
        grid=(steps,),
        in_specs=[
            pl.BlockSpec((groups, rows // steps, total), lambda i: (0, i, 0)),
            *[part(a) for a in tall],
            pl.BlockSpec(gains.shape, lambda i: (0, 0)),
        ],
        out_specs=[part(o) for o in outs],
        out_shape=outs,
        compiler_params=pltpu.CompilerParams(vmem_limit_bytes=48 * 2**20),
        name="final",
    )(gw, *tall, gains)


def gather_kernel(
    dims, w_in, dt_in, wo_in, small_in, tok_in, cot_in,
    turned_o, cot_o, pj_o, sg_o, w_o, wo_o, small_o,
    tok, cot, wbig, wo, small, pjv, sgv, turned,
    szu, szd, rz, sy, ry, wsu, wsd, wrz, wsy, wry, bx_s, bx_r, bc_s, bc_r, loc, out,
):
    deep, pieces, rows, inner, part, length, groups = dims
    d = lax.axis_index("dp")
    s = lax.axis_index("seq")
    z = d // 2
    y = d % 2
    top = deep - 1
    up, down, side = (d + 2, s), (d - 2, s), (d + 1 - 2 * y, s)
    across, twin = (d, s + 2 - 4 * (s // 2)), (d, s + 1 - 2 * (s % 2))
    opposite = across[1]

    bar = pltpu.get_barrier_semaphore()

    @pl.when(z < top)
    def _():
        pl.semaphore_signal(bar, inc=1, device_id=up, device_id_type=MESH)

    @pl.when(z > 0)
    def _():
        pl.semaphore_signal(bar, inc=1, device_id=down, device_id_type=MESH)

    for who in (side, across, twin):
        pl.semaphore_signal(bar, inc=1, device_id=who, device_id_type=MESH)
    pl.semaphore_wait(bar, 3 + jnp.minimum(z, 1) + jnp.minimum(top - z, 1))

    def send(src, dst, ssem, rsem, who):
        return pltpu.make_async_remote_copy(
            src_ref=src, dst_ref=dst, send_sem=ssem, recv_sem=rsem,
            device_id=who, device_id_type=MESH,
        )

    width = 2 * inner

    def cols(k):
        return pl.ds(width + 256, 128) if k == 1 else pl.ds(width if k == 2 else (k - 3) * 256, 256)

    def held(k, owner):
        if k == 0:
            return small.at[owner]
        return wbig.at[pl.ds(pl.multiple_of(owner * rows, 16), rows), cols(k)]

    def source(k):
        if k == 0:
            return small_in.at[...]
        if k == 1:
            return dt_in.at[...]
        if k == 2:
            return w_in.at[:, pl.ds(width * groups, 256)]
        return w_in.at[:, pl.ds(pl.multiple_of(s * width + (k - 3) * 256, 128), 256)]

    def own_send(k):
        src, dst = source(k), held(k, d)

        @pl.when(z < top)
        def _():
            send(src, dst, szu.at[k, z], rz.at[k, z], up).start()

        @pl.when(z > 0)
        def _():
            send(src, dst, szd.at[k, z], rz.at[k, z], down).start()

        send(src, dst, sy.at[k, z], ry.at[k, z], side).start()

    def hop(k, h):
        below, above = z - h, z + h

        @pl.when(below >= 0)
        def _():
            ref = held(k, below * 2 + y)
            send(ref, ref, szu.at[k, below], rz.at[k, below], up).wait_recv()

            @pl.when(z < top)
            def _():
                send(ref, ref, szu.at[k, below], rz.at[k, below], up).start()

            send(ref, ref, sy.at[k, below], ry.at[k, below], side).start()

        @pl.when(above <= top)
        def _():
            ref = held(k, above * 2 + y)
            send(ref, ref, szd.at[k, above], rz.at[k, above], down).wait_recv()

            @pl.when(z > 0)
            def _():
                send(ref, ref, szd.at[k, above], rz.at[k, above], down).start()

            send(ref, ref, sy.at[k, above], ry.at[k, above], side).start()

    def arrive(k):
        for e in range(deep):
            ref = held(k, e * 2 + 1 - y)
            send(ref, ref, sy.at[k, e], ry.at[k, e], side).wait_recv()

    def own_copy(src, dst, sem):
        return pltpu.make_async_copy(src, dst, sem)

    here = pl.multiple_of(s * part, 16)
    there = pl.multiple_of(opposite * part, 16)
    locals_ = [
        own_copy(small_in, small.at[d], loc.at[0]),
        own_copy(
            w_in.at[:, pl.ds(pl.multiple_of(s * width, 128), width)],
            wbig.at[pl.ds(pl.multiple_of(d * rows, 16), rows), pl.ds(0, width)],
            loc.at[1],
        ),
    ]
    for q in range(2):
        locals_.append(own_copy(tok_in.at[q], tok.at[q, pl.ds(here, part)], loc.at[2 + q]))
        locals_.append(own_copy(cot_in.at[q], cot.at[q, pl.ds(here, part)], loc.at[4 + q]))
    for k in (1, 2):
        locals_.append(own_copy(source(k), held(k, d), loc.at[6 + k]))
    half = wo_in.shape[0]
    mine = z == s

    def root_copy():
        return own_copy(wo_in, wo.at[pl.ds(pl.multiple_of(y * half, 16), half)], loc.at[6])

    def block_sends(which, src, dst, q):
        spot = dst.at[q, pl.ds(here, part)]
        i = which * 2 + q
        send(src.at[q], spot, bx_s.at[i], bx_r.at[i], across).start()
        send(src.at[q], spot, bc_s.at[0, i], bc_r.at[0, i], twin).start()

    def block_forward(which, dst, q):
        spot = dst.at[q, pl.ds(there, part)]
        i = which * 2 + q
        send(spot, spot, bx_s.at[i], bx_r.at[i], across).wait_recv()
        send(spot, spot, bc_s.at[1, i], bc_r.at[1, i], twin).start()

    def block_arrive(which, dst, q):
        i = which * 2 + q
        for n in range(2):
            spot = dst.at[q, pl.ds(here, part)]
            send(spot, spot, bc_s.at[n, i], bc_r.at[n, i], twin).wait_recv()

    lump = half // LUMPS

    def wo_piece(i, col):
        m = col * LUMPS + i
        return m, wo.at[pl.ds(pl.multiple_of(m * lump, 16), lump)]

    def wo_send(i, src=None):
        m, ref = wo_piece(i, y)
        src = ref if src is None else src

        @pl.when((z >= s) & (z < top))
        def _():
            send(src, ref, wsu.at[m], wrz.at[m], up).start()

        @pl.when((z <= s) & (z > 0))
        def _():
            send(src, ref, wsd.at[m], wrz.at[m], down).start()

        send(src, ref, wsy.at[m], wry.at[m], side).start()

    def wo_root(i):
        @pl.when(mine)
        def _():
            wo_send(i, wo_in.at[pl.ds(i * lump, lump)])

    def wo_hop(i, h):
        @pl.when((z - s == h) | (s - z == h))
        def _():
            m, ref = wo_piece(i, y)
            send(ref, ref, wsu.at[m], wrz.at[m], up).wait_recv()
            wo_send(i)

    def wo_arrive(i):
        m, ref = wo_piece(i, 1 - y)
        send(ref, ref, wsy.at[m], wry.at[m], side).wait_recv()

    tile = 256

    def project(k):
        c = pl.ds(width, 384) if k == 2 else cols(k)

        def step(i, _):
            q, r = i // (length // tile), i % (length // tile)
            at = pl.multiple_of(r * tile, tile)
            pjv[q, pl.ds(at, tile), c] = mm(tok[q, pl.ds(at, tile), :], wbig[:, c]).astype(BF16)
            return 0

        lax.fori_loop(0, 2 * length // tile, step, 0)
        own_copy(pjv.at[:, :, c], pj_o.at[:, :, c], out.at[k]).start()

    for c in locals_:
        c.start()

    @pl.when(mine)
    def _():
        root_copy().start()

    for q in range(2):
        block_sends(0, tok_in, tok, q)
    ahead = 3
    for k in range(ahead):
        own_send(k)
    done = []

    def hops(t):
        for h in range(1, deep):
            if 0 <= t - h < pieces:
                hop(t - h, h)
        for h in range(1, deep):
            if 0 <= t - h - WOFF < LUMPS:
                wo_hop(t - h - WOFF, h)
        if 0 <= t - WOFF < LUMPS:
            wo_root(t - WOFF)
        if ahead <= t + ahead - 1 < pieces:
            own_send(t + ahead - 1)

    steps = max(pieces, WOFF + LUMPS) + deep - 1
    count = dict(next=1)

    def ready(n):
        for _ in range(n):
            if count["next"] < pieces:
                arrive(count["next"])
                if count["next"] > 1:
                    project(count["next"])
                count["next"] += 1

    share = tok.shape[2] // (2 * deep)

    def norm_step(i, _):
        q, r = i // (length // 64), i % (length // 64)
        at = pl.multiple_of(r * 64, 64)
        x = tok[q, pl.ds(at, 64), :].astype(F32)
        inv = lax.rsqrt(jnp.mean(x * x, axis=1, keepdims=True) + EPSILON)
        gains = jnp.concatenate([small[e, 0:1, :share] for e in range(2 * deep)], axis=1)
        tok[q, pl.ds(at, 64), :] = (x * inv * gains.astype(F32)).astype(BF16)
        return 0

    for t in range(1, steps):
        hops(t)
        if t == 3:
            block_forward(0, tok, 0)
        if t == 6:
            block_forward(0, tok, 1)
            for q in range(2):
                block_sends(1, cot_in, cot, q)
        if t == 7:
            for i in (0, 1, 2, 4, 6, 7):
                locals_[i].wait()
            block_arrive(0, tok, 0)
            block_arrive(0, tok, 1)
            for q in range(2):
                spot = tok.at[q, pl.ds(there, part)]
                send(spot, spot, bc_s.at[1, q], bc_r.at[1, q], twin).wait_send()
            arrive(0)
            own_copy(small, small_o, out.at[0]).start()
            lax.fori_loop(0, 2 * length // 64, norm_step, 0)
        if t > 7:
            ready(2 if t == 8 else 1)
    for i in range(LUMPS):
        wo_arrive(i)

    @pl.when(mine)
    def _():
        root_copy().wait()

    block_forward(1, cot, 0)
    ready(pieces)
    own_copy(wbig, w_o, out.at[pieces + 1]).start()
    own_copy(wo, wo_o, out.at[pieces + 2]).start()

    def turn_step(i, _):
        q, r = i // (length // tile), i % (length // tile)
        at = pl.multiple_of(r * tile, tile)
        to = pl.multiple_of(i * tile, tile)
        for j in range(0, tok.shape[2], 128):
            turned[j : j + 128, pl.ds(to, tile)] = tok[q, pl.ds(at, tile), j : j + 128].T
        return 0

    lax.fori_loop(0, 2 * length // tile, turn_step, 0)
    own_copy(turned, turned_o, out.at[pieces]).start()
    block_forward(1, cot, 1)
    locals_[3].wait()
    locals_[5].wait()
    block_arrive(1, cot, 0)
    block_arrive(1, cot, 1)
    own_copy(cot, cot_o, out.at[pieces + 3]).start()

    def grad_step(i, _):
        q, r = i // (length // tile), i % (length // tile)
        at = pl.multiple_of(r * tile, tile)
        sgv[q, pl.ds(at, tile), :] = nt(cot[q, pl.ds(at, tile), :], wo[...]).astype(BF16)
        return 0

    lax.fori_loop(0, 2 * length // tile, grad_step, 0)
    own_copy(sgv, sg_o, out.at[pieces + 4]).start()

    for k in range(pieces):
        for e in range(deep):
            ref = held(k, e * 2 + y)

            @pl.when((z >= e) & (z < top))
            def _():
                send(ref, ref, szu.at[k, e], rz.at[k, e], up).wait_send()

            @pl.when((z <= e) & (z > 0))
            def _():
                send(ref, ref, szd.at[k, e], rz.at[k, e], down).wait_send()

            send(ref, ref, sy.at[k, e], ry.at[k, e], side).wait_send()
    for i in range(LUMPS):
        m, ref = wo_piece(i, y)

        @pl.when((z >= s) & (z < top))
        def _():
            send(ref, ref, wsu.at[m], wrz.at[m], up).wait_send()

        @pl.when((z <= s) & (z > 0))
        def _():
            send(ref, ref, wsd.at[m], wrz.at[m], down).wait_send()

        send(ref, ref, wsy.at[m], wry.at[m], side).wait_send()
    for which, dst in ((0, tok), (1, cot)):
        for q in range(2):
            i = which * 2 + q
            spot = dst.at[q, pl.ds(here, part)]
            send(spot, spot, bx_s.at[i], bx_r.at[i], across).wait_send()
            for n in range(1 + which):
                send(spot, spot, bc_s.at[n, i], bc_r.at[n, i], twin).wait_send()
    own_copy(small, small_o, out.at[0]).wait()
    for k in range(2, pieces):
        c = pl.ds(width, 384) if k == 2 else cols(k)
        own_copy(pjv.at[:, :, c], pj_o.at[:, :, c], out.at[k]).wait()
    own_copy(turned, turned_o, out.at[pieces]).wait()
    own_copy(wbig, w_o, out.at[pieces + 1]).wait()
    own_copy(wo, wo_o, out.at[pieces + 2]).wait()
    own_copy(cot, cot_o, out.at[pieces + 3]).wait()
    own_copy(sgv, sg_o, out.at[pieces + 4]).wait()


def gather(w_in, dt_in, w_out, small, tokens, cotangent, inner, shards, groups):
    rows = w_in.shape[0]
    total = 2 * inner + 384
    seqs, part, model = tokens.shape
    length = part * groups
    deep = shards // 2
    pieces = inner // 128 + 3
    any_ = pl.BlockSpec(memory_space=pl.ANY)
    dma = pltpu.SemaphoreType.DMA
    small_rows, small_cols = small.shape
    full = (shards * rows, total)
    shapes = [
        (model, seqs * length), (seqs, length, model), (seqs, length, total), (seqs, length, inner),
        full, (inner, model), (shards, small_rows, small_cols),
    ]
    return pl.pallas_call(
        functools.partial(gather_kernel, (deep, pieces, rows, inner, part, length, groups)),
        in_specs=[any_] * 6,
        out_specs=[any_] * 7,
        out_shape=[jax.ShapeDtypeStruct(n, BF16) for n in shapes],
        scratch_shapes=[
            pltpu.VMEM(shapes[1], BF16),
            pltpu.VMEM(shapes[1], BF16),
            pltpu.VMEM(full, BF16),
            pltpu.VMEM((inner, model), BF16),
            pltpu.VMEM(shapes[6], BF16),
            pltpu.VMEM(shapes[2], BF16),
            pltpu.VMEM(shapes[3], BF16),
            pltpu.VMEM(shapes[0], BF16),
            dma((pieces, deep)), dma((pieces, deep)), dma((pieces, deep)),
            dma((pieces, deep)), dma((pieces, deep)),
            *[dma((2 * LUMPS,))] * 5,
            dma((4,)), dma((4,)), dma((2, 4)), dma((2, 4)),
            dma((9,)), dma((pieces + 5,)),
        ],
        compiler_params=pltpu.CompilerParams(
            collective_id=1, has_side_effects=True, vmem_limit_bytes=56 * 2**20
        ),
        name="gather_project",
    )(w_in, dt_in, w_out, small, tokens, cotangent)


def greet(z, y, s, deep, others):
    bar = pltpu.get_barrier_semaphore()
    for e in range(deep):
        @pl.when(z != e)
        def _():
            pl.semaphore_signal(bar, inc=1, device_id=(2 * e + y, s), device_id_type=MESH)

    for who in others:
        pl.semaphore_signal(bar, inc=1, device_id=who, device_id_type=MESH)
    pl.semaphore_wait(bar, len(others) + deep - 1)


def send(src, dst, ssem, rsem, who):
    return pltpu.make_async_remote_copy(
        src_ref=src, dst_ref=dst, send_sem=ssem, recv_sem=rsem, device_id=who, device_id_type=MESH
    )


def add_into(dst, src):
    count = dst.shape[0]
    some = next(n for n in (64, 48, 32, 16) if count % n == 0)

    def step(i, _):
        at = pl.ds(pl.multiple_of(i * some, 16), some)
        dst[at, :] = (dst[at, :].astype(F32) + src[at, :].astype(F32)).astype(BF16)
        return 0

    lax.fori_loop(0, count // some, step, 0)


CUTS = ((0, 512), (512, 512), (1536, 384), (1024, 256), (1280, 256))
PARTS = len(CUTS)


def scatter_kernel(
    dims, nt_in, pg_in, st_in, sc_in, cot_in, wo_in, wi_in, ch_in, he_in,
    gw_o, wo_o, out_o, ng_o, sm_o,
    nt_v, pg_v, st_v, sc_v, wo_v, cw, pv, yb, zb, tw, xr, stage, gw, ybw, zbw, ch_v, he_v,
    vec, vgot, vall,
    sy, ry, su, sd, rz, gx_s, gx_r, gc_s, gc_r, tw_s, tw_r, xr_s, xr_r,
    wy_s, wy_r, wu_s, wd_s, wz_r, bx_s, bx_r, bc_s, bc_r, v_s, v_r, loc, out,
):
    deep, rows, part, length = dims
    d = lax.axis_index("dp")
    s = lax.axis_index("seq")
    z = d // 2
    y = d % 2
    x = s // 2
    c = s % 2
    top = deep - 1
    model = wi_in.shape[0]
    up, down, side = (d + 2, s), (d - 2, s), (d + 1 - 2 * y, s)
    across, twin = (d, s + 2 - 4 * x), (d, s + 1 - 2 * c)
    greet(z, y, s, deep, (side, across, twin))

    def cut(k):
        return pl.ds(*CUTS[k])

    def lines(ref, i, count=rows):
        return ref.at[pl.ds(pl.multiple_of(i * count, 16), count)]

    cot_v = cw.at[:, pl.ds(0, model)]
    wi_v = cw.at[pl.ds(0, model), :]
    loads = dict(
        ch=pltpu.make_async_copy(ch_in, ch_v, loc.at[2]),
        he=pltpu.make_async_copy(he_in, he_v, loc.at[3]),
        st=pltpu.make_async_copy(st_in, st_v, loc.at[0]),
        cot=pltpu.make_async_copy(cot_in, cot_v, loc.at[1]),
        sc=pltpu.make_async_copy(sc_in, sc_v, loc.at[6]),
        wo=pltpu.make_async_copy(wo_in, wo_v, loc.at[7]),
        nt=pltpu.make_async_copy(nt_in, nt_v, loc.at[4]),
        pg=pltpu.make_async_copy(pg_in, pg_v, loc.at[5]),
    )
    for load in loads.values():
        load.start()
    load_wi = pltpu.make_async_copy(wi_in, wi_v, loc.at[8])

    def v_send(n, src, dst, who):
        return send(src, dst, v_s.at[n], v_r.at[n], who)

    def v_y():
        return v_send(0, vec, vgot.at[deep], side)

    def v_z(e):
        return send(vec, vgot.at[z], v_s.at[1 + e], v_r.at[1 + z], (2 * e + y, s))

    def v_from(e):
        return send(vec, vgot.at[e], v_s.at[1 + e], v_r.at[1 + e], (2 * e + y, s))

    def v_seq(n, owner, who):
        return v_send(1 + deep + n, vall.at[owner], vall.at[owner], who)

    def v_start():
        vec[...] = jnp.concatenate(
            [
                jnp.sum(ch_v[...], axis=1),
                jnp.concatenate(
                    [jnp.sum(he_v[...], axis=1), jnp.zeros((3, vec.shape[1] - 128), F32)], axis=1
                ),
            ],
            axis=0,
        )
        v_y().start()

    def v_sum():
        v_y().wait()
        vec[...] = vec[...] + vgot[deep]
        for e in range(deep):
            @pl.when(z != e)
            def _():
                v_z(e).start()

    def v_total():
        for e in range(deep):
            @pl.when(z != e)
            def _():
                v_z(e).wait_send()
                v_from(e).wait_recv()

            @pl.when(z == e)
            def _():
                vgot[e] = vec[...]

        total = vgot[0]
        for e in range(1, deep):
            total = total + vgot[e]
        vall[s] = total
        v_seq(0, s, across).start()
        v_seq(1, s, twin).start()

    def v_spread():
        v_seq(0, across[1], across).wait_recv()
        v_seq(2, across[1], twin).start()

    both = ((0, out_o), (1, ng_o))

    def twin_send(n, turn, q):
        return send(stage.at[q], tw.at[n, turn, q], tw_s.at[q], tw_r.at[n, turn, q], twin)

    def product(n, q, owner, j):
        at = pl.ds(pl.multiple_of(q * length + owner * part, 16), part)
        if n == 0:
            return mm(sc_v[at, :], wo_v[:, j : j + 512])
        return nt(pg_v[at, :], cw[j : j + 512, :])

    def exchange(n, turn):
        half = 1 - x if turn == 0 else x
        for q in range(2):
            if (n, turn) != (0, 0):
                twin_send(n, turn, q).wait_send()
            for j in range(0, model, 512):
                stage[q, :, j : j + 512] = product(n, q, 2 * half + 1 - c, j).astype(BF16)
            twin_send(n, turn, q).start()
        for q in range(2):
            twin_send(n, turn, q).wait_recv()
            for j in range(0, model, 512):
                tw[n, turn, q, :, j : j + 512] = (
                    tw[n, turn, q, :, j : j + 512].astype(F32) + product(n, q, 2 * half + c, j)
                ).astype(BF16)
            if turn == 0:
                x_send(n, q).start()

    def x_send(n, q):
        return send(tw.at[n, 0, q], xr.at[n, q], xr_s.at[n, q], xr_r.at[n, q], across)

    def x_finish(n, dst):
        for q in range(2):
            x_send(n, q).wait_recv()
            add_into(xr.at[n, q], tw.at[n, 1, q])
            pltpu.make_async_copy(xr.at[n, q], dst.at[q], out.at[2 + 2 * n + q]).start()

    def weigh(k):
        def step(i, _):
            at = pl.ds(pl.multiple_of(i * rows, 16), rows)
            pv[at, cut(k)] = mm(nt_v[at, :], pg_v[:, cut(k)]).astype(BF16)
            return 0

        lax.fori_loop(0, 2 * deep, step, 0)

    def block(e, k):
        return pv.at[pl.ds(pl.multiple_of((2 * e + y) * rows, 16), rows), cut(k)]

    def y_send(k, e):
        src = pv.at[pl.ds(pl.multiple_of((2 * e + 1 - y) * rows, 16), rows), cut(k)]
        return send(src, lines(yb, e).at[:, cut(k)], sy.at[k, e], ry.at[k, e], side)

    def y_start(k):
        for e in range(deep):
            y_send(k, e).start()

    def y_add(k):
        for e in range(deep):
            y_send(k, e).wait_recv()
            add_into(block(e, k), lines(yb, e).at[:, cut(k)])

    def z_send(k, e, slot, sem, who):
        return send(block(e, k), lines(zb, slot).at[:, cut(k)], sem.at[k, e], rz.at[k, slot], who)

    def hop(k, h):
        @pl.when(z == h - 1)
        def _():
            for e in range(top, h - 1, -1):
                if h > 1:
                    z_send(k, e, e, su, up).wait_recv()
                    add_into(block(e, k), lines(zb, e).at[:, cut(k)])
                z_send(k, e, e, su, up).start()

        @pl.when(z == deep - h)
        def _():
            for e in range(deep - h):
                if h > 1:
                    z_send(k, e, e, sd, down).wait_recv()
                    add_into(block(e, k), lines(zb, e).at[:, cut(k)])
                z_send(k, e, deep if e == deep - h - 1 else e, sd, down).start()

    def g_spot(who, k):
        return gw_o.at[who, :, cut(k)]

    def finish(k):
        mine = block(z, k)

        @pl.when(z > 0)
        def _():
            z_send(k, z, z, su, up).wait_recv()
            add_into(mine, lines(zb, z).at[:, cut(k)])

        @pl.when(z < top)
        def _():
            z_send(k, z, deep, sd, down).wait_recv()
            add_into(mine, lines(zb, deep).at[:, cut(k)])

        send(mine, g_spot(s, k), gx_s.at[k], gx_r.at[k], across).start()
        send(mine, g_spot(s, k), gc_s.at[0, k], gc_r.at[0, k], twin).start()
        pltpu.make_async_copy(mine, g_spot(s, k), loc.at[9 + k]).start()

    def spread(k):
        spot = g_spot(across[1], k)
        send(spot, spot, gx_s.at[k], gx_r.at[k], across).wait_recv()
        send(spot, spot, gc_s.at[1, k], gc_r.at[1, k], twin).start()

    half = gw.shape[0] // 2
    lump = half // LUMPS

    def w_rows(col, i):
        return gw.at[pl.ds(pl.multiple_of(col * half + i * lump, 16), lump)]

    def piece(ref, i):
        return ref.at[pl.ds(i * lump, lump)]

    def wy_send(i):
        return send(w_rows(1 - y, i), piece(ybw, i), wy_s.at[i], wy_r.at[i], side)

    def w_compute():
        tall = 2 * lump
        for n in range(LUMPS):
            col, i = (1 - y, n) if n < LUMPS // 2 else (y, n - LUMPS // 2)
            at = pl.ds(pl.multiple_of(col * half + i * tall, 16), tall)
            for j in range(0, model, 512):
                gw[at, j : j + 512] = mm(st_v[at, :], cw[:, j : j + 512]).astype(BF16)
            if n < LUMPS // 2:
                wy_send(2 * i).start()
                wy_send(2 * i + 1).start()

    def from_below(i):
        return send(w_rows(y, i), piece(zbw.at[0], i), wu_s.at[i], wz_r.at[0, i], up)

    def from_above(i):
        return send(w_rows(y, i), piece(zbw.at[1], i), wd_s.at[i], wz_r.at[1, i], down)

    def w_cast(i, who, ssem, rsem):
        return send(piece(wo_o, i), piece(wo_o, i), ssem.at[i], rsem.at[i], who)

    def w_root(i, who, ssem, rsem):
        return send(w_rows(y, i), piece(wo_o, i), ssem.at[i], rsem.at[i], who)

    def w_keep(i):
        return pltpu.make_async_copy(w_rows(y, i), piece(wo_o, i), loc.at[9 + PARTS + i])

    root = z == s

    def w_chain(i, h):
        last = h == deep - 1
        below = root & (z > 0) if last else (z < s) & (z == h) & (h > 0)
        above = root & (z < top) if last else (z > s) & (top - z == h) & (h > 0)

        @pl.when(root if last else ((z < s) & (z == h)) | ((z > s) & (top - z == h)))
        def _():
            wy_send(i).wait_recv()
            add_into(w_rows(y, i), piece(ybw, i))

        @pl.when(below)
        def _():
            from_below(i).wait_recv()
            add_into(w_rows(y, i), piece(zbw.at[0], i))

        @pl.when(above)
        def _():
            from_above(i).wait_recv()
            add_into(w_rows(y, i), piece(zbw.at[1], i))

        if last:

            @pl.when(root)
            def _():
                w_keep(i).start()
                w_root(i, across, bx_s, bx_r).start()
                w_root(i, twin, bc_s, bc_r).start()

        else:

            @pl.when((z < s) & (z == h))
            def _():
                from_below(i).start()

            @pl.when((z > s) & (top - z == h))
            def _():
                from_above(i).start()

    def w_spread(i):
        @pl.when(across[1] == z)
        def _():
            w_cast(i, across, bx_s, bx_r).wait_recv()
            w_cast(i, twin, bc_s, bc_r).start()

        @pl.when((across[1] != z) & jnp.logical_not(root))
        def _():
            w_cast(i, twin, bc_s, bc_r).wait_recv()

    def w_step(t):
        for h in range(deep):
            if 0 <= t - h < LUMPS:
                w_chain(t - h, h)

    loads["ch"].wait()
    loads["he"].wait()
    v_start()
    loads["st"].wait()
    loads["cot"].wait()
    w_compute()
    load_wi.start()
    loads["sc"].wait()
    loads["wo"].wait()
    exchange(0, 0)
    w_step(0)
    loads["nt"].wait()
    loads["pg"].wait()
    weigh(0)
    y_start(0)
    v_sum()
    w_step(1)
    exchange(0, 1)
    w_step(2)
    load_wi.wait()
    exchange(1, 0)
    w_step(3)
    v_total()
    weigh(1)
    y_start(1)
    w_step(4)
    exchange(1, 1)
    w_step(5)
    y_add(0)
    hop(0, 1)
    weigh(2)
    y_start(2)
    w_step(6)
    hop(0, 2)
    weigh(3)
    y_start(3)
    weigh(4)
    y_start(4)
    w_step(7)
    hop(0, 3)
    y_add(1)
    hop(1, 1)
    w_step(8)
    finish(0)
    hop(1, 2)
    hop(1, 3)
    y_add(2)
    hop(2, 1)
    finish(1)
    hop(2, 2)
    x_finish(0, out_o)
    y_add(3)
    hop(3, 1)
    y_add(4)
    hop(4, 1)
    hop(2, 3)
    hop(3, 2)
    hop(4, 2)
    finish(2)
    hop(3, 3)
    hop(4, 3)
    finish(3)
    finish(4)
    x_finish(1, ng_o)
    v_spread()
    for i in range(LUMPS):
        w_spread(i)
    for n in (1, 2):
        v_seq(n, twin[1], twin).wait_recv()
    keep = pltpu.make_async_copy(vall, sm_o, out.at[0])
    keep.start()
    for k in range(PARTS):
        spread(k)
    for k in range(PARTS):
        for n in range(2):
            spot = g_spot(twin[1], k)
            send(spot, spot, gc_s.at[n, k], gc_r.at[n, k], twin).wait_recv()
        pltpu.make_async_copy(g_spot(s, k), g_spot(s, k), loc.at[9 + k]).wait()
    keep.wait()
    v_seq(0, s, across).wait_send()
    v_seq(1, s, twin).wait_send()
    v_seq(2, s, twin).wait_send()
    for n, dst in both:
        for q in range(2):
            x_send(n, q).wait_send()
            pltpu.make_async_copy(xr.at[n, q], dst.at[q], out.at[2 + 2 * n + q]).wait()
    for q in range(2):
        twin_send(1, 1, q).wait_send()
    for k in range(PARTS):
        for e in range(deep):
            y_send(k, e).wait_send()

            @pl.when(z < e)
            def _():
                z_send(k, e, e, su, up).wait_send()

            @pl.when(z > e)
            def _():
                z_send(k, e, e, sd, down).wait_send()

        spot = g_spot(s, k)
        send(spot, spot, gx_s.at[k], gx_r.at[k], across).wait_send()
        for n in range(2):
            send(spot, spot, gc_s.at[n, k], gc_r.at[n, k], twin).wait_send()
    for i in range(LUMPS):
        wy_send(i).wait_send()

        @pl.when(z < s)
        def _():
            from_below(i).wait_send()

        @pl.when(z > s)
        def _():
            from_above(i).wait_send()

        @pl.when(root)
        def _():
            w_keep(i).wait()
            w_root(i, across, bx_s, bx_r).wait_send()

        @pl.when(root | (across[1] == z))
        def _():
            w_cast(i, twin, bc_s, bc_r).wait_send()


def scatter(normed_t, pg, scaled_t, scaled, cot, wo, wi, chacc, hacc, length, shards, groups):
    model, count = normed_t.shape
    total = pg.shape[1]
    inner = scaled_t.shape[0]
    seqs = count // length
    part = length // groups
    deep = shards // 2
    rows = model // shards
    any_ = pl.BlockSpec(memory_space=pl.ANY)
    dma = pltpu.SemaphoreType.DMA
    v = pltpu.VMEM
    small = (8, chacc.shape[2])
    return pl.pallas_call(
        functools.partial(scatter_kernel, (deep, rows, part, length)),
        in_specs=[any_] * 9,
        out_specs=[any_] * 5,
        out_shape=[
            jax.ShapeDtypeStruct((groups, rows, total), BF16),
            jax.ShapeDtypeStruct((inner // 2, model), BF16),
            jax.ShapeDtypeStruct((seqs, part, model), BF16),
            jax.ShapeDtypeStruct((seqs, part, model), BF16),
            jax.ShapeDtypeStruct((groups, *small), F32),
        ],
        scratch_shapes=[
            v((model, count), BF16),
            v((count, total), BF16),
            v((inner, count), BF16),
            v((count, inner), BF16),
            v((inner, model), BF16),
            v((count, total), BF16),
            v((model, total), BF16),
            v((deep * rows, total), BF16),
            v(((deep + 1) * rows, total), BF16),
            v((2, 2, 2, part, model), BF16),
            v((2, 2, part, model), BF16),
            v((2, part, model), BF16),
            v((inner, model), BF16),
            v((inner // 2, model), BF16),
            v((2, inner // 2, model), BF16),
            v(chacc.shape, F32),
            v(hacc.shape, F32),
            v(small, F32),
            v((deep + 1, *small), F32),
            v((groups, *small), F32),
            dma((PARTS, deep)), dma((PARTS, deep)), dma((PARTS, deep)), dma((PARTS, deep)),
            dma((PARTS, deep + 1)),
            dma((PARTS,)), dma((PARTS,)), dma((2, PARTS)), dma((2, PARTS)),
            dma((2,)), dma((2, 2, 2)), dma((2, 2)), dma((2, 2)),
            dma((LUMPS,)), dma((LUMPS,)), dma((LUMPS,)), dma((LUMPS,)), dma((2, LUMPS)),
            dma((LUMPS,)), dma((LUMPS,)), dma((LUMPS,)), dma((LUMPS,)),
            dma((deep + 4,)), dma((deep + 4,)),
            dma((9 + PARTS + LUMPS,)), dma((6,)),
        ],
        compiler_params=pltpu.CompilerParams(
            collective_id=2, has_side_effects=True, vmem_limit_bytes=60 * 2**20
        ),
        name="weigh_scatter",
    )(normed_t, pg, scaled_t, scaled, cot, wo, wi, chacc, hacc)


def local(
    tokens,
    segment_ids,
    w_in,
    w_out,
    conv_weight,
    conv_bias,
    norm_gain,
    gated_gain,
    dt_bias,
    a_log,
    skip_weight,
    cotangent,
):
    groups = lax.axis_size("seq")
    shards = lax.axis_size("dp")
    place = lax.axis_index("seq")
    owner = lax.axis_index("dp")
    seqs, part, model = tokens.shape
    length = part * groups
    rows_in = w_in.shape[0]
    rows_out = w_out.shape[0]
    wide = rows_out * shards
    heads = dt_bias.shape[0]
    size = wide // heads
    mine = heads // groups
    inner = mine * size
    span = 2 * inner
    taps = conv_weight.shape[1]
    state2 = w_in.shape[1] - 2 * wide - heads
    channels = wide + state2
    share = channels // shards
    ratio = shards // groups
    small_slice = groups == 4 and shards == 8

    def own(a):
        return lax.dynamic_slice_in_dim(a, place * inner, inner, 0)

    def own_heads(a):
        return lax.dynamic_slice_in_dim(a, place * mine, mine, 0)

    step_cols = jnp.pad(
        lax.dynamic_slice_in_dim(w_in, 2 * wide + state2 + place * mine, mine, 1),
        ((0, 0), (0, 128 - mine)),
    )
    def rows256(a):
        flat = a.reshape(-1)
        count = -(-flat.shape[0] // 256)
        return jnp.pad(flat, (0, count * 256 - flat.shape[0])).reshape(count, 256), count

    packs = [rows256(a) for a in (norm_gain, conv_bias, gated_gain, conv_weight)]
    small = jnp.concatenate([p[0] for p in packs])
    tall = -(-small.shape[0] // 16) * 16
    small = jnp.pad(small, ((0, tall - small.shape[0]), (0, 0)))
    if small_slice:
        turned, cot, pj, sg, w_full, wo, small_all = gather(
            w_in, step_cols, w_out, small, tokens, cotangent, inner, shards, groups
        )
    else:
        small_all = lax.all_gather(small, "dp", axis=0, tiled=False)
    small_all = small_all.astype(F32)
    cut = [0]
    for pack in packs:
        cut.append(cut[-1] + pack[1])

    def unpack(i, count):
        return small_all[:, cut[i] : cut[i + 1]].reshape(shards, -1)[:, :count].reshape(-1)

    norm_all = unpack(0, rows_in)
    conv_b = unpack(1, share)
    gain_all = unpack(2, rows_out)
    conv_w = unpack(3, share * taps).reshape(channels, taps)
    if not small_slice:
        floats = tokens.astype(F32)
        inverse = lax.rsqrt(jnp.mean(floats * floats, axis=-1, keepdims=True) + EPSILON)
        unit = floats * inverse
        w_mine = jnp.concatenate(
            [
                lax.dynamic_slice_in_dim(w_in, place * span, span, 1),
                w_in[:, 2 * wide : 2 * wide + state2],
                step_cols,
            ],
            axis=1,
        )
        normed = lax.all_gather((unit * norm_all).astype(BF16), "seq", axis=1, tiled=True)
        cot = lax.all_gather(cotangent, "seq", axis=1, tiled=True)
        w_full = lax.all_gather(w_mine, "dp", axis=0, tiled=True)
        held = jnp.where(
            (owner // ratio == place) & (jnp.arange(ratio)[:, None, None] == owner % ratio),
            w_out[None],
            jnp.zeros((), BF16),
        ).reshape(inner, model)
        wo = lax.psum(held, "dp")
        sg = jnp.einsum("std,cd->stc", cot, wo, preferred_element_type=F32).astype(BF16)
        pj = jnp.einsum("std,de->ste", normed, w_full, preferred_element_type=F32).astype(BF16)

    def pad(v):
        return jnp.pad(v, (0, 128 - mine))

    rate = -jnp.exp(own_heads(a_log))
    hp = jnp.stack([pad(own_heads(dt_bias)), pad(rate * LOG2E), pad(rate)] + [jnp.zeros(128)] * 5)
    blank = jnp.zeros((state2,), F32)
    ch = jnp.concatenate(
        [
            jnp.concatenate([own(conv_w), conv_w[wide:]]).T,
            jnp.concatenate([own(conv_b), conv_b[wide:]])[None],
            jnp.concatenate([jnp.repeat(own_heads(skip_weight), size), blank])[None],
            jnp.concatenate([own(gain_all), blank])[None],
            jnp.zeros((1, inner + state2), F32),
        ]
    )
    cols = columns(segment_ids)
    pre, ys, st, red = mix_forward(pj, cols, sg, hp, ch)
    if small_slice:
        rk = norms(red, wide, groups)
    else:
        totals = lax.psum(red[:, :2], "seq")
        rho = lax.rsqrt(totals[:, 0] / wide + EPSILON)
        rk = jnp.stack([rho, rho**3 * totals[:, 1] / wide] + [jnp.zeros_like(rho)] * 6, axis=1)
    pg, chacc, hacc, scaled_t, scaled = mix_backward(
        pj, cols, rk, sg, pre, ys, st, hp, ch, selectors(inner // 128)
    )
    flat_pg = pg.reshape(seqs * length, -1)
    flat_cot = cot.reshape(seqs * length, -1)
    if small_slice:
        win_grad, wo_grad, out_sum, ngrad, sums = scatter(
            turned, flat_pg, scaled_t, scaled.reshape(seqs * length, -1), flat_cot, wo, w_full,
            chacc, hacc, length, shards, groups,
        )
    else:
        product = jnp.einsum("stc,cd->std", scaled, wo, preferred_element_type=F32).astype(BF16)
        out_sum = lax.psum_scatter(product, "seq", scatter_dimension=1, tiled=True)
        product = jnp.einsum("ste,de->std", pg, w_full, preferred_element_type=F32).astype(BF16)
        ngrad = lax.psum_scatter(product, "seq", scatter_dimension=1, tiled=True)
        win_grad = jnp.einsum("std,ste->de", normed, pg, preferred_element_type=F32)
        win_grad = lax.psum_scatter(win_grad.astype(BF16), "dp", scatter_dimension=0, tiled=True)
        win_grad = lax.all_gather(win_grad, "seq", axis=0, tiled=False)
        wo_grad = jnp.dot(scaled_t, flat_cot, preferred_element_type=F32)
        wo_grad = lax.psum(wo_grad.astype(BF16), "dp").reshape(ratio, rows_out, model)
        wo_grad = lax.dynamic_index_in_dim(wo_grad, owner % ratio, 0, False)
        wo_grad = lax.psum(
            jnp.where(owner // ratio == place, wo_grad, jnp.zeros((), BF16)), "seq"
        )
        sums = jnp.concatenate(
            [
                jnp.sum(chacc, axis=1),
                jnp.pad(jnp.sum(hacc, axis=1), ((0, 0), (0, inner + state2 - 128))),
            ]
        )
        sums = lax.all_gather(lax.psum(sums, "dp"), "seq", axis=0, tiled=False)
    flat = (seqs * part, model)
    result, tokens_grad, w_in_grad, wo_grad, norm_sum, gain_sum = final(
        win_grad, w_in, wo_grad, w_out, out_sum.reshape(flat), ngrad.reshape(flat),
        tokens.reshape(flat), cotangent.reshape(flat), norm_all[None], span, mine,
    )
    chan = jnp.concatenate(
        [*[sums[g, : taps + 1, :inner] for g in range(groups)],
         jnp.sum(sums[:, : taps + 1, inner:], axis=0)],
        axis=1,
    )
    chan = lax.dynamic_slice_in_dim(chan, owner * share, share, 1)
    per_head = sums[:, taps + 1 : taps + 4, :mine].transpose(1, 0, 2).reshape(3, heads)
    return (
        result.reshape(tokens.shape),
        tokens_grad.reshape(tokens.shape),
        w_in_grad,
        wo_grad,
        chan[:taps].T,
        chan[taps],
        norm_sum[:, 0] / norm_gain.astype(F32),
        gain_sum[:, 0] / gated_gain.astype(F32),
        per_head[0],
        -jnp.exp(a_log) * per_head[1],
        per_head[2],
    )


def solution(mesh):
    return jax.shard_map(
        local,
        mesh=mesh,
        in_specs=(
            P("dp", "seq", None),
            P("dp", None),
            P("dp", None),
            P("dp", None),
            P("dp", None),
            P("dp"),
            P("dp"),
            P("dp"),
            P(),
            P(),
            P(),
            P("dp", "seq", None),
        ),
        out_specs=(
            P("dp", "seq", None),
            P("dp", "seq", None),
            P("dp", None),
            P("dp", None),
            P("dp", None),
            P("dp"),
            P("dp"),
            P("dp"),
            P(),
            P(),
            P(),
        ),
        check_vma=False,
    )
```

```python
import functools

import jax
import jax.numpy as jnp
from jax import lax
from jax.experimental import pallas as pl
from jax.experimental.pallas import tpu as pltpu
from jax.sharding import PartitionSpec as P

Q = 128
EXACT = lax.Precision.HIGHEST
EPSILON = 1e-05
LOG2E = 1.4426950408889634
RESET = 160.0
F32 = jnp.float32
BF16 = jnp.bfloat16
LUMPS = 6
WOFF = 1
MESH = pl.DeviceIdType.MESH


def sigmoid(x):
    return 0.5 * jnp.tanh(0.5 * x) + 0.5


def softplus(x):
    return jnp.maximum(x, 0.0) + jnp.log1p(jnp.exp(-jnp.abs(x)))


def nt(a, b):
    return lax.dot_general(a, b, (((1,), (1,)), ((), ())), preferred_element_type=F32)


def mm(a, b):
    return jnp.dot(a, b, preferred_element_type=F32)


def decays(pj, tall, hp, width):
    arg = pj[0, :, width + 256 : width + 384].astype(F32) + hp[0:1, :]
    dt = softplus(arg)
    rows = lax.broadcasted_iota(jnp.int32, (Q, Q), 0)
    lanes = lax.broadcasted_iota(jnp.int32, (Q, Q), 1)
    lower = (rows >= lanes).astype(F32)
    level = jnp.dot(lower, dt * hp[1:2, :], precision=EXACT, preferred_element_type=F32)
    level = level + tall[:, 3:4]
    return arg, dt, level, rows, lanes


def fwd_kernel(pairs, pj, marks, sg, hp, ch, pre, ys, st, red, state, tail):
    width = pairs * 256
    inner = pairs * 128
    chunk = pl.program_id(1)

    @pl.when(chunk == 0)
    def _():
        state[...] = jnp.zeros_like(state)
        tail[...] = jnp.zeros_like(tail)

    tall = jnp.concatenate([marks[0], jnp.zeros((Q - 8, Q), F32)], axis=0).T
    _, dt, level, rows, lanes = decays(pj, tall, hp, width)
    level_t = level.T
    low = lanes < 64
    masks = [tall[:, d : d + 1] for d in range(3)]

    def conv(raw, at):
        ext = jnp.concatenate([tail[:, at : at + 128], raw], axis=0)
        total = raw * ch[3:4, at : at + 128] + ch[4:5, at : at + 128]
        for d in (1, 2, 3):
            moved = pltpu.roll(ext, d, 0)[8:]
            total = total + moved * masks[d - 1] * ch[3 - d : 4 - d, at : at + 128]
        tail[:, at : at + 128] = raw[Q - 8 :]
        pre[0, :, at : at + 128] = total
        return total * sigmoid(total)

    b_rows = conv(pj[0, :, width : width + 128].astype(F32), inner)
    c_rows = conv(pj[0, :, width + 128 : width + 256].astype(F32), inner + 128)
    b_t = b_rows.T.astype(BF16)
    b_low = b_rows.astype(BF16)
    c_low = c_rows.astype(BF16)
    scores = jnp.where(rows >= lanes, nt(c_low, b_low), 0.0)
    old = state[...].astype(BF16)
    st[0, 0] = old
    carried_all = mm(c_low, old)
    squares = jnp.zeros((Q, 128), F32)
    cross = jnp.zeros((Q, 128), F32)
    for p in range(pairs):
        at = p * 128
        one = pj[0, :, p * 256 : p * 256 + 128].astype(F32)
        two = pj[0, :, p * 256 + 128 : p * 256 + 256].astype(F32)
        z = jnp.where(low, one, pltpu.roll(two, 64, 1))
        v = jnp.where(low, pltpu.roll(one, 64, 1), two)
        xc = conv(v, at)
        l0 = jnp.broadcast_to(level[:, 2 * p : 2 * p + 1], (Q, Q))
        l1 = jnp.broadcast_to(level[:, 2 * p + 1 : 2 * p + 2], (Q, Q))
        le = jnp.where(low, l0, l1)
        dte = jnp.where(low, dt[:, 2 * p : 2 * p + 1], dt[:, 2 * p + 1 : 2 * p + 2])
        u = xc * dte
        w0 = jnp.exp2(jnp.minimum(l0 - level_t[2 * p : 2 * p + 1, :], 0.0)) * scores
        w1 = jnp.exp2(jnp.minimum(l1 - level_t[2 * p + 1 : 2 * p + 2, :], 0.0)) * scores
        wide = jnp.concatenate([w0.astype(BF16), w1.astype(BF16)], axis=1)
        blocks = jnp.concatenate(
            [jnp.where(low, u, 0.0).astype(BF16), jnp.where(low, 0.0, u).astype(BF16)], axis=0
        )
        part = mm(wide, blocks) + carried_all[:, at : at + 128] * jnp.exp2(le)
        ys[0, :, at : at + 128] = part
        gated = (part + ch[5:6, at : at + 128] * xc) * (z * sigmoid(z))
        scaled = gated * ch[6:7, at : at + 128]
        squares = squares + gated * gated
        cross = cross + sg[0, :, at : at + 128].astype(F32) * scaled
        last = le[Q - 1 : Q, :]
        ul = (u * jnp.exp2(last - le)).astype(BF16)
        state[:, at : at + 128] = state[:, at : at + 128] * jnp.exp2(last) + mm(b_t, ul)
    both = jnp.where(
        lanes == 0, jnp.sum(squares, axis=1, keepdims=True), jnp.sum(cross, axis=1, keepdims=True)
    )
    red[0] = both.T[0:8]


def mix_forward(pj, marks, sg, hp, ch):
    seqs, length, total = pj.shape
    width = total - 384
    inner = width // 2
    pairs = inner // 128
    chunks = length // Q

    def row(n):
        return pl.BlockSpec((1, Q, n), lambda s, c: (s, c, 0))

    def whole(a):
        return pl.BlockSpec(a.shape, lambda s, c: (0,) * a.ndim)

    return pl.pallas_call(
        functools.partial(fwd_kernel, pairs),
        grid=(seqs, chunks),
        in_specs=[
            row(total),
            pl.BlockSpec((1, 8, Q), lambda s, c: (s, 0, c)),
            row(inner),
            whole(hp),
            whole(ch),
        ],
        out_specs=[
            row(inner + 256),
            row(inner),
            pl.BlockSpec((1, 1, 128, inner), lambda s, c: (s, c, 0, 0)),
            pl.BlockSpec((1, 8, Q), lambda s, c: (s, 0, c)),
        ],
        out_shape=[
            jax.ShapeDtypeStruct((seqs, length, inner + 256), F32),
            jax.ShapeDtypeStruct((seqs, length, inner), F32),
            jax.ShapeDtypeStruct((seqs, chunks, 128, inner), BF16),
            jax.ShapeDtypeStruct((seqs, 8, length), F32),
        ],
        scratch_shapes=[pltpu.VMEM((128, inner), F32), pltpu.VMEM((8, inner + 256), F32)],
        compiler_params=pltpu.CompilerParams(vmem_limit_bytes=60 * 2**20),
        name="mix_forward",
    )(pj, marks, sg, hp, ch)


def bwd_kernel(
    pairs, pj, marks, rk, sg, pre, ys, st, hp, ch, sel, pg, chacc, hacc, sct, scl,
    dstate, halo, edy_all, ul_all,
):
    width = pairs * 256
    inner = pairs * 128
    first = (pl.program_id(0) == 0) & (pl.program_id(1) == 0)

    @pl.when(pl.program_id(1) == 0)
    def _():
        dstate[...] = jnp.zeros_like(dstate)
        halo[...] = jnp.zeros_like(halo)

    @pl.when(first)
    def _():
        chacc[...] = jnp.zeros_like(chacc)
        hacc[...] = jnp.zeros_like(hacc)

    tall = jnp.concatenate([marks[0], rk[0], jnp.zeros((Q - 16, Q), F32)], axis=0).T
    arg, dt, level, rows, lanes = decays(pj, tall, hp, width)
    level_t = level.T
    low = lanes < 64
    masks = [tall[:, 3 + d : 4 + d] for d in (1, 2, 3)]
    rho = jnp.broadcast_to(tall[:, 8:9], (Q, 128))
    k2 = jnp.broadcast_to(tall[:, 9:10], (Q, 128))

    def fold(x):
        return jnp.sum(x.reshape(Q // 8, 8, 128), axis=0)

    def conv_back(grad, raw, at):
        ext = jnp.concatenate([grad, halo[:, at : at + 128]], axis=0)
        out = grad * ch[3:4, at : at + 128]
        chacc[3, :, at : at + 128] += fold(grad * raw)
        chacc[4, :, at : at + 128] += fold(grad)
        for d in (1, 2, 3):
            moved = pltpu.roll(ext, Q + 8 - d, 0)[:Q] * masks[d - 1]
            out = out + moved * ch[3 - d : 4 - d, at : at + 128]
            chacc[3 - d, :, at : at + 128] += fold(moved * raw)
        halo[:, at : at + 128] = grad[:8]
        return out

    pre_b = pre[0, :, inner : inner + 128]
    pre_c = pre[0, :, inner + 128 : inner + 256]
    sig_b, sig_c = sigmoid(pre_b), sigmoid(pre_c)
    b_rows, c_rows = pre_b * sig_b, pre_c * sig_c
    b_low, c_low = b_rows.astype(BF16), c_rows.astype(BF16)
    c_t = c_rows.T.astype(BF16)
    upper = lanes >= rows
    scores = jnp.where(upper, nt(b_low, c_low), 0.0)
    dlow = dstate[...].astype(BF16)
    dsb_all = mm(b_low, dlow)
    dscores = jnp.zeros((Q, Q), F32)
    sums = jnp.zeros((6 * Q, 128), F32)
    keep = jnp.zeros((8, 128), F32)
    for p in range(pairs):
        at = p * 128
        one = pj[0, :, p * 256 : p * 256 + 128].astype(F32)
        two = pj[0, :, p * 256 + 128 : p * 256 + 256].astype(F32)
        z = jnp.where(low, one, pltpu.roll(two, 64, 1))
        v = jnp.where(low, pltpu.roll(one, 64, 1), two)
        pr = pre[0, :, at : at + 128]
        sp = sigmoid(pr)
        xc = pr * sp
        l0 = jnp.broadcast_to(level[:, 2 * p : 2 * p + 1], (Q, Q))
        l1 = jnp.broadcast_to(level[:, 2 * p + 1 : 2 * p + 2], (Q, Q))
        le = jnp.where(low, l0, l1)
        dte = jnp.where(low, dt[:, 2 * p : 2 * p + 1], dt[:, 2 * p + 1 : 2 * p + 2])
        u = xc * dte
        skip = ch[5:6, at : at + 128]
        part = ys[0, :, at : at + 128]
        y = part + skip * xc
        sz = sigmoid(z)
        silz = z * sz
        gated = y * silz
        graw = sg[0, :, at : at + 128].astype(F32)
        scaled_rho = graw * rho
        scaled = gated * rho * ch[6:7, at : at + 128]
        sct[at : at + 128, :] = scaled.T.astype(BF16)
        scl[0, :, at : at + 128] = scaled.astype(BF16)
        gg = scaled_rho * ch[6:7, at : at + 128] - k2 * gated
        dy = gg * silz
        dz = gg * y * (sz + silz * (1.0 - sz))
        ulow = u.astype(BF16)
        dylow = dy.astype(BF16)
        w0 = jnp.exp2(jnp.minimum(level_t[2 * p : 2 * p + 1, :] - l0, 0.0))
        w1 = jnp.exp2(jnp.minimum(level_t[2 * p + 1 : 2 * p + 2, :] - l1, 0.0))
        wide = jnp.concatenate([(w0 * scores).astype(BF16), (w1 * scores).astype(BF16)], axis=1)
        dyb = jnp.concatenate(
            [jnp.where(low, dy, 0.0).astype(BF16), jnp.where(low, 0.0, dy).astype(BF16)], axis=0
        )
        ub = jnp.concatenate(
            [jnp.where(low, u, 0.0).astype(BF16), jnp.where(low, 0.0, u).astype(BF16)], axis=0
        )
        duw = mm(wide, dyb)
        gt = nt(ub, dylow)
        dscores = dscores + w0 * gt[:Q] + w1 * gt[Q:]
        last = le[Q - 1 : Q, :]
        lve = jnp.exp2(last - le)
        edy = (dy * jnp.exp2(le)).astype(BF16)
        ul = (u * lve).astype(BF16)
        edy_all[:, at : at + 128] = edy
        ul_all[:, at : at + 128] = ul
        dsb = dsb_all[:, at : at + 128]
        du = duw + lve * dsb
        r1 = dylow.astype(F32) * part - ulow.astype(F32) * duw
        r2 = ul.astype(F32) * dsb
        r1h, r2h = r1.astype(BF16), r2.astype(BF16)
        stacked = jnp.concatenate(
            [
                r1h,
                (r1 - r1h.astype(F32)).astype(BF16),
                r2h,
                (r2 - r2h.astype(F32)).astype(BF16),
                (dy * xc).astype(BF16),
                (du * xc).astype(BF16),
            ],
            axis=0,
        )
        sums = sums + mm(stacked, sel[p])
        decay = jnp.exp2(last)
        kept = fold(dlow[:, at : at + 128].astype(F32) * st[0, 0, :, at : at + 128].astype(F32)) * decay
        kept_high = kept.astype(BF16)
        keep = keep + mm(kept_high, sel[p]) + mm((kept - kept_high.astype(F32)).astype(BF16), sel[p])
        dstate[:, at : at + 128] = dstate[:, at : at + 128] * decay + mm(c_t, edy)
        dv = conv_back((du * dte + skip * dy) * (sp + xc * (1.0 - sp)), v, at)
        pg[0, :, p * 256 : p * 256 + 128] = jnp.where(low, dz, pltpu.roll(dv, 64, 1)).astype(BF16)
        pg[0, :, p * 256 + 128 : p * 256 + 256] = jnp.where(low, pltpu.roll(dz, 64, 1), dv).astype(BF16)
    dsc = jnp.where(upper, dscores, 0.0)
    db = mm(dsc.astype(BF16), c_low) + nt(ul_all[...], dlow)
    dc = mm(dsc.T.astype(BF16), b_low) + nt(edy_all[...], st[0, 0])
    raw_b = pj[0, :, width : width + 128].astype(F32)
    raw_c = pj[0, :, width + 128 : width + 256].astype(F32)
    pg[0, :, width : width + 128] = conv_back(
        db * (sig_b + b_rows * (1.0 - sig_b)), raw_b, inner
    ).astype(BF16)
    pg[0, :, width + 128 : width + 256] = conv_back(
        dc * (sig_c + c_rows * (1.0 - sig_c)), raw_c, inner + 128
    ).astype(BF16)
    r1 = sums[:Q] + sums[Q : 2 * Q]
    r2 = sums[2 * Q : 3 * Q] + sums[3 * Q : 4 * Q]
    da = (
        jnp.dot(upper.astype(F32), r1, precision=EXACT, preferred_element_type=F32)
        + jnp.dot((rows > lanes).astype(F32), r2, precision=EXACT, preferred_element_type=F32)
        + jnp.sum(keep, axis=0, keepdims=True)
    )
    ddt = da * hp[2:3, :] + sums[5 * Q :]
    ds = ddt * sigmoid(arg)
    pg[0, :, width + 256 : width + 384] = ds.astype(BF16)
    hacc[0] += fold(ds)
    hacc[1] += fold(da * dt)
    hacc[2] += fold(sums[4 * Q : 5 * Q])


def mix_backward(pj, marks, rk, sg, pre, ys, st, hp, ch, sel):
    seqs, length, total = pj.shape
    width = total - 384
    inner = width // 2
    pairs = inner // 128
    chunks = length // Q

    def row(n):
        return pl.BlockSpec((1, Q, n), lambda s, c: (s, chunks - 1 - c, 0))

    def whole(shape):
        return pl.BlockSpec(shape, lambda s, c: (0,) * len(shape))

    return pl.pallas_call(
        functools.partial(bwd_kernel, pairs),
        grid=(seqs, chunks),
        in_specs=[
            row(total),
            pl.BlockSpec((1, 8, Q), lambda s, c: (s, 0, chunks - 1 - c)),
            pl.BlockSpec((1, 8, Q), lambda s, c: (s, 0, chunks - 1 - c)),
            row(inner),
            row(inner + 256),
            row(inner),
            pl.BlockSpec((1, 1, 128, inner), lambda s, c: (s, chunks - 1 - c, 0, 0)),
            whole(hp.shape),
            whole(ch.shape),
            whole(sel.shape),
        ],
        out_specs=[
            row(total),
            whole((5, 8, inner + 256)),
            whole((3, 8, 128)),
            pl.BlockSpec((inner, Q), lambda s, c: (0, s * chunks + chunks - 1 - c)),
            row(inner),
        ],
        out_shape=[
            jax.ShapeDtypeStruct((seqs, length, total), BF16),
            jax.ShapeDtypeStruct((5, 8, inner + 256), F32),
            jax.ShapeDtypeStruct((3, 8, 128), F32),
            jax.ShapeDtypeStruct((inner, seqs * length), BF16),
            jax.ShapeDtypeStruct((seqs, length, inner), BF16),
        ],
        scratch_shapes=[
            pltpu.VMEM((128, inner), F32),
            pltpu.VMEM((8, inner + 256), F32),
            pltpu.VMEM((Q, inner), BF16),
            pltpu.VMEM((Q, inner), BF16),
        ],
        compiler_params=pltpu.CompilerParams(vmem_limit_bytes=60 * 2**20),
        name="mix_backward",
    )(pj, marks, rk, sg, pre, ys, st, hp, ch, sel)


def marks_kernel(seg, marks):
    seqs, length = seg.shape
    ids = seg[...].astype(F32)
    lane = lax.broadcasted_iota(jnp.int32, (seqs, length), 1)
    back = [
        jnp.where((pltpu.roll(ids, d, 1) == ids) & (lane >= d), 1.0, 0.0) for d in (1, 2, 3)
    ]
    ahead = [
        jnp.where((pltpu.roll(ids, length - d, 1) == ids) & (lane < length - d), 1.0, 0.0)
        for d in (1, 2, 3)
    ]
    before = [ids[:, 0:1]] + [ids[:, at - 1 : at] for at in range(Q, length, Q)]
    level = jnp.concatenate(
        [-RESET * (ids[:, n * Q : (n + 1) * Q] - b) for n, b in enumerate(before)], axis=1
    )
    all_rows = [*back, level, *ahead, jnp.zeros((seqs, length), F32)]
    for n in range(seqs):
        marks[n] = jnp.concatenate([r[n : n + 1, :] for r in all_rows], axis=0)


def marks_of(seg):
    return pl.pallas_call(
        marks_kernel,
        out_shape=jax.ShapeDtypeStruct((seg.shape[0], 8, seg.shape[1]), F32),
        name="marks",
    )(seg)


def selectors(pairs):
    lane = lax.broadcasted_iota(jnp.int32, (pairs, 128, 128), 1)
    pair = lax.broadcasted_iota(jnp.int32, (pairs, 128, 128), 0)
    out = lax.broadcasted_iota(jnp.int32, (pairs, 128, 128), 2)
    return (out == 2 * pair + lane // 64).astype(BF16)


def norm_kernel(wide, red, rk, got, ssem, rsem):
    d = lax.axis_index("dp")
    s = lax.axis_index("seq")
    groups = got.shape[0]
    bar = pltpu.get_barrier_semaphore()
    for j in range(1, groups):
        pl.semaphore_signal(bar, inc=1, device_id=(d, lax.rem(s + j, groups)), device_id_type=MESH)
    pl.semaphore_wait(bar, groups - 1)
    sends = [
        pltpu.make_async_remote_copy(
            src_ref=red, dst_ref=got.at[j], send_sem=ssem.at[j], recv_sem=rsem.at[j],
            device_id=(d, lax.rem(s + j, groups)), device_id_type=MESH,
        )
        for j in range(1, groups)
    ]
    for copy in sends:
        copy.start()
    total = red[...]
    for j, copy in enumerate(sends):
        copy.wait()
        total = total + got[j + 1]
    rho = lax.rsqrt(total[:, 0:1] / wide + EPSILON)
    rk[...] = jnp.concatenate(
        [rho, rho * rho * rho * total[:, 1:2] / wide, jnp.zeros_like(total[:, 2:])], axis=1
    )


def norms(red, wide, groups):
    vmem = pl.BlockSpec(memory_space=pltpu.VMEM)
    return pl.pallas_call(
        functools.partial(norm_kernel, wide),
        in_specs=[vmem],
        out_specs=vmem,
        out_shape=jax.ShapeDtypeStruct(red.shape, F32),
        scratch_shapes=[
            pltpu.VMEM((groups, *red.shape), F32),
            pltpu.SemaphoreType.DMA((groups,)),
            pltpu.SemaphoreType.DMA((groups,)),
        ],
        compiler_params=pltpu.CompilerParams(collective_id=3, has_side_effects=True),
        name="norms",
    )(red)


def final_kernel(
    groups, span, mine, share, gw, w_in, wog, w_out, osum, ngrad, tok, cot, gains, sums,
    res, tgrad, wig, wgr, nsum, gsum, chan, head,
):
    @pl.when(pl.program_id(0) == 0)
    def _():
        inner = span // 2
        shared = sums[0, :, inner:]
        heads = sums[0, :, :128]
        for g in range(1, groups):
            shared = shared + sums[g, :, inner:]
            heads = heads + pltpu.roll(sums[g, :, :128], g * mine, 1)
        row = jnp.concatenate([*[sums[g, :, :inner] for g in range(groups)], shared], axis=1)
        first = lax.axis_index("dp") * share
        own = pltpu.roll(row, row.shape[1] - first, 1)[:, : chan.shape[0]]
        chan[...] = own.T
        head[...] = heads

    total = jnp.zeros((w_in.shape[0], 1), F32)
    for g in range(groups):
        here = slice(g * span, (g + 1) * span)
        grad = gw[g, :, :span].astype(F32)
        wig[:, here] = grad
        total = total + jnp.sum(grad * w_in[:, here].astype(F32), axis=1, keepdims=True)
    at = groups * span
    width = gw.shape[2] - 128
    shared = gw[0, :, span:width].astype(F32)
    steps = gw[0, :, width:].astype(F32)
    for g in range(1, groups):
        shared = shared + gw[g, :, span:width].astype(F32)
        steps = steps + pltpu.roll(gw[g, :, width:].astype(F32), g * mine, 1)
    mid = at + width - span
    wig[:, at:mid] = shared
    wig[:, mid:] = steps[:, : groups * mine]
    total = total + jnp.sum(shared * w_in[:, at:mid].astype(F32), axis=1, keepdims=True)
    total = total + jnp.sum(
        steps[:, : groups * mine] * w_in[:, mid:].astype(F32), axis=1, keepdims=True
    )
    nsum[...] = jnp.broadcast_to(total, nsum.shape)
    grad = wog[...].astype(F32)
    wgr[...] = grad
    gsum[...] = jnp.broadcast_to(
        jnp.sum(grad * w_out[...].astype(F32), axis=1, keepdims=True), gsum.shape
    )
    x = tok[...].astype(F32)
    res[...] = (x + osum[...].astype(F32)).astype(BF16)
    inverse = lax.rsqrt(jnp.mean(x * x, axis=1, keepdims=True) + EPSILON)
    unit = x * inverse
    grad = ngrad[...].astype(F32) * gains[0:1, :]
    tgrad[...] = cot[...].astype(F32) + inverse * (
        grad - unit * jnp.mean(grad * unit, axis=1, keepdims=True)
    )


def final(gw, w_in, wog, w_out, osum, ngrad, tok, cot, gains, sums, span, mine, share):
    groups, rows, total = gw.shape
    steps = next(n for n in (4, 2, 1) if rows % (16 * n) == 0)

    def part(a):
        return pl.BlockSpec((a.shape[0] // steps, a.shape[1]), lambda i: (i, 0))

    tall = [w_in, wog, w_out, osum, ngrad, tok, cot]
    shapes = [
        (tok.shape, BF16), (tok.shape, F32), (w_in.shape, F32), (wog.shape, F32),
        ((rows, 128), F32), ((wog.shape[0], 128), F32),
    ]
    outs = [jax.ShapeDtypeStruct(*n) for n in shapes]
    chan = jax.ShapeDtypeStruct((-(-share // 128) * 128, 8), F32)
    head = jax.ShapeDtypeStruct((8, 128), F32)
    return pl.pallas_call(
        functools.partial(final_kernel, groups, span, mine, share),
        grid=(steps,),
        in_specs=[
            pl.BlockSpec((groups, rows // steps, total), lambda i: (0, i, 0)),
            *[part(a) for a in tall],
            pl.BlockSpec(gains.shape, lambda i: (0, 0)),
            pl.BlockSpec(sums.shape, lambda i: (0, 0, 0)),
        ],
        out_specs=[
            *[part(o) for o in outs],
            pl.BlockSpec(chan.shape, lambda i: (0, 0)),
            pl.BlockSpec(head.shape, lambda i: (0, 0)),
        ],
        out_shape=[*outs, chan, head],
        compiler_params=pltpu.CompilerParams(vmem_limit_bytes=60 * 2**20),
        name="final",
    )(gw, *tall, gains, sums)


def gather_kernel(
    dims, w_in, dt_in, wo_in, small_in, tok_in, cot_in,
    turned_o, cot_o, pj_o, sg_o, w_o, wo_o, small_o,
    tok, cot, wbig, wo, small, pjv, sgv, turned,
    szu, szd, rz, sy, ry, wsu, wsd, wrz, wsy, wry, bx_s, bx_r, bc_s, bc_r, loc, out,
):
    deep, pieces, rows, inner, part, length, groups = dims
    d = lax.axis_index("dp")
    s = lax.axis_index("seq")
    z = d // 2
    y = d % 2
    top = deep - 1
    up, down, side = (d + 2, s), (d - 2, s), (d + 1 - 2 * y, s)
    across, twin = (d, s + 2 - 4 * (s // 2)), (d, s + 1 - 2 * (s % 2))
    opposite = across[1]

    bar = pltpu.get_barrier_semaphore()

    @pl.when(z < top)
    def _():
        pl.semaphore_signal(bar, inc=1, device_id=up, device_id_type=MESH)

    @pl.when(z > 0)
    def _():
        pl.semaphore_signal(bar, inc=1, device_id=down, device_id_type=MESH)

    for who in (side, across, twin):
        pl.semaphore_signal(bar, inc=1, device_id=who, device_id_type=MESH)
    pl.semaphore_wait(bar, 3 + jnp.minimum(z, 1) + jnp.minimum(top - z, 1))

    def send(src, dst, ssem, rsem, who):
        return pltpu.make_async_remote_copy(
            src_ref=src, dst_ref=dst, send_sem=ssem, recv_sem=rsem,
            device_id=who, device_id_type=MESH,
        )

    width = 2 * inner

    def cols(k):
        return pl.ds(width + 256, 128) if k == 1 else pl.ds(width if k == 2 else (k - 3) * 256, 256)

    def held(k, owner):
        if k == 0:
            return small.at[owner]
        return wbig.at[pl.ds(pl.multiple_of(owner * rows, 16), rows), cols(k)]

    def source(k):
        if k == 0:
            return small_in.at[...]
        if k == 1:
            return dt_in.at[...]
        if k == 2:
            return w_in.at[:, pl.ds(width * groups, 256)]
        return w_in.at[:, pl.ds(pl.multiple_of(s * width + (k - 3) * 256, 128), 256)]

    def own_send(k):
        src, dst = source(k), held(k, d)

        @pl.when(z < top)
        def _():
            send(src, dst, szu.at[k, z], rz.at[k, z], up).start()

        @pl.when(z > 0)
        def _():
            send(src, dst, szd.at[k, z], rz.at[k, z], down).start()

        send(src, dst, sy.at[k, z], ry.at[k, z], side).start()

    def hop(k, h):
        below, above = z - h, z + h

        @pl.when(below >= 0)
        def _():
            ref = held(k, below * 2 + y)
            send(ref, ref, szu.at[k, below], rz.at[k, below], up).wait_recv()

            @pl.when(z < top)
            def _():
                send(ref, ref, szu.at[k, below], rz.at[k, below], up).start()

            send(ref, ref, sy.at[k, below], ry.at[k, below], side).start()

        @pl.when(above <= top)
        def _():
            ref = held(k, above * 2 + y)
            send(ref, ref, szd.at[k, above], rz.at[k, above], down).wait_recv()

            @pl.when(z > 0)
            def _():
                send(ref, ref, szd.at[k, above], rz.at[k, above], down).start()

            send(ref, ref, sy.at[k, above], ry.at[k, above], side).start()

    def arrive(k):
        for e in range(deep):
            ref = held(k, e * 2 + 1 - y)
            send(ref, ref, sy.at[k, e], ry.at[k, e], side).wait_recv()

    def own_copy(src, dst, sem):
        return pltpu.make_async_copy(src, dst, sem)

    here = pl.multiple_of(s * part, 16)
    there = pl.multiple_of(opposite * part, 16)
    locals_ = [
        own_copy(small_in, small.at[d], loc.at[0]),
        own_copy(
            w_in.at[:, pl.ds(pl.multiple_of(s * width, 128), width)],
            wbig.at[pl.ds(pl.multiple_of(d * rows, 16), rows), pl.ds(0, width)],
            loc.at[1],
        ),
    ]
    for q in range(2):
        locals_.append(own_copy(tok_in.at[q], tok.at[q, pl.ds(here, part)], loc.at[2 + q]))
        locals_.append(own_copy(cot_in.at[q], cot.at[q, pl.ds(here, part)], loc.at[4 + q]))
    for k in (1, 2):
        locals_.append(own_copy(source(k), held(k, d), loc.at[6 + k]))
    half = wo_in.shape[0]
    mine = z == s

    def root_copy():
        return own_copy(wo_in, wo.at[pl.ds(pl.multiple_of(y * half, 16), half)], loc.at[6])

    def block_sends(which, src, dst, q):
        spot = dst.at[q, pl.ds(here, part)]
        i = which * 2 + q
        send(src.at[q], spot, bx_s.at[i], bx_r.at[i], across).start()
        send(src.at[q], spot, bc_s.at[0, i], bc_r.at[0, i], twin).start()

    def block_forward(which, dst, q):
        spot = dst.at[q, pl.ds(there, part)]
        i = which * 2 + q
        send(spot, spot, bx_s.at[i], bx_r.at[i], across).wait_recv()
        send(spot, spot, bc_s.at[1, i], bc_r.at[1, i], twin).start()

    def block_arrive(which, dst, q):
        i = which * 2 + q
        for n in range(2):
            spot = dst.at[q, pl.ds(here, part)]
            send(spot, spot, bc_s.at[n, i], bc_r.at[n, i], twin).wait_recv()

    lump = half // LUMPS

    def wo_piece(i, col):
        m = col * LUMPS + i
        return m, wo.at[pl.ds(pl.multiple_of(m * lump, 16), lump)]

    def wo_send(i, src=None):
        m, ref = wo_piece(i, y)
        src = ref if src is None else src

        @pl.when((z >= s) & (z < top))
        def _():
            send(src, ref, wsu.at[m], wrz.at[m], up).start()

        @pl.when((z <= s) & (z > 0))
        def _():
            send(src, ref, wsd.at[m], wrz.at[m], down).start()

        send(src, ref, wsy.at[m], wry.at[m], side).start()

    def wo_root(i):
        @pl.when(mine)
        def _():
            wo_send(i, wo_in.at[pl.ds(i * lump, lump)])

    def wo_hop(i, h):
        @pl.when((z - s == h) | (s - z == h))
        def _():
            m, ref = wo_piece(i, y)
            send(ref, ref, wsu.at[m], wrz.at[m], up).wait_recv()
            wo_send(i)

    def wo_arrive(i):
        m, ref = wo_piece(i, 1 - y)
        send(ref, ref, wsy.at[m], wry.at[m], side).wait_recv()

    tile = 256
    long = 512

    def project(k):
        c = pl.ds(width, 384) if k == 2 else cols(k)

        def step(i, _):
            q, r = i // (length // long), i % (length // long)
            at = pl.ds(pl.multiple_of(r * long, long), long)
            pjv[q, at, c] = mm(tok[q, at, :], wbig[:, c]).astype(BF16)
            return 0

        lax.fori_loop(0, 2 * length // long, step, 0)
        own_copy(pjv.at[:, :, c], pj_o.at[:, :, c], out.at[k]).start()

    for c in locals_:
        c.start()

    @pl.when(mine)
    def _():
        root_copy().start()

    for q in range(2):
        block_sends(0, tok_in, tok, q)
    ahead = 3
    for k in range(ahead):
        own_send(k)
    done = []

    def hops(t):
        for h in range(1, deep):
            if 0 <= t - h < pieces:
                hop(t - h, h)
        for h in range(1, deep):
            if 0 <= t - h - WOFF < LUMPS:
                wo_hop(t - h - WOFF, h)
        if 0 <= t - WOFF < LUMPS:
            wo_root(t - WOFF)
        if ahead <= t + ahead - 1 < pieces:
            own_send(t + ahead - 1)

    steps = max(pieces, WOFF + LUMPS) + deep - 1
    count = dict(next=1)

    def ready(n):
        for _ in range(n):
            if count["next"] < pieces:
                arrive(count["next"])
                if count["next"] > 1:
                    project(count["next"])
                count["next"] += 1

    share = tok.shape[2] // (2 * deep)

    def norm_step(i, _):
        q, r = i // (length // 64), i % (length // 64)
        at = pl.multiple_of(r * 64, 64)
        x = tok[q, pl.ds(at, 64), :].astype(F32)
        inv = lax.rsqrt(jnp.mean(x * x, axis=1, keepdims=True) + EPSILON)
        gains = jnp.concatenate([small[e, 0:1, :share] for e in range(2 * deep)], axis=1)
        tok[q, pl.ds(at, 64), :] = (x * inv * gains.astype(F32)).astype(BF16)
        return 0

    def turn_step(i, _):
        q, r = i // (length // tile), i % (length // tile)
        at = pl.multiple_of(r * tile, tile)
        to = pl.multiple_of(i * tile, tile)
        for j in range(0, tok.shape[2], 128):
            turned[j : j + 128, pl.ds(to, tile)] = tok[q, pl.ds(at, tile), j : j + 128].T
        return 0

    def grad_step(i, _):
        q, r = i // (length // long), i % (length // long)
        at = pl.ds(pl.multiple_of(r * long, long), long)
        sgv[q, at, :] = nt(cot[q, at, :], wo[...]).astype(BF16)
        return 0

    for t in range(1, steps):
        hops(t)
        if t == 3:
            block_forward(0, tok, 0)
        if t == 6:
            block_forward(0, tok, 1)
            for q in range(2):
                block_sends(1, cot_in, cot, q)
        if t == 7:
            for i in (0, 1, 2, 4, 6, 7):
                locals_[i].wait()
            block_arrive(0, tok, 0)
            block_arrive(0, tok, 1)
            for q in range(2):
                spot = tok.at[q, pl.ds(there, part)]
                send(spot, spot, bc_s.at[1, q], bc_r.at[1, q], twin).wait_send()
            arrive(0)
            own_copy(small, small_o, out.at[0]).start()
            lax.fori_loop(0, 2 * length // 64, norm_step, 0)
            lax.fori_loop(0, 2 * length // tile, turn_step, 0)
            own_copy(turned, turned_o, out.at[pieces]).start()
        if t == 10:
            block_forward(1, cot, 0)
        if t == 11:
            block_forward(1, cot, 1)
        if t > 7:
            ready(2 if t == 8 else 1)

    @pl.when(mine)
    def _():
        root_copy().wait()

    locals_[3].wait()
    locals_[5].wait()
    for i in range(LUMPS):
        wo_arrive(i)
    own_copy(wo, wo_o, out.at[pieces + 2]).start()
    block_arrive(1, cot, 0)
    block_arrive(1, cot, 1)
    own_copy(cot, cot_o, out.at[pieces + 3]).start()
    lax.fori_loop(0, 2 * length // long, grad_step, 0)
    own_copy(sgv, sg_o, out.at[pieces + 4]).start()
    ready(pieces)
    own_copy(wbig, w_o, out.at[pieces + 1]).start()
    for k in range(pieces):
        for e in range(deep):
            ref = held(k, e * 2 + y)

            @pl.when((z >= e) & (z < top))
            def _():
                send(ref, ref, szu.at[k, e], rz.at[k, e], up).wait_send()

            @pl.when((z <= e) & (z > 0))
            def _():
                send(ref, ref, szd.at[k, e], rz.at[k, e], down).wait_send()

            send(ref, ref, sy.at[k, e], ry.at[k, e], side).wait_send()
    for i in range(LUMPS):
        m, ref = wo_piece(i, y)

        @pl.when((z >= s) & (z < top))
        def _():
            send(ref, ref, wsu.at[m], wrz.at[m], up).wait_send()

        @pl.when((z <= s) & (z > 0))
        def _():
            send(ref, ref, wsd.at[m], wrz.at[m], down).wait_send()

        send(ref, ref, wsy.at[m], wry.at[m], side).wait_send()
    for which, dst in ((0, tok), (1, cot)):
        for q in range(2):
            i = which * 2 + q
            spot = dst.at[q, pl.ds(here, part)]
            send(spot, spot, bx_s.at[i], bx_r.at[i], across).wait_send()
            for n in range(1 + which):
                send(spot, spot, bc_s.at[n, i], bc_r.at[n, i], twin).wait_send()
    own_copy(small, small_o, out.at[0]).wait()
    for k in range(2, pieces):
        c = pl.ds(width, 384) if k == 2 else cols(k)
        own_copy(pjv.at[:, :, c], pj_o.at[:, :, c], out.at[k]).wait()
    own_copy(turned, turned_o, out.at[pieces]).wait()
    own_copy(wbig, w_o, out.at[pieces + 1]).wait()
    own_copy(wo, wo_o, out.at[pieces + 2]).wait()
    own_copy(cot, cot_o, out.at[pieces + 3]).wait()
    own_copy(sgv, sg_o, out.at[pieces + 4]).wait()


def gather(w_in, dt_in, w_out, small, tokens, cotangent, inner, shards, groups):
    rows = w_in.shape[0]
    total = 2 * inner + 384
    seqs, part, model = tokens.shape
    length = part * groups
    deep = shards // 2
    pieces = inner // 128 + 3
    any_ = pl.BlockSpec(memory_space=pl.ANY)
    dma = pltpu.SemaphoreType.DMA
    small_rows, small_cols = small.shape
    full = (shards * rows, total)
    shapes = [
        (model, seqs * length), (seqs, length, model), (seqs, length, total), (seqs, length, inner),
        full, (inner, model), (shards, small_rows, small_cols),
    ]
    return pl.pallas_call(
        functools.partial(gather_kernel, (deep, pieces, rows, inner, part, length, groups)),
        in_specs=[any_] * 6,
        out_specs=[any_] * 7,
        out_shape=[jax.ShapeDtypeStruct(n, BF16) for n in shapes],
        scratch_shapes=[
            pltpu.VMEM(shapes[1], BF16),
            pltpu.VMEM(shapes[1], BF16),
            pltpu.VMEM(full, BF16),
            pltpu.VMEM((inner, model), BF16),
            pltpu.VMEM(shapes[6], BF16),
            pltpu.VMEM(shapes[2], BF16),
            pltpu.VMEM(shapes[3], BF16),
            pltpu.VMEM(shapes[0], BF16),
            dma((pieces, deep)), dma((pieces, deep)), dma((pieces, deep)),
            dma((pieces, deep)), dma((pieces, deep)),
            *[dma((2 * LUMPS,))] * 5,
            dma((4,)), dma((4,)), dma((2, 4)), dma((2, 4)),
            dma((9,)), dma((pieces + 5,)),
        ],
        compiler_params=pltpu.CompilerParams(
            collective_id=1, has_side_effects=True, vmem_limit_bytes=56 * 2**20
        ),
        name="gather_project",
    )(w_in, dt_in, w_out, small, tokens, cotangent)


def greet(z, y, s, deep, others):
    bar = pltpu.get_barrier_semaphore()
    for e in range(deep):
        @pl.when(z != e)
        def _():
            pl.semaphore_signal(bar, inc=1, device_id=(2 * e + y, s), device_id_type=MESH)

    for who in others:
        pl.semaphore_signal(bar, inc=1, device_id=who, device_id_type=MESH)
    pl.semaphore_wait(bar, len(others) + deep - 1)


def send(src, dst, ssem, rsem, who):
    return pltpu.make_async_remote_copy(
        src_ref=src, dst_ref=dst, send_sem=ssem, recv_sem=rsem, device_id=who, device_id_type=MESH
    )


def add_into(dst, src):
    count = dst.shape[0]
    some = next(n for n in (64, 48, 32, 16) if count % n == 0)

    def step(i, _):
        at = pl.ds(pl.multiple_of(i * some, 16), some)
        dst[at, :] = (dst[at, :].astype(F32) + src[at, :].astype(F32)).astype(BF16)
        return 0

    lax.fori_loop(0, count // some, step, 0)


CUTS = ((0, 512), (512, 512), (1536, 384), (1024, 256), (1280, 256))
PARTS = len(CUTS)


def scatter_kernel(
    dims, nt_in, pg_in, st_in, sc_in, cot_in, wo_in, wi_in, ch_in, he_in,
    gw_o, wo_o, out_o, ng_o, sm_o,
    nt_v, pg_v, st_v, sc_v, wo_v, cw, pv, yb, zb, tw, xr, stage, gw, ybw, zbw, ch_v, he_v,
    vec, vgot, vall,
    sy, ry, su, sd, rz, gx_s, gx_r, gc_s, gc_r, tw_s, tw_r, xr_s, xr_r,
    wy_s, wy_r, wu_s, wd_s, wz_r, bx_s, bx_r, bc_s, bc_r, v_s, v_r, loc, out,
):
    deep, rows, part, length = dims
    d = lax.axis_index("dp")
    s = lax.axis_index("seq")
    z = d // 2
    y = d % 2
    x = s // 2
    c = s % 2
    top = deep - 1
    model = wi_in.shape[0]
    up, down, side = (d + 2, s), (d - 2, s), (d + 1 - 2 * y, s)
    across, twin = (d, s + 2 - 4 * x), (d, s + 1 - 2 * c)
    greet(z, y, s, deep, (side, across, twin))

    def cut(k):
        return pl.ds(*CUTS[k])

    def lines(ref, i, count=rows):
        return ref.at[pl.ds(pl.multiple_of(i * count, 16), count)]

    cot_v = cw.at[:, pl.ds(0, model)]
    wi_v = cw.at[pl.ds(0, model), :]
    loads = dict(
        ch=pltpu.make_async_copy(ch_in, ch_v, loc.at[2]),
        he=pltpu.make_async_copy(he_in, he_v, loc.at[3]),
        st=pltpu.make_async_copy(st_in, st_v, loc.at[0]),
        cot=pltpu.make_async_copy(cot_in, cot_v, loc.at[1]),
        sc=pltpu.make_async_copy(sc_in, sc_v, loc.at[6]),
        wo=pltpu.make_async_copy(wo_in, wo_v, loc.at[7]),
        nt=pltpu.make_async_copy(nt_in, nt_v, loc.at[4]),
        pg=pltpu.make_async_copy(pg_in, pg_v, loc.at[5]),
    )
    for load in loads.values():
        load.start()
    load_wi = pltpu.make_async_copy(wi_in, wi_v, loc.at[8])

    def v_send(n, src, dst, who):
        return send(src, dst, v_s.at[n], v_r.at[n], who)

    def v_y():
        return v_send(0, vec, vgot.at[deep], side)

    def v_z(e):
        return send(vec, vgot.at[z], v_s.at[1 + e], v_r.at[1 + z], (2 * e + y, s))

    def v_from(e):
        return send(vec, vgot.at[e], v_s.at[1 + e], v_r.at[1 + e], (2 * e + y, s))

    def v_seq(n, owner, who):
        return v_send(1 + deep + n, vall.at[owner], vall.at[owner], who)

    def v_start():
        vec[...] = jnp.concatenate(
            [
                jnp.sum(ch_v[...], axis=1),
                jnp.concatenate(
                    [jnp.sum(he_v[...], axis=1), jnp.zeros((3, vec.shape[1] - 128), F32)], axis=1
                ),
            ],
            axis=0,
        )
        v_y().start()

    def v_sum():
        v_y().wait()
        vec[...] = vec[...] + vgot[deep]
        for e in range(deep):
            @pl.when(z != e)
            def _():
                v_z(e).start()

    def v_total():
        for e in range(deep):
            @pl.when(z != e)
            def _():
                v_z(e).wait_send()
                v_from(e).wait_recv()

            @pl.when(z == e)
            def _():
                vgot[e] = vec[...]

        total = vgot[0]
        for e in range(1, deep):
            total = total + vgot[e]
        vall[s] = total
        v_seq(0, s, across).start()
        v_seq(1, s, twin).start()

    def v_spread():
        v_seq(0, across[1], across).wait_recv()
        v_seq(2, across[1], twin).start()

    both = ((0, out_o), (1, ng_o))

    def twin_send(n, turn, q):
        return send(stage.at[q], tw.at[n, turn, q], tw_s.at[q], tw_r.at[n, turn, q], twin)

    def product(n, q, owner, j):
        at = pl.ds(pl.multiple_of(q * length + owner * part, 16), part)
        if n == 0:
            return mm(sc_v[at, :], wo_v[:, j : j + 512])
        return nt(pg_v[at, :], cw[j : j + 512, :])

    def exchange(n, turn):
        half = 1 - x if turn == 0 else x
        for q in range(2):
            if (n, turn) != (0, 0):
                twin_send(n, turn, q).wait_send()
            for j in range(0, model, 512):
                stage[q, :, j : j + 512] = product(n, q, 2 * half + 1 - c, j).astype(BF16)
            twin_send(n, turn, q).start()
        for q in range(2):
            twin_send(n, turn, q).wait_recv()
            for j in range(0, model, 512):
                tw[n, turn, q, :, j : j + 512] = (
                    tw[n, turn, q, :, j : j + 512].astype(F32) + product(n, q, 2 * half + c, j)
                ).astype(BF16)
            if turn == 0:
                x_send(n, q).start()

    def x_send(n, q):
        return send(tw.at[n, 0, q], xr.at[n, q], xr_s.at[n, q], xr_r.at[n, q], across)

    def x_finish(n, dst):
        for q in range(2):
            x_send(n, q).wait_recv()
            add_into(xr.at[n, q], tw.at[n, 1, q])
            pltpu.make_async_copy(xr.at[n, q], dst.at[q], out.at[2 + 2 * n + q]).start()

    def weigh(k):
        def step(i, _):
            at = pl.ds(pl.multiple_of(i * rows, 16), rows)
            pv[at, cut(k)] = mm(nt_v[at, :], pg_v[:, cut(k)]).astype(BF16)
            return 0

        lax.fori_loop(0, 2 * deep, step, 0)

    def block(e, k):
        return pv.at[pl.ds(pl.multiple_of((2 * e + y) * rows, 16), rows), cut(k)]

    def y_send(k, e):
        src = pv.at[pl.ds(pl.multiple_of((2 * e + 1 - y) * rows, 16), rows), cut(k)]
        return send(src, lines(yb, e).at[:, cut(k)], sy.at[k, e], ry.at[k, e], side)

    def y_start(k):
        for e in range(deep):
            y_send(k, e).start()

    def y_add(k):
        for e in range(deep):
            y_send(k, e).wait_recv()
            add_into(block(e, k), lines(yb, e).at[:, cut(k)])

    def z_send(k, e, slot, sem, who):
        return send(block(e, k), lines(zb, slot).at[:, cut(k)], sem.at[k, e], rz.at[k, slot], who)

    def hop(k, h):
        @pl.when(z == h - 1)
        def _():
            for e in range(top, h - 1, -1):
                if h > 1:
                    z_send(k, e, e, su, up).wait_recv()
                    add_into(block(e, k), lines(zb, e).at[:, cut(k)])
                z_send(k, e, e, su, up).start()

        @pl.when(z == deep - h)
        def _():
            for e in range(deep - h):
                if h > 1:
                    z_send(k, e, e, sd, down).wait_recv()
                    add_into(block(e, k), lines(zb, e).at[:, cut(k)])
                z_send(k, e, deep if e == deep - h - 1 else e, sd, down).start()

    def g_spot(who, k):
        return gw_o.at[who, :, cut(k)]

    def finish(k):
        mine = block(z, k)

        @pl.when(z > 0)
        def _():
            z_send(k, z, z, su, up).wait_recv()
            add_into(mine, lines(zb, z).at[:, cut(k)])

        @pl.when(z < top)
        def _():
            z_send(k, z, deep, sd, down).wait_recv()
            add_into(mine, lines(zb, deep).at[:, cut(k)])

        send(mine, g_spot(s, k), gx_s.at[k], gx_r.at[k], across).start()
        send(mine, g_spot(s, k), gc_s.at[0, k], gc_r.at[0, k], twin).start()
        pltpu.make_async_copy(mine, g_spot(s, k), loc.at[9 + k]).start()

    def spread(k):
        spot = g_spot(across[1], k)
        send(spot, spot, gx_s.at[k], gx_r.at[k], across).wait_recv()
        send(spot, spot, gc_s.at[1, k], gc_r.at[1, k], twin).start()

    half = gw.shape[0] // 2
    lump = half // LUMPS

    def w_rows(col, i):
        return gw.at[pl.ds(pl.multiple_of(col * half + i * lump, 16), lump)]

    def piece(ref, i):
        return ref.at[pl.ds(i * lump, lump)]

    def wy_send(i):
        return send(w_rows(1 - y, i), piece(ybw, i), wy_s.at[i], wy_r.at[i], side)

    def w_compute():
        tall = 2 * lump
        for n in range(LUMPS):
            col, i = (1 - y, n) if n < LUMPS // 2 else (y, n - LUMPS // 2)
            at = pl.ds(pl.multiple_of(col * half + i * tall, 16), tall)
            for j in range(0, model, 512):
                gw[at, j : j + 512] = mm(st_v[at, :], cw[:, j : j + 512]).astype(BF16)
            if n < LUMPS // 2:
                wy_send(2 * i).start()
                wy_send(2 * i + 1).start()

    def from_below(i):
        return send(w_rows(y, i), piece(zbw.at[0], i), wu_s.at[i], wz_r.at[0, i], up)

    def from_above(i):
        return send(w_rows(y, i), piece(zbw.at[1], i), wd_s.at[i], wz_r.at[1, i], down)

    def w_cast(i, who, ssem, rsem):
        return send(piece(wo_o, i), piece(wo_o, i), ssem.at[i], rsem.at[i], who)

    def w_root(i, who, ssem, rsem):
        return send(w_rows(y, i), piece(wo_o, i), ssem.at[i], rsem.at[i], who)

    def w_keep(i):
        return pltpu.make_async_copy(w_rows(y, i), piece(wo_o, i), loc.at[9 + PARTS + i])

    root = z == s

    def w_chain(i, h):
        last = h == deep - 1
        below = root & (z > 0) if last else (z < s) & (z == h) & (h > 0)
        above = root & (z < top) if last else (z > s) & (top - z == h) & (h > 0)

        @pl.when(root if last else ((z < s) & (z == h)) | ((z > s) & (top - z == h)))
        def _():
            wy_send(i).wait_recv()
            add_into(w_rows(y, i), piece(ybw, i))

        @pl.when(below)
        def _():
            from_below(i).wait_recv()
            add_into(w_rows(y, i), piece(zbw.at[0], i))

        @pl.when(above)
        def _():
            from_above(i).wait_recv()
            add_into(w_rows(y, i), piece(zbw.at[1], i))

        if last:

            @pl.when(root)
            def _():
                w_keep(i).start()
                w_root(i, across, bx_s, bx_r).start()
                w_root(i, twin, bc_s, bc_r).start()

        else:

            @pl.when((z < s) & (z == h))
            def _():
                from_below(i).start()

            @pl.when((z > s) & (top - z == h))
            def _():
                from_above(i).start()

    def w_spread(i):
        @pl.when(across[1] == z)
        def _():
            w_cast(i, across, bx_s, bx_r).wait_recv()
            w_cast(i, twin, bc_s, bc_r).start()

        @pl.when((across[1] != z) & jnp.logical_not(root))
        def _():
            w_cast(i, twin, bc_s, bc_r).wait_recv()

    def w_step(t):
        for h in range(deep):
            if 0 <= t - h < LUMPS:
                w_chain(t - h, h)

    loads["ch"].wait()
    loads["he"].wait()
    v_start()
    loads["st"].wait()
    loads["cot"].wait()
    w_compute()
    load_wi.start()
    loads["sc"].wait()
    loads["wo"].wait()
    exchange(0, 0)
    w_step(0)
    loads["nt"].wait()
    loads["pg"].wait()
    weigh(0)
    y_start(0)
    v_sum()
    w_step(1)
    exchange(0, 1)
    w_step(2)
    load_wi.wait()
    exchange(1, 0)
    w_step(3)
    v_total()
    weigh(1)
    y_start(1)
    w_step(4)
    exchange(1, 1)
    w_step(5)
    y_add(0)
    hop(0, 1)
    weigh(2)
    y_start(2)
    w_step(6)
    hop(0, 2)
    weigh(3)
    y_start(3)
    weigh(4)
    y_start(4)
    w_step(7)
    hop(0, 3)
    y_add(1)
    hop(1, 1)
    w_step(8)
    finish(0)
    hop(1, 2)
    hop(1, 3)
    y_add(2)
    hop(2, 1)
    finish(1)
    hop(2, 2)
    x_finish(0, out_o)
    y_add(3)
    hop(3, 1)
    y_add(4)
    hop(4, 1)
    hop(2, 3)
    hop(3, 2)
    hop(4, 2)
    finish(2)
    hop(3, 3)
    hop(4, 3)
    finish(3)
    finish(4)
    x_finish(1, ng_o)
    v_spread()
    for i in range(LUMPS):
        w_spread(i)
    for n in (1, 2):
        v_seq(n, twin[1], twin).wait_recv()
    keep = pltpu.make_async_copy(vall, sm_o, out.at[0])
    keep.start()
    for k in range(PARTS):
        spread(k)
    for k in range(PARTS):
        for n in range(2):
            spot = g_spot(twin[1], k)
            send(spot, spot, gc_s.at[n, k], gc_r.at[n, k], twin).wait_recv()
        pltpu.make_async_copy(g_spot(s, k), g_spot(s, k), loc.at[9 + k]).wait()
    keep.wait()
    v_seq(0, s, across).wait_send()
    v_seq(1, s, twin).wait_send()
    v_seq(2, s, twin).wait_send()
    for n, dst in both:
        for q in range(2):
            x_send(n, q).wait_send()
            pltpu.make_async_copy(xr.at[n, q], dst.at[q], out.at[2 + 2 * n + q]).wait()
    for q in range(2):
        twin_send(1, 1, q).wait_send()
    for k in range(PARTS):
        for e in range(deep):
            y_send(k, e).wait_send()

            @pl.when(z < e)
            def _():
                z_send(k, e, e, su, up).wait_send()

            @pl.when(z > e)
            def _():
                z_send(k, e, e, sd, down).wait_send()

        spot = g_spot(s, k)
        send(spot, spot, gx_s.at[k], gx_r.at[k], across).wait_send()
        for n in range(2):
            send(spot, spot, gc_s.at[n, k], gc_r.at[n, k], twin).wait_send()
    for i in range(LUMPS):
        wy_send(i).wait_send()

        @pl.when(z < s)
        def _():
            from_below(i).wait_send()

        @pl.when(z > s)
        def _():
            from_above(i).wait_send()

        @pl.when(root)
        def _():
            w_keep(i).wait()
            w_root(i, across, bx_s, bx_r).wait_send()

        @pl.when(root | (across[1] == z))
        def _():
            w_cast(i, twin, bc_s, bc_r).wait_send()


def scatter(normed_t, pg, scaled_t, scaled, cot, wo, wi, chacc, hacc, length, shards, groups):
    model, count = normed_t.shape
    total = pg.shape[1]
    inner = scaled_t.shape[0]
    seqs = count // length
    part = length // groups
    deep = shards // 2
    rows = model // shards
    any_ = pl.BlockSpec(memory_space=pl.ANY)
    dma = pltpu.SemaphoreType.DMA
    v = pltpu.VMEM
    small = (8, chacc.shape[2])
    return pl.pallas_call(
        functools.partial(scatter_kernel, (deep, rows, part, length)),
        in_specs=[any_] * 9,
        out_specs=[any_] * 5,
        out_shape=[
            jax.ShapeDtypeStruct((groups, rows, total), BF16),
            jax.ShapeDtypeStruct((inner // 2, model), BF16),
            jax.ShapeDtypeStruct((seqs, part, model), BF16),
            jax.ShapeDtypeStruct((seqs, part, model), BF16),
            jax.ShapeDtypeStruct((groups, *small), F32),
        ],
        scratch_shapes=[
            v((model, count), BF16),
            v((count, total), BF16),
            v((inner, count), BF16),
            v((count, inner), BF16),
            v((inner, model), BF16),
            v((count, total), BF16),
            v((model, total), BF16),
            v((deep * rows, total), BF16),
            v(((deep + 1) * rows, total), BF16),
            v((2, 2, 2, part, model), BF16),
            v((2, 2, part, model), BF16),
            v((2, part, model), BF16),
            v((inner, model), BF16),
            v((inner // 2, model), BF16),
            v((2, inner // 2, model), BF16),
            v(chacc.shape, F32),
            v(hacc.shape, F32),
            v(small, F32),
            v((deep + 1, *small), F32),
            v((groups, *small), F32),
            dma((PARTS, deep)), dma((PARTS, deep)), dma((PARTS, deep)), dma((PARTS, deep)),
            dma((PARTS, deep + 1)),
            dma((PARTS,)), dma((PARTS,)), dma((2, PARTS)), dma((2, PARTS)),
            dma((2,)), dma((2, 2, 2)), dma((2, 2)), dma((2, 2)),
            dma((LUMPS,)), dma((LUMPS,)), dma((LUMPS,)), dma((LUMPS,)), dma((2, LUMPS)),
            dma((LUMPS,)), dma((LUMPS,)), dma((LUMPS,)), dma((LUMPS,)),
            dma((deep + 4,)), dma((deep + 4,)),
            dma((9 + PARTS + LUMPS,)), dma((6,)),
        ],
        compiler_params=pltpu.CompilerParams(
            collective_id=2, has_side_effects=True, vmem_limit_bytes=60 * 2**20
        ),
        name="weigh_scatter",
    )(normed_t, pg, scaled_t, scaled, cot, wo, wi, chacc, hacc)


def local(
    tokens,
    segment_ids,
    w_in,
    w_out,
    conv_weight,
    conv_bias,
    norm_gain,
    gated_gain,
    dt_bias,
    a_log,
    skip_weight,
    cotangent,
):
    groups = lax.axis_size("seq")
    shards = lax.axis_size("dp")
    place = lax.axis_index("seq")
    owner = lax.axis_index("dp")
    seqs, part, model = tokens.shape
    length = part * groups
    rows_in = w_in.shape[0]
    rows_out = w_out.shape[0]
    wide = rows_out * shards
    heads = dt_bias.shape[0]
    size = wide // heads
    mine = heads // groups
    inner = mine * size
    span = 2 * inner
    taps = conv_weight.shape[1]
    state2 = w_in.shape[1] - 2 * wide - heads
    channels = wide + state2
    share = channels // shards
    ratio = shards // groups
    small_slice = groups == 4 and shards == 8

    def own(a):
        return lax.dynamic_slice_in_dim(a, place * inner, inner, 0)

    def own_heads(a):
        return lax.dynamic_slice_in_dim(a, place * mine, mine, 0)

    step_cols = jnp.pad(
        lax.dynamic_slice_in_dim(w_in, 2 * wide + state2 + place * mine, mine, 1),
        ((0, 0), (0, 128 - mine)),
    )
    flat = [norm_gain, conv_bias, gated_gain, conv_weight.reshape(-1)]
    small = jnp.concatenate(flat)
    tall = -(-small.shape[0] // 4096) * 4096
    small = jnp.pad(small, (0, tall - small.shape[0])).reshape(-1, 256)
    if small_slice:
        turned, cot, pj, sg, w_full, wo, small_all = gather(
            w_in, step_cols, w_out, small, tokens, cotangent, inner, shards, groups
        )
    else:
        small_all = lax.all_gather(small, "dp", axis=0, tiled=False)
    small_all = small_all.reshape(shards, -1).astype(F32)
    cut = [0]
    for a in flat:
        cut.append(cut[-1] + a.shape[0])
    norm_all, conv_b, gain_all, conv_w = (
        small_all[:, cut[i] : cut[i + 1]].reshape(-1) for i in range(4)
    )
    conv_w = conv_w.reshape(channels, taps)
    if not small_slice:
        floats = tokens.astype(F32)
        inverse = lax.rsqrt(jnp.mean(floats * floats, axis=-1, keepdims=True) + EPSILON)
        unit = floats * inverse
        w_mine = jnp.concatenate(
            [
                lax.dynamic_slice_in_dim(w_in, place * span, span, 1),
                w_in[:, 2 * wide : 2 * wide + state2],
                step_cols,
            ],
            axis=1,
        )
        normed = lax.all_gather((unit * norm_all).astype(BF16), "seq", axis=1, tiled=True)
        cot = lax.all_gather(cotangent, "seq", axis=1, tiled=True)
        w_full = lax.all_gather(w_mine, "dp", axis=0, tiled=True)
        held = jnp.where(
            (owner // ratio == place) & (jnp.arange(ratio)[:, None, None] == owner % ratio),
            w_out[None],
            jnp.zeros((), BF16),
        ).reshape(inner, model)
        wo = lax.psum(held, "dp")
        sg = jnp.einsum("std,cd->stc", cot, wo, preferred_element_type=F32).astype(BF16)
        pj = jnp.einsum("std,de->ste", normed, w_full, preferred_element_type=F32).astype(BF16)

    def pad(v):
        return jnp.pad(v, (0, 128 - mine))

    rate = -jnp.exp(own_heads(a_log))
    hp = jnp.stack([pad(own_heads(dt_bias)), pad(rate * LOG2E), pad(rate)] + [jnp.zeros(128)] * 5)
    blank = jnp.zeros((state2,), F32)
    ch = jnp.concatenate(
        [
            jnp.concatenate([own(conv_w), conv_w[wide:]]).T,
            jnp.concatenate([own(conv_b), conv_b[wide:]])[None],
            jnp.concatenate([jnp.repeat(own_heads(skip_weight), size), blank])[None],
            jnp.concatenate([own(gain_all), blank])[None],
            jnp.zeros((1, inner + state2), F32),
        ]
    )
    marks = marks_of(segment_ids)
    pre, ys, st, red = mix_forward(pj, marks, sg, hp, ch)
    if small_slice:
        rk = norms(red, wide, groups)
    else:
        totals = lax.psum(red[:, :2], "seq")
        rho = lax.rsqrt(totals[:, 0] / wide + EPSILON)
        rk = jnp.stack([rho, rho**3 * totals[:, 1] / wide] + [jnp.zeros_like(rho)] * 6, axis=1)
    pg, chacc, hacc, scaled_t, scaled = mix_backward(
        pj, marks, rk, sg, pre, ys, st, hp, ch, selectors(inner // 128)
    )
    flat_pg = pg.reshape(seqs * length, -1)
    flat_cot = cot.reshape(seqs * length, -1)
    if small_slice:
        win_grad, wo_grad, out_sum, ngrad, sums = scatter(
            turned, flat_pg, scaled_t, scaled.reshape(seqs * length, -1), flat_cot, wo, w_full,
            chacc, hacc, length, shards, groups,
        )
    else:
        product = jnp.einsum("stc,cd->std", scaled, wo, preferred_element_type=F32).astype(BF16)
        out_sum = lax.psum_scatter(product, "seq", scatter_dimension=1, tiled=True)
        product = jnp.einsum("ste,de->std", pg, w_full, preferred_element_type=F32).astype(BF16)
        ngrad = lax.psum_scatter(product, "seq", scatter_dimension=1, tiled=True)
        win_grad = jnp.einsum("std,ste->de", normed, pg, preferred_element_type=F32)
        win_grad = lax.psum_scatter(win_grad.astype(BF16), "dp", scatter_dimension=0, tiled=True)
        win_grad = lax.all_gather(win_grad, "seq", axis=0, tiled=False)
        wo_grad = jnp.dot(scaled_t, flat_cot, preferred_element_type=F32)
        wo_grad = lax.psum(wo_grad.astype(BF16), "dp").reshape(ratio, rows_out, model)
        wo_grad = lax.dynamic_index_in_dim(wo_grad, owner % ratio, 0, False)
        wo_grad = lax.psum(
            jnp.where(owner // ratio == place, wo_grad, jnp.zeros((), BF16)), "seq"
        )
        sums = jnp.concatenate(
            [
                jnp.sum(chacc, axis=1),
                jnp.pad(jnp.sum(hacc, axis=1), ((0, 0), (0, inner + state2 - 128))),
            ]
        )
        sums = lax.all_gather(lax.psum(sums, "dp"), "seq", axis=0, tiled=False)
    flat = (seqs * part, model)
    result, tokens_grad, w_in_grad, wo_grad, norm_sum, gain_sum, chan, per_head = final(
        win_grad, w_in, wo_grad, w_out, out_sum.reshape(flat), ngrad.reshape(flat),
        tokens.reshape(flat), cotangent.reshape(flat), norm_all[None], sums, span, mine, share,
    )
    return (
        result.reshape(tokens.shape),
        tokens_grad.reshape(tokens.shape),
        w_in_grad,
        wo_grad,
        chan[:share, :taps],
        chan[:share, taps],
        norm_sum[:, 0] / norm_gain.astype(F32),
        gain_sum[:, 0] / gated_gain.astype(F32),
        per_head[taps + 1, :heads],
        -jnp.exp(a_log) * per_head[taps + 2, :heads],
        per_head[taps + 3, :heads],
    )


def solution(mesh):
    return jax.shard_map(
        local,
        mesh=mesh,
        in_specs=(
            P("dp", "seq", None),
            P("dp", None),
            P("dp", None),
            P("dp", None),
            P("dp", None),
            P("dp"),
            P("dp"),
            P("dp"),
            P(),
            P(),
            P(),
            P("dp", "seq", None),
        ),
        out_specs=(
            P("dp", "seq", None),
            P("dp", "seq", None),
            P("dp", None),
            P("dp", None),
            P("dp", None),
            P("dp"),
            P("dp"),
            P("dp"),
            P(),
            P(),
            P(),
        ),
        check_vma=False,
    )
```

```python
import functools

import jax
import jax.numpy as jnp
from jax import lax
from jax.experimental import pallas as pl
from jax.experimental.pallas import tpu as pltpu
from jax.sharding import PartitionSpec as P

Q = 128
EXACT = lax.Precision.HIGHEST
EPSILON = 1e-05
LOG2E = 1.4426950408889634
RESET = 160.0
F32 = jnp.float32
BF16 = jnp.bfloat16
LUMPS = 6
WOFF = 1
MESH = pl.DeviceIdType.MESH


def sigmoid(x):
    return 0.5 * jnp.tanh(0.5 * x) + 0.5


def softplus(x):
    return jnp.maximum(x, 0.0) + jnp.log1p(jnp.exp(-jnp.abs(x)))


def nt(a, b):
    return lax.dot_general(a, b, (((1,), (1,)), ((), ())), preferred_element_type=F32)


def mm(a, b):
    return jnp.dot(a, b, preferred_element_type=F32)


def decays(pj, tall, hp, width):
    arg = pj[0, :, width + 256 : width + 384].astype(F32) + hp[0:1, :]
    dt = softplus(arg)
    rows = lax.broadcasted_iota(jnp.int32, (Q, Q), 0)
    lanes = lax.broadcasted_iota(jnp.int32, (Q, Q), 1)
    lower = (rows >= lanes).astype(F32)
    level = jnp.dot(lower, dt * hp[1:2, :], precision=EXACT, preferred_element_type=F32)
    level = level + tall[:, 3:4]
    return arg, dt, level, rows, lanes


def fwd_kernel(pairs, pj, marks, sg, hp, ch, pre, ys, st, red, state, tail):
    width = pairs * 256
    inner = pairs * 128
    chunk = pl.program_id(1)

    @pl.when(chunk == 0)
    def _():
        state[...] = jnp.zeros_like(state)
        tail[...] = jnp.zeros_like(tail)

    tall = jnp.concatenate([marks[0], jnp.zeros((Q - 8, Q), F32)], axis=0).T
    _, dt, level, rows, lanes = decays(pj, tall, hp, width)
    level_t = level.T
    low = lanes < 64
    masks = [tall[:, d : d + 1] for d in range(3)]

    def conv(raw, at):
        ext = jnp.concatenate([tail[:, at : at + 128], raw], axis=0)
        total = raw * ch[3:4, at : at + 128] + ch[4:5, at : at + 128]
        for d in (1, 2, 3):
            moved = pltpu.roll(ext, d, 0)[8:]
            total = total + moved * masks[d - 1] * ch[3 - d : 4 - d, at : at + 128]
        tail[:, at : at + 128] = raw[Q - 8 :]
        pre[0, :, at : at + 128] = total
        return total * sigmoid(total)

    b_rows = conv(pj[0, :, width : width + 128].astype(F32), inner)
    c_rows = conv(pj[0, :, width + 128 : width + 256].astype(F32), inner + 128)
    b_t = b_rows.T.astype(BF16)
    b_low = b_rows.astype(BF16)
    c_low = c_rows.astype(BF16)
    scores = jnp.where(rows >= lanes, nt(c_low, b_low), 0.0)
    old = state[...].astype(BF16)
    st[0, 0] = old
    carried_all = mm(c_low, old)
    squares = jnp.zeros((Q, 128), F32)
    cross = jnp.zeros((Q, 128), F32)
    for p in range(pairs):
        at = p * 128
        one = pj[0, :, p * 256 : p * 256 + 128].astype(F32)
        two = pj[0, :, p * 256 + 128 : p * 256 + 256].astype(F32)
        z = jnp.where(low, one, pltpu.roll(two, 64, 1))
        v = jnp.where(low, pltpu.roll(one, 64, 1), two)
        xc = conv(v, at)
        l0 = jnp.broadcast_to(level[:, 2 * p : 2 * p + 1], (Q, Q))
        l1 = jnp.broadcast_to(level[:, 2 * p + 1 : 2 * p + 2], (Q, Q))
        le = jnp.where(low, l0, l1)
        dte = jnp.where(low, dt[:, 2 * p : 2 * p + 1], dt[:, 2 * p + 1 : 2 * p + 2])
        u = xc * dte
        w0 = jnp.exp2(jnp.minimum(l0 - level_t[2 * p : 2 * p + 1, :], 0.0)) * scores
        w1 = jnp.exp2(jnp.minimum(l1 - level_t[2 * p + 1 : 2 * p + 2, :], 0.0)) * scores
        wide = jnp.concatenate([w0.astype(BF16), w1.astype(BF16)], axis=1)
        blocks = jnp.concatenate(
            [jnp.where(low, u, 0.0).astype(BF16), jnp.where(low, 0.0, u).astype(BF16)], axis=0
        )
        part = mm(wide, blocks) + carried_all[:, at : at + 128] * jnp.exp2(le)
        ys[0, :, at : at + 128] = part
        gated = (part + ch[5:6, at : at + 128] * xc) * (z * sigmoid(z))
        scaled = gated * ch[6:7, at : at + 128]
        squares = squares + gated * gated
        cross = cross + sg[0, :, at : at + 128].astype(F32) * scaled
        last = le[Q - 1 : Q, :]
        ul = (u * jnp.exp2(last - le)).astype(BF16)
        state[:, at : at + 128] = state[:, at : at + 128] * jnp.exp2(last) + mm(b_t, ul)
    both = jnp.where(
        lanes == 0, jnp.sum(squares, axis=1, keepdims=True), jnp.sum(cross, axis=1, keepdims=True)
    )
    red[0] = both.T[0:8]


def mix_forward(pj, marks, sg, hp, ch):
    seqs, length, total = pj.shape
    width = total - 384
    inner = width // 2
    pairs = inner // 128
    chunks = length // Q

    def row(n):
        return pl.BlockSpec((1, Q, n), lambda s, c: (s, c, 0))

    def whole(a):
        return pl.BlockSpec(a.shape, lambda s, c: (0,) * a.ndim)

    return pl.pallas_call(
        functools.partial(fwd_kernel, pairs),
        grid=(seqs, chunks),
        in_specs=[
            row(total),
            pl.BlockSpec((1, 8, Q), lambda s, c: (s, 0, c)),
            row(inner),
            whole(hp),
            whole(ch),
        ],
        out_specs=[
            row(inner + 256),
            row(inner),
            pl.BlockSpec((1, 1, 128, inner), lambda s, c: (s, c, 0, 0)),
            pl.BlockSpec((1, 8, Q), lambda s, c: (s, 0, c)),
        ],
        out_shape=[
            jax.ShapeDtypeStruct((seqs, length, inner + 256), F32),
            jax.ShapeDtypeStruct((seqs, length, inner), F32),
            jax.ShapeDtypeStruct((seqs, chunks, 128, inner), BF16),
            jax.ShapeDtypeStruct((seqs, 8, length), F32),
        ],
        scratch_shapes=[pltpu.VMEM((128, inner), F32), pltpu.VMEM((8, inner + 256), F32)],
        compiler_params=pltpu.CompilerParams(vmem_limit_bytes=60 * 2**20),
        name="mix_forward",
    )(pj, marks, sg, hp, ch)


def bwd_kernel(
    pairs, pj, marks, rk, sg, pre, ys, st, hp, ch, sel, pg, chacc, hacc, sct, scl,
    dstate, halo, edy_all, ul_all,
):
    width = pairs * 256
    inner = pairs * 128
    first = (pl.program_id(0) == 0) & (pl.program_id(1) == 0)

    @pl.when(pl.program_id(1) == 0)
    def _():
        dstate[...] = jnp.zeros_like(dstate)
        halo[...] = jnp.zeros_like(halo)

    @pl.when(first)
    def _():
        chacc[...] = jnp.zeros_like(chacc)
        hacc[...] = jnp.zeros_like(hacc)

    tall = jnp.concatenate([marks[0], rk[0], jnp.zeros((Q - 16, Q), F32)], axis=0).T
    arg, dt, level, rows, lanes = decays(pj, tall, hp, width)
    level_t = level.T
    low = lanes < 64
    masks = [tall[:, 3 + d : 4 + d] for d in (1, 2, 3)]
    rho = jnp.broadcast_to(tall[:, 8:9], (Q, 128))
    k2 = jnp.broadcast_to(tall[:, 9:10], (Q, 128))

    def fold(x):
        return jnp.sum(x.reshape(Q // 8, 8, 128), axis=0)

    def conv_back(grad, raw, at):
        ext = jnp.concatenate([grad, halo[:, at : at + 128]], axis=0)
        out = grad * ch[3:4, at : at + 128]
        chacc[3, :, at : at + 128] += fold(grad * raw)
        chacc[4, :, at : at + 128] += fold(grad)
        for d in (1, 2, 3):
            moved = pltpu.roll(ext, Q + 8 - d, 0)[:Q] * masks[d - 1]
            out = out + moved * ch[3 - d : 4 - d, at : at + 128]
            chacc[3 - d, :, at : at + 128] += fold(moved * raw)
        halo[:, at : at + 128] = grad[:8]
        return out

    pre_b = pre[0, :, inner : inner + 128]
    pre_c = pre[0, :, inner + 128 : inner + 256]
    sig_b, sig_c = sigmoid(pre_b), sigmoid(pre_c)
    b_rows, c_rows = pre_b * sig_b, pre_c * sig_c
    b_low, c_low = b_rows.astype(BF16), c_rows.astype(BF16)
    c_t = c_rows.T.astype(BF16)
    upper = lanes >= rows
    scores = jnp.where(upper, nt(b_low, c_low), 0.0)
    dlow = dstate[...].astype(BF16)
    dsb_all = mm(b_low, dlow)
    dscores = jnp.zeros((Q, Q), F32)
    sums = jnp.zeros((6 * Q, 128), F32)
    keep = jnp.zeros((8, 128), F32)
    for p in range(pairs):
        at = p * 128
        one = pj[0, :, p * 256 : p * 256 + 128].astype(F32)
        two = pj[0, :, p * 256 + 128 : p * 256 + 256].astype(F32)
        z = jnp.where(low, one, pltpu.roll(two, 64, 1))
        v = jnp.where(low, pltpu.roll(one, 64, 1), two)
        pr = pre[0, :, at : at + 128]
        sp = sigmoid(pr)
        xc = pr * sp
        l0 = jnp.broadcast_to(level[:, 2 * p : 2 * p + 1], (Q, Q))
        l1 = jnp.broadcast_to(level[:, 2 * p + 1 : 2 * p + 2], (Q, Q))
        le = jnp.where(low, l0, l1)
        dte = jnp.where(low, dt[:, 2 * p : 2 * p + 1], dt[:, 2 * p + 1 : 2 * p + 2])
        u = xc * dte
        skip = ch[5:6, at : at + 128]
        part = ys[0, :, at : at + 128]
        y = part + skip * xc
        sz = sigmoid(z)
        silz = z * sz
        gated = y * silz
        graw = sg[0, :, at : at + 128].astype(F32)
        scaled_rho = graw * rho
        scaled = gated * rho * ch[6:7, at : at + 128]
        sct[at : at + 128, :] = scaled.T.astype(BF16)
        scl[0, :, at : at + 128] = scaled.astype(BF16)
        gg = scaled_rho * ch[6:7, at : at + 128] - k2 * gated
        dy = gg * silz
        dz = gg * y * (sz + silz * (1.0 - sz))
        ulow = u.astype(BF16)
        dylow = dy.astype(BF16)
        w0 = jnp.exp2(jnp.minimum(level_t[2 * p : 2 * p + 1, :] - l0, 0.0))
        w1 = jnp.exp2(jnp.minimum(level_t[2 * p + 1 : 2 * p + 2, :] - l1, 0.0))
        wide = jnp.concatenate([(w0 * scores).astype(BF16), (w1 * scores).astype(BF16)], axis=1)
        dyb = jnp.concatenate(
            [jnp.where(low, dy, 0.0).astype(BF16), jnp.where(low, 0.0, dy).astype(BF16)], axis=0
        )
        ub = jnp.concatenate(
            [jnp.where(low, u, 0.0).astype(BF16), jnp.where(low, 0.0, u).astype(BF16)], axis=0
        )
        duw = mm(wide, dyb)
        gt = nt(ub, dylow)
        dscores = dscores + w0 * gt[:Q] + w1 * gt[Q:]
        last = le[Q - 1 : Q, :]
        lve = jnp.exp2(last - le)
        edy = (dy * jnp.exp2(le)).astype(BF16)
        ul = (u * lve).astype(BF16)
        edy_all[:, at : at + 128] = edy
        ul_all[:, at : at + 128] = ul
        dsb = dsb_all[:, at : at + 128]
        du = duw + lve * dsb
        r1 = dylow.astype(F32) * part - ulow.astype(F32) * duw
        r2 = ul.astype(F32) * dsb
        r1h, r2h = r1.astype(BF16), r2.astype(BF16)
        stacked = jnp.concatenate(
            [
                r1h,
                (r1 - r1h.astype(F32)).astype(BF16),
                r2h,
                (r2 - r2h.astype(F32)).astype(BF16),
                (dy * xc).astype(BF16),
                (du * xc).astype(BF16),
            ],
            axis=0,
        )
        sums = sums + mm(stacked, sel[p])
        decay = jnp.exp2(last)
        kept = fold(dlow[:, at : at + 128].astype(F32) * st[0, 0, :, at : at + 128].astype(F32)) * decay
        kept_high = kept.astype(BF16)
        keep = keep + mm(kept_high, sel[p]) + mm((kept - kept_high.astype(F32)).astype(BF16), sel[p])
        dstate[:, at : at + 128] = dstate[:, at : at + 128] * decay + mm(c_t, edy)
        dv = conv_back((du * dte + skip * dy) * (sp + xc * (1.0 - sp)), v, at)
        pg[0, :, p * 256 : p * 256 + 128] = jnp.where(low, dz, pltpu.roll(dv, 64, 1)).astype(BF16)
        pg[0, :, p * 256 + 128 : p * 256 + 256] = jnp.where(low, pltpu.roll(dz, 64, 1), dv).astype(BF16)
    dsc = jnp.where(upper, dscores, 0.0)
    db = mm(dsc.astype(BF16), c_low) + nt(ul_all[...], dlow)
    dc = mm(dsc.T.astype(BF16), b_low) + nt(edy_all[...], st[0, 0])
    raw_b = pj[0, :, width : width + 128].astype(F32)
    raw_c = pj[0, :, width + 128 : width + 256].astype(F32)
    pg[0, :, width : width + 128] = conv_back(
        db * (sig_b + b_rows * (1.0 - sig_b)), raw_b, inner
    ).astype(BF16)
    pg[0, :, width + 128 : width + 256] = conv_back(
        dc * (sig_c + c_rows * (1.0 - sig_c)), raw_c, inner + 128
    ).astype(BF16)
    r1 = sums[:Q] + sums[Q : 2 * Q]
    r2 = sums[2 * Q : 3 * Q] + sums[3 * Q : 4 * Q]
    da = (
        jnp.dot(upper.astype(F32), r1, precision=EXACT, preferred_element_type=F32)
        + jnp.dot((rows > lanes).astype(F32), r2, precision=EXACT, preferred_element_type=F32)
        + jnp.sum(keep, axis=0, keepdims=True)
    )
    ddt = da * hp[2:3, :] + sums[5 * Q :]
    ds = ddt * sigmoid(arg)
    pg[0, :, width + 256 : width + 384] = ds.astype(BF16)
    hacc[0] += fold(ds)
    hacc[1] += fold(da * dt)
    hacc[2] += fold(sums[4 * Q : 5 * Q])


def mix_backward(pj, marks, rk, sg, pre, ys, st, hp, ch, sel):
    seqs, length, total = pj.shape
    width = total - 384
    inner = width // 2
    pairs = inner // 128
    chunks = length // Q

    def row(n):
        return pl.BlockSpec((1, Q, n), lambda s, c: (s, chunks - 1 - c, 0))

    def whole(shape):
        return pl.BlockSpec(shape, lambda s, c: (0,) * len(shape))

    return pl.pallas_call(
        functools.partial(bwd_kernel, pairs),
        grid=(seqs, chunks),
        in_specs=[
            row(total),
            pl.BlockSpec((1, 8, Q), lambda s, c: (s, 0, chunks - 1 - c)),
            pl.BlockSpec((1, 8, Q), lambda s, c: (s, 0, chunks - 1 - c)),
            row(inner),
            row(inner + 256),
            row(inner),
            pl.BlockSpec((1, 1, 128, inner), lambda s, c: (s, chunks - 1 - c, 0, 0)),
            whole(hp.shape),
            whole(ch.shape),
            whole(sel.shape),
        ],
        out_specs=[
            row(total),
            whole((5, 8, inner + 256)),
            whole((3, 8, 128)),
            pl.BlockSpec((inner, Q), lambda s, c: (0, s * chunks + chunks - 1 - c)),
            row(inner),
        ],
        out_shape=[
            jax.ShapeDtypeStruct((seqs, length, total), BF16),
            jax.ShapeDtypeStruct((5, 8, inner + 256), F32),
            jax.ShapeDtypeStruct((3, 8, 128), F32),
            jax.ShapeDtypeStruct((inner, seqs * length), BF16),
            jax.ShapeDtypeStruct((seqs, length, inner), BF16),
        ],
        scratch_shapes=[
            pltpu.VMEM((128, inner), F32),
            pltpu.VMEM((8, inner + 256), F32),
            pltpu.VMEM((Q, inner), BF16),
            pltpu.VMEM((Q, inner), BF16),
        ],
        compiler_params=pltpu.CompilerParams(vmem_limit_bytes=60 * 2**20),
        name="mix_backward",
    )(pj, marks, rk, sg, pre, ys, st, hp, ch, sel)


def prep_kernel(mine, at, seg, heads, cols, marks, hp, sel, steps):
    lane8 = lax.broadcasted_iota(jnp.int32, (8, 128), 1)
    shift = 128 - lax.axis_index("seq") * mine
    own = jnp.where(lane8 < mine, pltpu.roll(heads[...], shift, 1), 0.0)
    rate = jnp.where(lane8 < mine, -jnp.exp(own), 0.0)[1:2, :]
    hp[...] = jnp.concatenate([own[0:1, :], rate * LOG2E, rate, jnp.zeros((5, 128), F32)], axis=0)
    last = cols[:, at:].astype(F32)
    last = jnp.concatenate(
        [last, jnp.zeros((last.shape[0], 128 - last.shape[1]), F32)], axis=1
    )
    lane = lax.broadcasted_iota(jnp.int32, last.shape, 1)
    moved = pltpu.roll(last, shift, 1)
    steps[...] = jnp.where(lane < mine, moved, 0.0).astype(BF16)
    lane = lax.broadcasted_iota(jnp.int32, (128, 128), 0)
    out = lax.broadcasted_iota(jnp.int32, (128, 128), 1)
    for p in range(sel.shape[0]):
        sel[p] = jnp.where(out == 2 * p + lane // 64, 1.0, 0.0).astype(BF16)
    seqs, length = seg.shape
    ids = seg[...].astype(F32)
    lane = lax.broadcasted_iota(jnp.int32, (seqs, length), 1)
    back = [
        jnp.where((pltpu.roll(ids, d, 1) == ids) & (lane >= d), 1.0, 0.0) for d in (1, 2, 3)
    ]
    ahead = [
        jnp.where((pltpu.roll(ids, length - d, 1) == ids) & (lane < length - d), 1.0, 0.0)
        for d in (1, 2, 3)
    ]
    before = [ids[:, 0:1]] + [ids[:, at - 1 : at] for at in range(Q, length, Q)]
    level = jnp.concatenate(
        [-RESET * (ids[:, n * Q : (n + 1) * Q] - b) for n, b in enumerate(before)], axis=1
    )
    all_rows = [*back, level, *ahead, jnp.zeros((seqs, length), F32)]
    for n in range(seqs):
        marks[n] = jnp.concatenate([r[n : n + 1, :] for r in all_rows], axis=0)


def prepare(seg, heads, w_in, mine, at):
    rows = w_in.shape[0]
    pairs = mine // 2
    shapes = [
        ((seg.shape[0], 8, seg.shape[1]), F32), ((8, 128), F32), ((pairs, 128, 128), BF16),
        ((rows, 128), BF16),
    ]

    def whole(shape):
        return pl.BlockSpec(shape, lambda i: (0,) * len(shape))

    return pl.pallas_call(
        functools.partial(prep_kernel, mine, at),
        grid=(1,),
        in_specs=[
            whole(seg.shape),
            whole(heads.shape),
            whole(w_in.shape),
        ],
        out_specs=[whole(n) for n, _ in shapes],
        out_shape=[jax.ShapeDtypeStruct(*n) for n in shapes],
        name="prepare",
    )(seg, heads, w_in)


def norm_kernel(wide, red, rk, got, ssem, rsem):
    d = lax.axis_index("dp")
    s = lax.axis_index("seq")
    groups = got.shape[0]
    bar = pltpu.get_barrier_semaphore()
    for j in range(1, groups):
        pl.semaphore_signal(bar, inc=1, device_id=(d, lax.rem(s + j, groups)), device_id_type=MESH)
    pl.semaphore_wait(bar, groups - 1)
    sends = [
        pltpu.make_async_remote_copy(
            src_ref=red, dst_ref=got.at[j], send_sem=ssem.at[j], recv_sem=rsem.at[j],
            device_id=(d, lax.rem(s + j, groups)), device_id_type=MESH,
        )
        for j in range(1, groups)
    ]
    for copy in sends:
        copy.start()
    total = red[...]
    for j, copy in enumerate(sends):
        copy.wait()
        total = total + got[j + 1]
    rho = lax.rsqrt(total[:, 0:1] / wide + EPSILON)
    rk[...] = jnp.concatenate(
        [rho, rho * rho * rho * total[:, 1:2] / wide, jnp.zeros_like(total[:, 2:])], axis=1
    )


def norms(red, wide, groups):
    vmem = pl.BlockSpec(memory_space=pltpu.VMEM)
    return pl.pallas_call(
        functools.partial(norm_kernel, wide),
        in_specs=[vmem],
        out_specs=vmem,
        out_shape=jax.ShapeDtypeStruct(red.shape, F32),
        scratch_shapes=[
            pltpu.VMEM((groups, *red.shape), F32),
            pltpu.SemaphoreType.DMA((groups,)),
            pltpu.SemaphoreType.DMA((groups,)),
        ],
        compiler_params=pltpu.CompilerParams(collective_id=3, has_side_effects=True),
        name="norms",
    )(red)


def final_kernel(
    groups, span, mine, gw, w_in, wog, w_out, osum, ngrad, tok, cot, gains, sums, nrow, grow, log,
    res, tgrad, wig, wgr, nout, gout, cout, bout, hout, nsum, gsum,
):
    step = pl.program_id(0)

    @pl.when(step == 0)
    def _():
        inner = span // 2
        shared = sums[0, :, inner:]
        heads = sums[0, :, :128]
        for g in range(1, groups):
            shared = shared + sums[g, :, inner:]
            heads = heads + pltpu.roll(sums[g, :, :128], g * mine, 1)
        row = jnp.concatenate([*[sums[g, :, :inner] for g in range(groups)], shared], axis=1)
        share, taps = cout.shape
        first = lax.axis_index("dp") * share
        tall = -(-share // 128) * 128
        own = pltpu.roll(row, row.shape[1] - first, 1)[:, :tall]
        cout[...] = own.T[:share, :taps]
        bout[...] = own[taps : taps + 1, :share]
        count = groups * mine
        hout[0:1, :] = heads[taps + 1 : taps + 2, :count]
        hout[1:2, :] = -jnp.exp(log[...]) * heads[taps + 2 : taps + 3, :count]
        hout[2:3, :] = heads[taps + 3 : taps + 4, :count]

    total = jnp.zeros((w_in.shape[0], 1), F32)
    for g in range(groups):
        here = slice(g * span, (g + 1) * span)
        grad = gw[g, :, :span].astype(F32)
        wig[:, here] = grad
        total = total + jnp.sum(grad * w_in[:, here].astype(F32), axis=1, keepdims=True)
    at = groups * span
    width = gw.shape[2] - 128
    shared = gw[0, :, span:width].astype(F32)
    steps = gw[0, :, width:].astype(F32)
    for g in range(1, groups):
        shared = shared + gw[g, :, span:width].astype(F32)
        steps = steps + pltpu.roll(gw[g, :, width:].astype(F32), g * mine, 1)
    mid = at + width - span
    wig[:, at:mid] = shared
    wig[:, mid:] = steps[:, : groups * mine]
    total = total + jnp.sum(shared * w_in[:, at:mid].astype(F32), axis=1, keepdims=True)
    total = total + jnp.sum(
        steps[:, : groups * mine] * w_in[:, mid:].astype(F32), axis=1, keepdims=True
    )
    tall = w_in.shape[0]
    nsum[pl.ds(pl.multiple_of(step * tall, 16), tall), :] = jnp.broadcast_to(total, (tall, 128))
    grad = wog[...].astype(F32)
    wgr[...] = grad
    tall = wog.shape[0]
    gsum[pl.ds(pl.multiple_of(step * tall, 16), tall), :] = jnp.broadcast_to(
        jnp.sum(grad * w_out[...].astype(F32), axis=1, keepdims=True), (tall, 128)
    )

    @pl.when(step == pl.num_programs(0) - 1)
    def _():
        nout[...] = nsum[...].T[0:1, : nout.shape[1]] / nrow[...].astype(F32)
        gout[...] = gsum[...].T[0:1, : gout.shape[1]] / grow[...].astype(F32)

    x = tok[...].astype(F32)
    res[...] = (x + osum[...].astype(F32)).astype(BF16)
    inverse = lax.rsqrt(jnp.mean(x * x, axis=1, keepdims=True) + EPSILON)
    unit = x * inverse
    grad = ngrad[...].astype(F32) * gains[0:1, :]
    tgrad[...] = cot[...].astype(F32) + inverse * (
        grad - unit * jnp.mean(grad * unit, axis=1, keepdims=True)
    )


def final(gw, w_in, wog, w_out, osum, ngrad, tok, cot, rows, span, mine, taps, share):
    groups, count, total = gw.shape
    steps = next(n for n in (4, 2, 1) if count % (16 * n) == 0)

    def part(a):
        return pl.BlockSpec((a.shape[0] // steps, a.shape[1]), lambda i: (i, 0))

    def whole(a):
        return pl.BlockSpec(a.shape, lambda i: (0,) * len(a.shape))

    def up(n):
        return -(-n // 128) * 128

    tall = [w_in, wog, w_out, osum, ngrad, tok, cot]
    big = [(tok.shape, BF16), (tok.shape, F32), (w_in.shape, F32), (wog.shape, F32)]
    little = [(1, count), (1, wog.shape[0]), (share, taps), (1, share), (3, groups * mine)]
    outs = [jax.ShapeDtypeStruct(*n) for n in big]
    extra = [jax.ShapeDtypeStruct(n, F32) for n in little]
    return pl.pallas_call(
        functools.partial(final_kernel, groups, span, mine),
        grid=(steps,),
        in_specs=[
            pl.BlockSpec((groups, count // steps, total), lambda i: (0, i, 0)),
            *[part(a) for a in tall],
            *[whole(a) for a in rows],
        ],
        out_specs=[*[part(o) for o in outs], *[whole(o) for o in extra]],
        out_shape=[*outs, *extra],
        scratch_shapes=[
            pltpu.VMEM((up(count), 128), F32),
            pltpu.VMEM((up(wog.shape[0]), 128), F32),
        ],
        compiler_params=pltpu.CompilerParams(vmem_limit_bytes=60 * 2**20),
        name="final",
    )(gw, *tall, *rows)


def gather_kernel(
    dims, w_in, dt_in, wo_in, small_in, tok_in, cot_in,
    turned_o, cot_o, pj_o, sg_o, w_o, wo_o, small_o,
    tok, cot, wbig, wo, small, pjv, sgv, turned,
    szu, szd, rz, sy, ry, wsu, wsd, wrz, wsy, wry, bx_s, bx_r, bc_s, bc_r, loc, out,
):
    deep, pieces, rows, inner, part, length, groups = dims
    d = lax.axis_index("dp")
    s = lax.axis_index("seq")
    z = d // 2
    y = d % 2
    top = deep - 1
    up, down, side = (d + 2, s), (d - 2, s), (d + 1 - 2 * y, s)
    across, twin = (d, s + 2 - 4 * (s // 2)), (d, s + 1 - 2 * (s % 2))
    opposite = across[1]

    bar = pltpu.get_barrier_semaphore()

    @pl.when(z < top)
    def _():
        pl.semaphore_signal(bar, inc=1, device_id=up, device_id_type=MESH)

    @pl.when(z > 0)
    def _():
        pl.semaphore_signal(bar, inc=1, device_id=down, device_id_type=MESH)

    for who in (side, across, twin):
        pl.semaphore_signal(bar, inc=1, device_id=who, device_id_type=MESH)
    pl.semaphore_wait(bar, 3 + jnp.minimum(z, 1) + jnp.minimum(top - z, 1))

    def send(src, dst, ssem, rsem, who):
        return pltpu.make_async_remote_copy(
            src_ref=src, dst_ref=dst, send_sem=ssem, recv_sem=rsem,
            device_id=who, device_id_type=MESH,
        )

    width = 2 * inner

    def cols(k):
        return pl.ds(width + 256, 128) if k == 1 else pl.ds(width if k == 2 else (k - 3) * 256, 256)

    def held(k, owner):
        if k == 0:
            return small.at[owner]
        return wbig.at[pl.ds(pl.multiple_of(owner * rows, 16), rows), cols(k)]

    def source(k):
        if k == 0:
            return small_in.at[...]
        if k == 1:
            return dt_in.at[...]
        if k == 2:
            return w_in.at[:, pl.ds(width * groups, 256)]
        return w_in.at[:, pl.ds(pl.multiple_of(s * width + (k - 3) * 256, 128), 256)]

    def own_send(k):
        src, dst = source(k), held(k, d)

        @pl.when(z < top)
        def _():
            send(src, dst, szu.at[k, z], rz.at[k, z], up).start()

        @pl.when(z > 0)
        def _():
            send(src, dst, szd.at[k, z], rz.at[k, z], down).start()

        send(src, dst, sy.at[k, z], ry.at[k, z], side).start()

    def hop(k, h):
        below, above = z - h, z + h

        @pl.when(below >= 0)
        def _():
            ref = held(k, below * 2 + y)
            send(ref, ref, szu.at[k, below], rz.at[k, below], up).wait_recv()

            @pl.when(z < top)
            def _():
                send(ref, ref, szu.at[k, below], rz.at[k, below], up).start()

            send(ref, ref, sy.at[k, below], ry.at[k, below], side).start()

        @pl.when(above <= top)
        def _():
            ref = held(k, above * 2 + y)
            send(ref, ref, szd.at[k, above], rz.at[k, above], down).wait_recv()

            @pl.when(z > 0)
            def _():
                send(ref, ref, szd.at[k, above], rz.at[k, above], down).start()

            send(ref, ref, sy.at[k, above], ry.at[k, above], side).start()

    def arrive(k):
        for e in range(deep):
            ref = held(k, e * 2 + 1 - y)
            send(ref, ref, sy.at[k, e], ry.at[k, e], side).wait_recv()

    def own_copy(src, dst, sem):
        return pltpu.make_async_copy(src, dst, sem)

    here = pl.multiple_of(s * part, 16)
    there = pl.multiple_of(opposite * part, 16)
    locals_ = [
        own_copy(small_in, small.at[d], loc.at[0]),
        own_copy(
            w_in.at[:, pl.ds(pl.multiple_of(s * width, 128), width)],
            wbig.at[pl.ds(pl.multiple_of(d * rows, 16), rows), pl.ds(0, width)],
            loc.at[1],
        ),
    ]
    for q in range(2):
        locals_.append(own_copy(tok_in.at[q], tok.at[q, pl.ds(here, part)], loc.at[2 + q]))
        locals_.append(own_copy(cot_in.at[q], cot.at[q, pl.ds(here, part)], loc.at[4 + q]))
    for k in (1, 2):
        locals_.append(own_copy(source(k), held(k, d), loc.at[6 + k]))
    half = wo_in.shape[0]
    mine = z == s

    def root_copy():
        return own_copy(wo_in, wo.at[pl.ds(pl.multiple_of(y * half, 16), half)], loc.at[6])

    def block_sends(which, src, dst, q):
        spot = dst.at[q, pl.ds(here, part)]
        i = which * 2 + q
        send(src.at[q], spot, bx_s.at[i], bx_r.at[i], across).start()
        send(src.at[q], spot, bc_s.at[0, i], bc_r.at[0, i], twin).start()

    def block_forward(which, dst, q):
        spot = dst.at[q, pl.ds(there, part)]
        i = which * 2 + q
        send(spot, spot, bx_s.at[i], bx_r.at[i], across).wait_recv()
        send(spot, spot, bc_s.at[1, i], bc_r.at[1, i], twin).start()

    def block_arrive(which, dst, q):
        i = which * 2 + q
        for n in range(2):
            spot = dst.at[q, pl.ds(here, part)]
            send(spot, spot, bc_s.at[n, i], bc_r.at[n, i], twin).wait_recv()

    lump = half // LUMPS

    def wo_piece(i, col):
        m = col * LUMPS + i
        return m, wo.at[pl.ds(pl.multiple_of(m * lump, 16), lump)]

    def wo_send(i, src=None):
        m, ref = wo_piece(i, y)
        src = ref if src is None else src

        @pl.when((z >= s) & (z < top))
        def _():
            send(src, ref, wsu.at[m], wrz.at[m], up).start()

        @pl.when((z <= s) & (z > 0))
        def _():
            send(src, ref, wsd.at[m], wrz.at[m], down).start()

        send(src, ref, wsy.at[m], wry.at[m], side).start()

    def wo_root(i):
        @pl.when(mine)
        def _():
            wo_send(i, wo_in.at[pl.ds(i * lump, lump)])

    def wo_hop(i, h):
        @pl.when((z - s == h) | (s - z == h))
        def _():
            m, ref = wo_piece(i, y)
            send(ref, ref, wsu.at[m], wrz.at[m], up).wait_recv()
            wo_send(i)

    def wo_arrive(i):
        m, ref = wo_piece(i, 1 - y)
        send(ref, ref, wsy.at[m], wry.at[m], side).wait_recv()

    tile = 256
    long = 512

    def project(k):
        c = pl.ds(width, 384) if k == 2 else cols(k)

        def step(i, _):
            q, r = i // (length // long), i % (length // long)
            at = pl.ds(pl.multiple_of(r * long, long), long)
            pjv[q, at, c] = mm(tok[q, at, :], wbig[:, c]).astype(BF16)
            return 0

        lax.fori_loop(0, 2 * length // long, step, 0)
        own_copy(pjv.at[:, :, c], pj_o.at[:, :, c], out.at[k]).start()

    for c in locals_:
        c.start()

    @pl.when(mine)
    def _():
        root_copy().start()

    for q in range(2):
        block_sends(0, tok_in, tok, q)
    ahead = 3
    for k in range(ahead):
        own_send(k)
    done = []

    def hops(t):
        for h in range(1, deep):
            if 0 <= t - h < pieces:
                hop(t - h, h)
        for h in range(1, deep):
            if 0 <= t - h - WOFF < LUMPS:
                wo_hop(t - h - WOFF, h)
        if 0 <= t - WOFF < LUMPS:
            wo_root(t - WOFF)
        if ahead <= t + ahead - 1 < pieces:
            own_send(t + ahead - 1)

    steps = max(pieces, WOFF + LUMPS) + deep - 1
    count = dict(next=1)

    def ready(n):
        for _ in range(n):
            if count["next"] < pieces:
                arrive(count["next"])
                if count["next"] > 1:
                    project(count["next"])
                count["next"] += 1

    share = tok.shape[2] // (2 * deep)

    def norm_step(i, _):
        q, r = i // (length // 64), i % (length // 64)
        at = pl.multiple_of(r * 64, 64)
        x = tok[q, pl.ds(at, 64), :].astype(F32)
        inv = lax.rsqrt(jnp.mean(x * x, axis=1, keepdims=True) + EPSILON)
        gains = jnp.concatenate([small[e, 0:1, :share] for e in range(2 * deep)], axis=1)
        tok[q, pl.ds(at, 64), :] = (x * inv * gains.astype(F32)).astype(BF16)
        return 0

    def turn_step(i, _):
        q, r = i // (length // tile), i % (length // tile)
        at = pl.multiple_of(r * tile, tile)
        to = pl.multiple_of(i * tile, tile)
        for j in range(0, tok.shape[2], 128):
            turned[j : j + 128, pl.ds(to, tile)] = tok[q, pl.ds(at, tile), j : j + 128].T
        return 0

    def grad_step(i, _):
        q, r = i // (length // long), i % (length // long)
        at = pl.ds(pl.multiple_of(r * long, long), long)
        sgv[q, at, :] = nt(cot[q, at, :], wo[...]).astype(BF16)
        return 0

    for t in range(1, steps):
        hops(t)
        if t == 3:
            block_forward(0, tok, 0)
        if t == 6:
            block_forward(0, tok, 1)
            for q in range(2):
                block_sends(1, cot_in, cot, q)
        if t == 7:
            for i in (0, 1, 2, 4, 6, 7):
                locals_[i].wait()
            block_arrive(0, tok, 0)
            block_arrive(0, tok, 1)
            for q in range(2):
                spot = tok.at[q, pl.ds(there, part)]
                send(spot, spot, bc_s.at[1, q], bc_r.at[1, q], twin).wait_send()
            arrive(0)
            own_copy(small, small_o, out.at[0]).start()
            lax.fori_loop(0, 2 * length // 64, norm_step, 0)
            lax.fori_loop(0, 2 * length // tile, turn_step, 0)
            own_copy(turned, turned_o, out.at[pieces]).start()
        if t == 10:
            block_forward(1, cot, 0)
        if t == 11:
            block_forward(1, cot, 1)
        if t > 7:
            ready(2 if t == 8 else 1)

    @pl.when(mine)
    def _():
        root_copy().wait()

    locals_[3].wait()
    locals_[5].wait()
    for i in range(LUMPS):
        wo_arrive(i)
    own_copy(wo, wo_o, out.at[pieces + 2]).start()
    block_arrive(1, cot, 0)
    block_arrive(1, cot, 1)
    own_copy(cot, cot_o, out.at[pieces + 3]).start()
    lax.fori_loop(0, 2 * length // long, grad_step, 0)
    own_copy(sgv, sg_o, out.at[pieces + 4]).start()
    ready(pieces)
    own_copy(wbig, w_o, out.at[pieces + 1]).start()
    for k in range(pieces):
        for e in range(deep):
            ref = held(k, e * 2 + y)

            @pl.when((z >= e) & (z < top))
            def _():
                send(ref, ref, szu.at[k, e], rz.at[k, e], up).wait_send()

            @pl.when((z <= e) & (z > 0))
            def _():
                send(ref, ref, szd.at[k, e], rz.at[k, e], down).wait_send()

            send(ref, ref, sy.at[k, e], ry.at[k, e], side).wait_send()
    for i in range(LUMPS):
        m, ref = wo_piece(i, y)

        @pl.when((z >= s) & (z < top))
        def _():
            send(ref, ref, wsu.at[m], wrz.at[m], up).wait_send()

        @pl.when((z <= s) & (z > 0))
        def _():
            send(ref, ref, wsd.at[m], wrz.at[m], down).wait_send()

        send(ref, ref, wsy.at[m], wry.at[m], side).wait_send()
    for which, dst in ((0, tok), (1, cot)):
        for q in range(2):
            i = which * 2 + q
            spot = dst.at[q, pl.ds(here, part)]
            send(spot, spot, bx_s.at[i], bx_r.at[i], across).wait_send()
            for n in range(1 + which):
                send(spot, spot, bc_s.at[n, i], bc_r.at[n, i], twin).wait_send()
    own_copy(small, small_o, out.at[0]).wait()
    for k in range(2, pieces):
        c = pl.ds(width, 384) if k == 2 else cols(k)
        own_copy(pjv.at[:, :, c], pj_o.at[:, :, c], out.at[k]).wait()
    own_copy(turned, turned_o, out.at[pieces]).wait()
    own_copy(wbig, w_o, out.at[pieces + 1]).wait()
    own_copy(wo, wo_o, out.at[pieces + 2]).wait()
    own_copy(cot, cot_o, out.at[pieces + 3]).wait()
    own_copy(sgv, sg_o, out.at[pieces + 4]).wait()


def gather(w_in, dt_in, w_out, small, tokens, cotangent, inner, shards, groups):
    rows = w_in.shape[0]
    total = 2 * inner + 384
    seqs, part, model = tokens.shape
    length = part * groups
    deep = shards // 2
    pieces = inner // 128 + 3
    any_ = pl.BlockSpec(memory_space=pl.ANY)
    dma = pltpu.SemaphoreType.DMA
    small_rows, small_cols = small.shape
    full = (shards * rows, total)
    shapes = [
        (model, seqs * length), (seqs, length, model), (seqs, length, total), (seqs, length, inner),
        full, (inner, model), (shards, small_rows, small_cols),
    ]
    return pl.pallas_call(
        functools.partial(gather_kernel, (deep, pieces, rows, inner, part, length, groups)),
        in_specs=[any_] * 6,
        out_specs=[any_] * 7,
        out_shape=[jax.ShapeDtypeStruct(n, BF16) for n in shapes],
        scratch_shapes=[
            pltpu.VMEM(shapes[1], BF16),
            pltpu.VMEM(shapes[1], BF16),
            pltpu.VMEM(full, BF16),
            pltpu.VMEM((inner, model), BF16),
            pltpu.VMEM(shapes[6], BF16),
            pltpu.VMEM(shapes[2], BF16),
            pltpu.VMEM(shapes[3], BF16),
            pltpu.VMEM(shapes[0], BF16),
            dma((pieces, deep)), dma((pieces, deep)), dma((pieces, deep)),
            dma((pieces, deep)), dma((pieces, deep)),
            *[dma((2 * LUMPS,))] * 5,
            dma((4,)), dma((4,)), dma((2, 4)), dma((2, 4)),
            dma((9,)), dma((pieces + 5,)),
        ],
        compiler_params=pltpu.CompilerParams(
            collective_id=1, has_side_effects=True, vmem_limit_bytes=56 * 2**20
        ),
        name="gather_project",
    )(w_in, dt_in, w_out, small, tokens, cotangent)


def greet(z, y, s, deep, others):
    bar = pltpu.get_barrier_semaphore()
    for e in range(deep):
        @pl.when(z != e)
        def _():
            pl.semaphore_signal(bar, inc=1, device_id=(2 * e + y, s), device_id_type=MESH)

    for who in others:
        pl.semaphore_signal(bar, inc=1, device_id=who, device_id_type=MESH)
    pl.semaphore_wait(bar, len(others) + deep - 1)


def send(src, dst, ssem, rsem, who):
    return pltpu.make_async_remote_copy(
        src_ref=src, dst_ref=dst, send_sem=ssem, recv_sem=rsem, device_id=who, device_id_type=MESH
    )


def add_into(dst, src):
    count = dst.shape[0]
    some = next(n for n in (64, 48, 32, 16) if count % n == 0)

    def step(i, _):
        at = pl.ds(pl.multiple_of(i * some, 16), some)
        dst[at, :] = (dst[at, :].astype(F32) + src[at, :].astype(F32)).astype(BF16)
        return 0

    lax.fori_loop(0, count // some, step, 0)


CUTS = ((0, 512), (512, 512), (1536, 384), (1024, 256), (1280, 128), (1408, 128))
PARTS = len(CUTS)


def scatter_kernel(
    dims, nt_in, pg_in, st_in, sc_in, cot_in, wo_in, wi_in, ch_in, he_in,
    gw_o, wo_o, out_o, ng_o, sm_o,
    nt_v, pg_v, st_v, sc_v, wo_v, cw, pv, yb, zb, tw, xr, stage, gw, ybw, zbw, ch_v, he_v,
    vec, vgot, vall,
    sy, ry, su, sd, rz, gx_s, gx_r, gc_s, gc_r, tw_s, tw_r, xr_s, xr_r,
    wy_s, wy_r, wu_s, wd_s, wz_r, bx_s, bx_r, bc_s, bc_r, v_s, v_r, loc, out,
):
    deep, rows, part, length = dims
    d = lax.axis_index("dp")
    s = lax.axis_index("seq")
    z = d // 2
    y = d % 2
    x = s // 2
    c = s % 2
    top = deep - 1
    model = wi_in.shape[0]
    up, down, side = (d + 2, s), (d - 2, s), (d + 1 - 2 * y, s)
    across, twin = (d, s + 2 - 4 * x), (d, s + 1 - 2 * c)
    greet(z, y, s, deep, (side, across, twin))

    def cut(k):
        return pl.ds(*CUTS[k])

    def lines(ref, i, count=rows):
        return ref.at[pl.ds(pl.multiple_of(i * count, 16), count)]

    cot_v = cw.at[:, pl.ds(0, model)]
    wi_v = cw.at[pl.ds(0, model), :]
    loads = dict(
        ch=pltpu.make_async_copy(ch_in, ch_v, loc.at[2]),
        he=pltpu.make_async_copy(he_in, he_v, loc.at[3]),
        st=pltpu.make_async_copy(st_in, st_v, loc.at[0]),
        cot=pltpu.make_async_copy(cot_in, cot_v, loc.at[1]),
        sc=pltpu.make_async_copy(sc_in, sc_v, loc.at[6]),
        wo=pltpu.make_async_copy(wo_in, wo_v, loc.at[7]),
        nt=pltpu.make_async_copy(nt_in, nt_v, loc.at[4]),
        pg=pltpu.make_async_copy(pg_in, pg_v, loc.at[5]),
    )
    for load in loads.values():
        load.start()
    load_wi = pltpu.make_async_copy(wi_in, wi_v, loc.at[8])

    def v_send(n, src, dst, who):
        return send(src, dst, v_s.at[n], v_r.at[n], who)

    def v_y():
        return v_send(0, vec, vgot.at[deep], side)

    def v_z(e):
        return send(vec, vgot.at[z], v_s.at[1 + e], v_r.at[1 + z], (2 * e + y, s))

    def v_from(e):
        return send(vec, vgot.at[e], v_s.at[1 + e], v_r.at[1 + e], (2 * e + y, s))

    def v_seq(n, owner, who):
        return v_send(1 + deep + n, vall.at[owner], vall.at[owner], who)

    def v_start():
        vec[...] = jnp.concatenate(
            [
                jnp.sum(ch_v[...], axis=1),
                jnp.concatenate(
                    [jnp.sum(he_v[...], axis=1), jnp.zeros((3, vec.shape[1] - 128), F32)], axis=1
                ),
            ],
            axis=0,
        )
        v_y().start()

    def v_sum():
        v_y().wait()
        vec[...] = vec[...] + vgot[deep]
        for e in range(deep):
            @pl.when(z != e)
            def _():
                v_z(e).start()

    def v_total():
        for e in range(deep):
            @pl.when(z != e)
            def _():
                v_z(e).wait_send()
                v_from(e).wait_recv()

            @pl.when(z == e)
            def _():
                vgot[e] = vec[...]

        total = vgot[0]
        for e in range(1, deep):
            total = total + vgot[e]
        vall[s] = total
        v_seq(0, s, across).start()
        v_seq(1, s, twin).start()

    def v_spread():
        v_seq(0, across[1], across).wait_recv()
        v_seq(2, across[1], twin).start()

    both = ((0, out_o), (1, ng_o))

    def twin_send(n, turn, q):
        return send(stage.at[q], tw.at[n, turn, q], tw_s.at[q], tw_r.at[n, turn, q], twin)

    def product(n, q, owner, j):
        at = pl.ds(pl.multiple_of(q * length + owner * part, 16), part)
        if n == 0:
            return mm(sc_v[at, :], wo_v[:, j : j + 512])
        return nt(pg_v[at, :], cw[j : j + 512, :])

    def exchange(n, turn):
        half = 1 - x if turn == 0 else x
        for q in range(2):
            if (n, turn) != (0, 0):
                twin_send(n, turn, q).wait_send()
            for j in range(0, model, 512):
                stage[q, :, j : j + 512] = product(n, q, 2 * half + 1 - c, j).astype(BF16)
            twin_send(n, turn, q).start()
        for q in range(2):
            twin_send(n, turn, q).wait_recv()
            for j in range(0, model, 512):
                tw[n, turn, q, :, j : j + 512] = (
                    tw[n, turn, q, :, j : j + 512].astype(F32) + product(n, q, 2 * half + c, j)
                ).astype(BF16)
            if turn == 0:
                x_send(n, q).start()

    def x_send(n, q):
        return send(tw.at[n, 0, q], xr.at[n, q], xr_s.at[n, q], xr_r.at[n, q], across)

    def x_finish(n, dst):
        for q in range(2):
            x_send(n, q).wait_recv()
            add_into(xr.at[n, q], tw.at[n, 1, q])
            pltpu.make_async_copy(xr.at[n, q], dst.at[q], out.at[2 + 2 * n + q]).start()

    def weigh(k):
        def step(i, _):
            at = pl.ds(pl.multiple_of(i * rows, 16), rows)
            pv[at, cut(k)] = mm(nt_v[at, :], pg_v[:, cut(k)]).astype(BF16)
            return 0

        lax.fori_loop(0, 2 * deep, step, 0)

    def block(e, k):
        return pv.at[pl.ds(pl.multiple_of((2 * e + y) * rows, 16), rows), cut(k)]

    def y_send(k, e):
        src = pv.at[pl.ds(pl.multiple_of((2 * e + 1 - y) * rows, 16), rows), cut(k)]
        return send(src, lines(yb, e).at[:, cut(k)], sy.at[k, e], ry.at[k, e], side)

    def y_start(k):
        for e in range(deep):
            y_send(k, e).start()

    def y_add(k):
        for e in range(deep):
            y_send(k, e).wait_recv()
            add_into(block(e, k), lines(yb, e).at[:, cut(k)])

    def z_send(k, e, slot, sem, who):
        return send(block(e, k), lines(zb, slot).at[:, cut(k)], sem.at[k, e], rz.at[k, slot], who)

    def hop(k, h):
        @pl.when(z == h - 1)
        def _():
            for e in range(top, h - 1, -1):
                if h > 1:
                    z_send(k, e, e, su, up).wait_recv()
                    add_into(block(e, k), lines(zb, e).at[:, cut(k)])
                z_send(k, e, e, su, up).start()

        @pl.when(z == deep - h)
        def _():
            for e in range(deep - h):
                if h > 1:
                    z_send(k, e, e, sd, down).wait_recv()
                    add_into(block(e, k), lines(zb, e).at[:, cut(k)])
                z_send(k, e, deep if e == deep - h - 1 else e, sd, down).start()

    def g_spot(who, k):
        return gw_o.at[who, :, cut(k)]

    def finish(k):
        mine = block(z, k)

        @pl.when(z > 0)
        def _():
            z_send(k, z, z, su, up).wait_recv()
            add_into(mine, lines(zb, z).at[:, cut(k)])

        @pl.when(z < top)
        def _():
            z_send(k, z, deep, sd, down).wait_recv()
            add_into(mine, lines(zb, deep).at[:, cut(k)])

        send(mine, g_spot(s, k), gx_s.at[k], gx_r.at[k], across).start()
        send(mine, g_spot(s, k), gc_s.at[0, k], gc_r.at[0, k], twin).start()
        pltpu.make_async_copy(mine, g_spot(s, k), loc.at[9 + k]).start()

    def spread(k):
        spot = g_spot(across[1], k)
        send(spot, spot, gx_s.at[k], gx_r.at[k], across).wait_recv()
        send(spot, spot, gc_s.at[1, k], gc_r.at[1, k], twin).start()

    half = gw.shape[0] // 2
    lump = half // LUMPS

    def w_rows(col, i):
        return gw.at[pl.ds(pl.multiple_of(col * half + i * lump, 16), lump)]

    def piece(ref, i):
        return ref.at[pl.ds(i * lump, lump)]

    def wy_send(i):
        return send(w_rows(1 - y, i), piece(ybw, i), wy_s.at[i], wy_r.at[i], side)

    def w_compute():
        tall = 2 * lump
        for n in range(LUMPS):
            col, i = (1 - y, n) if n < LUMPS // 2 else (y, n - LUMPS // 2)
            at = pl.ds(pl.multiple_of(col * half + i * tall, 16), tall)
            for j in range(0, model, 512):
                gw[at, j : j + 512] = mm(st_v[at, :], cw[:, j : j + 512]).astype(BF16)
            if n < LUMPS // 2:
                wy_send(2 * i).start()
                wy_send(2 * i + 1).start()

    def from_below(i):
        return send(w_rows(y, i), piece(zbw.at[0], i), wu_s.at[i], wz_r.at[0, i], up)

    def from_above(i):
        return send(w_rows(y, i), piece(zbw.at[1], i), wd_s.at[i], wz_r.at[1, i], down)

    def w_cast(i, who, ssem, rsem):
        return send(piece(wo_o, i), piece(wo_o, i), ssem.at[i], rsem.at[i], who)

    def w_root(i, who, ssem, rsem):
        return send(w_rows(y, i), piece(wo_o, i), ssem.at[i], rsem.at[i], who)

    def w_keep(i):
        return pltpu.make_async_copy(w_rows(y, i), piece(wo_o, i), loc.at[9 + PARTS + i])

    root = z == s

    def w_chain(i, h):
        last = h == deep - 1
        below = root & (z > 0) if last else (z < s) & (z == h) & (h > 0)
        above = root & (z < top) if last else (z > s) & (top - z == h) & (h > 0)

        @pl.when(root if last else ((z < s) & (z == h)) | ((z > s) & (top - z == h)))
        def _():
            wy_send(i).wait_recv()
            add_into(w_rows(y, i), piece(ybw, i))

        @pl.when(below)
        def _():
            from_below(i).wait_recv()
            add_into(w_rows(y, i), piece(zbw.at[0], i))

        @pl.when(above)
        def _():
            from_above(i).wait_recv()
            add_into(w_rows(y, i), piece(zbw.at[1], i))

        if last:

            @pl.when(root)
            def _():
                w_keep(i).start()
                w_root(i, across, bx_s, bx_r).start()
                w_root(i, twin, bc_s, bc_r).start()

        else:

            @pl.when((z < s) & (z == h))
            def _():
                from_below(i).start()

            @pl.when((z > s) & (top - z == h))
            def _():
                from_above(i).start()

    def w_spread(i):
        @pl.when(across[1] == z)
        def _():
            w_cast(i, across, bx_s, bx_r).wait_recv()
            w_cast(i, twin, bc_s, bc_r).start()

        @pl.when((across[1] != z) & jnp.logical_not(root))
        def _():
            w_cast(i, twin, bc_s, bc_r).wait_recv()

    def w_step(t):
        for h in range(deep):
            if 0 <= t - h < LUMPS:
                w_chain(t - h, h)

    loads["ch"].wait()
    loads["he"].wait()
    v_start()
    loads["st"].wait()
    loads["cot"].wait()
    w_compute()
    load_wi.start()
    loads["sc"].wait()
    loads["wo"].wait()
    exchange(0, 0)
    w_step(0)
    loads["nt"].wait()
    loads["pg"].wait()
    weigh(0)
    y_start(0)
    v_sum()
    w_step(1)
    exchange(0, 1)
    w_step(2)
    load_wi.wait()
    exchange(1, 0)
    w_step(3)
    v_total()
    weigh(1)
    y_start(1)
    w_step(4)
    exchange(1, 1)
    w_step(5)
    y_add(0)
    hop(0, 1)
    weigh(2)
    y_start(2)
    w_step(6)
    hop(0, 2)
    weigh(3)
    y_start(3)
    for k in range(4, PARTS):
        weigh(k)
        y_start(k)
    w_step(7)
    hop(0, 3)
    y_add(1)
    hop(1, 1)
    w_step(8)
    finish(0)
    hop(1, 2)
    hop(1, 3)
    y_add(2)
    hop(2, 1)
    finish(1)
    hop(2, 2)
    x_finish(0, out_o)
    y_add(3)
    hop(3, 1)
    hop(2, 3)
    y_add(4)
    hop(4, 1)
    hop(3, 2)
    finish(2)
    y_add(5)
    hop(5, 1)
    hop(3, 3)
    hop(4, 2)
    hop(5, 2)
    finish(3)
    hop(4, 3)
    hop(5, 3)
    finish(4)
    finish(5)
    x_finish(1, ng_o)
    v_spread()
    for i in range(LUMPS):
        w_spread(i)
    for n in (1, 2):
        v_seq(n, twin[1], twin).wait_recv()
    keep = pltpu.make_async_copy(vall, sm_o, out.at[0])
    keep.start()
    for k in range(PARTS):
        spread(k)
    for k in range(PARTS):
        for n in range(2):
            spot = g_spot(twin[1], k)
            send(spot, spot, gc_s.at[n, k], gc_r.at[n, k], twin).wait_recv()
        pltpu.make_async_copy(g_spot(s, k), g_spot(s, k), loc.at[9 + k]).wait()
    keep.wait()
    v_seq(0, s, across).wait_send()
    v_seq(1, s, twin).wait_send()
    v_seq(2, s, twin).wait_send()
    for n, dst in both:
        for q in range(2):
            x_send(n, q).wait_send()
            pltpu.make_async_copy(xr.at[n, q], dst.at[q], out.at[2 + 2 * n + q]).wait()
    for q in range(2):
        twin_send(1, 1, q).wait_send()
    for k in range(PARTS):
        for e in range(deep):
            y_send(k, e).wait_send()

            @pl.when(z < e)
            def _():
                z_send(k, e, e, su, up).wait_send()

            @pl.when(z > e)
            def _():
                z_send(k, e, e, sd, down).wait_send()

        spot = g_spot(s, k)
        send(spot, spot, gx_s.at[k], gx_r.at[k], across).wait_send()
        for n in range(2):
            send(spot, spot, gc_s.at[n, k], gc_r.at[n, k], twin).wait_send()
    for i in range(LUMPS):
        wy_send(i).wait_send()

        @pl.when(z < s)
        def _():
            from_below(i).wait_send()

        @pl.when(z > s)
        def _():
            from_above(i).wait_send()

        @pl.when(root)
        def _():
            w_keep(i).wait()
            w_root(i, across, bx_s, bx_r).wait_send()

        @pl.when(root | (across[1] == z))
        def _():
            w_cast(i, twin, bc_s, bc_r).wait_send()


def scatter(normed_t, pg, scaled_t, scaled, cot, wo, wi, chacc, hacc, length, shards, groups):
    model, count = normed_t.shape
    total = pg.shape[1]
    inner = scaled_t.shape[0]
    seqs = count // length
    part = length // groups
    deep = shards // 2
    rows = model // shards
    any_ = pl.BlockSpec(memory_space=pl.ANY)
    dma = pltpu.SemaphoreType.DMA
    v = pltpu.VMEM
    small = (8, chacc.shape[2])
    return pl.pallas_call(
        functools.partial(scatter_kernel, (deep, rows, part, length)),
        in_specs=[any_] * 9,
        out_specs=[any_] * 5,
        out_shape=[
            jax.ShapeDtypeStruct((groups, rows, total), BF16),
            jax.ShapeDtypeStruct((inner // 2, model), BF16),
            jax.ShapeDtypeStruct((seqs, part, model), BF16),
            jax.ShapeDtypeStruct((seqs, part, model), BF16),
            jax.ShapeDtypeStruct((groups, *small), F32),
        ],
        scratch_shapes=[
            v((model, count), BF16),
            v((count, total), BF16),
            v((inner, count), BF16),
            v((count, inner), BF16),
            v((inner, model), BF16),
            v((count, total), BF16),
            v((model, total), BF16),
            v((deep * rows, total), BF16),
            v(((deep + 1) * rows, total), BF16),
            v((2, 2, 2, part, model), BF16),
            v((2, 2, part, model), BF16),
            v((2, part, model), BF16),
            v((inner, model), BF16),
            v((inner // 2, model), BF16),
            v((2, inner // 2, model), BF16),
            v(chacc.shape, F32),
            v(hacc.shape, F32),
            v(small, F32),
            v((deep + 1, *small), F32),
            v((groups, *small), F32),
            dma((PARTS, deep)), dma((PARTS, deep)), dma((PARTS, deep)), dma((PARTS, deep)),
            dma((PARTS, deep + 1)),
            dma((PARTS,)), dma((PARTS,)), dma((2, PARTS)), dma((2, PARTS)),
            dma((2,)), dma((2, 2, 2)), dma((2, 2)), dma((2, 2)),
            dma((LUMPS,)), dma((LUMPS,)), dma((LUMPS,)), dma((LUMPS,)), dma((2, LUMPS)),
            dma((LUMPS,)), dma((LUMPS,)), dma((LUMPS,)), dma((LUMPS,)),
            dma((deep + 4,)), dma((deep + 4,)),
            dma((9 + PARTS + LUMPS,)), dma((6,)),
        ],
        compiler_params=pltpu.CompilerParams(
            collective_id=2, has_side_effects=True, vmem_limit_bytes=60 * 2**20
        ),
        name="weigh_scatter",
    )(normed_t, pg, scaled_t, scaled, cot, wo, wi, chacc, hacc)


def local(
    tokens,
    segment_ids,
    w_in,
    w_out,
    conv_weight,
    conv_bias,
    norm_gain,
    gated_gain,
    dt_bias,
    a_log,
    skip_weight,
    cotangent,
):
    groups = lax.axis_size("seq")
    shards = lax.axis_size("dp")
    place = lax.axis_index("seq")
    owner = lax.axis_index("dp")
    seqs, part, model = tokens.shape
    length = part * groups
    rows_in = w_in.shape[0]
    rows_out = w_out.shape[0]
    wide = rows_out * shards
    heads = dt_bias.shape[0]
    size = wide // heads
    mine = heads // groups
    inner = mine * size
    span = 2 * inner
    taps = conv_weight.shape[1]
    state2 = w_in.shape[1] - 2 * wide - heads
    channels = wide + state2
    share = channels // shards
    ratio = shards // groups
    small_slice = groups == 4 and shards == 8

    def own(a):
        return lax.dynamic_slice_in_dim(a, place * inner, inner, 0)

    def own_heads(a):
        return lax.dynamic_slice_in_dim(a, place * mine, mine, 0)

    head_rows = jnp.pad(jnp.stack([dt_bias, a_log]), ((0, 6), (0, 128 - heads)))
    marks, hp, sel, step_cols = prepare(segment_ids, head_rows, w_in, mine, 2 * wide + state2)
    flat = [norm_gain, conv_bias, gated_gain, conv_weight.reshape(-1)]
    small = jnp.concatenate(flat)
    tall = -(-small.shape[0] // 4096) * 4096
    small = jnp.pad(small, (0, tall - small.shape[0])).reshape(-1, 256)
    if small_slice:
        turned, cot, pj, sg, w_full, wo, small_all = gather(
            w_in, step_cols, w_out, small, tokens, cotangent, inner, shards, groups
        )
    else:
        small_all = lax.all_gather(small, "dp", axis=0, tiled=False)
    small_all = small_all.reshape(shards, -1).astype(F32)
    cut = [0]
    for a in flat:
        cut.append(cut[-1] + a.shape[0])
    norm_all, conv_b, gain_all, conv_w = (
        small_all[:, cut[i] : cut[i + 1]].reshape(-1) for i in range(4)
    )
    conv_w = conv_w.reshape(channels, taps)
    if not small_slice:
        floats = tokens.astype(F32)
        inverse = lax.rsqrt(jnp.mean(floats * floats, axis=-1, keepdims=True) + EPSILON)
        unit = floats * inverse
        w_mine = jnp.concatenate(
            [
                lax.dynamic_slice_in_dim(w_in, place * span, span, 1),
                w_in[:, 2 * wide : 2 * wide + state2],
                step_cols,
            ],
            axis=1,
        )
        normed = lax.all_gather((unit * norm_all).astype(BF16), "seq", axis=1, tiled=True)
        cot = lax.all_gather(cotangent, "seq", axis=1, tiled=True)
        w_full = lax.all_gather(w_mine, "dp", axis=0, tiled=True)
        held = jnp.where(
            (owner // ratio == place) & (jnp.arange(ratio)[:, None, None] == owner % ratio),
            w_out[None],
            jnp.zeros((), BF16),
        ).reshape(inner, model)
        wo = lax.psum(held, "dp")
        sg = jnp.einsum("std,cd->stc", cot, wo, preferred_element_type=F32).astype(BF16)
        pj = jnp.einsum("std,de->ste", normed, w_full, preferred_element_type=F32).astype(BF16)

    blank = jnp.zeros((state2,), F32)
    ch = jnp.concatenate(
        [
            jnp.concatenate([own(conv_w), conv_w[wide:]]).T,
            jnp.concatenate([own(conv_b), conv_b[wide:]])[None],
            jnp.concatenate([jnp.repeat(own_heads(skip_weight), size), blank])[None],
            jnp.concatenate([own(gain_all), blank])[None],
            jnp.zeros((1, inner + state2), F32),
        ]
    )
    pre, ys, st, red = mix_forward(pj, marks, sg, hp, ch)
    if small_slice:
        rk = norms(red, wide, groups)
    else:
        totals = lax.psum(red[:, :2], "seq")
        rho = lax.rsqrt(totals[:, 0] / wide + EPSILON)
        rk = jnp.stack([rho, rho**3 * totals[:, 1] / wide] + [jnp.zeros_like(rho)] * 6, axis=1)
    pg, chacc, hacc, scaled_t, scaled = mix_backward(
        pj, marks, rk, sg, pre, ys, st, hp, ch, sel
    )
    flat_pg = pg.reshape(seqs * length, -1)
    flat_cot = cot.reshape(seqs * length, -1)
    if small_slice:
        win_grad, wo_grad, out_sum, ngrad, sums = scatter(
            turned, flat_pg, scaled_t, scaled.reshape(seqs * length, -1), flat_cot, wo, w_full,
            chacc, hacc, length, shards, groups,
        )
    else:
        product = jnp.einsum("stc,cd->std", scaled, wo, preferred_element_type=F32).astype(BF16)
        out_sum = lax.psum_scatter(product, "seq", scatter_dimension=1, tiled=True)
        product = jnp.einsum("ste,de->std", pg, w_full, preferred_element_type=F32).astype(BF16)
        ngrad = lax.psum_scatter(product, "seq", scatter_dimension=1, tiled=True)
        win_grad = jnp.einsum("std,ste->de", normed, pg, preferred_element_type=F32)
        win_grad = lax.psum_scatter(win_grad.astype(BF16), "dp", scatter_dimension=0, tiled=True)
        win_grad = lax.all_gather(win_grad, "seq", axis=0, tiled=False)
        wo_grad = jnp.dot(scaled_t, flat_cot, preferred_element_type=F32)
        wo_grad = lax.psum(wo_grad.astype(BF16), "dp").reshape(ratio, rows_out, model)
        wo_grad = lax.dynamic_index_in_dim(wo_grad, owner % ratio, 0, False)
        wo_grad = lax.psum(
            jnp.where(owner // ratio == place, wo_grad, jnp.zeros((), BF16)), "seq"
        )
        sums = jnp.concatenate(
            [
                jnp.sum(chacc, axis=1),
                jnp.pad(jnp.sum(hacc, axis=1), ((0, 0), (0, inner + state2 - 128))),
            ]
        )
        sums = lax.all_gather(lax.psum(sums, "dp"), "seq", axis=0, tiled=False)
    flat = (seqs * part, model)
    rows = [norm_all[None], sums, norm_gain[None], gated_gain[None], a_log[None]]
    (result, tokens_grad, w_in_grad, wo_grad, norm_grad, gain_grad, conv_grad, bias_grad, per_head) = (
        final(
            win_grad, w_in, wo_grad, w_out, out_sum.reshape(flat), ngrad.reshape(flat),
            tokens.reshape(flat), cotangent.reshape(flat), rows, span, mine, taps, share,
        )
    )
    return (
        result.reshape(tokens.shape),
        tokens_grad.reshape(tokens.shape),
        w_in_grad,
        wo_grad,
        conv_grad,
        bias_grad[0],
        norm_grad[0],
        gain_grad[0],
        per_head[0],
        per_head[1],
        per_head[2],
    )


def solution(mesh):
    return jax.shard_map(
        local,
        mesh=mesh,
        in_specs=(
            P("dp", "seq", None),
            P("dp", None),
            P("dp", None),
            P("dp", None),
            P("dp", None),
            P("dp"),
            P("dp"),
            P("dp"),
            P(),
            P(),
            P(),
            P("dp", "seq", None),
        ),
        out_specs=(
            P("dp", "seq", None),
            P("dp", "seq", None),
            P("dp", None),
            P("dp", None),
            P("dp", None),
            P("dp"),
            P("dp"),
            P("dp"),
            P(),
            P(),
            P(),
        ),
        check_vma=False,
    )
```

```python
import functools

import jax
import jax.numpy as jnp
from jax import lax
from jax.experimental import pallas as pl
from jax.experimental.pallas import tpu as pltpu
from jax.sharding import PartitionSpec as P

Q = 128
EXACT = lax.Precision.HIGHEST
EPSILON = 1e-05
LOG2E = 1.4426950408889634
RESET = 160.0
F32 = jnp.float32
BF16 = jnp.bfloat16
LUMPS = 6
WOFF = 1
MESH = pl.DeviceIdType.MESH


def sigmoid(x):
    return 0.5 * jnp.tanh(0.5 * x) + 0.5


def softplus(x):
    return jnp.maximum(x, 0.0) + jnp.log1p(jnp.exp(-jnp.abs(x)))


def nt(a, b):
    return lax.dot_general(a, b, (((1,), (1,)), ((), ())), preferred_element_type=F32)


def mm(a, b):
    return jnp.dot(a, b, preferred_element_type=F32)


def decays(pj, tall, hp, width):
    arg = pj[0, :, width + 256 : width + 384].astype(F32) + hp[0:1, :]
    dt = softplus(arg)
    rows = lax.broadcasted_iota(jnp.int32, (Q, Q), 0)
    lanes = lax.broadcasted_iota(jnp.int32, (Q, Q), 1)
    lower = (rows >= lanes).astype(F32)
    level = jnp.dot(lower, dt * hp[1:2, :], precision=EXACT, preferred_element_type=F32)
    level = level + tall[:, 3:4]
    return arg, dt, level, rows, lanes


def fwd_kernel(pairs, pj, marks, sg, hp, ch, pre, ys, st, red, state, tail):
    width = pairs * 256
    inner = pairs * 128
    chunk = pl.program_id(1)

    @pl.when(chunk == 0)
    def _():
        state[...] = jnp.zeros_like(state)
        tail[...] = jnp.zeros_like(tail)

    tall = jnp.concatenate([marks[0], jnp.zeros((Q - 8, Q), F32)], axis=0).T
    _, dt, level, rows, lanes = decays(pj, tall, hp, width)
    level_t = level.T
    low = lanes < 64
    masks = [tall[:, d : d + 1] for d in range(3)]

    def conv(raw, at):
        ext = jnp.concatenate([tail[:, at : at + 128], raw], axis=0)
        total = raw * ch[3:4, at : at + 128] + ch[4:5, at : at + 128]
        for d in (1, 2, 3):
            moved = pltpu.roll(ext, d, 0)[8:]
            total = total + moved * masks[d - 1] * ch[3 - d : 4 - d, at : at + 128]
        tail[:, at : at + 128] = raw[Q - 8 :]
        pre[0, :, at : at + 128] = total
        return total * sigmoid(total)

    b_rows = conv(pj[0, :, width : width + 128].astype(F32), inner)
    c_rows = conv(pj[0, :, width + 128 : width + 256].astype(F32), inner + 128)
    b_t = b_rows.T.astype(BF16)
    b_low = b_rows.astype(BF16)
    c_low = c_rows.astype(BF16)
    scores = jnp.where(rows >= lanes, nt(c_low, b_low), 0.0)
    old = state[...].astype(BF16)
    st[0, 0] = old
    carried_all = mm(c_low, old)
    squares = jnp.zeros((Q, 128), F32)
    cross = jnp.zeros((Q, 128), F32)
    for p in range(pairs):
        at = p * 128
        one = pj[0, :, p * 256 : p * 256 + 128].astype(F32)
        two = pj[0, :, p * 256 + 128 : p * 256 + 256].astype(F32)
        z = jnp.where(low, one, pltpu.roll(two, 64, 1))
        v = jnp.where(low, pltpu.roll(one, 64, 1), two)
        xc = conv(v, at)
        l0 = jnp.broadcast_to(level[:, 2 * p : 2 * p + 1], (Q, Q))
        l1 = jnp.broadcast_to(level[:, 2 * p + 1 : 2 * p + 2], (Q, Q))
        le = jnp.where(low, l0, l1)
        dte = jnp.where(low, dt[:, 2 * p : 2 * p + 1], dt[:, 2 * p + 1 : 2 * p + 2])
        u = xc * dte
        w0 = jnp.exp2(jnp.minimum(l0 - level_t[2 * p : 2 * p + 1, :], 0.0)) * scores
        w1 = jnp.exp2(jnp.minimum(l1 - level_t[2 * p + 1 : 2 * p + 2, :], 0.0)) * scores
        wide = jnp.concatenate([w0.astype(BF16), w1.astype(BF16)], axis=1)
        blocks = jnp.concatenate(
            [jnp.where(low, u, 0.0).astype(BF16), jnp.where(low, 0.0, u).astype(BF16)], axis=0
        )
        part = mm(wide, blocks) + carried_all[:, at : at + 128] * jnp.exp2(le)
        ys[0, :, at : at + 128] = part
        gated = (part + ch[5:6, at : at + 128] * xc) * (z * sigmoid(z))
        scaled = gated * ch[6:7, at : at + 128]
        squares = squares + gated * gated
        cross = cross + sg[0, :, at : at + 128].astype(F32) * scaled
        last = le[Q - 1 : Q, :]
        ul = (u * jnp.exp2(last - le)).astype(BF16)
        state[:, at : at + 128] = state[:, at : at + 128] * jnp.exp2(last) + mm(b_t, ul)
    both = jnp.where(
        lanes == 0, jnp.sum(squares, axis=1, keepdims=True), jnp.sum(cross, axis=1, keepdims=True)
    )
    red[0] = both.T[0:8]


def mix_forward(pj, marks, sg, hp, ch):
    seqs, length, total = pj.shape
    width = total - 384
    inner = width // 2
    pairs = inner // 128
    chunks = length // Q

    def row(n):
        return pl.BlockSpec((1, Q, n), lambda s, c: (s, c, 0))

    def whole(a):
        return pl.BlockSpec(a.shape, lambda s, c: (0,) * a.ndim)

    return pl.pallas_call(
        functools.partial(fwd_kernel, pairs),
        grid=(seqs, chunks),
        in_specs=[
            row(total),
            pl.BlockSpec((1, 8, Q), lambda s, c: (s, 0, c)),
            row(inner),
            whole(hp),
            whole(ch),
        ],
        out_specs=[
            row(inner + 256),
            row(inner),
            pl.BlockSpec((1, 1, 128, inner), lambda s, c: (s, c, 0, 0)),
            pl.BlockSpec((1, 8, Q), lambda s, c: (s, 0, c)),
        ],
        out_shape=[
            jax.ShapeDtypeStruct((seqs, length, inner + 256), F32),
            jax.ShapeDtypeStruct((seqs, length, inner), F32),
            jax.ShapeDtypeStruct((seqs, chunks, 128, inner), BF16),
            jax.ShapeDtypeStruct((seqs, 8, length), F32),
        ],
        scratch_shapes=[pltpu.VMEM((128, inner), F32), pltpu.VMEM((8, inner + 256), F32)],
        compiler_params=pltpu.CompilerParams(vmem_limit_bytes=60 * 2**20),
        name="mix_forward",
    )(pj, marks, sg, hp, ch)


def bwd_kernel(
    pairs, pj, marks, rk, sg, pre, ys, st, hp, ch, sel, pg, chacc, hacc, sct, scl,
    dstate, halo, edy_all, ul_all,
):
    width = pairs * 256
    inner = pairs * 128
    first = (pl.program_id(0) == 0) & (pl.program_id(1) == 0)

    @pl.when(pl.program_id(1) == 0)
    def _():
        dstate[...] = jnp.zeros_like(dstate)
        halo[...] = jnp.zeros_like(halo)

    @pl.when(first)
    def _():
        chacc[...] = jnp.zeros_like(chacc)
        hacc[...] = jnp.zeros_like(hacc)

    tall = jnp.concatenate([marks[0], rk[0], jnp.zeros((Q - 16, Q), F32)], axis=0).T
    arg, dt, level, rows, lanes = decays(pj, tall, hp, width)
    level_t = level.T
    low = lanes < 64
    masks = [tall[:, 3 + d : 4 + d] for d in (1, 2, 3)]
    rho = jnp.broadcast_to(tall[:, 8:9], (Q, 128))
    k2 = jnp.broadcast_to(tall[:, 9:10], (Q, 128))

    def fold(x):
        return jnp.sum(x.reshape(Q // 8, 8, 128), axis=0)

    def conv_back(grad, raw, at):
        ext = jnp.concatenate([grad, halo[:, at : at + 128]], axis=0)
        out = grad * ch[3:4, at : at + 128]
        chacc[3, :, at : at + 128] += fold(grad * raw)
        chacc[4, :, at : at + 128] += fold(grad)
        for d in (1, 2, 3):
            moved = pltpu.roll(ext, Q + 8 - d, 0)[:Q] * masks[d - 1]
            out = out + moved * ch[3 - d : 4 - d, at : at + 128]
            chacc[3 - d, :, at : at + 128] += fold(moved * raw)
        halo[:, at : at + 128] = grad[:8]
        return out

    pre_b = pre[0, :, inner : inner + 128]
    pre_c = pre[0, :, inner + 128 : inner + 256]
    sig_b, sig_c = sigmoid(pre_b), sigmoid(pre_c)
    b_rows, c_rows = pre_b * sig_b, pre_c * sig_c
    b_low, c_low = b_rows.astype(BF16), c_rows.astype(BF16)
    c_t = c_rows.T.astype(BF16)
    upper = lanes >= rows
    scores = jnp.where(upper, nt(b_low, c_low), 0.0)
    dlow = dstate[...].astype(BF16)
    dsb_all = mm(b_low, dlow)
    dscores = jnp.zeros((Q, Q), F32)
    sums = jnp.zeros((6 * Q, 128), F32)
    keep = jnp.zeros((8, 128), F32)
    for p in range(pairs):
        at = p * 128
        one = pj[0, :, p * 256 : p * 256 + 128].astype(F32)
        two = pj[0, :, p * 256 + 128 : p * 256 + 256].astype(F32)
        z = jnp.where(low, one, pltpu.roll(two, 64, 1))
        v = jnp.where(low, pltpu.roll(one, 64, 1), two)
        pr = pre[0, :, at : at + 128]
        sp = sigmoid(pr)
        xc = pr * sp
        l0 = jnp.broadcast_to(level[:, 2 * p : 2 * p + 1], (Q, Q))
        l1 = jnp.broadcast_to(level[:, 2 * p + 1 : 2 * p + 2], (Q, Q))
        le = jnp.where(low, l0, l1)
        dte = jnp.where(low, dt[:, 2 * p : 2 * p + 1], dt[:, 2 * p + 1 : 2 * p + 2])
        u = xc * dte
        skip = ch[5:6, at : at + 128]
        part = ys[0, :, at : at + 128]
        y = part + skip * xc
        sz = sigmoid(z)
        silz = z * sz
        gated = y * silz
        graw = sg[0, :, at : at + 128].astype(F32)
        scaled_rho = graw * rho
        scaled = gated * rho * ch[6:7, at : at + 128]
        sct[at : at + 128, :] = scaled.T.astype(BF16)
        scl[0, :, at : at + 128] = scaled.astype(BF16)
        gg = scaled_rho * ch[6:7, at : at + 128] - k2 * gated
        dy = gg * silz
        dz = gg * y * (sz + silz * (1.0 - sz))
        ulow = u.astype(BF16)
        dylow = dy.astype(BF16)
        w0 = jnp.exp2(jnp.minimum(level_t[2 * p : 2 * p + 1, :] - l0, 0.0))
        w1 = jnp.exp2(jnp.minimum(level_t[2 * p + 1 : 2 * p + 2, :] - l1, 0.0))
        wide = jnp.concatenate([(w0 * scores).astype(BF16), (w1 * scores).astype(BF16)], axis=1)
        dyb = jnp.concatenate(
            [jnp.where(low, dy, 0.0).astype(BF16), jnp.where(low, 0.0, dy).astype(BF16)], axis=0
        )
        ub = jnp.concatenate(
            [jnp.where(low, u, 0.0).astype(BF16), jnp.where(low, 0.0, u).astype(BF16)], axis=0
        )
        duw = mm(wide, dyb)
        gt = nt(ub, dylow)
        dscores = dscores + w0 * gt[:Q] + w1 * gt[Q:]
        last = le[Q - 1 : Q, :]
        lve = jnp.exp2(last - le)
        edy = (dy * jnp.exp2(le)).astype(BF16)
        ul = (u * lve).astype(BF16)
        edy_all[:, at : at + 128] = edy
        ul_all[:, at : at + 128] = ul
        dsb = dsb_all[:, at : at + 128]
        du = duw + lve * dsb
        r1 = dylow.astype(F32) * part - ulow.astype(F32) * duw
        r2 = ul.astype(F32) * dsb
        r1h, r2h = r1.astype(BF16), r2.astype(BF16)
        stacked = jnp.concatenate(
            [
                r1h,
                (r1 - r1h.astype(F32)).astype(BF16),
                r2h,
                (r2 - r2h.astype(F32)).astype(BF16),
                (dy * xc).astype(BF16),
                (du * xc).astype(BF16),
            ],
            axis=0,
        )
        sums = sums + mm(stacked, sel[p])
        decay = jnp.exp2(last)
        kept = fold(dlow[:, at : at + 128].astype(F32) * st[0, 0, :, at : at + 128].astype(F32)) * decay
        kept_high = kept.astype(BF16)
        keep = keep + mm(kept_high, sel[p]) + mm((kept - kept_high.astype(F32)).astype(BF16), sel[p])
        dstate[:, at : at + 128] = dstate[:, at : at + 128] * decay + mm(c_t, edy)
        dv = conv_back((du * dte + skip * dy) * (sp + xc * (1.0 - sp)), v, at)
        pg[0, :, p * 256 : p * 256 + 128] = jnp.where(low, dz, pltpu.roll(dv, 64, 1)).astype(BF16)
        pg[0, :, p * 256 + 128 : p * 256 + 256] = jnp.where(low, pltpu.roll(dz, 64, 1), dv).astype(BF16)
    dsc = jnp.where(upper, dscores, 0.0)
    db = mm(dsc.astype(BF16), c_low) + nt(ul_all[...], dlow)
    dc = mm(dsc.T.astype(BF16), b_low) + nt(edy_all[...], st[0, 0])
    raw_b = pj[0, :, width : width + 128].astype(F32)
    raw_c = pj[0, :, width + 128 : width + 256].astype(F32)
    pg[0, :, width : width + 128] = conv_back(
        db * (sig_b + b_rows * (1.0 - sig_b)), raw_b, inner
    ).astype(BF16)
    pg[0, :, width + 128 : width + 256] = conv_back(
        dc * (sig_c + c_rows * (1.0 - sig_c)), raw_c, inner + 128
    ).astype(BF16)
    r1 = sums[:Q] + sums[Q : 2 * Q]
    r2 = sums[2 * Q : 3 * Q] + sums[3 * Q : 4 * Q]
    da = (
        jnp.dot(upper.astype(F32), r1, precision=EXACT, preferred_element_type=F32)
        + jnp.dot((rows > lanes).astype(F32), r2, precision=EXACT, preferred_element_type=F32)
        + jnp.sum(keep, axis=0, keepdims=True)
    )
    ddt = da * hp[2:3, :] + sums[5 * Q :]
    ds = ddt * sigmoid(arg)
    pg[0, :, width + 256 : width + 384] = ds.astype(BF16)
    hacc[0] += fold(ds)
    hacc[1] += fold(da * dt)
    hacc[2] += fold(sums[4 * Q : 5 * Q])


def mix_backward(pj, marks, rk, sg, pre, ys, st, hp, ch, sel):
    seqs, length, total = pj.shape
    width = total - 384
    inner = width // 2
    pairs = inner // 128
    chunks = length // Q

    def row(n):
        return pl.BlockSpec((1, Q, n), lambda s, c: (s, chunks - 1 - c, 0))

    def whole(shape):
        return pl.BlockSpec(shape, lambda s, c: (0,) * len(shape))

    return pl.pallas_call(
        functools.partial(bwd_kernel, pairs),
        grid=(seqs, chunks),
        in_specs=[
            row(total),
            pl.BlockSpec((1, 8, Q), lambda s, c: (s, 0, chunks - 1 - c)),
            pl.BlockSpec((1, 8, Q), lambda s, c: (s, 0, chunks - 1 - c)),
            row(inner),
            row(inner + 256),
            row(inner),
            pl.BlockSpec((1, 1, 128, inner), lambda s, c: (s, chunks - 1 - c, 0, 0)),
            whole(hp.shape),
            whole(ch.shape),
            whole(sel.shape),
        ],
        out_specs=[
            row(total),
            whole((5, 8, inner + 256)),
            whole((3, 8, 128)),
            pl.BlockSpec((inner, Q), lambda s, c: (0, s * chunks + chunks - 1 - c)),
            row(inner),
        ],
        out_shape=[
            jax.ShapeDtypeStruct((seqs, length, total), BF16),
            jax.ShapeDtypeStruct((5, 8, inner + 256), F32),
            jax.ShapeDtypeStruct((3, 8, 128), F32),
            jax.ShapeDtypeStruct((inner, seqs * length), BF16),
            jax.ShapeDtypeStruct((seqs, length, inner), BF16),
        ],
        scratch_shapes=[
            pltpu.VMEM((128, inner), F32),
            pltpu.VMEM((8, inner + 256), F32),
            pltpu.VMEM((Q, inner), BF16),
            pltpu.VMEM((Q, inner), BF16),
        ],
        compiler_params=pltpu.CompilerParams(vmem_limit_bytes=60 * 2**20),
        name="mix_backward",
    )(pj, marks, rk, sg, pre, ys, st, hp, ch, sel)


def prep_kernel(mine, at, seg, heads, cols, marks, hp, sel, steps):
    lane8 = lax.broadcasted_iota(jnp.int32, (8, 128), 1)
    shift = 128 - lax.axis_index("seq") * mine
    own = jnp.where(lane8 < mine, pltpu.roll(heads[...], shift, 1), 0.0)
    rate = jnp.where(lane8 < mine, -jnp.exp(own), 0.0)[1:2, :]
    hp[...] = jnp.concatenate([own[0:1, :], rate * LOG2E, rate, jnp.zeros((5, 128), F32)], axis=0)
    last = cols[:, at:].astype(F32)
    last = jnp.concatenate(
        [last, jnp.zeros((last.shape[0], 128 - last.shape[1]), F32)], axis=1
    )
    lane = lax.broadcasted_iota(jnp.int32, last.shape, 1)
    moved = pltpu.roll(last, shift, 1)
    steps[...] = jnp.where(lane < mine, moved, 0.0).astype(BF16)
    lane = lax.broadcasted_iota(jnp.int32, (128, 128), 0)
    out = lax.broadcasted_iota(jnp.int32, (128, 128), 1)
    for p in range(sel.shape[0]):
        sel[p] = jnp.where(out == 2 * p + lane // 64, 1.0, 0.0).astype(BF16)
    seqs, length = seg.shape
    ids = seg[...].astype(F32)
    lane = lax.broadcasted_iota(jnp.int32, (seqs, length), 1)
    back = [
        jnp.where((pltpu.roll(ids, d, 1) == ids) & (lane >= d), 1.0, 0.0) for d in (1, 2, 3)
    ]
    ahead = [
        jnp.where((pltpu.roll(ids, length - d, 1) == ids) & (lane < length - d), 1.0, 0.0)
        for d in (1, 2, 3)
    ]
    before = [ids[:, 0:1]] + [ids[:, at - 1 : at] for at in range(Q, length, Q)]
    level = jnp.concatenate(
        [-RESET * (ids[:, n * Q : (n + 1) * Q] - b) for n, b in enumerate(before)], axis=1
    )
    all_rows = [*back, level, *ahead, jnp.zeros((seqs, length), F32)]
    for n in range(seqs):
        marks[n] = jnp.concatenate([r[n : n + 1, :] for r in all_rows], axis=0)


def prepare(seg, heads, w_in, mine, at):
    rows = w_in.shape[0]
    pairs = mine // 2
    shapes = [
        ((seg.shape[0], 8, seg.shape[1]), F32), ((8, 128), F32), ((pairs, 128, 128), BF16),
        ((rows, 128), BF16),
    ]

    def whole(shape):
        return pl.BlockSpec(shape, lambda i: (0,) * len(shape))

    return pl.pallas_call(
        functools.partial(prep_kernel, mine, at),
        grid=(1,),
        in_specs=[
            whole(seg.shape),
            whole(heads.shape),
            whole(w_in.shape),
        ],
        out_specs=[whole(n) for n, _ in shapes],
        out_shape=[jax.ShapeDtypeStruct(*n) for n in shapes],
        name="prepare",
    )(seg, heads, w_in)


def norm_kernel(wide, red, rk, got, ssem, rsem):
    d = lax.axis_index("dp")
    s = lax.axis_index("seq")
    groups = got.shape[0]
    bar = pltpu.get_barrier_semaphore()
    for j in range(1, groups):
        pl.semaphore_signal(bar, inc=1, device_id=(d, lax.rem(s + j, groups)), device_id_type=MESH)
    pl.semaphore_wait(bar, groups - 1)
    sends = [
        pltpu.make_async_remote_copy(
            src_ref=red, dst_ref=got.at[j], send_sem=ssem.at[j], recv_sem=rsem.at[j],
            device_id=(d, lax.rem(s + j, groups)), device_id_type=MESH,
        )
        for j in range(1, groups)
    ]
    for copy in sends:
        copy.start()
    total = red[...]
    for j, copy in enumerate(sends):
        copy.wait()
        total = total + got[j + 1]
    rho = lax.rsqrt(total[:, 0:1] / wide + EPSILON)
    rk[...] = jnp.concatenate(
        [rho, rho * rho * rho * total[:, 1:2] / wide, jnp.zeros_like(total[:, 2:])], axis=1
    )


def norms(red, wide, groups):
    vmem = pl.BlockSpec(memory_space=pltpu.VMEM)
    return pl.pallas_call(
        functools.partial(norm_kernel, wide),
        in_specs=[vmem],
        out_specs=vmem,
        out_shape=jax.ShapeDtypeStruct(red.shape, F32),
        scratch_shapes=[
            pltpu.VMEM((groups, *red.shape), F32),
            pltpu.SemaphoreType.DMA((groups,)),
            pltpu.SemaphoreType.DMA((groups,)),
        ],
        compiler_params=pltpu.CompilerParams(collective_id=3, has_side_effects=True),
        name="norms",
    )(red)


def final_kernel(
    groups, span, mine, gw, w_in, wog, w_out, osum, ngrad, tok, cot, gains, sums, nrow, grow, log,
    res, tgrad, wig, wgr, nout, gout, cout, bout, hout, nsum, gsum,
):
    step = pl.program_id(0)

    @pl.when(step == 0)
    def _():
        inner = span // 2
        shared = sums[0, :, inner:]
        heads = sums[0, :, :128]
        for g in range(1, groups):
            shared = shared + sums[g, :, inner:]
            heads = heads + pltpu.roll(sums[g, :, :128], g * mine, 1)
        row = jnp.concatenate([*[sums[g, :, :inner] for g in range(groups)], shared], axis=1)
        share, taps = cout.shape
        first = lax.axis_index("dp") * share
        tall = -(-share // 128) * 128
        own = pltpu.roll(row, row.shape[1] - first, 1)[:, :tall]
        cout[...] = own.T[:share, :taps]
        bout[...] = own[taps : taps + 1, :share]
        count = groups * mine
        hout[0:1, :] = heads[taps + 1 : taps + 2, :count]
        hout[1:2, :] = -jnp.exp(log[...]) * heads[taps + 2 : taps + 3, :count]
        hout[2:3, :] = heads[taps + 3 : taps + 4, :count]

    total = jnp.zeros((w_in.shape[0], 1), F32)
    for g in range(groups):
        here = slice(g * span, (g + 1) * span)
        grad = gw[g, :, :span].astype(F32)
        wig[:, here] = grad
        total = total + jnp.sum(grad * w_in[:, here].astype(F32), axis=1, keepdims=True)
    at = groups * span
    width = gw.shape[2] - 128
    shared = gw[0, :, span:width].astype(F32)
    steps = gw[0, :, width:].astype(F32)
    for g in range(1, groups):
        shared = shared + gw[g, :, span:width].astype(F32)
        steps = steps + pltpu.roll(gw[g, :, width:].astype(F32), g * mine, 1)
    mid = at + width - span
    wig[:, at:mid] = shared
    wig[:, mid:] = steps[:, : groups * mine]
    total = total + jnp.sum(shared * w_in[:, at:mid].astype(F32), axis=1, keepdims=True)
    total = total + jnp.sum(
        steps[:, : groups * mine] * w_in[:, mid:].astype(F32), axis=1, keepdims=True
    )
    tall = w_in.shape[0]
    nsum[pl.ds(pl.multiple_of(step * tall, 16), tall), :] = jnp.broadcast_to(total, (tall, 128))
    grad = wog[...].astype(F32)
    wgr[...] = grad
    tall = wog.shape[0]
    gsum[pl.ds(pl.multiple_of(step * tall, 16), tall), :] = jnp.broadcast_to(
        jnp.sum(grad * w_out[...].astype(F32), axis=1, keepdims=True), (tall, 128)
    )

    @pl.when(step == pl.num_programs(0) - 1)
    def _():
        nout[...] = nsum[...].T[0:1, : nout.shape[1]] / nrow[...].astype(F32)
        gout[...] = gsum[...].T[0:1, : gout.shape[1]] / grow[...].astype(F32)

    x = tok[...].astype(F32)
    res[...] = (x + osum[...].astype(F32)).astype(BF16)
    inverse = lax.rsqrt(jnp.mean(x * x, axis=1, keepdims=True) + EPSILON)
    unit = x * inverse
    grad = ngrad[...].astype(F32) * gains[0:1, :]
    tgrad[...] = cot[...].astype(F32) + inverse * (
        grad - unit * jnp.mean(grad * unit, axis=1, keepdims=True)
    )


def final(gw, w_in, wog, w_out, osum, ngrad, tok, cot, rows, span, mine, taps, share):
    groups, count, total = gw.shape
    steps = next(n for n in (4, 2, 1) if count % (16 * n) == 0)

    def part(a):
        return pl.BlockSpec((a.shape[0] // steps, a.shape[1]), lambda i: (i, 0))

    def whole(a):
        return pl.BlockSpec(a.shape, lambda i: (0,) * len(a.shape))

    def up(n):
        return -(-n // 128) * 128

    tall = [w_in, wog, w_out, osum, ngrad, tok, cot]
    big = [(tok.shape, BF16), (tok.shape, F32), (w_in.shape, F32), (wog.shape, F32)]
    little = [(1, count), (1, wog.shape[0]), (share, taps), (1, share), (3, groups * mine)]
    outs = [jax.ShapeDtypeStruct(*n) for n in big]
    extra = [jax.ShapeDtypeStruct(n, F32) for n in little]
    return pl.pallas_call(
        functools.partial(final_kernel, groups, span, mine),
        grid=(steps,),
        in_specs=[
            pl.BlockSpec((groups, count // steps, total), lambda i: (0, i, 0)),
            *[part(a) for a in tall],
            *[whole(a) for a in rows],
        ],
        out_specs=[*[part(o) for o in outs], *[whole(o) for o in extra]],
        out_shape=[*outs, *extra],
        scratch_shapes=[
            pltpu.VMEM((up(count), 128), F32),
            pltpu.VMEM((up(wog.shape[0]), 128), F32),
        ],
        compiler_params=pltpu.CompilerParams(vmem_limit_bytes=60 * 2**20),
        name="final",
    )(gw, *tall, *rows)


def gather_kernel(
    dims, w_in, dt_in, wo_in, small_in, tok_in, cot_in,
    turned_o, cot_o, pj_o, sg_o, w_o, wo_o, small_o,
    tok, cot, wbig, wo, small, pjv, sgv, turned,
    szu, szd, rz, sy, ry, wsu, wsd, wrz, wsy, wry, bx_s, bx_r, bc_s, bc_r, bs, br, loc, out,
):
    deep, pieces, rows, inner, part, length, groups = dims
    d = lax.axis_index("dp")
    s = lax.axis_index("seq")
    z = d // 2
    y = d % 2
    core = s % 2
    top = deep - 1
    up, down, side = (d + 2, s), (d - 2, s), (d + 1 - 2 * y, s)
    across, twin = (d, s + 2 - 4 * (s // 2)), (d, s + 1 - 2 * (s % 2))
    opposite = across[1]

    bar = pltpu.get_barrier_semaphore()

    @pl.when(z < top)
    def _():
        pl.semaphore_signal(bar, inc=1, device_id=up, device_id_type=MESH)

    @pl.when(z > 0)
    def _():
        pl.semaphore_signal(bar, inc=1, device_id=down, device_id_type=MESH)

    for who in (side, across, twin):
        pl.semaphore_signal(bar, inc=1, device_id=who, device_id_type=MESH)
    pl.semaphore_wait(bar, 3 + jnp.minimum(z, 1) + jnp.minimum(top - z, 1))

    def send(src, dst, ssem, rsem, who):
        return pltpu.make_async_remote_copy(
            src_ref=src, dst_ref=dst, send_sem=ssem, recv_sem=rsem,
            device_id=who, device_id_type=MESH,
        )

    width = 2 * inner

    def cols(k):
        return pl.ds(width + 256, 128) if k == 1 else pl.ds(width if k == 2 else (k - 3) * 256, 256)

    def held(k, owner):
        if k == 0:
            return small.at[owner]
        if k == 2:
            return shared(owner, core)
        return wbig.at[pl.ds(pl.multiple_of(owner * rows, 16), rows), cols(k)]

    def shared(owner, half):
        at = pl.multiple_of(owner * rows + half * (rows // 2), 16)
        return wbig.at[pl.ds(at, rows // 2), pl.ds(width, 256)]

    def shared_send(owner, half):
        ref = shared(owner, half)
        return send(ref, ref, bs.at[owner], br.at[owner], twin)

    def share_columns():
        for e in range(2 * deep):
            @pl.when(d != e)
            def _():
                shared_send(e, core).start()

        for e in range(2 * deep):
            @pl.when(d != e)
            def _():
                shared_send(e, 1 - core).wait_recv()

    def source(k):
        if k == 0:
            return small_in.at[...]
        if k == 1:
            return dt_in.at[...]
        if k == 2:
            at = pl.multiple_of(core * (rows // 2), 16)
            return w_in.at[pl.ds(at, rows // 2), pl.ds(width * groups, 256)]
        return w_in.at[:, pl.ds(pl.multiple_of(s * width + (k - 3) * 256, 128), 256)]

    def own_send(k):
        src, dst = source(k), held(k, d)

        @pl.when(z < top)
        def _():
            send(src, dst, szu.at[k, z], rz.at[k, z], up).start()

        @pl.when(z > 0)
        def _():
            send(src, dst, szd.at[k, z], rz.at[k, z], down).start()

        send(src, dst, sy.at[k, z], ry.at[k, z], side).start()

    def hop(k, h):
        below, above = z - h, z + h

        @pl.when(below >= 0)
        def _():
            ref = held(k, below * 2 + y)
            send(ref, ref, szu.at[k, below], rz.at[k, below], up).wait_recv()

            @pl.when(z < top)
            def _():
                send(ref, ref, szu.at[k, below], rz.at[k, below], up).start()

            send(ref, ref, sy.at[k, below], ry.at[k, below], side).start()

        @pl.when(above <= top)
        def _():
            ref = held(k, above * 2 + y)
            send(ref, ref, szd.at[k, above], rz.at[k, above], down).wait_recv()

            @pl.when(z > 0)
            def _():
                send(ref, ref, szd.at[k, above], rz.at[k, above], down).start()

            send(ref, ref, sy.at[k, above], ry.at[k, above], side).start()

    def arrive(k):
        for e in range(deep):
            ref = held(k, e * 2 + 1 - y)
            send(ref, ref, sy.at[k, e], ry.at[k, e], side).wait_recv()

    def own_copy(src, dst, sem):
        return pltpu.make_async_copy(src, dst, sem)

    here = pl.multiple_of(s * part, 16)
    there = pl.multiple_of(opposite * part, 16)
    locals_ = [
        own_copy(small_in, small.at[d], loc.at[0]),
        own_copy(
            w_in.at[:, pl.ds(pl.multiple_of(s * width, 128), width)],
            wbig.at[pl.ds(pl.multiple_of(d * rows, 16), rows), pl.ds(0, width)],
            loc.at[1],
        ),
    ]
    for q in range(2):
        locals_.append(own_copy(tok_in.at[q], tok.at[q, pl.ds(here, part)], loc.at[2 + q]))
        locals_.append(own_copy(cot_in.at[q], cot.at[q, pl.ds(here, part)], loc.at[4 + q]))
    locals_.append(own_copy(source(1), held(1, d), loc.at[7]))
    locals_.append(
        own_copy(
            w_in.at[:, pl.ds(width * groups, 256)],
            wbig.at[pl.ds(pl.multiple_of(d * rows, 16), rows), pl.ds(width, 256)],
            loc.at[8],
        )
    )
    half = wo_in.shape[0]
    mine = z == s

    def root_copy():
        return own_copy(wo_in, wo.at[pl.ds(pl.multiple_of(y * half, 16), half)], loc.at[6])

    def block_sends(which, src, dst, q):
        spot = dst.at[q, pl.ds(here, part)]
        i = which * 2 + q
        send(src.at[q], spot, bx_s.at[i], bx_r.at[i], across).start()
        send(src.at[q], spot, bc_s.at[0, i], bc_r.at[0, i], twin).start()

    def block_forward(which, dst, q):
        spot = dst.at[q, pl.ds(there, part)]
        i = which * 2 + q
        send(spot, spot, bx_s.at[i], bx_r.at[i], across).wait_recv()
        send(spot, spot, bc_s.at[1, i], bc_r.at[1, i], twin).start()

    def block_arrive(which, dst, q):
        i = which * 2 + q
        for n in range(2):
            spot = dst.at[q, pl.ds(here, part)]
            send(spot, spot, bc_s.at[n, i], bc_r.at[n, i], twin).wait_recv()

    lump = half // LUMPS

    def wo_piece(i, col):
        m = col * LUMPS + i
        return m, wo.at[pl.ds(pl.multiple_of(m * lump, 16), lump)]

    def wo_send(i, src=None):
        m, ref = wo_piece(i, y)
        src = ref if src is None else src

        @pl.when((z >= s) & (z < top))
        def _():
            send(src, ref, wsu.at[m], wrz.at[m], up).start()

        @pl.when((z <= s) & (z > 0))
        def _():
            send(src, ref, wsd.at[m], wrz.at[m], down).start()

        send(src, ref, wsy.at[m], wry.at[m], side).start()

    def wo_root(i):
        @pl.when(mine)
        def _():
            wo_send(i, wo_in.at[pl.ds(i * lump, lump)])

    def wo_hop(i, h):
        @pl.when((z - s == h) | (s - z == h))
        def _():
            m, ref = wo_piece(i, y)
            send(ref, ref, wsu.at[m], wrz.at[m], up).wait_recv()
            wo_send(i)

    def wo_arrive(i):
        m, ref = wo_piece(i, 1 - y)
        send(ref, ref, wsy.at[m], wry.at[m], side).wait_recv()

    tile = 256
    long = 512

    def project(k):
        c = pl.ds(width, 384) if k == 2 else cols(k)

        def step(i, _):
            q, r = i // (length // long), i % (length // long)
            at = pl.ds(pl.multiple_of(r * long, long), long)
            pjv[q, at, c] = mm(tok[q, at, :], wbig[:, c]).astype(BF16)
            return 0

        lax.fori_loop(0, 2 * length // long, step, 0)
        own_copy(pjv.at[:, :, c], pj_o.at[:, :, c], out.at[k]).start()

    for c in locals_:
        c.start()

    @pl.when(mine)
    def _():
        root_copy().start()

    for q in range(2):
        block_sends(0, tok_in, tok, q)
    for q in range(2):
        block_sends(1, cot_in, cot, q)
    ahead = 3
    for k in range(ahead):
        own_send(k)
    done = []

    def hops(t):
        for h in range(1, deep):
            if 0 <= t - h < pieces:
                hop(t - h, h)
        for h in range(1, deep):
            if 0 <= t - h - WOFF < LUMPS:
                wo_hop(t - h - WOFF, h)
        if 0 <= t - WOFF < LUMPS:
            wo_root(t - WOFF)
        if ahead <= t + ahead - 1 < pieces:
            own_send(t + ahead - 1)

    steps = max(pieces, WOFF + LUMPS) + deep - 1
    count = dict(next=1)

    def ready(n):
        for _ in range(n):
            if count["next"] < pieces:
                arrive(count["next"])
                if count["next"] == 2:
                    share_columns()
                if count["next"] > 1:
                    project(count["next"])
                count["next"] += 1

    share = tok.shape[2] // (2 * deep)

    def norm_step(i, _):
        q, r = i // (length // 64), i % (length // 64)
        at = pl.multiple_of(r * 64, 64)
        x = tok[q, pl.ds(at, 64), :].astype(F32)
        inv = lax.rsqrt(jnp.mean(x * x, axis=1, keepdims=True) + EPSILON)
        gains = jnp.concatenate([small[e, 0:1, :share] for e in range(2 * deep)], axis=1)
        tok[q, pl.ds(at, 64), :] = (x * inv * gains.astype(F32)).astype(BF16)
        return 0

    def turn_step(i, _):
        q, r = i // (length // tile), i % (length // tile)
        at = pl.multiple_of(r * tile, tile)
        to = pl.multiple_of(i * tile, tile)
        for j in range(0, tok.shape[2], 128):
            turned[j : j + 128, pl.ds(to, tile)] = tok[q, pl.ds(at, tile), j : j + 128].T
        return 0

    def grad_step(i, _):
        q, r = i // (length // long), i % (length // long)
        at = pl.ds(pl.multiple_of(r * long, long), long)
        sgv[q, at, :] = nt(cot[q, at, :], wo[...]).astype(BF16)
        return 0

    for t in range(1, steps):
        hops(t)
        if t == 3:
            block_forward(0, tok, 0)
        if t == 6:
            block_forward(0, tok, 1)
        if t == 7:
            for i in (0, 1, 2, 4, 6, 7):
                locals_[i].wait()
            block_arrive(0, tok, 0)
            block_arrive(0, tok, 1)
            for q in range(2):
                spot = tok.at[q, pl.ds(there, part)]
                send(spot, spot, bc_s.at[1, q], bc_r.at[1, q], twin).wait_send()
            arrive(0)
            own_copy(small, small_o, out.at[0]).start()
            lax.fori_loop(0, 2 * length // 64, norm_step, 0)
            lax.fori_loop(0, 2 * length // tile, turn_step, 0)
            own_copy(turned, turned_o, out.at[pieces]).start()
        if t == 10:
            block_forward(1, cot, 0)
        if t == 11:
            block_forward(1, cot, 1)
        if t > 7:
            ready(2 if t == 8 else 1)

    @pl.when(mine)
    def _():
        root_copy().wait()

    locals_[3].wait()
    locals_[5].wait()
    for i in range(LUMPS):
        wo_arrive(i)
    own_copy(wo, wo_o, out.at[pieces + 2]).start()
    block_arrive(1, cot, 0)
    block_arrive(1, cot, 1)
    own_copy(cot, cot_o, out.at[pieces + 3]).start()
    lax.fori_loop(0, 2 * length // long, grad_step, 0)
    own_copy(sgv, sg_o, out.at[pieces + 4]).start()
    ready(pieces)
    own_copy(wbig, w_o, out.at[pieces + 1]).start()
    for k in range(pieces):
        for e in range(deep):
            ref = held(k, e * 2 + y)

            @pl.when((z >= e) & (z < top))
            def _():
                send(ref, ref, szu.at[k, e], rz.at[k, e], up).wait_send()

            @pl.when((z <= e) & (z > 0))
            def _():
                send(ref, ref, szd.at[k, e], rz.at[k, e], down).wait_send()

            send(ref, ref, sy.at[k, e], ry.at[k, e], side).wait_send()
    for e in range(2 * deep):
        @pl.when(d != e)
        def _():
            shared_send(e, core).wait_send()

    for i in range(LUMPS):
        m, ref = wo_piece(i, y)

        @pl.when((z >= s) & (z < top))
        def _():
            send(ref, ref, wsu.at[m], wrz.at[m], up).wait_send()

        @pl.when((z <= s) & (z > 0))
        def _():
            send(ref, ref, wsd.at[m], wrz.at[m], down).wait_send()

        send(ref, ref, wsy.at[m], wry.at[m], side).wait_send()
    for which, dst in ((0, tok), (1, cot)):
        for q in range(2):
            i = which * 2 + q
            spot = dst.at[q, pl.ds(here, part)]
            send(spot, spot, bx_s.at[i], bx_r.at[i], across).wait_send()
            for n in range(1 + which):
                send(spot, spot, bc_s.at[n, i], bc_r.at[n, i], twin).wait_send()
    own_copy(small, small_o, out.at[0]).wait()
    for k in range(2, pieces):
        c = pl.ds(width, 384) if k == 2 else cols(k)
        own_copy(pjv.at[:, :, c], pj_o.at[:, :, c], out.at[k]).wait()
    own_copy(turned, turned_o, out.at[pieces]).wait()
    own_copy(wbig, w_o, out.at[pieces + 1]).wait()
    own_copy(wo, wo_o, out.at[pieces + 2]).wait()
    own_copy(cot, cot_o, out.at[pieces + 3]).wait()
    own_copy(sgv, sg_o, out.at[pieces + 4]).wait()


def gather(w_in, dt_in, w_out, small, tokens, cotangent, inner, shards, groups):
    rows = w_in.shape[0]
    total = 2 * inner + 384
    seqs, part, model = tokens.shape
    length = part * groups
    deep = shards // 2
    pieces = inner // 128 + 3
    any_ = pl.BlockSpec(memory_space=pl.ANY)
    dma = pltpu.SemaphoreType.DMA
    small_rows, small_cols = small.shape
    full = (shards * rows, total)
    shapes = [
        (model, seqs * length), (seqs, length, model), (seqs, length, total), (seqs, length, inner),
        full, (inner, model), (shards, small_rows, small_cols),
    ]
    return pl.pallas_call(
        functools.partial(gather_kernel, (deep, pieces, rows, inner, part, length, groups)),
        in_specs=[any_] * 6,
        out_specs=[any_] * 7,
        out_shape=[jax.ShapeDtypeStruct(n, BF16) for n in shapes],
        scratch_shapes=[
            pltpu.VMEM(shapes[1], BF16),
            pltpu.VMEM(shapes[1], BF16),
            pltpu.VMEM(full, BF16),
            pltpu.VMEM((inner, model), BF16),
            pltpu.VMEM(shapes[6], BF16),
            pltpu.VMEM(shapes[2], BF16),
            pltpu.VMEM(shapes[3], BF16),
            pltpu.VMEM(shapes[0], BF16),
            dma((pieces, deep)), dma((pieces, deep)), dma((pieces, deep)),
            dma((pieces, deep)), dma((pieces, deep)),
            *[dma((2 * LUMPS,))] * 5,
            dma((4,)), dma((4,)), dma((2, 4)), dma((2, 4)),
            dma((2 * deep,)), dma((2 * deep,)),
            dma((9,)), dma((pieces + 5,)),
        ],
        compiler_params=pltpu.CompilerParams(
            collective_id=1, has_side_effects=True, vmem_limit_bytes=56 * 2**20
        ),
        name="gather_project",
    )(w_in, dt_in, w_out, small, tokens, cotangent)


def greet(z, y, s, deep, others):
    bar = pltpu.get_barrier_semaphore()
    for e in range(deep):
        @pl.when(z != e)
        def _():
            pl.semaphore_signal(bar, inc=1, device_id=(2 * e + y, s), device_id_type=MESH)

    for who in others:
        pl.semaphore_signal(bar, inc=1, device_id=who, device_id_type=MESH)
    pl.semaphore_wait(bar, len(others) + deep - 1)


def send(src, dst, ssem, rsem, who):
    return pltpu.make_async_remote_copy(
        src_ref=src, dst_ref=dst, send_sem=ssem, recv_sem=rsem, device_id=who, device_id_type=MESH
    )


def add_into(dst, src):
    count = dst.shape[0]
    some = next(n for n in (64, 48, 32, 16) if count % n == 0)

    def step(i, _):
        at = pl.ds(pl.multiple_of(i * some, 16), some)
        dst[at, :] = (dst[at, :].astype(F32) + src[at, :].astype(F32)).astype(BF16)
        return 0

    lax.fori_loop(0, count // some, step, 0)


CUTS = ((0, 512), (512, 512), (1536, 384), (1024, 256), (1280, 128), (1408, 128))
PARTS = len(CUTS)


def scatter_kernel(
    dims, nt_in, pg_in, st_in, sc_in, cot_in, wo_in, wi_in, ch_in, he_in,
    gw_o, wo_o, out_o, ng_o, sm_o,
    nt_v, pg_v, st_v, sc_v, wo_v, cw, pv, yb, zb, tw, xr, stage, gw, ybw, zbw, ch_v, he_v,
    vec, vgot, vall,
    sy, ry, su, sd, rz, gx_s, gx_r, gc_s, gc_r, tw_s, tw_r, xr_s, xr_r,
    wy_s, wy_r, wu_s, wd_s, wz_r, bx_s, bx_r, bc_s, bc_r, v_s, v_r, loc, out,
):
    deep, rows, part, length = dims
    d = lax.axis_index("dp")
    s = lax.axis_index("seq")
    z = d // 2
    y = d % 2
    x = s // 2
    c = s % 2
    top = deep - 1
    model = wi_in.shape[0]
    up, down, side = (d + 2, s), (d - 2, s), (d + 1 - 2 * y, s)
    across, twin = (d, s + 2 - 4 * x), (d, s + 1 - 2 * c)
    greet(z, y, s, deep, (side, across, twin))

    def cut(k):
        return pl.ds(*CUTS[k])

    def lines(ref, i, count=rows):
        return ref.at[pl.ds(pl.multiple_of(i * count, 16), count)]

    cot_v = cw.at[:, pl.ds(0, model)]
    wi_v = cw.at[pl.ds(0, model), :]
    loads = dict(
        ch=pltpu.make_async_copy(ch_in, ch_v, loc.at[2]),
        he=pltpu.make_async_copy(he_in, he_v, loc.at[3]),
        st=pltpu.make_async_copy(st_in, st_v, loc.at[0]),
        cot=pltpu.make_async_copy(cot_in, cot_v, loc.at[1]),
        sc=pltpu.make_async_copy(sc_in, sc_v, loc.at[6]),
        wo=pltpu.make_async_copy(wo_in, wo_v, loc.at[7]),
        nt=pltpu.make_async_copy(nt_in, nt_v, loc.at[4]),
        pg=pltpu.make_async_copy(pg_in, pg_v, loc.at[5]),
    )
    for load in loads.values():
        load.start()
    load_wi = pltpu.make_async_copy(wi_in, wi_v, loc.at[8])

    def v_send(n, src, dst, who):
        return send(src, dst, v_s.at[n], v_r.at[n], who)

    def v_y():
        return v_send(0, vec, vgot.at[deep], side)

    def v_z(e):
        return send(vec, vgot.at[z], v_s.at[1 + e], v_r.at[1 + z], (2 * e + y, s))

    def v_from(e):
        return send(vec, vgot.at[e], v_s.at[1 + e], v_r.at[1 + e], (2 * e + y, s))

    def v_seq(n, owner, who):
        return v_send(1 + deep + n, vall.at[owner], vall.at[owner], who)

    def v_start():
        vec[...] = jnp.concatenate(
            [
                jnp.sum(ch_v[...], axis=1),
                jnp.concatenate(
                    [jnp.sum(he_v[...], axis=1), jnp.zeros((3, vec.shape[1] - 128), F32)], axis=1
                ),
            ],
            axis=0,
        )
        v_y().start()

    def v_sum():
        v_y().wait()
        vec[...] = vec[...] + vgot[deep]
        for e in range(deep):
            @pl.when(z != e)
            def _():
                v_z(e).start()

    def v_total():
        for e in range(deep):
            @pl.when(z != e)
            def _():
                v_z(e).wait_send()
                v_from(e).wait_recv()

            @pl.when(z == e)
            def _():
                vgot[e] = vec[...]

        total = vgot[0]
        for e in range(1, deep):
            total = total + vgot[e]
        vall[s] = total
        v_seq(0, s, across).start()
        v_seq(1, s, twin).start()

    def v_spread():
        v_seq(0, across[1], across).wait_recv()
        v_seq(2, across[1], twin).start()

    both = ((0, out_o), (1, ng_o))

    def twin_send(n, turn, q):
        return send(stage.at[q], tw.at[n, turn, q], tw_s.at[q], tw_r.at[n, turn, q], twin)

    def product(n, q, owner, j):
        at = pl.ds(pl.multiple_of(q * length + owner * part, 16), part)
        if n == 0:
            return mm(sc_v[at, :], wo_v[:, j : j + 512])
        return nt(pg_v[at, :], cw[j : j + 512, :])

    def exchange(n, turn):
        half = 1 - x if turn == 0 else x
        for q in range(2):
            if (n, turn) != (0, 0):
                twin_send(n, turn, q).wait_send()
            for j in range(0, model, 512):
                stage[q, :, j : j + 512] = product(n, q, 2 * half + 1 - c, j).astype(BF16)
            twin_send(n, turn, q).start()
        for q in range(2):
            twin_send(n, turn, q).wait_recv()
            for j in range(0, model, 512):
                tw[n, turn, q, :, j : j + 512] = (
                    tw[n, turn, q, :, j : j + 512].astype(F32) + product(n, q, 2 * half + c, j)
                ).astype(BF16)
            if turn == 0:
                x_send(n, q).start()

    def x_send(n, q):
        return send(tw.at[n, 0, q], xr.at[n, q], xr_s.at[n, q], xr_r.at[n, q], across)

    def x_finish(n, dst):
        for q in range(2):
            x_send(n, q).wait_recv()
            add_into(xr.at[n, q], tw.at[n, 1, q])
            pltpu.make_async_copy(xr.at[n, q], dst.at[q], out.at[2 + 2 * n + q]).start()

    def weigh(k):
        tall = 2 * rows

        def step(i, _):
            at = pl.ds(pl.multiple_of(i * tall, 16), tall)
            pv[at, cut(k)] = mm(nt_v[at, :], pg_v[:, cut(k)]).astype(BF16)
            return 0

        lax.fori_loop(0, deep, step, 0)

    def block(e, k):
        return pv.at[pl.ds(pl.multiple_of((2 * e + y) * rows, 16), rows), cut(k)]

    def y_send(k, e):
        src = pv.at[pl.ds(pl.multiple_of((2 * e + 1 - y) * rows, 16), rows), cut(k)]
        return send(src, lines(yb, e).at[:, cut(k)], sy.at[k, e], ry.at[k, e], side)

    def y_start(k):
        for e in range(deep):
            y_send(k, e).start()

    def y_add(k):
        for e in range(deep):
            y_send(k, e).wait_recv()
            add_into(block(e, k), lines(yb, e).at[:, cut(k)])

    def z_send(k, e, slot, sem, who):
        return send(block(e, k), lines(zb, slot).at[:, cut(k)], sem.at[k, e], rz.at[k, slot], who)

    def hop(k, h):
        @pl.when(z == h - 1)
        def _():
            for e in range(top, h - 1, -1):
                if h > 1:
                    z_send(k, e, e, su, up).wait_recv()
                    add_into(block(e, k), lines(zb, e).at[:, cut(k)])
                z_send(k, e, e, su, up).start()

        @pl.when(z == deep - h)
        def _():
            for e in range(deep - h):
                if h > 1:
                    z_send(k, e, e, sd, down).wait_recv()
                    add_into(block(e, k), lines(zb, e).at[:, cut(k)])
                z_send(k, e, deep if e == deep - h - 1 else e, sd, down).start()

    def g_spot(who, k):
        return gw_o.at[who, :, cut(k)]

    def finish(k):
        mine = block(z, k)

        @pl.when(z > 0)
        def _():
            z_send(k, z, z, su, up).wait_recv()
            add_into(mine, lines(zb, z).at[:, cut(k)])

        @pl.when(z < top)
        def _():
            z_send(k, z, deep, sd, down).wait_recv()
            add_into(mine, lines(zb, deep).at[:, cut(k)])

        send(mine, g_spot(s, k), gx_s.at[k], gx_r.at[k], across).start()
        send(mine, g_spot(s, k), gc_s.at[0, k], gc_r.at[0, k], twin).start()
        pltpu.make_async_copy(mine, g_spot(s, k), loc.at[9 + k]).start()

    def spread(k):
        spot = g_spot(across[1], k)
        send(spot, spot, gx_s.at[k], gx_r.at[k], across).wait_recv()
        send(spot, spot, gc_s.at[1, k], gc_r.at[1, k], twin).start()

    half = gw.shape[0] // 2
    lump = half // LUMPS

    def w_rows(col, i):
        return gw.at[pl.ds(pl.multiple_of(col * half + i * lump, 16), lump)]

    def piece(ref, i):
        return ref.at[pl.ds(i * lump, lump)]

    def wy_send(i):
        return send(w_rows(1 - y, i), piece(ybw, i), wy_s.at[i], wy_r.at[i], side)

    def w_compute():
        tall = 2 * lump
        for n in range(LUMPS):
            col, i = (1 - y, n) if n < LUMPS // 2 else (y, n - LUMPS // 2)
            at = pl.ds(pl.multiple_of(col * half + i * tall, 16), tall)
            for j in range(0, model, 512):
                gw[at, j : j + 512] = mm(st_v[at, :], cw[:, j : j + 512]).astype(BF16)
            if n < LUMPS // 2:
                wy_send(2 * i).start()
                wy_send(2 * i + 1).start()

    def from_below(i):
        return send(w_rows(y, i), piece(zbw.at[0], i), wu_s.at[i], wz_r.at[0, i], up)

    def from_above(i):
        return send(w_rows(y, i), piece(zbw.at[1], i), wd_s.at[i], wz_r.at[1, i], down)

    def w_cast(i, who, ssem, rsem):
        return send(piece(wo_o, i), piece(wo_o, i), ssem.at[i], rsem.at[i], who)

    def w_root(i, who, ssem, rsem):
        return send(w_rows(y, i), piece(wo_o, i), ssem.at[i], rsem.at[i], who)

    def w_keep(i):
        return pltpu.make_async_copy(w_rows(y, i), piece(wo_o, i), loc.at[9 + PARTS + i])

    root = z == s

    def w_chain(i, h):
        last = h == deep - 1
        below = root & (z > 0) if last else (z < s) & (z == h) & (h > 0)
        above = root & (z < top) if last else (z > s) & (top - z == h) & (h > 0)

        @pl.when(root if last else ((z < s) & (z == h)) | ((z > s) & (top - z == h)))
        def _():
            wy_send(i).wait_recv()
            add_into(w_rows(y, i), piece(ybw, i))

        @pl.when(below)
        def _():
            from_below(i).wait_recv()
            add_into(w_rows(y, i), piece(zbw.at[0], i))

        @pl.when(above)
        def _():
            from_above(i).wait_recv()
            add_into(w_rows(y, i), piece(zbw.at[1], i))

        if last:

            @pl.when(root)
            def _():
                w_keep(i).start()
                w_root(i, across, bx_s, bx_r).start()
                w_root(i, twin, bc_s, bc_r).start()

        else:

            @pl.when((z < s) & (z == h))
            def _():
                from_below(i).start()

            @pl.when((z > s) & (top - z == h))
            def _():
                from_above(i).start()

    def w_spread(i):
        @pl.when(across[1] == z)
        def _():
            w_cast(i, across, bx_s, bx_r).wait_recv()
            w_cast(i, twin, bc_s, bc_r).start()

        @pl.when((across[1] != z) & jnp.logical_not(root))
        def _():
            w_cast(i, twin, bc_s, bc_r).wait_recv()

    def w_step(t):
        for h in range(deep):
            if 0 <= t - h < LUMPS:
                w_chain(t - h, h)

    loads["ch"].wait()
    loads["he"].wait()
    v_start()
    loads["st"].wait()
    loads["cot"].wait()
    w_compute()
    load_wi.start()
    loads["sc"].wait()
    loads["wo"].wait()
    exchange(0, 0)
    w_step(0)
    loads["nt"].wait()
    loads["pg"].wait()
    weigh(0)
    y_start(0)
    v_sum()
    w_step(1)
    exchange(0, 1)
    w_step(2)
    load_wi.wait()
    exchange(1, 0)
    w_step(3)
    v_total()
    weigh(1)
    y_start(1)
    w_step(4)
    exchange(1, 1)
    w_step(5)
    y_add(0)
    hop(0, 1)
    weigh(2)
    y_start(2)
    w_step(6)
    hop(0, 2)
    weigh(3)
    y_start(3)
    for k in range(4, PARTS):
        weigh(k)
        y_start(k)
    w_step(7)
    hop(0, 3)
    y_add(1)
    hop(1, 1)
    w_step(8)
    finish(0)
    hop(1, 2)
    hop(1, 3)
    y_add(2)
    hop(2, 1)
    finish(1)
    hop(2, 2)
    x_finish(0, out_o)
    y_add(3)
    hop(3, 1)
    hop(2, 3)
    y_add(4)
    hop(4, 1)
    hop(3, 2)
    finish(2)
    y_add(5)
    hop(5, 1)
    hop(3, 3)
    hop(4, 2)
    hop(5, 2)
    finish(3)
    hop(4, 3)
    hop(5, 3)
    finish(4)
    finish(5)
    x_finish(1, ng_o)
    v_spread()
    for i in range(LUMPS):
        w_spread(i)
    for n in (1, 2):
        v_seq(n, twin[1], twin).wait_recv()
    keep = pltpu.make_async_copy(vall, sm_o, out.at[0])
    keep.start()
    for k in range(PARTS):
        spread(k)
    for k in range(PARTS):
        for n in range(2):
            spot = g_spot(twin[1], k)
            send(spot, spot, gc_s.at[n, k], gc_r.at[n, k], twin).wait_recv()
        pltpu.make_async_copy(g_spot(s, k), g_spot(s, k), loc.at[9 + k]).wait()
    keep.wait()
    v_seq(0, s, across).wait_send()
    v_seq(1, s, twin).wait_send()
    v_seq(2, s, twin).wait_send()
    for n, dst in both:
        for q in range(2):
            x_send(n, q).wait_send()
            pltpu.make_async_copy(xr.at[n, q], dst.at[q], out.at[2 + 2 * n + q]).wait()
    for q in range(2):
        twin_send(1, 1, q).wait_send()
    for k in range(PARTS):
        for e in range(deep):
            y_send(k, e).wait_send()

            @pl.when(z < e)
            def _():
                z_send(k, e, e, su, up).wait_send()

            @pl.when(z > e)
            def _():
                z_send(k, e, e, sd, down).wait_send()

        spot = g_spot(s, k)
        send(spot, spot, gx_s.at[k], gx_r.at[k], across).wait_send()
        for n in range(2):
            send(spot, spot, gc_s.at[n, k], gc_r.at[n, k], twin).wait_send()
    for i in range(LUMPS):
        wy_send(i).wait_send()

        @pl.when(z < s)
        def _():
            from_below(i).wait_send()

        @pl.when(z > s)
        def _():
            from_above(i).wait_send()

        @pl.when(root)
        def _():
            w_keep(i).wait()
            w_root(i, across, bx_s, bx_r).wait_send()

        @pl.when(root | (across[1] == z))
        def _():
            w_cast(i, twin, bc_s, bc_r).wait_send()


def scatter(normed_t, pg, scaled_t, scaled, cot, wo, wi, chacc, hacc, length, shards, groups):
    model, count = normed_t.shape
    total = pg.shape[1]
    inner = scaled_t.shape[0]
    seqs = count // length
    part = length // groups
    deep = shards // 2
    rows = model // shards
    any_ = pl.BlockSpec(memory_space=pl.ANY)
    dma = pltpu.SemaphoreType.DMA
    v = pltpu.VMEM
    small = (8, chacc.shape[2])
    return pl.pallas_call(
        functools.partial(scatter_kernel, (deep, rows, part, length)),
        in_specs=[any_] * 9,
        out_specs=[any_] * 5,
        out_shape=[
            jax.ShapeDtypeStruct((groups, rows, total), BF16),
            jax.ShapeDtypeStruct((inner // 2, model), BF16),
            jax.ShapeDtypeStruct((seqs, part, model), BF16),
            jax.ShapeDtypeStruct((seqs, part, model), BF16),
            jax.ShapeDtypeStruct((groups, *small), F32),
        ],
        scratch_shapes=[
            v((model, count), BF16),
            v((count, total), BF16),
            v((inner, count), BF16),
            v((count, inner), BF16),
            v((inner, model), BF16),
            v((count, total), BF16),
            v((model, total), BF16),
            v((deep * rows, total), BF16),
            v(((deep + 1) * rows, total), BF16),
            v((2, 2, 2, part, model), BF16),
            v((2, 2, part, model), BF16),
            v((2, part, model), BF16),
            v((inner, model), BF16),
            v((inner // 2, model), BF16),
            v((2, inner // 2, model), BF16),
            v(chacc.shape, F32),
            v(hacc.shape, F32),
            v(small, F32),
            v((deep + 1, *small), F32),
            v((groups, *small), F32),
            dma((PARTS, deep)), dma((PARTS, deep)), dma((PARTS, deep)), dma((PARTS, deep)),
            dma((PARTS, deep + 1)),
            dma((PARTS,)), dma((PARTS,)), dma((2, PARTS)), dma((2, PARTS)),
            dma((2,)), dma((2, 2, 2)), dma((2, 2)), dma((2, 2)),
            dma((LUMPS,)), dma((LUMPS,)), dma((LUMPS,)), dma((LUMPS,)), dma((2, LUMPS)),
            dma((LUMPS,)), dma((LUMPS,)), dma((LUMPS,)), dma((LUMPS,)),
            dma((deep + 4,)), dma((deep + 4,)),
            dma((9 + PARTS + LUMPS,)), dma((6,)),
        ],
        compiler_params=pltpu.CompilerParams(
            collective_id=2, has_side_effects=True, vmem_limit_bytes=60 * 2**20
        ),
        name="weigh_scatter",
    )(normed_t, pg, scaled_t, scaled, cot, wo, wi, chacc, hacc)


def local(
    tokens,
    segment_ids,
    w_in,
    w_out,
    conv_weight,
    conv_bias,
    norm_gain,
    gated_gain,
    dt_bias,
    a_log,
    skip_weight,
    cotangent,
):
    groups = lax.axis_size("seq")
    shards = lax.axis_size("dp")
    place = lax.axis_index("seq")
    owner = lax.axis_index("dp")
    seqs, part, model = tokens.shape
    length = part * groups
    rows_in = w_in.shape[0]
    rows_out = w_out.shape[0]
    wide = rows_out * shards
    heads = dt_bias.shape[0]
    size = wide // heads
    mine = heads // groups
    inner = mine * size
    span = 2 * inner
    taps = conv_weight.shape[1]
    state2 = w_in.shape[1] - 2 * wide - heads
    channels = wide + state2
    share = channels // shards
    ratio = shards // groups
    small_slice = groups == 4 and shards == 8

    def own(a):
        return lax.dynamic_slice_in_dim(a, place * inner, inner, 0)

    def own_heads(a):
        return lax.dynamic_slice_in_dim(a, place * mine, mine, 0)

    head_rows = jnp.pad(jnp.stack([dt_bias, a_log]), ((0, 6), (0, 128 - heads)))
    marks, hp, sel, step_cols = prepare(segment_ids, head_rows, w_in, mine, 2 * wide + state2)
    flat = [norm_gain, conv_bias, gated_gain, conv_weight.reshape(-1)]
    small = jnp.concatenate(flat)
    tall = -(-small.shape[0] // 4096) * 4096
    small = jnp.pad(small, (0, tall - small.shape[0])).reshape(-1, 256)
    if small_slice:
        turned, cot, pj, sg, w_full, wo, small_all = gather(
            w_in, step_cols, w_out, small, tokens, cotangent, inner, shards, groups
        )
    else:
        small_all = lax.all_gather(small, "dp", axis=0, tiled=False)
    small_all = small_all.reshape(shards, -1).astype(F32)
    cut = [0]
    for a in flat:
        cut.append(cut[-1] + a.shape[0])
    norm_all, conv_b, gain_all, conv_w = (
        small_all[:, cut[i] : cut[i + 1]].reshape(-1) for i in range(4)
    )
    conv_w = conv_w.reshape(channels, taps)
    if not small_slice:
        floats = tokens.astype(F32)
        inverse = lax.rsqrt(jnp.mean(floats * floats, axis=-1, keepdims=True) + EPSILON)
        unit = floats * inverse
        w_mine = jnp.concatenate(
            [
                lax.dynamic_slice_in_dim(w_in, place * span, span, 1),
                w_in[:, 2 * wide : 2 * wide + state2],
                step_cols,
            ],
            axis=1,
        )
        normed = lax.all_gather((unit * norm_all).astype(BF16), "seq", axis=1, tiled=True)
        cot = lax.all_gather(cotangent, "seq", axis=1, tiled=True)
        w_full = lax.all_gather(w_mine, "dp", axis=0, tiled=True)
        held = jnp.where(
            (owner // ratio == place) & (jnp.arange(ratio)[:, None, None] == owner % ratio),
            w_out[None],
            jnp.zeros((), BF16),
        ).reshape(inner, model)
        wo = lax.psum(held, "dp")
        sg = jnp.einsum("std,cd->stc", cot, wo, preferred_element_type=F32).astype(BF16)
        pj = jnp.einsum("std,de->ste", normed, w_full, preferred_element_type=F32).astype(BF16)

    blank = jnp.zeros((state2,), F32)
    ch = jnp.concatenate(
        [
            jnp.concatenate([own(conv_w), conv_w[wide:]]).T,
            jnp.concatenate([own(conv_b), conv_b[wide:]])[None],
            jnp.concatenate([jnp.repeat(own_heads(skip_weight), size), blank])[None],
            jnp.concatenate([own(gain_all), blank])[None],
            jnp.zeros((1, inner + state2), F32),
        ]
    )
    pre, ys, st, red = mix_forward(pj, marks, sg, hp, ch)
    if small_slice:
        rk = norms(red, wide, groups)
    else:
        totals = lax.psum(red[:, :2], "seq")
        rho = lax.rsqrt(totals[:, 0] / wide + EPSILON)
        rk = jnp.stack([rho, rho**3 * totals[:, 1] / wide] + [jnp.zeros_like(rho)] * 6, axis=1)
    pg, chacc, hacc, scaled_t, scaled = mix_backward(
        pj, marks, rk, sg, pre, ys, st, hp, ch, sel
    )
    flat_pg = pg.reshape(seqs * length, -1)
    flat_cot = cot.reshape(seqs * length, -1)
    if small_slice:
        win_grad, wo_grad, out_sum, ngrad, sums = scatter(
            turned, flat_pg, scaled_t, scaled.reshape(seqs * length, -1), flat_cot, wo, w_full,
            chacc, hacc, length, shards, groups,
        )
    else:
        product = jnp.einsum("stc,cd->std", scaled, wo, preferred_element_type=F32).astype(BF16)
        out_sum = lax.psum_scatter(product, "seq", scatter_dimension=1, tiled=True)
        product = jnp.einsum("ste,de->std", pg, w_full, preferred_element_type=F32).astype(BF16)
        ngrad = lax.psum_scatter(product, "seq", scatter_dimension=1, tiled=True)
        win_grad = jnp.einsum("std,ste->de", normed, pg, preferred_element_type=F32)
        win_grad = lax.psum_scatter(win_grad.astype(BF16), "dp", scatter_dimension=0, tiled=True)
        win_grad = lax.all_gather(win_grad, "seq", axis=0, tiled=False)
        wo_grad = jnp.dot(scaled_t, flat_cot, preferred_element_type=F32)
        wo_grad = lax.psum(wo_grad.astype(BF16), "dp").reshape(ratio, rows_out, model)
        wo_grad = lax.dynamic_index_in_dim(wo_grad, owner % ratio, 0, False)
        wo_grad = lax.psum(
            jnp.where(owner // ratio == place, wo_grad, jnp.zeros((), BF16)), "seq"
        )
        sums = jnp.concatenate(
            [
                jnp.sum(chacc, axis=1),
                jnp.pad(jnp.sum(hacc, axis=1), ((0, 0), (0, inner + state2 - 128))),
            ]
        )
        sums = lax.all_gather(lax.psum(sums, "dp"), "seq", axis=0, tiled=False)
    flat = (seqs * part, model)
    rows = [norm_all[None], sums, norm_gain[None], gated_gain[None], a_log[None]]
    (result, tokens_grad, w_in_grad, wo_grad, norm_grad, gain_grad, conv_grad, bias_grad, per_head) = (
        final(
            win_grad, w_in, wo_grad, w_out, out_sum.reshape(flat), ngrad.reshape(flat),
            tokens.reshape(flat), cotangent.reshape(flat), rows, span, mine, taps, share,
        )
    )
    return (
        result.reshape(tokens.shape),
        tokens_grad.reshape(tokens.shape),
        w_in_grad,
        wo_grad,
        conv_grad,
        bias_grad[0],
        norm_grad[0],
        gain_grad[0],
        per_head[0],
        per_head[1],
        per_head[2],
    )


def solution(mesh):
    return jax.shard_map(
        local,
        mesh=mesh,
        in_specs=(
            P("dp", "seq", None),
            P("dp", None),
            P("dp", None),
            P("dp", None),
            P("dp", None),
            P("dp"),
            P("dp"),
            P("dp"),
            P(),
            P(),
            P(),
            P("dp", "seq", None),
        ),
        out_specs=(
            P("dp", "seq", None),
            P("dp", "seq", None),
            P("dp", None),
            P("dp", None),
            P("dp", None),
            P("dp"),
            P("dp"),
            P("dp"),
            P(),
            P(),
            P(),
        ),
        check_vma=False,
    )
```

```python
import functools

import jax
import jax.numpy as jnp
from jax import lax
from jax.experimental import pallas as pl
from jax.experimental.pallas import tpu as pltpu
from jax.sharding import PartitionSpec as P

Q = 128
EXACT = lax.Precision.HIGHEST
EPSILON = 1e-05
LOG2E = 1.4426950408889634
RESET = 160.0
F32 = jnp.float32
BF16 = jnp.bfloat16
LUMPS = 6
WOFF = 1
MESH = pl.DeviceIdType.MESH


def sigmoid(x):
    return 0.5 * jnp.tanh(0.5 * x) + 0.5


def softplus(x):
    return jnp.maximum(x, 0.0) + jnp.log1p(jnp.exp(-jnp.abs(x)))


def nt(a, b):
    return lax.dot_general(a, b, (((1,), (1,)), ((), ())), preferred_element_type=F32)


def mm(a, b):
    return jnp.dot(a, b, preferred_element_type=F32)


def decays(pj, tall, hp, width):
    arg = pj[0, :, width + 256 : width + 384].astype(F32) + hp[0:1, :]
    dt = softplus(arg)
    rows = lax.broadcasted_iota(jnp.int32, (Q, Q), 0)
    lanes = lax.broadcasted_iota(jnp.int32, (Q, Q), 1)
    lower = (rows >= lanes).astype(F32)
    level = jnp.dot(lower, dt * hp[1:2, :], precision=EXACT, preferred_element_type=F32)
    level = level + tall[:, 3:4]
    return arg, dt, level, rows, lanes


def fwd_kernel(pairs, pj, marks, sg, hp, ch, pre, ys, st, red, state, tail):
    width = pairs * 256
    inner = pairs * 128
    chunk = pl.program_id(1)

    @pl.when(chunk == 0)
    def _():
        state[...] = jnp.zeros_like(state)
        tail[...] = jnp.zeros_like(tail)

    tall = jnp.concatenate([marks[0], jnp.zeros((Q - 8, Q), F32)], axis=0).T
    _, dt, level, rows, lanes = decays(pj, tall, hp, width)
    level_t = level.T
    low = lanes < 64
    masks = [tall[:, d : d + 1] for d in range(3)]

    def conv(raw, at):
        ext = jnp.concatenate([tail[:, at : at + 128], raw], axis=0)
        total = raw * ch[3:4, at : at + 128] + ch[4:5, at : at + 128]
        for d in (1, 2, 3):
            moved = pltpu.roll(ext, d, 0)[8:]
            total = total + moved * masks[d - 1] * ch[3 - d : 4 - d, at : at + 128]
        tail[:, at : at + 128] = raw[Q - 8 :]
        pre[0, :, at : at + 128] = total
        return total * sigmoid(total)

    b_rows = conv(pj[0, :, width : width + 128].astype(F32), inner)
    c_rows = conv(pj[0, :, width + 128 : width + 256].astype(F32), inner + 128)
    b_t = b_rows.T.astype(BF16)
    b_low = b_rows.astype(BF16)
    c_low = c_rows.astype(BF16)
    scores = jnp.where(rows >= lanes, nt(c_low, b_low), 0.0)
    old = state[...].astype(BF16)
    st[0, 0] = old
    carried_all = mm(c_low, old)
    squares = jnp.zeros((Q, 128), F32)
    cross = jnp.zeros((Q, 128), F32)
    for p in range(pairs):
        at = p * 128
        one = pj[0, :, p * 256 : p * 256 + 128].astype(F32)
        two = pj[0, :, p * 256 + 128 : p * 256 + 256].astype(F32)
        z = jnp.where(low, one, pltpu.roll(two, 64, 1))
        v = jnp.where(low, pltpu.roll(one, 64, 1), two)
        xc = conv(v, at)
        l0 = jnp.broadcast_to(level[:, 2 * p : 2 * p + 1], (Q, Q))
        l1 = jnp.broadcast_to(level[:, 2 * p + 1 : 2 * p + 2], (Q, Q))
        le = jnp.where(low, l0, l1)
        dte = jnp.where(low, dt[:, 2 * p : 2 * p + 1], dt[:, 2 * p + 1 : 2 * p + 2])
        u = xc * dte
        w0 = jnp.exp2(jnp.minimum(l0 - level_t[2 * p : 2 * p + 1, :], 0.0)) * scores
        w1 = jnp.exp2(jnp.minimum(l1 - level_t[2 * p + 1 : 2 * p + 2, :], 0.0)) * scores
        wide = jnp.concatenate([w0.astype(BF16), w1.astype(BF16)], axis=1)
        blocks = jnp.concatenate(
            [jnp.where(low, u, 0.0).astype(BF16), jnp.where(low, 0.0, u).astype(BF16)], axis=0
        )
        part = mm(wide, blocks) + carried_all[:, at : at + 128] * jnp.exp2(le)
        ys[0, :, at : at + 128] = part
        gated = (part + ch[5:6, at : at + 128] * xc) * (z * sigmoid(z))
        scaled = gated * ch[6:7, at : at + 128]
        squares = squares + gated * gated
        cross = cross + sg[0, :, at : at + 128].astype(F32) * scaled
        last = le[Q - 1 : Q, :]
        ul = (u * jnp.exp2(last - le)).astype(BF16)
        state[:, at : at + 128] = state[:, at : at + 128] * jnp.exp2(last) + mm(b_t, ul)
    both = jnp.where(
        lanes == 0, jnp.sum(squares, axis=1, keepdims=True), jnp.sum(cross, axis=1, keepdims=True)
    )
    red[0] = both.T[0:8]


def mix_forward(pj, marks, sg, hp, ch):
    seqs, length, total = pj.shape
    width = total - 384
    inner = width // 2
    pairs = inner // 128
    chunks = length // Q

    def row(n):
        return pl.BlockSpec((1, Q, n), lambda s, c: (s, c, 0))

    def whole(a):
        return pl.BlockSpec(a.shape, lambda s, c: (0,) * a.ndim)

    return pl.pallas_call(
        functools.partial(fwd_kernel, pairs),
        grid=(seqs, chunks),
        in_specs=[
            row(total),
            pl.BlockSpec((1, 8, Q), lambda s, c: (s, 0, c)),
            row(inner),
            whole(hp),
            whole(ch),
        ],
        out_specs=[
            row(inner + 256),
            row(inner),
            pl.BlockSpec((1, 1, 128, inner), lambda s, c: (s, c, 0, 0)),
            pl.BlockSpec((1, 8, Q), lambda s, c: (s, 0, c)),
        ],
        out_shape=[
            jax.ShapeDtypeStruct((seqs, length, inner + 256), F32),
            jax.ShapeDtypeStruct((seqs, length, inner), F32),
            jax.ShapeDtypeStruct((seqs, chunks, 128, inner), BF16),
            jax.ShapeDtypeStruct((seqs, 8, length), F32),
        ],
        scratch_shapes=[pltpu.VMEM((128, inner), F32), pltpu.VMEM((8, inner + 256), F32)],
        compiler_params=pltpu.CompilerParams(vmem_limit_bytes=60 * 2**20),
        name="mix_forward",
    )(pj, marks, sg, hp, ch)


def bwd_kernel(
    pairs, pj, marks, rk, sg, pre, ys, st, hp, ch, sel, pg, chacc, hacc, sct, scl,
    dstate, halo, edy_all, ul_all,
):
    width = pairs * 256
    inner = pairs * 128
    first = (pl.program_id(0) == 0) & (pl.program_id(1) == 0)

    @pl.when(pl.program_id(1) == 0)
    def _():
        dstate[...] = jnp.zeros_like(dstate)
        halo[...] = jnp.zeros_like(halo)

    @pl.when(first)
    def _():
        chacc[...] = jnp.zeros_like(chacc)
        hacc[...] = jnp.zeros_like(hacc)

    tall = jnp.concatenate([marks[0], rk[0], jnp.zeros((Q - 16, Q), F32)], axis=0).T
    arg, dt, level, rows, lanes = decays(pj, tall, hp, width)
    level_t = level.T
    low = lanes < 64
    masks = [tall[:, 3 + d : 4 + d] for d in (1, 2, 3)]
    rho = jnp.broadcast_to(tall[:, 8:9], (Q, 128))
    k2 = jnp.broadcast_to(tall[:, 9:10], (Q, 128))

    def fold(x):
        return jnp.sum(x.reshape(Q // 8, 8, 128), axis=0)

    def conv_back(grad, raw, at):
        ext = jnp.concatenate([grad, halo[:, at : at + 128]], axis=0)
        out = grad * ch[3:4, at : at + 128]
        chacc[3, :, at : at + 128] += fold(grad * raw)
        chacc[4, :, at : at + 128] += fold(grad)
        for d in (1, 2, 3):
            moved = pltpu.roll(ext, Q + 8 - d, 0)[:Q] * masks[d - 1]
            out = out + moved * ch[3 - d : 4 - d, at : at + 128]
            chacc[3 - d, :, at : at + 128] += fold(moved * raw)
        halo[:, at : at + 128] = grad[:8]
        return out

    pre_b = pre[0, :, inner : inner + 128]
    pre_c = pre[0, :, inner + 128 : inner + 256]
    sig_b, sig_c = sigmoid(pre_b), sigmoid(pre_c)
    b_rows, c_rows = pre_b * sig_b, pre_c * sig_c
    b_low, c_low = b_rows.astype(BF16), c_rows.astype(BF16)
    c_t = c_rows.T.astype(BF16)
    upper = lanes >= rows
    scores = jnp.where(upper, nt(b_low, c_low), 0.0)
    dlow = dstate[...].astype(BF16)
    dsb_all = mm(b_low, dlow)
    dscores = jnp.zeros((Q, Q), F32)
    sums = jnp.zeros((6 * Q, 128), F32)
    keep = jnp.zeros((8, 128), F32)
    for p in range(pairs):
        at = p * 128
        one = pj[0, :, p * 256 : p * 256 + 128].astype(F32)
        two = pj[0, :, p * 256 + 128 : p * 256 + 256].astype(F32)
        z = jnp.where(low, one, pltpu.roll(two, 64, 1))
        v = jnp.where(low, pltpu.roll(one, 64, 1), two)
        pr = pre[0, :, at : at + 128]
        sp = sigmoid(pr)
        xc = pr * sp
        l0 = jnp.broadcast_to(level[:, 2 * p : 2 * p + 1], (Q, Q))
        l1 = jnp.broadcast_to(level[:, 2 * p + 1 : 2 * p + 2], (Q, Q))
        le = jnp.where(low, l0, l1)
        dte = jnp.where(low, dt[:, 2 * p : 2 * p + 1], dt[:, 2 * p + 1 : 2 * p + 2])
        u = xc * dte
        skip = ch[5:6, at : at + 128]
        part = ys[0, :, at : at + 128]
        y = part + skip * xc
        sz = sigmoid(z)
        silz = z * sz
        gated = y * silz
        graw = sg[0, :, at : at + 128].astype(F32)
        scaled_rho = graw * rho
        scaled = gated * rho * ch[6:7, at : at + 128]
        sct[at : at + 128, :] = scaled.T.astype(BF16)
        scl[0, :, at : at + 128] = scaled.astype(BF16)
        gg = scaled_rho * ch[6:7, at : at + 128] - k2 * gated
        dy = gg * silz
        dz = gg * y * (sz + silz * (1.0 - sz))
        ulow = u.astype(BF16)
        dylow = dy.astype(BF16)
        w0 = jnp.exp2(jnp.minimum(level_t[2 * p : 2 * p + 1, :] - l0, 0.0))
        w1 = jnp.exp2(jnp.minimum(level_t[2 * p + 1 : 2 * p + 2, :] - l1, 0.0))
        wide = jnp.concatenate([(w0 * scores).astype(BF16), (w1 * scores).astype(BF16)], axis=1)
        dyb = jnp.concatenate(
            [jnp.where(low, dy, 0.0).astype(BF16), jnp.where(low, 0.0, dy).astype(BF16)], axis=0
        )
        ub = jnp.concatenate(
            [jnp.where(low, u, 0.0).astype(BF16), jnp.where(low, 0.0, u).astype(BF16)], axis=0
        )
        duw = mm(wide, dyb)
        gt = nt(ub, dylow)
        dscores = dscores + w0 * gt[:Q] + w1 * gt[Q:]
        last = le[Q - 1 : Q, :]
        lve = jnp.exp2(last - le)
        edy = (dy * jnp.exp2(le)).astype(BF16)
        ul = (u * lve).astype(BF16)
        edy_all[:, at : at + 128] = edy
        ul_all[:, at : at + 128] = ul
        dsb = dsb_all[:, at : at + 128]
        du = duw + lve * dsb
        r1 = dylow.astype(F32) * part - ulow.astype(F32) * duw
        r2 = ul.astype(F32) * dsb
        r1h, r2h = r1.astype(BF16), r2.astype(BF16)
        stacked = jnp.concatenate(
            [
                r1h,
                (r1 - r1h.astype(F32)).astype(BF16),
                r2h,
                (r2 - r2h.astype(F32)).astype(BF16),
                (dy * xc).astype(BF16),
                (du * xc).astype(BF16),
            ],
            axis=0,
        )
        sums = sums + mm(stacked, sel[p])
        decay = jnp.exp2(last)
        kept = fold(dlow[:, at : at + 128].astype(F32) * st[0, 0, :, at : at + 128].astype(F32)) * decay
        kept_high = kept.astype(BF16)
        keep = keep + mm(kept_high, sel[p]) + mm((kept - kept_high.astype(F32)).astype(BF16), sel[p])
        dstate[:, at : at + 128] = dstate[:, at : at + 128] * decay + mm(c_t, edy)
        dv = conv_back((du * dte + skip * dy) * (sp + xc * (1.0 - sp)), v, at)
        pg[0, :, p * 256 : p * 256 + 128] = jnp.where(low, dz, pltpu.roll(dv, 64, 1)).astype(BF16)
        pg[0, :, p * 256 + 128 : p * 256 + 256] = jnp.where(low, pltpu.roll(dz, 64, 1), dv).astype(BF16)
    dsc = jnp.where(upper, dscores, 0.0)
    db = mm(dsc.astype(BF16), c_low) + nt(ul_all[...], dlow)
    dc = mm(dsc.T.astype(BF16), b_low) + nt(edy_all[...], st[0, 0])
    raw_b = pj[0, :, width : width + 128].astype(F32)
    raw_c = pj[0, :, width + 128 : width + 256].astype(F32)
    pg[0, :, width : width + 128] = conv_back(
        db * (sig_b + b_rows * (1.0 - sig_b)), raw_b, inner
    ).astype(BF16)
    pg[0, :, width + 128 : width + 256] = conv_back(
        dc * (sig_c + c_rows * (1.0 - sig_c)), raw_c, inner + 128
    ).astype(BF16)
    r1 = sums[:Q] + sums[Q : 2 * Q]
    r2 = sums[2 * Q : 3 * Q] + sums[3 * Q : 4 * Q]
    da = (
        jnp.dot(upper.astype(F32), r1, precision=EXACT, preferred_element_type=F32)
        + jnp.dot((rows > lanes).astype(F32), r2, precision=EXACT, preferred_element_type=F32)
        + jnp.sum(keep, axis=0, keepdims=True)
    )
    ddt = da * hp[2:3, :] + sums[5 * Q :]
    ds = ddt * sigmoid(arg)
    pg[0, :, width + 256 : width + 384] = ds.astype(BF16)
    hacc[0] += fold(ds)
    hacc[1] += fold(da * dt)
    hacc[2] += fold(sums[4 * Q : 5 * Q])


def mix_backward(pj, marks, rk, sg, pre, ys, st, hp, ch, sel):
    seqs, length, total = pj.shape
    width = total - 384
    inner = width // 2
    pairs = inner // 128
    chunks = length // Q

    def row(n):
        return pl.BlockSpec((1, Q, n), lambda s, c: (s, chunks - 1 - c, 0))

    def whole(shape):
        return pl.BlockSpec(shape, lambda s, c: (0,) * len(shape))

    return pl.pallas_call(
        functools.partial(bwd_kernel, pairs),
        grid=(seqs, chunks),
        in_specs=[
            row(total),
            pl.BlockSpec((1, 8, Q), lambda s, c: (s, 0, chunks - 1 - c)),
            pl.BlockSpec((1, 8, Q), lambda s, c: (s, 0, chunks - 1 - c)),
            row(inner),
            row(inner + 256),
            row(inner),
            pl.BlockSpec((1, 1, 128, inner), lambda s, c: (s, chunks - 1 - c, 0, 0)),
            whole(hp.shape),
            whole(ch.shape),
            whole(sel.shape),
        ],
        out_specs=[
            row(total),
            whole((5, 8, inner + 256)),
            whole((3, 8, 128)),
            pl.BlockSpec((inner, Q), lambda s, c: (0, s * chunks + chunks - 1 - c)),
            row(inner),
        ],
        out_shape=[
            jax.ShapeDtypeStruct((seqs, length, total), BF16),
            jax.ShapeDtypeStruct((5, 8, inner + 256), F32),
            jax.ShapeDtypeStruct((3, 8, 128), F32),
            jax.ShapeDtypeStruct((inner, seqs * length), BF16),
            jax.ShapeDtypeStruct((seqs, length, inner), BF16),
        ],
        scratch_shapes=[
            pltpu.VMEM((128, inner), F32),
            pltpu.VMEM((8, inner + 256), F32),
            pltpu.VMEM((Q, inner), BF16),
            pltpu.VMEM((Q, inner), BF16),
        ],
        compiler_params=pltpu.CompilerParams(vmem_limit_bytes=60 * 2**20),
        name="mix_backward",
    )(pj, marks, rk, sg, pre, ys, st, hp, ch, sel)


def prep_kernel(mine, at, seg, heads, cols, marks, hp, sel, steps):
    lane8 = lax.broadcasted_iota(jnp.int32, (8, 128), 1)
    shift = 128 - lax.axis_index("seq") * mine
    own = jnp.where(lane8 < mine, pltpu.roll(heads[...], shift, 1), 0.0)
    rate = jnp.where(lane8 < mine, -jnp.exp(own), 0.0)[1:2, :]
    hp[...] = jnp.concatenate([own[0:1, :], rate * LOG2E, rate, jnp.zeros((5, 128), F32)], axis=0)
    last = cols[:, at:].astype(F32)
    last = jnp.concatenate(
        [last, jnp.zeros((last.shape[0], 128 - last.shape[1]), F32)], axis=1
    )
    lane = lax.broadcasted_iota(jnp.int32, last.shape, 1)
    moved = pltpu.roll(last, shift, 1)
    steps[...] = jnp.where(lane < mine, moved, 0.0).astype(BF16)
    lane = lax.broadcasted_iota(jnp.int32, (128, 128), 0)
    out = lax.broadcasted_iota(jnp.int32, (128, 128), 1)
    for p in range(sel.shape[0]):
        sel[p] = jnp.where(out == 2 * p + lane // 64, 1.0, 0.0).astype(BF16)
    seqs, length = seg.shape
    ids = seg[...].astype(F32)
    lane = lax.broadcasted_iota(jnp.int32, (seqs, length), 1)
    back = [
        jnp.where((pltpu.roll(ids, d, 1) == ids) & (lane >= d), 1.0, 0.0) for d in (1, 2, 3)
    ]
    ahead = [
        jnp.where((pltpu.roll(ids, length - d, 1) == ids) & (lane < length - d), 1.0, 0.0)
        for d in (1, 2, 3)
    ]
    before = [ids[:, 0:1]] + [ids[:, at - 1 : at] for at in range(Q, length, Q)]
    level = jnp.concatenate(
        [-RESET * (ids[:, n * Q : (n + 1) * Q] - b) for n, b in enumerate(before)], axis=1
    )
    all_rows = [*back, level, *ahead, jnp.zeros((seqs, length), F32)]
    for n in range(seqs):
        marks[n] = jnp.concatenate([r[n : n + 1, :] for r in all_rows], axis=0)


def prepare(seg, heads, w_in, mine, at):
    rows = w_in.shape[0]
    pairs = mine // 2
    shapes = [
        ((seg.shape[0], 8, seg.shape[1]), F32), ((8, 128), F32), ((pairs, 128, 128), BF16),
        ((rows, 128), BF16),
    ]

    def whole(shape):
        return pl.BlockSpec(shape, lambda i: (0,) * len(shape))

    return pl.pallas_call(
        functools.partial(prep_kernel, mine, at),
        grid=(1,),
        in_specs=[
            whole(seg.shape),
            whole(heads.shape),
            whole(w_in.shape),
        ],
        out_specs=[whole(n) for n, _ in shapes],
        out_shape=[jax.ShapeDtypeStruct(*n) for n in shapes],
        name="prepare",
    )(seg, heads, w_in)


def norm_kernel(wide, red, rk, got, ssem, rsem):
    d = lax.axis_index("dp")
    s = lax.axis_index("seq")
    groups = got.shape[0]
    bar = pltpu.get_barrier_semaphore()
    for j in range(1, groups):
        pl.semaphore_signal(bar, inc=1, device_id=(d, lax.rem(s + j, groups)), device_id_type=MESH)
    pl.semaphore_wait(bar, groups - 1)
    sends = [
        pltpu.make_async_remote_copy(
            src_ref=red, dst_ref=got.at[j], send_sem=ssem.at[j], recv_sem=rsem.at[j],
            device_id=(d, lax.rem(s + j, groups)), device_id_type=MESH,
        )
        for j in range(1, groups)
    ]
    for copy in sends:
        copy.start()
    total = red[...]
    for j, copy in enumerate(sends):
        copy.wait()
        total = total + got[j + 1]
    rho = lax.rsqrt(total[:, 0:1] / wide + EPSILON)
    rk[...] = jnp.concatenate(
        [rho, rho * rho * rho * total[:, 1:2] / wide, jnp.zeros_like(total[:, 2:])], axis=1
    )


def norms(red, wide, groups):
    vmem = pl.BlockSpec(memory_space=pltpu.VMEM)
    return pl.pallas_call(
        functools.partial(norm_kernel, wide),
        in_specs=[vmem],
        out_specs=vmem,
        out_shape=jax.ShapeDtypeStruct(red.shape, F32),
        scratch_shapes=[
            pltpu.VMEM((groups, *red.shape), F32),
            pltpu.SemaphoreType.DMA((groups,)),
            pltpu.SemaphoreType.DMA((groups,)),
        ],
        compiler_params=pltpu.CompilerParams(collective_id=3, has_side_effects=True),
        name="norms",
    )(red)


def final_kernel(
    groups, span, mine, gw, w_in, wog, w_out, osum, ngrad, tok, cot, gains, sums, nrow, grow, log,
    res, tgrad, wig, wgr, nout, gout, cout, bout, hout0, hout1, hout2, nsum, gsum,
):
    step = pl.program_id(0)

    @pl.when(step == 0)
    def _():
        inner = span // 2
        shared = sums[0, :, inner:]
        heads = sums[0, :, :128]
        for g in range(1, groups):
            shared = shared + sums[g, :, inner:]
            heads = heads + pltpu.roll(sums[g, :, :128], g * mine, 1)
        row = jnp.concatenate([*[sums[g, :, :inner] for g in range(groups)], shared], axis=1)
        share, taps = cout.shape
        first = lax.axis_index("dp") * share
        tall = -(-share // 128) * 128
        own = pltpu.roll(row, row.shape[1] - first, 1)[:, :tall]
        cout[...] = own.T[:share, :taps]
        bout[...] = own[taps, :share]
        count = groups * mine
        hout0[...] = heads[taps + 1, :count]
        hout1[...] = -jnp.exp(log[...]) * heads[taps + 2, :count]
        hout2[...] = heads[taps + 3, :count]

    total = jnp.zeros((w_in.shape[0], 1), F32)
    for g in range(groups):
        here = slice(g * span, (g + 1) * span)
        grad = gw[g, :, :span].astype(F32)
        wig[:, here] = grad
        total = total + jnp.sum(grad * w_in[:, here].astype(F32), axis=1, keepdims=True)
    at = groups * span
    width = gw.shape[2] - 128
    shared = gw[0, :, span:width].astype(F32)
    steps = gw[0, :, width:].astype(F32)
    for g in range(1, groups):
        shared = shared + gw[g, :, span:width].astype(F32)
        steps = steps + pltpu.roll(gw[g, :, width:].astype(F32), g * mine, 1)
    mid = at + width - span
    wig[:, at:mid] = shared
    wig[:, mid:] = steps[:, : groups * mine]
    total = total + jnp.sum(shared * w_in[:, at:mid].astype(F32), axis=1, keepdims=True)
    total = total + jnp.sum(
        steps[:, : groups * mine] * w_in[:, mid:].astype(F32), axis=1, keepdims=True
    )
    tall = w_in.shape[0]
    nsum[pl.ds(pl.multiple_of(step * tall, 16), tall), :] = jnp.broadcast_to(total, (tall, 128))
    grad = wog[...].astype(F32)
    wgr[...] = grad
    tall = wog.shape[0]
    gsum[pl.ds(pl.multiple_of(step * tall, 16), tall), :] = jnp.broadcast_to(
        jnp.sum(grad * w_out[...].astype(F32), axis=1, keepdims=True), (tall, 128)
    )

    @pl.when(step == pl.num_programs(0) - 1)
    def _():
        nout[...] = nsum[...].T[0, : nout.shape[0]] / nrow[...].astype(F32)
        gout[...] = gsum[...].T[0, : gout.shape[0]] / grow[...].astype(F32)

    x = tok[...].astype(F32)
    res[...] = (x + osum[...].astype(F32)).astype(BF16)
    inverse = lax.rsqrt(jnp.mean(x * x, axis=1, keepdims=True) + EPSILON)
    unit = x * inverse
    grad = ngrad[...].astype(F32) * gains[0:1, :]
    tgrad[...] = cot[...].astype(F32) + inverse * (
        grad - unit * jnp.mean(grad * unit, axis=1, keepdims=True)
    )


def final(gw, w_in, wog, w_out, osum, ngrad, tok, cot, rows, span, mine, taps, share):
    groups, count, total = gw.shape
    steps = next(n for n in (4, 2, 1) if count % (16 * n) == 0)

    def part(a):
        return pl.BlockSpec((a.shape[0] // steps, a.shape[1]), lambda i: (i, 0))

    def whole(a):
        return pl.BlockSpec(a.shape, lambda i: (0,) * len(a.shape))

    def up(n):
        return -(-n // 128) * 128

    tall = [w_in, wog, w_out, osum, ngrad, tok, cot]
    big = [(tok.shape, BF16), (tok.shape, F32), (w_in.shape, F32), (wog.shape, F32)]
    little = [(count,), (wog.shape[0],), (share, taps), (share,), *[(groups * mine,)] * 3]
    outs = [jax.ShapeDtypeStruct(*n) for n in big]
    extra = [jax.ShapeDtypeStruct(n, F32) for n in little]
    return pl.pallas_call(
        functools.partial(final_kernel, groups, span, mine),
        grid=(steps,),
        in_specs=[
            pl.BlockSpec((groups, count // steps, total), lambda i: (0, i, 0)),
            *[part(a) for a in tall],
            *[whole(a) for a in rows],
        ],
        out_specs=[*[part(o) for o in outs], *[whole(o) for o in extra]],
        out_shape=[*outs, *extra],
        scratch_shapes=[
            pltpu.VMEM((up(count), 128), F32),
            pltpu.VMEM((up(wog.shape[0]), 128), F32),
        ],
        compiler_params=pltpu.CompilerParams(vmem_limit_bytes=60 * 2**20),
        name="final",
    )(gw, *tall, *rows)


def gather_kernel(
    dims, w_in, dt_in, wo_in, small_in, tok_in, cot_in,
    turned_o, cot_o, pj_o, sg_o, w_o, wo_o, small_o,
    tok, cot, wbig, wo, small, pjv, sgv, turned,
    szu, szd, rz, sy, ry, wsu, wsd, wrz, wsy, wry, bx_s, bx_r, bc_s, bc_r, bs, br, loc, out,
):
    deep, pieces, rows, inner, part, length, groups = dims
    d = lax.axis_index("dp")
    s = lax.axis_index("seq")
    z = d // 2
    y = d % 2
    core = s % 2
    top = deep - 1
    up, down, side = (d + 2, s), (d - 2, s), (d + 1 - 2 * y, s)
    across, twin = (d, s + 2 - 4 * (s // 2)), (d, s + 1 - 2 * (s % 2))
    opposite = across[1]

    bar = pltpu.get_barrier_semaphore()

    @pl.when(z < top)
    def _():
        pl.semaphore_signal(bar, inc=1, device_id=up, device_id_type=MESH)

    @pl.when(z > 0)
    def _():
        pl.semaphore_signal(bar, inc=1, device_id=down, device_id_type=MESH)

    for who in (side, across, twin):
        pl.semaphore_signal(bar, inc=1, device_id=who, device_id_type=MESH)
    pl.semaphore_wait(bar, 3 + jnp.minimum(z, 1) + jnp.minimum(top - z, 1))

    def send(src, dst, ssem, rsem, who):
        return pltpu.make_async_remote_copy(
            src_ref=src, dst_ref=dst, send_sem=ssem, recv_sem=rsem,
            device_id=who, device_id_type=MESH,
        )

    width = 2 * inner

    def cols(k):
        return pl.ds(width + 256, 128) if k == 1 else pl.ds(width if k == 2 else (k - 3) * 256, 256)

    def held(k, owner):
        if k == 0:
            return small.at[owner]
        if k == 2:
            return shared(owner, core)
        return wbig.at[pl.ds(pl.multiple_of(owner * rows, 16), rows), cols(k)]

    def shared(owner, half):
        at = pl.multiple_of(owner * rows + half * (rows // 2), 16)
        return wbig.at[pl.ds(at, rows // 2), pl.ds(width, 256)]

    def shared_send(owner, half):
        ref = shared(owner, half)
        return send(ref, ref, bs.at[owner], br.at[owner], twin)

    def share_columns():
        for e in range(2 * deep):
            @pl.when(d != e)
            def _():
                shared_send(e, core).start()

        for e in range(2 * deep):
            @pl.when(d != e)
            def _():
                shared_send(e, 1 - core).wait_recv()

    def source(k):
        if k == 0:
            return small_in.at[...]
        if k == 1:
            return dt_in.at[...]
        if k == 2:
            at = pl.multiple_of(core * (rows // 2), 16)
            return w_in.at[pl.ds(at, rows // 2), pl.ds(width * groups, 256)]
        return w_in.at[:, pl.ds(pl.multiple_of(s * width + (k - 3) * 256, 128), 256)]

    def own_send(k):
        src, dst = source(k), held(k, d)

        @pl.when(z < top)
        def _():
            send(src, dst, szu.at[k, z], rz.at[k, z], up).start()

        @pl.when(z > 0)
        def _():
            send(src, dst, szd.at[k, z], rz.at[k, z], down).start()

        send(src, dst, sy.at[k, z], ry.at[k, z], side).start()

    def hop(k, h):
        below, above = z - h, z + h

        @pl.when(below >= 0)
        def _():
            ref = held(k, below * 2 + y)
            send(ref, ref, szu.at[k, below], rz.at[k, below], up).wait_recv()

            @pl.when(z < top)
            def _():
                send(ref, ref, szu.at[k, below], rz.at[k, below], up).start()

            send(ref, ref, sy.at[k, below], ry.at[k, below], side).start()

        @pl.when(above <= top)
        def _():
            ref = held(k, above * 2 + y)
            send(ref, ref, szd.at[k, above], rz.at[k, above], down).wait_recv()

            @pl.when(z > 0)
            def _():
                send(ref, ref, szd.at[k, above], rz.at[k, above], down).start()

            send(ref, ref, sy.at[k, above], ry.at[k, above], side).start()

    def arrive(k):
        for e in range(deep):
            ref = held(k, e * 2 + 1 - y)
            send(ref, ref, sy.at[k, e], ry.at[k, e], side).wait_recv()

    def own_copy(src, dst, sem):
        return pltpu.make_async_copy(src, dst, sem)

    here = pl.multiple_of(s * part, 16)
    there = pl.multiple_of(opposite * part, 16)
    locals_ = [
        own_copy(small_in, small.at[d], loc.at[0]),
        own_copy(
            w_in.at[:, pl.ds(pl.multiple_of(s * width, 128), width)],
            wbig.at[pl.ds(pl.multiple_of(d * rows, 16), rows), pl.ds(0, width)],
            loc.at[1],
        ),
    ]
    for q in range(2):
        locals_.append(own_copy(tok_in.at[q], tok.at[q, pl.ds(here, part)], loc.at[2 + q]))
        locals_.append(own_copy(cot_in.at[q], cot.at[q, pl.ds(here, part)], loc.at[4 + q]))
    locals_.append(own_copy(source(1), held(1, d), loc.at[7]))
    locals_.append(
        own_copy(
            w_in.at[:, pl.ds(width * groups, 256)],
            wbig.at[pl.ds(pl.multiple_of(d * rows, 16), rows), pl.ds(width, 256)],
            loc.at[8],
        )
    )
    half = wo_in.shape[0]
    mine = z == s

    def root_copy():
        return own_copy(wo_in, wo.at[pl.ds(pl.multiple_of(y * half, 16), half)], loc.at[6])

    def block_sends(which, src, dst, q):
        spot = dst.at[q, pl.ds(here, part)]
        i = which * 2 + q
        send(src.at[q], spot, bx_s.at[i], bx_r.at[i], across).start()
        send(src.at[q], spot, bc_s.at[0, i], bc_r.at[0, i], twin).start()

    def block_forward(which, dst, q):
        spot = dst.at[q, pl.ds(there, part)]
        i = which * 2 + q
        send(spot, spot, bx_s.at[i], bx_r.at[i], across).wait_recv()
        send(spot, spot, bc_s.at[1, i], bc_r.at[1, i], twin).start()

    def block_arrive(which, dst, q):
        i = which * 2 + q
        for n in range(2):
            spot = dst.at[q, pl.ds(here, part)]
            send(spot, spot, bc_s.at[n, i], bc_r.at[n, i], twin).wait_recv()

    lump = half // LUMPS

    def wo_piece(i, col):
        m = col * LUMPS + i
        return m, wo.at[pl.ds(pl.multiple_of(m * lump, 16), lump)]

    def wo_send(i, src=None):
        m, ref = wo_piece(i, y)
        src = ref if src is None else src

        @pl.when((z >= s) & (z < top))
        def _():
            send(src, ref, wsu.at[m], wrz.at[m], up).start()

        @pl.when((z <= s) & (z > 0))
        def _():
            send(src, ref, wsd.at[m], wrz.at[m], down).start()

        send(src, ref, wsy.at[m], wry.at[m], side).start()

    def wo_root(i):
        @pl.when(mine)
        def _():
            wo_send(i, wo_in.at[pl.ds(i * lump, lump)])

    def wo_hop(i, h):
        @pl.when((z - s == h) | (s - z == h))
        def _():
            m, ref = wo_piece(i, y)
            send(ref, ref, wsu.at[m], wrz.at[m], up).wait_recv()
            wo_send(i)

    def wo_arrive(i):
        m, ref = wo_piece(i, 1 - y)
        send(ref, ref, wsy.at[m], wry.at[m], side).wait_recv()

    tile = 256
    long = 512

    def project(k):
        c = pl.ds(width, 384) if k == 2 else cols(k)

        def step(i, _):
            q, r = i // (length // long), i % (length // long)
            at = pl.ds(pl.multiple_of(r * long, long), long)
            pjv[q, at, c] = mm(tok[q, at, :], wbig[:, c]).astype(BF16)
            return 0

        lax.fori_loop(0, 2 * length // long, step, 0)
        own_copy(pjv.at[:, :, c], pj_o.at[:, :, c], out.at[k]).start()

    for c in locals_:
        c.start()

    @pl.when(mine)
    def _():
        root_copy().start()

    for q in range(2):
        block_sends(0, tok_in, tok, q)
    for q in range(2):
        block_sends(1, cot_in, cot, q)
    ahead = 3
    for k in range(ahead):
        own_send(k)
    done = []

    def hops(t):
        for h in range(1, deep):
            if 0 <= t - h < pieces:
                hop(t - h, h)
        for h in range(1, deep):
            if 0 <= t - h - WOFF < LUMPS:
                wo_hop(t - h - WOFF, h)
        if 0 <= t - WOFF < LUMPS:
            wo_root(t - WOFF)
        if ahead <= t + ahead - 1 < pieces:
            own_send(t + ahead - 1)

    steps = max(pieces, WOFF + LUMPS) + deep - 1
    count = dict(next=1)

    def ready(n):
        for _ in range(n):
            if count["next"] < pieces:
                arrive(count["next"])
                if count["next"] == 2:
                    share_columns()
                if count["next"] > 1:
                    project(count["next"])
                count["next"] += 1

    share = tok.shape[2] // (2 * deep)

    def norm_step(i, _):
        q, r = i // (length // 64), i % (length // 64)
        at = pl.multiple_of(r * 64, 64)
        x = tok[q, pl.ds(at, 64), :].astype(F32)
        inv = lax.rsqrt(jnp.mean(x * x, axis=1, keepdims=True) + EPSILON)
        gains = jnp.concatenate([small[e, 0:1, :share] for e in range(2 * deep)], axis=1)
        tok[q, pl.ds(at, 64), :] = (x * inv * gains.astype(F32)).astype(BF16)
        return 0

    def turn_step(i, _):
        q, r = i // (length // tile), i % (length // tile)
        at = pl.multiple_of(r * tile, tile)
        to = pl.multiple_of(i * tile, tile)
        for j in range(0, tok.shape[2], 128):
            turned[j : j + 128, pl.ds(to, tile)] = tok[q, pl.ds(at, tile), j : j + 128].T
        return 0

    def grad_step(i, _):
        q, r = i // (length // long), i % (length // long)
        at = pl.ds(pl.multiple_of(r * long, long), long)
        sgv[q, at, :] = nt(cot[q, at, :], wo[...]).astype(BF16)
        return 0

    for t in range(1, steps):
        hops(t)
        if t == 3:
            block_forward(0, tok, 0)
        if t == 6:
            block_forward(0, tok, 1)
        if t == 7:
            for i in (0, 1, 2, 4, 6, 7):
                locals_[i].wait()
            block_arrive(0, tok, 0)
            block_arrive(0, tok, 1)
            for q in range(2):
                spot = tok.at[q, pl.ds(there, part)]
                send(spot, spot, bc_s.at[1, q], bc_r.at[1, q], twin).wait_send()
            arrive(0)
            own_copy(small, small_o, out.at[0]).start()
            lax.fori_loop(0, 2 * length // 64, norm_step, 0)
            lax.fori_loop(0, 2 * length // tile, turn_step, 0)
            own_copy(turned, turned_o, out.at[pieces]).start()
        if t == 10:
            block_forward(1, cot, 0)
        if t == 11:
            block_forward(1, cot, 1)
        if t > 7:
            ready(2 if t == 8 else 1)

    @pl.when(mine)
    def _():
        root_copy().wait()

    locals_[3].wait()
    locals_[5].wait()
    for i in range(LUMPS):
        wo_arrive(i)
    own_copy(wo, wo_o, out.at[pieces + 2]).start()
    block_arrive(1, cot, 0)
    block_arrive(1, cot, 1)
    own_copy(cot, cot_o, out.at[pieces + 3]).start()
    lax.fori_loop(0, 2 * length // long, grad_step, 0)
    own_copy(sgv, sg_o, out.at[pieces + 4]).start()
    ready(pieces)
    own_copy(wbig, w_o, out.at[pieces + 1]).start()
    for k in range(pieces):
        for e in range(deep):
            ref = held(k, e * 2 + y)

            @pl.when((z >= e) & (z < top))
            def _():
                send(ref, ref, szu.at[k, e], rz.at[k, e], up).wait_send()

            @pl.when((z <= e) & (z > 0))
            def _():
                send(ref, ref, szd.at[k, e], rz.at[k, e], down).wait_send()

            send(ref, ref, sy.at[k, e], ry.at[k, e], side).wait_send()
    for e in range(2 * deep):
        @pl.when(d != e)
        def _():
            shared_send(e, core).wait_send()

    for i in range(LUMPS):
        m, ref = wo_piece(i, y)

        @pl.when((z >= s) & (z < top))
        def _():
            send(ref, ref, wsu.at[m], wrz.at[m], up).wait_send()

        @pl.when((z <= s) & (z > 0))
        def _():
            send(ref, ref, wsd.at[m], wrz.at[m], down).wait_send()

        send(ref, ref, wsy.at[m], wry.at[m], side).wait_send()
    for which, dst in ((0, tok), (1, cot)):
        for q in range(2):
            i = which * 2 + q
            spot = dst.at[q, pl.ds(here, part)]
            send(spot, spot, bx_s.at[i], bx_r.at[i], across).wait_send()
            for n in range(1 + which):
                send(spot, spot, bc_s.at[n, i], bc_r.at[n, i], twin).wait_send()
    own_copy(small, small_o, out.at[0]).wait()
    for k in range(2, pieces):
        c = pl.ds(width, 384) if k == 2 else cols(k)
        own_copy(pjv.at[:, :, c], pj_o.at[:, :, c], out.at[k]).wait()
    own_copy(turned, turned_o, out.at[pieces]).wait()
    own_copy(wbig, w_o, out.at[pieces + 1]).wait()
    own_copy(wo, wo_o, out.at[pieces + 2]).wait()
    own_copy(cot, cot_o, out.at[pieces + 3]).wait()
    own_copy(sgv, sg_o, out.at[pieces + 4]).wait()


def gather(w_in, dt_in, w_out, small, tokens, cotangent, inner, shards, groups):
    rows = w_in.shape[0]
    total = 2 * inner + 384
    seqs, part, model = tokens.shape
    length = part * groups
    deep = shards // 2
    pieces = inner // 128 + 3
    any_ = pl.BlockSpec(memory_space=pl.ANY)
    dma = pltpu.SemaphoreType.DMA
    small_rows, small_cols = small.shape
    full = (shards * rows, total)
    shapes = [
        (model, seqs * length), (seqs, length, model), (seqs, length, total), (seqs, length, inner),
        full, (inner, model), (shards, small_rows, small_cols),
    ]
    return pl.pallas_call(
        functools.partial(gather_kernel, (deep, pieces, rows, inner, part, length, groups)),
        in_specs=[any_] * 6,
        out_specs=[any_] * 7,
        out_shape=[jax.ShapeDtypeStruct(n, BF16) for n in shapes],
        scratch_shapes=[
            pltpu.VMEM(shapes[1], BF16),
            pltpu.VMEM(shapes[1], BF16),
            pltpu.VMEM(full, BF16),
            pltpu.VMEM((inner, model), BF16),
            pltpu.VMEM(shapes[6], BF16),
            pltpu.VMEM(shapes[2], BF16),
            pltpu.VMEM(shapes[3], BF16),
            pltpu.VMEM(shapes[0], BF16),
            dma((pieces, deep)), dma((pieces, deep)), dma((pieces, deep)),
            dma((pieces, deep)), dma((pieces, deep)),
            *[dma((2 * LUMPS,))] * 5,
            dma((4,)), dma((4,)), dma((2, 4)), dma((2, 4)),
            dma((2 * deep,)), dma((2 * deep,)),
            dma((9,)), dma((pieces + 5,)),
        ],
        compiler_params=pltpu.CompilerParams(
            collective_id=1, has_side_effects=True, vmem_limit_bytes=56 * 2**20
        ),
        name="gather_project",
    )(w_in, dt_in, w_out, small, tokens, cotangent)


def greet(z, y, s, deep, others):
    bar = pltpu.get_barrier_semaphore()
    for e in range(deep):
        @pl.when(z != e)
        def _():
            pl.semaphore_signal(bar, inc=1, device_id=(2 * e + y, s), device_id_type=MESH)

    for who in others:
        pl.semaphore_signal(bar, inc=1, device_id=who, device_id_type=MESH)
    pl.semaphore_wait(bar, len(others) + deep - 1)


def send(src, dst, ssem, rsem, who):
    return pltpu.make_async_remote_copy(
        src_ref=src, dst_ref=dst, send_sem=ssem, recv_sem=rsem, device_id=who, device_id_type=MESH
    )


def add_into(dst, src):
    count = dst.shape[0]
    some = next(n for n in (64, 48, 32, 16) if count % n == 0)

    def step(i, _):
        at = pl.ds(pl.multiple_of(i * some, 16), some)
        dst[at, :] = (dst[at, :].astype(F32) + src[at, :].astype(F32)).astype(BF16)
        return 0

    lax.fori_loop(0, count // some, step, 0)


CUTS = ((0, 512), (512, 512), (1536, 384), (1024, 256), (1280, 128), (1408, 128))
PARTS = len(CUTS)


def scatter_kernel(
    dims, nt_in, pg_in, st_in, sc_in, cot_in, wo_in, wi_in, ch_in, he_in,
    gw_o, wo_o, out_o, ng_o, sm_o,
    nt_v, pg_v, st_v, sc_v, wo_v, cw, pv, yb, zb, tw, xr, stage, gw, ybw, zbw, ch_v, he_v,
    vec, vgot, vall,
    sy, ry, su, sd, rz, gx_s, gx_r, gc_s, gc_r, tw_s, tw_r, xr_s, xr_r,
    wy_s, wy_r, wu_s, wd_s, wz_r, bx_s, bx_r, bc_s, bc_r, v_s, v_r, loc, out,
):
    deep, rows, part, length = dims
    d = lax.axis_index("dp")
    s = lax.axis_index("seq")
    z = d // 2
    y = d % 2
    x = s // 2
    c = s % 2
    top = deep - 1
    model = wi_in.shape[0]
    up, down, side = (d + 2, s), (d - 2, s), (d + 1 - 2 * y, s)
    across, twin = (d, s + 2 - 4 * x), (d, s + 1 - 2 * c)
    greet(z, y, s, deep, (side, across, twin))

    def cut(k):
        return pl.ds(*CUTS[k])

    def lines(ref, i, count=rows):
        return ref.at[pl.ds(pl.multiple_of(i * count, 16), count)]

    cot_v = cw.at[:, pl.ds(0, model)]
    wi_v = cw.at[pl.ds(0, model), :]
    loads = dict(
        ch=pltpu.make_async_copy(ch_in, ch_v, loc.at[2]),
        he=pltpu.make_async_copy(he_in, he_v, loc.at[3]),
        st=pltpu.make_async_copy(st_in, st_v, loc.at[0]),
        cot=pltpu.make_async_copy(cot_in, cot_v, loc.at[1]),
        sc=pltpu.make_async_copy(sc_in, sc_v, loc.at[6]),
        wo=pltpu.make_async_copy(wo_in, wo_v, loc.at[7]),
        nt=pltpu.make_async_copy(nt_in, nt_v, loc.at[4]),
        pg=pltpu.make_async_copy(pg_in, pg_v, loc.at[5]),
    )
    for load in loads.values():
        load.start()
    load_wi = pltpu.make_async_copy(wi_in, wi_v, loc.at[8])

    def v_send(n, src, dst, who):
        return send(src, dst, v_s.at[n], v_r.at[n], who)

    def v_y():
        return v_send(0, vec, vgot.at[deep], side)

    def v_z(e):
        return send(vec, vgot.at[z], v_s.at[1 + e], v_r.at[1 + z], (2 * e + y, s))

    def v_from(e):
        return send(vec, vgot.at[e], v_s.at[1 + e], v_r.at[1 + e], (2 * e + y, s))

    def v_seq(n, owner, who):
        return v_send(1 + deep + n, vall.at[owner], vall.at[owner], who)

    def v_start():
        vec[...] = jnp.concatenate(
            [
                jnp.sum(ch_v[...], axis=1),
                jnp.concatenate(
                    [jnp.sum(he_v[...], axis=1), jnp.zeros((3, vec.shape[1] - 128), F32)], axis=1
                ),
            ],
            axis=0,
        )
        v_y().start()

    def v_sum():
        v_y().wait()
        vec[...] = vec[...] + vgot[deep]
        for e in range(deep):
            @pl.when(z != e)
            def _():
                v_z(e).start()

    def v_total():
        for e in range(deep):
            @pl.when(z != e)
            def _():
                v_z(e).wait_send()
                v_from(e).wait_recv()

            @pl.when(z == e)
            def _():
                vgot[e] = vec[...]

        total = vgot[0]
        for e in range(1, deep):
            total = total + vgot[e]
        vall[s] = total
        v_seq(0, s, across).start()
        v_seq(1, s, twin).start()

    def v_spread():
        v_seq(0, across[1], across).wait_recv()
        v_seq(2, across[1], twin).start()

    both = ((0, out_o), (1, ng_o))

    def twin_send(n, turn, q):
        return send(stage.at[q], tw.at[n, turn, q], tw_s.at[q], tw_r.at[n, turn, q], twin)

    def product(n, q, owner, j):
        at = pl.ds(pl.multiple_of(q * length + owner * part, 16), part)
        if n == 0:
            return mm(sc_v[at, :], wo_v[:, j : j + 512])
        return nt(pg_v[at, :], cw[j : j + 512, :])

    def exchange(n, turn):
        half = 1 - x if turn == 0 else x
        for q in range(2):
            if (n, turn) != (0, 0):
                twin_send(n, turn, q).wait_send()
            for j in range(0, model, 512):
                stage[q, :, j : j + 512] = product(n, q, 2 * half + 1 - c, j).astype(BF16)
            twin_send(n, turn, q).start()
        for q in range(2):
            twin_send(n, turn, q).wait_recv()
            for j in range(0, model, 512):
                tw[n, turn, q, :, j : j + 512] = (
                    tw[n, turn, q, :, j : j + 512].astype(F32) + product(n, q, 2 * half + c, j)
                ).astype(BF16)
            if turn == 0:
                x_send(n, q).start()

    def x_send(n, q):
        return send(tw.at[n, 0, q], xr.at[n, q], xr_s.at[n, q], xr_r.at[n, q], across)

    def x_finish(n, dst):
        for q in range(2):
            x_send(n, q).wait_recv()
            add_into(xr.at[n, q], tw.at[n, 1, q])
            pltpu.make_async_copy(xr.at[n, q], dst.at[q], out.at[2 + 2 * n + q]).start()

    def weigh(k):
        tall = 2 * rows

        def step(i, _):
            at = pl.ds(pl.multiple_of(i * tall, 16), tall)
            pv[at, cut(k)] = mm(nt_v[at, :], pg_v[:, cut(k)]).astype(BF16)
            return 0

        lax.fori_loop(0, deep, step, 0)

    def block(e, k):
        return pv.at[pl.ds(pl.multiple_of((2 * e + y) * rows, 16), rows), cut(k)]

    def y_send(k, e):
        src = pv.at[pl.ds(pl.multiple_of((2 * e + 1 - y) * rows, 16), rows), cut(k)]
        return send(src, lines(yb, e).at[:, cut(k)], sy.at[k, e], ry.at[k, e], side)

    def y_start(k):
        for e in range(deep):
            y_send(k, e).start()

    def y_add(k):
        for e in range(deep):
            y_send(k, e).wait_recv()
            add_into(block(e, k), lines(yb, e).at[:, cut(k)])

    def z_send(k, e, slot, sem, who):
        return send(block(e, k), lines(zb, slot).at[:, cut(k)], sem.at[k, e], rz.at[k, slot], who)

    def hop(k, h):
        @pl.when(z == h - 1)
        def _():
            for e in range(top, h - 1, -1):
                if h > 1:
                    z_send(k, e, e, su, up).wait_recv()
                    add_into(block(e, k), lines(zb, e).at[:, cut(k)])
                z_send(k, e, e, su, up).start()

        @pl.when(z == deep - h)
        def _():
            for e in range(deep - h):
                if h > 1:
                    z_send(k, e, e, sd, down).wait_recv()
                    add_into(block(e, k), lines(zb, e).at[:, cut(k)])
                z_send(k, e, deep if e == deep - h - 1 else e, sd, down).start()

    def g_spot(who, k):
        return gw_o.at[who, :, cut(k)]

    def finish(k):
        mine = block(z, k)

        @pl.when(z > 0)
        def _():
            z_send(k, z, z, su, up).wait_recv()
            add_into(mine, lines(zb, z).at[:, cut(k)])

        @pl.when(z < top)
        def _():
            z_send(k, z, deep, sd, down).wait_recv()
            add_into(mine, lines(zb, deep).at[:, cut(k)])

        send(mine, g_spot(s, k), gx_s.at[k], gx_r.at[k], across).start()
        send(mine, g_spot(s, k), gc_s.at[0, k], gc_r.at[0, k], twin).start()
        pltpu.make_async_copy(mine, g_spot(s, k), loc.at[9 + k]).start()

    def spread(k):
        spot = g_spot(across[1], k)
        send(spot, spot, gx_s.at[k], gx_r.at[k], across).wait_recv()
        send(spot, spot, gc_s.at[1, k], gc_r.at[1, k], twin).start()

    half = gw.shape[0] // 2
    lump = half // LUMPS

    def w_rows(col, i):
        return gw.at[pl.ds(pl.multiple_of(col * half + i * lump, 16), lump)]

    def piece(ref, i):
        return ref.at[pl.ds(i * lump, lump)]

    def wy_send(i):
        return send(w_rows(1 - y, i), piece(ybw, i), wy_s.at[i], wy_r.at[i], side)

    def w_compute():
        tall = 2 * lump
        for n in range(LUMPS):
            col, i = (1 - y, n) if n < LUMPS // 2 else (y, n - LUMPS // 2)
            at = pl.ds(pl.multiple_of(col * half + i * tall, 16), tall)
            for j in range(0, model, 512):
                gw[at, j : j + 512] = mm(st_v[at, :], cw[:, j : j + 512]).astype(BF16)
            if n < LUMPS // 2:
                wy_send(2 * i).start()
                wy_send(2 * i + 1).start()

    def from_below(i):
        return send(w_rows(y, i), piece(zbw.at[0], i), wu_s.at[i], wz_r.at[0, i], up)

    def from_above(i):
        return send(w_rows(y, i), piece(zbw.at[1], i), wd_s.at[i], wz_r.at[1, i], down)

    def w_cast(i, who, ssem, rsem):
        return send(piece(wo_o, i), piece(wo_o, i), ssem.at[i], rsem.at[i], who)

    def w_root(i, who, ssem, rsem):
        return send(w_rows(y, i), piece(wo_o, i), ssem.at[i], rsem.at[i], who)

    def w_keep(i):
        return pltpu.make_async_copy(w_rows(y, i), piece(wo_o, i), loc.at[9 + PARTS + i])

    root = z == s

    def w_chain(i, h):
        last = h == deep - 1
        below = root & (z > 0) if last else (z < s) & (z == h) & (h > 0)
        above = root & (z < top) if last else (z > s) & (top - z == h) & (h > 0)

        @pl.when(root if last else ((z < s) & (z == h)) | ((z > s) & (top - z == h)))
        def _():
            wy_send(i).wait_recv()
            add_into(w_rows(y, i), piece(ybw, i))

        @pl.when(below)
        def _():
            from_below(i).wait_recv()
            add_into(w_rows(y, i), piece(zbw.at[0], i))

        @pl.when(above)
        def _():
            from_above(i).wait_recv()
            add_into(w_rows(y, i), piece(zbw.at[1], i))

        if last:

            @pl.when(root)
            def _():
                w_keep(i).start()
                w_root(i, across, bx_s, bx_r).start()
                w_root(i, twin, bc_s, bc_r).start()

        else:

            @pl.when((z < s) & (z == h))
            def _():
                from_below(i).start()

            @pl.when((z > s) & (top - z == h))
            def _():
                from_above(i).start()

    def w_spread(i):
        @pl.when(across[1] == z)
        def _():
            w_cast(i, across, bx_s, bx_r).wait_recv()
            w_cast(i, twin, bc_s, bc_r).start()

        @pl.when((across[1] != z) & jnp.logical_not(root))
        def _():
            w_cast(i, twin, bc_s, bc_r).wait_recv()

    def w_step(t):
        for h in range(deep):
            if 0 <= t - h < LUMPS:
                w_chain(t - h, h)

    loads["ch"].wait()
    loads["he"].wait()
    v_start()
    loads["st"].wait()
    loads["cot"].wait()
    w_compute()
    load_wi.start()
    loads["sc"].wait()
    loads["wo"].wait()
    exchange(0, 0)
    w_step(0)
    loads["nt"].wait()
    loads["pg"].wait()
    weigh(0)
    y_start(0)
    v_sum()
    w_step(1)
    exchange(0, 1)
    w_step(2)
    load_wi.wait()
    exchange(1, 0)
    w_step(3)
    v_total()
    weigh(1)
    y_start(1)
    w_step(4)
    exchange(1, 1)
    w_step(5)
    y_add(0)
    hop(0, 1)
    weigh(2)
    y_start(2)
    w_step(6)
    hop(0, 2)
    weigh(3)
    y_start(3)
    for k in range(4, PARTS):
        weigh(k)
        y_start(k)
    w_step(7)
    hop(0, 3)
    y_add(1)
    hop(1, 1)
    w_step(8)
    finish(0)
    hop(1, 2)
    hop(1, 3)
    y_add(2)
    hop(2, 1)
    finish(1)
    hop(2, 2)
    x_finish(0, out_o)
    y_add(3)
    hop(3, 1)
    hop(2, 3)
    y_add(4)
    hop(4, 1)
    hop(3, 2)
    finish(2)
    y_add(5)
    hop(5, 1)
    hop(3, 3)
    hop(4, 2)
    hop(5, 2)
    finish(3)
    hop(4, 3)
    hop(5, 3)
    finish(4)
    finish(5)
    x_finish(1, ng_o)
    v_spread()
    for i in range(LUMPS):
        w_spread(i)
    for n in (1, 2):
        v_seq(n, twin[1], twin).wait_recv()
    keep = pltpu.make_async_copy(vall, sm_o, out.at[0])
    keep.start()
    for k in range(PARTS):
        spread(k)
    for k in range(PARTS):
        for n in range(2):
            spot = g_spot(twin[1], k)
            send(spot, spot, gc_s.at[n, k], gc_r.at[n, k], twin).wait_recv()
        pltpu.make_async_copy(g_spot(s, k), g_spot(s, k), loc.at[9 + k]).wait()
    keep.wait()
    v_seq(0, s, across).wait_send()
    v_seq(1, s, twin).wait_send()
    v_seq(2, s, twin).wait_send()
    for n, dst in both:
        for q in range(2):
            x_send(n, q).wait_send()
            pltpu.make_async_copy(xr.at[n, q], dst.at[q], out.at[2 + 2 * n + q]).wait()
    for q in range(2):
        twin_send(1, 1, q).wait_send()
    for k in range(PARTS):
        for e in range(deep):
            y_send(k, e).wait_send()

            @pl.when(z < e)
            def _():
                z_send(k, e, e, su, up).wait_send()

            @pl.when(z > e)
            def _():
                z_send(k, e, e, sd, down).wait_send()

        spot = g_spot(s, k)
        send(spot, spot, gx_s.at[k], gx_r.at[k], across).wait_send()
        for n in range(2):
            send(spot, spot, gc_s.at[n, k], gc_r.at[n, k], twin).wait_send()
    for i in range(LUMPS):
        wy_send(i).wait_send()

        @pl.when(z < s)
        def _():
            from_below(i).wait_send()

        @pl.when(z > s)
        def _():
            from_above(i).wait_send()

        @pl.when(root)
        def _():
            w_keep(i).wait()
            w_root(i, across, bx_s, bx_r).wait_send()

        @pl.when(root | (across[1] == z))
        def _():
            w_cast(i, twin, bc_s, bc_r).wait_send()


def scatter(normed_t, pg, scaled_t, scaled, cot, wo, wi, chacc, hacc, length, shards, groups):
    model, count = normed_t.shape
    total = pg.shape[1]
    inner = scaled_t.shape[0]
    seqs = count // length
    part = length // groups
    deep = shards // 2
    rows = model // shards
    any_ = pl.BlockSpec(memory_space=pl.ANY)
    dma = pltpu.SemaphoreType.DMA
    v = pltpu.VMEM
    small = (8, chacc.shape[2])
    return pl.pallas_call(
        functools.partial(scatter_kernel, (deep, rows, part, length)),
        in_specs=[any_] * 9,
        out_specs=[any_] * 5,
        out_shape=[
            jax.ShapeDtypeStruct((groups, rows, total), BF16),
            jax.ShapeDtypeStruct((inner // 2, model), BF16),
            jax.ShapeDtypeStruct((seqs, part, model), BF16),
            jax.ShapeDtypeStruct((seqs, part, model), BF16),
            jax.ShapeDtypeStruct((groups, *small), F32),
        ],
        scratch_shapes=[
            v((model, count), BF16),
            v((count, total), BF16),
            v((inner, count), BF16),
            v((count, inner), BF16),
            v((inner, model), BF16),
            v((count, total), BF16),
            v((model, total), BF16),
            v((deep * rows, total), BF16),
            v(((deep + 1) * rows, total), BF16),
            v((2, 2, 2, part, model), BF16),
            v((2, 2, part, model), BF16),
            v((2, part, model), BF16),
            v((inner, model), BF16),
            v((inner // 2, model), BF16),
            v((2, inner // 2, model), BF16),
            v(chacc.shape, F32),
            v(hacc.shape, F32),
            v(small, F32),
            v((deep + 1, *small), F32),
            v((groups, *small), F32),
            dma((PARTS, deep)), dma((PARTS, deep)), dma((PARTS, deep)), dma((PARTS, deep)),
            dma((PARTS, deep + 1)),
            dma((PARTS,)), dma((PARTS,)), dma((2, PARTS)), dma((2, PARTS)),
            dma((2,)), dma((2, 2, 2)), dma((2, 2)), dma((2, 2)),
            dma((LUMPS,)), dma((LUMPS,)), dma((LUMPS,)), dma((LUMPS,)), dma((2, LUMPS)),
            dma((LUMPS,)), dma((LUMPS,)), dma((LUMPS,)), dma((LUMPS,)),
            dma((deep + 4,)), dma((deep + 4,)),
            dma((9 + PARTS + LUMPS,)), dma((6,)),
        ],
        compiler_params=pltpu.CompilerParams(
            collective_id=2, has_side_effects=True, vmem_limit_bytes=60 * 2**20
        ),
        name="weigh_scatter",
    )(normed_t, pg, scaled_t, scaled, cot, wo, wi, chacc, hacc)


def local(
    tokens,
    segment_ids,
    w_in,
    w_out,
    conv_weight,
    conv_bias,
    norm_gain,
    gated_gain,
    dt_bias,
    a_log,
    skip_weight,
    cotangent,
):
    groups = lax.axis_size("seq")
    shards = lax.axis_size("dp")
    place = lax.axis_index("seq")
    owner = lax.axis_index("dp")
    seqs, part, model = tokens.shape
    length = part * groups
    rows_in = w_in.shape[0]
    rows_out = w_out.shape[0]
    wide = rows_out * shards
    heads = dt_bias.shape[0]
    size = wide // heads
    mine = heads // groups
    inner = mine * size
    span = 2 * inner
    taps = conv_weight.shape[1]
    state2 = w_in.shape[1] - 2 * wide - heads
    channels = wide + state2
    share = channels // shards
    ratio = shards // groups
    small_slice = groups == 4 and shards == 8

    def own(a):
        return lax.dynamic_slice_in_dim(a, place * inner, inner, 0)

    def own_heads(a):
        return lax.dynamic_slice_in_dim(a, place * mine, mine, 0)

    head_rows = jnp.pad(jnp.stack([dt_bias, a_log]), ((0, 6), (0, 128 - heads)))
    marks, hp, sel, step_cols = prepare(segment_ids, head_rows, w_in, mine, 2 * wide + state2)
    flat = [norm_gain, conv_bias, gated_gain, conv_weight.reshape(-1)]
    small = jnp.concatenate(flat)
    tall = -(-small.shape[0] // 4096) * 4096
    small = jnp.pad(small, (0, tall - small.shape[0])).reshape(-1, 256)
    if small_slice:
        turned, cot, pj, sg, w_full, wo, small_all = gather(
            w_in, step_cols, w_out, small, tokens, cotangent, inner, shards, groups
        )
    else:
        small_all = lax.all_gather(small, "dp", axis=0, tiled=False)
    small_all = small_all.reshape(shards, -1).astype(F32)
    cut = [0]
    for a in flat:
        cut.append(cut[-1] + a.shape[0])
    norm_all, conv_b, gain_all, conv_w = (
        small_all[:, cut[i] : cut[i + 1]].reshape(-1) for i in range(4)
    )
    conv_w = conv_w.reshape(channels, taps)
    if not small_slice:
        floats = tokens.astype(F32)
        inverse = lax.rsqrt(jnp.mean(floats * floats, axis=-1, keepdims=True) + EPSILON)
        unit = floats * inverse
        w_mine = jnp.concatenate(
            [
                lax.dynamic_slice_in_dim(w_in, place * span, span, 1),
                w_in[:, 2 * wide : 2 * wide + state2],
                step_cols,
            ],
            axis=1,
        )
        normed = lax.all_gather((unit * norm_all).astype(BF16), "seq", axis=1, tiled=True)
        cot = lax.all_gather(cotangent, "seq", axis=1, tiled=True)
        w_full = lax.all_gather(w_mine, "dp", axis=0, tiled=True)
        held = jnp.where(
            (owner // ratio == place) & (jnp.arange(ratio)[:, None, None] == owner % ratio),
            w_out[None],
            jnp.zeros((), BF16),
        ).reshape(inner, model)
        wo = lax.psum(held, "dp")
        sg = jnp.einsum("std,cd->stc", cot, wo, preferred_element_type=F32).astype(BF16)
        pj = jnp.einsum("std,de->ste", normed, w_full, preferred_element_type=F32).astype(BF16)

    blank = jnp.zeros((state2,), F32)
    ch = jnp.concatenate(
        [
            jnp.concatenate([own(conv_w), conv_w[wide:]]).T,
            jnp.concatenate([own(conv_b), conv_b[wide:]])[None],
            jnp.concatenate([jnp.repeat(own_heads(skip_weight), size), blank])[None],
            jnp.concatenate([own(gain_all), blank])[None],
            jnp.zeros((1, inner + state2), F32),
        ]
    )
    pre, ys, st, red = mix_forward(pj, marks, sg, hp, ch)
    if small_slice:
        rk = norms(red, wide, groups)
    else:
        totals = lax.psum(red[:, :2], "seq")
        rho = lax.rsqrt(totals[:, 0] / wide + EPSILON)
        rk = jnp.stack([rho, rho**3 * totals[:, 1] / wide] + [jnp.zeros_like(rho)] * 6, axis=1)
    pg, chacc, hacc, scaled_t, scaled = mix_backward(
        pj, marks, rk, sg, pre, ys, st, hp, ch, sel
    )
    flat_pg = pg.reshape(seqs * length, -1)
    flat_cot = cot.reshape(seqs * length, -1)
    if small_slice:
        win_grad, wo_grad, out_sum, ngrad, sums = scatter(
            turned, flat_pg, scaled_t, scaled.reshape(seqs * length, -1), flat_cot, wo, w_full,
            chacc, hacc, length, shards, groups,
        )
    else:
        product = jnp.einsum("stc,cd->std", scaled, wo, preferred_element_type=F32).astype(BF16)
        out_sum = lax.psum_scatter(product, "seq", scatter_dimension=1, tiled=True)
        product = jnp.einsum("ste,de->std", pg, w_full, preferred_element_type=F32).astype(BF16)
        ngrad = lax.psum_scatter(product, "seq", scatter_dimension=1, tiled=True)
        win_grad = jnp.einsum("std,ste->de", normed, pg, preferred_element_type=F32)
        win_grad = lax.psum_scatter(win_grad.astype(BF16), "dp", scatter_dimension=0, tiled=True)
        win_grad = lax.all_gather(win_grad, "seq", axis=0, tiled=False)
        wo_grad = jnp.dot(scaled_t, flat_cot, preferred_element_type=F32)
        wo_grad = lax.psum(wo_grad.astype(BF16), "dp").reshape(ratio, rows_out, model)
        wo_grad = lax.dynamic_index_in_dim(wo_grad, owner % ratio, 0, False)
        wo_grad = lax.psum(
            jnp.where(owner // ratio == place, wo_grad, jnp.zeros((), BF16)), "seq"
        )
        sums = jnp.concatenate(
            [
                jnp.sum(chacc, axis=1),
                jnp.pad(jnp.sum(hacc, axis=1), ((0, 0), (0, inner + state2 - 128))),
            ]
        )
        sums = lax.all_gather(lax.psum(sums, "dp"), "seq", axis=0, tiled=False)
    flat = (seqs * part, model)
    rows = [norm_all[None], sums, norm_gain, gated_gain, a_log]
    outs = final(
        win_grad, w_in, wo_grad, w_out, out_sum.reshape(flat), ngrad.reshape(flat),
        tokens.reshape(flat), cotangent.reshape(flat), rows, span, mine, taps, share,
    )
    result, tokens_grad, w_in_grad, wo_grad, norm_grad, gain_grad, conv_grad, bias_grad = outs[:8]
    return (
        result.reshape(tokens.shape),
        tokens_grad.reshape(tokens.shape),
        w_in_grad,
        wo_grad,
        conv_grad,
        bias_grad,
        norm_grad,
        gain_grad,
        *outs[8:],
    )


def solution(mesh):
    return jax.shard_map(
        local,
        mesh=mesh,
        in_specs=(
            P("dp", "seq", None),
            P("dp", None),
            P("dp", None),
            P("dp", None),
            P("dp", None),
            P("dp"),
            P("dp"),
            P("dp"),
            P(),
            P(),
            P(),
            P("dp", "seq", None),
        ),
        out_specs=(
            P("dp", "seq", None),
            P("dp", "seq", None),
            P("dp", None),
            P("dp", None),
            P("dp", None),
            P("dp"),
            P("dp"),
            P("dp"),
            P(),
            P(),
            P(),
        ),
        check_vma=False,
    )
```
